32 devices in a mesh: dp: 4 (over z), ctx: 8 (over y, x, core).
Axes of the slice: x: 2, y: 2, z: 4, core: 2. Of those that a mesh axis runs over, the one named last changes fastest.
Arguments:
- inputs: bfloat16 [4, 2048, 2048], P('dp', 'ctx'), may hold values from -6 to 6
- places: int32 [4, 2048], P('dp', 'ctx'), may hold values from 0 to 2047, as said below
- cotangent: bfloat16 [4, 2048, 2048], P('dp', 'ctx'), may hold values from -6 to 6
- attn_gain: float32 [2048], replicated, may hold values from 0.5 to 1.5
- w_qkv: bfloat16 [2048, 1536], P(('dp', 'ctx')), may hold values from -0.125 to 0.125
- q_gain: float32 [64], replicated, may hold values from 0.1 to 1.9
- k_gain: float32 [64], replicated, may hold values from 0.1 to 1.9
- w_out: bfloat16 [1024, 2048], P(('dp', 'ctx')), may hold values from -6 to 6
- ffn_gain: float32 [2048], replicated, may hold values from 0.5 to 1.5
- w_gateup: bfloat16 [2048, 2048], P(('dp', 'ctx')), may hold values from -0.125 to 0.125
- w_down: bfloat16 [1024, 2048], P(('dp', 'ctx')), may hold values from -0.1875 to 0.1875
Outputs:
- layer_output: bfloat16 [4, 2048, 2048], P('dp', 'ctx')
- grad_inputs: bfloat16 [4, 2048, 2048], P('dp', 'ctx')
- grad_attn_gain: float32 [2048], replicated
- grad_w_qkv: float32 [2048, 1536], P(('dp', 'ctx'))
- grad_q_gain: float32 [64], replicated
- grad_k_gain: float32 [64], replicated
- grad_w_out: float32 [1024, 2048], P(('dp', 'ctx'))
- grad_ffn_gain: float32 [2048], replicated
- grad_w_gateup: float32 [2048, 2048], P(('dp', 'ctx'))
- grad_w_down: float32 [1024, 2048], P(('dp', 'ctx'))
The draws below stay inside these ranges and needn't reach their ends.
Inputs may be any that keep to these rules, and one draw needn't show every extreme that they name: Each row of places holds every position 0 to 2047 once. Cut a sequence into 16 blocks of 128 consecutive positions; each aligned block of 256 entries (one device's tokens) is a block b in increasing order followed by block 15 - b in increasing order.
All inputs are finite; a program needn't handle non-finite values.
Results may differ from the reference program's by a relative error of at most 0.02.
Values may be sent and summed in bfloat16 or wider, within the bound.
A program may use at most 128 MiB of HBM per device.

```python
import math
import jax
import jax.numpy as jnp
from jax import lax

D = 2048
HEADS = 16
GROUPS = 4
HEAD_DIM = 64
FF = 1024
SEQ_TOK = 256
LEN = 2048
NSEQ = 4
QKV = 1536


def draw_places(key, part):
    key = jax.random.fold_in(key, 11)
    blocks = LEN // SEQ_TOK
    half_tok = SEQ_TOK // 2

    def draw_row(seq_index):
        block_order = jax.random.permutation(jax.random.fold_in(key, seq_index), blocks).astype(jnp.int32)
        pair_blocks = jnp.stack([block_order, 2 * blocks - 1 - block_order], axis=1)
        offsets = jnp.arange(half_tok, dtype=jnp.int32)
        return (pair_blocks[:, :, None] * half_tok + offsets[None, None, :]).reshape(LEN).astype(jnp.int32)
    return jax.vmap(draw_row)(jnp.arange(NSEQ, dtype=jnp.int32))


def level_of(rng, extent, pieces, low, top_value):
    level, own = 1.0, jax.random.fold_in(rng, 6)
    for dim, parts in pieces:
        steps = jnp.exp(jax.random.uniform(jax.random.fold_in(own, dim), (parts,), jnp.float32, low / len(pieces), top_value / len(pieces)))
        level = level * jnp.repeat(steps, extent[dim] // parts).reshape([-1 if axis == dim else 1 for axis in range(len(extent))])
    return level


def centred(own_key, dims, spread, limit, split=(), kind=jnp.bfloat16):
    array = jax.random.normal(own_key, dims, jnp.float32) * spread
    if len(split) > 0:
        array = level_of(own_key, dims, split, -0.22, 0.18) * array
    return jnp.clip(array, min=-limit, max=limit).astype(kind)


def setup_inputs(seed: int = 0) -> dict:
    arg_keys = jax.random.split(jax.random.key(seed), 12)
    inputs = centred(arg_keys[0], (NSEQ, LEN, D), 1.0, 6.0, ((0, 4), (1, 8)))
    places = draw_places(jax.random.fold_in(arg_keys[11], 71), 0)
    cotangent = centred(arg_keys[2], (NSEQ, LEN, D), 1.0, 6.0, ((0, 4), (1, 8)))
    attn_gain = jnp.clip(1.0 + 0.1 * jax.random.normal(arg_keys[3], (D,), jnp.float32), 0.5, 1.5)
    w_qkv = centred(arg_keys[4], (D, QKV), D ** -0.5, 0.125, ((0, 32),))
    q_gain = jnp.clip(1.0 + 0.18 * jax.random.normal(arg_keys[5], (HEAD_DIM,), jnp.float32), 0.1, 1.9)
    k_gain = jnp.clip(1.0 + 0.18 * jax.random.normal(arg_keys[6], (HEAD_DIM,), jnp.float32), 0.1, 1.9)
    w_out = centred(arg_keys[7], (HEADS * HEAD_DIM, D), ((LEN // 5) ** 0.5 * (HEADS * HEAD_DIM) ** -0.5), 6.0, ((0, 32),))
    ffn_gain = jnp.clip(1.0 + 0.1 * jax.random.normal(arg_keys[8], (D,), jnp.float32), 0.5, 1.5)
    w_gateup = centred(arg_keys[9], (D, 2 * FF), D ** -0.5, 0.125, ((0, 32),))
    w_down = centred(arg_keys[10], (FF, D), FF ** -0.5, 0.1875, ((0, 32),))
    return dict(inputs=inputs, places=places, cotangent=cotangent, attn_gain=attn_gain, w_qkv=w_qkv, q_gain=q_gain, k_gain=k_gain, w_out=w_out, ffn_gain=ffn_gain, w_gateup=w_gateup, w_down=w_down)


@jax.custom_vjp
def low(v):
    return lax.optimization_barrier(v.astype(jnp.bfloat16)).astype(jnp.float32)

@jax.custom_vjp
def low_back(v):
    return v

def low_keep(v):
    return (low(v), None)

def low_pass(kept, grad):
    return (grad,)

def back_keep(v):
    return (v, None)

def back_low(kept, grad):
    return (low(grad),)
low.defvjp(low_keep, low_pass)
low_back.defvjp(back_keep, back_low)
epsilon = 1e-06
HIGHEST = lax.Precision.HIGHEST

def norm_rows(values, gain_vec):
    return values * lax.rsqrt(lax.optimization_barrier(jnp.mean(values * values, axis=-1, keepdims=True)) + epsilon) * gain_vec

def rotate(values, positions):
    half_dim = values.shape[-1] // 2
    frequency = jnp.exp(jnp.arange(half_dim).astype(jnp.float32) * (-2.0 * math.log(10000.0) / values.shape[-1]))
    angles = positions.astype(jnp.float32)[:, None] * frequency[None, :]
    cosine = jnp.cos(angles)[:, None, :]
    sine = jnp.sin(angles)[:, None, :]
    first = values[..., :half_dim]
    second = values[..., half_dim:]
    return jnp.concatenate([first * cosine - second * sine, second * cosine + first * sine], axis=-1)

def project_heads(qkv_all, positions, q_gain, k_gain):
    tok_rows = qkv_all.shape[0]
    q_cols = HEADS * HEAD_DIM
    k_cols = GROUPS * HEAD_DIM
    queries = qkv_all[:, :q_cols].reshape(tok_rows, HEADS, HEAD_DIM)
    keys_raw = qkv_all[:, q_cols:q_cols + k_cols].reshape(tok_rows, GROUPS, HEAD_DIM)
    values = qkv_all[:, q_cols + k_cols:].reshape(tok_rows, GROUPS, HEAD_DIM)
    return (rotate(norm_rows(queries, q_gain), positions), rotate(norm_rows(keys_raw, k_gain), positions), values)

def gated(gate_up):
    return jax.nn.silu(gate_up[:, :FF]) * gate_up[:, FF:]

def layer(weights, layer_in, positions):
    attn_gain, w_qkv, q_gain, k_gain, w_out, ffn_gain, w_gateup, w_down = weights
    length = layer_in.shape[0]
    repeat = HEADS // GROUPS
    score_scale = HEAD_DIM ** (-0.5)
    h_attn = low(norm_rows(layer_in, attn_gain))
    qkv_all = low_back(jnp.dot(h_attn, w_qkv, precision=HIGHEST))
    queries, keys_f, values = project_heads(qkv_all, positions, q_gain, k_gain)
    queries = low(queries).reshape(length, GROUPS, repeat, HEAD_DIM)
    keys_f = low(keys_f)
    values = low(values)
    q_block = math.gcd(length, 512)
    q_blocks = length // q_block

    def attend(entries):
        q_part, q_places = entries
        scores = low_back(jnp.einsum('igrd,jgd->grij', q_part, keys_f, precision=HIGHEST) * score_scale)
        allowed = positions[None, :] <= q_places[:, None]
        scores = jnp.where(allowed, scores, -1e+30)
        row_top = lax.optimization_barrier(jnp.max(scores, axis=-1, keepdims=True))
        expo = jnp.exp(scores - row_top)
        weights_p = low(expo / lax.optimization_barrier(jnp.sum(expo, axis=-1, keepdims=True)))
        return jnp.einsum('grij,jgd->igrd', weights_p, values, precision=HIGHEST)
    mixed = lax.map(jax.checkpoint(attend), (queries.reshape(q_blocks, q_block, GROUPS, repeat, HEAD_DIM), positions.reshape(q_blocks, q_block)))
    mixed = low(low_back(mixed.reshape(length, HEADS * HEAD_DIM)))
    attn_out = low_back(jnp.dot(mixed, w_out, precision=HIGHEST))
    residual = layer_in + attn_out
    h_ffn = low(norm_rows(residual, ffn_gain))
    gate_up = low_back(jnp.dot(h_ffn, w_gateup, precision=HIGHEST))
    act_vals = low(gated(gate_up))
    return residual + jnp.dot(act_vals, w_down, precision=HIGHEST)

def reference(inputs, places, cotangent, attn_gain, w_qkv, q_gain, k_gain, w_out, ffn_gain, w_gateup, w_down):
    params = jax.tree.map(lambda weight_arr: weight_arr.astype(jnp.float32), (attn_gain, w_qkv, q_gain, k_gain, w_out, ffn_gain, w_gateup, w_down))

    def per_sequence(grad_total, entries):
        seq_inputs, seq_places, seq_cot = entries

        def forward(weights, layer_in):
            return layer(weights, layer_in, seq_places)
        result, pull_back = jax.vjp(forward, params, seq_inputs.astype(jnp.float32))
        grad_params, grad_in = pull_back(seq_cot.astype(jnp.float32))
        grad_total = jax.tree.map(jnp.add, grad_total, grad_params)
        return (grad_total, (result.astype(jnp.bfloat16), grad_in.astype(jnp.bfloat16)))
    zeros_tree = jax.tree.map(jnp.zeros_like, params)
    grads, (outputs, grad_inputs) = lax.scan(per_sequence, zeros_tree, (inputs, places, cotangent))
    return (outputs, grad_inputs, grads[0], grads[1], grads[2], grads[3], grads[4], grads[5], grads[6], grads[7])
```

```python
import functools
import math

import jax
import jax.numpy as jnp
from jax import lax
from jax.experimental import pallas as pl
from jax.experimental.pallas import tpu as pltpu
from jax.sharding import PartitionSpec as P
MESH = pl.DeviceIdType.MESH
NZ = 4
ZT=[0,1,2,3]
PT=[1.5,2.5,4,5.5]
CT=[3.5,5.2,6.2,7.2]

class Place:
    def __init__(self):
        self.z = lax.axis_index("dp")
        c = lax.axis_index("ctx")
        self.core = c % 2
        self.x = (c // 2) % 2
        self.y = c // 4
    def at(self, z=None, y=None, x=None, core=None):
        z = self.z if z is None else z
        y = self.y if y is None else y
        x = self.x if x is None else x
        core = self.core if core is None else core
        return (z, y * 4 + x * 2 + core)
    def xn(self): return self.at(x=1 - self.x)
    def yn(self): return self.at(y=1 - self.y)
    def sn(self): return self.at(core=1 - self.core)
    def up(self): return self.at(z=self.z + 1)
    def down(self): return self.at(z=self.z - 1)

def barrier(pc):
    bar = pltpu.get_barrier_semaphore()
    sig = lambda d: pl.semaphore_signal(bar, inc=1, device_id=d, device_id_type=MESH)
    for d in (pc.xn(), pc.yn(), pc.sn()): sig(d)
    @pl.when(pc.z < NZ - 1)
    def _(): sig(pc.up())
    @pl.when(pc.z > 0)
    def _(): sig(pc.down())
    pl.semaphore_wait(bar, 3 + (1 - pc.z // (NZ - 1)) + (pc.z + NZ - 1) // NZ)

KZ, KX, KY, KD0, KD1, KS = range(6)
KU = 6

class Gather:
    def __init__(self, pc, buf, send, recv):
        self.pc, self.buf, self.send, self.recv = pc, buf, send, recv
        R = buf.shape[-2]
        self.h = (pl.ds(0, R // 2), pl.ds(R // 2, R // 2))
    def cp(self, idx, dev, ks, kr, slot):
        ref = self.buf.at[idx]
        return pltpu.make_async_remote_copy(src_ref=ref, dst_ref=ref, send_sem=self.send.at[ks, slot], recv_sem=self.recv.at[kr, slot], device_id=dev, device_id_type=MESH)
    def c_up(self, z0): p = self.pc; return self.cp((z0, p.y, p.x, p.core), p.up(), KU, KZ, z0)
    def c_down(self, z0): p = self.pc; return self.cp((z0, p.y, p.x, p.core), p.down(), KZ, KZ, z0)
    def c_x(self, z0): p = self.pc; return self.cp((z0, p.y, p.x, p.core), p.xn(), KX, KX, z0)
    def c_y(self, z0): p = self.pc; return self.cp((z0, p.y, p.x, p.core), p.yn(), KY, KY, z0)
    def c_d0(self, z0): p = self.pc; return self.cp((z0, p.y, 1 - p.x, p.core, self.h[0]), p.yn(), KD0, KD0, z0)
    def c_d1(self, z0): p = self.pc; return self.cp((z0, 1 - p.y, p.x, p.core, self.h[1]), p.xn(), KD1, KD1, z0)
    def c_s(self, z0): p = self.pc; return self.cp((z0, slice(None), slice(None), p.core), p.sn(), KS, KS, z0)
    def plane_send(self, z0):
        self.c_x(z0).start(); self.c_y(z0).start()
    def own(self):
        z = self.pc.z
        @pl.when(z < NZ - 1)
        def _(): self.c_up(z).start()
        @pl.when(z > 0)
        def _(): self.c_down(z).start()
        self.plane_send(z)
    def z_event(self, s, below):
        z = self.pc.z
        if below:
            z0 = z - s
            @pl.when(z0 >= 0)
            def _():
                self.c_up(z0).wait_recv()
                @pl.when(z < NZ - 1)
                def _(): self.c_up(z0).start()
                self.plane_send(z0)
        else:
            z0 = z + s
            @pl.when(z0 < NZ)
            def _():
                self.c_down(z0).wait_recv()
                @pl.when(z > 0)
                def _(): self.c_down(z0).start()
                self.plane_send(z0)
    def plane_event(self, z0):
        self.c_x(z0).wait_recv()
        self.c_d0(z0).start()
        self.c_y(z0).wait_recv()
        self.c_d1(z0).start()
    def core_event(self, z0):
        self.c_d0(z0).wait_recv()
        self.c_d1(z0).wait_recv()
        self.c_s(z0).start()
    def done_event(self, z0):
        self.c_s(z0).wait_recv()
    def finish(self):
        z = self.pc.z
        for z0 in range(NZ):
            for c in (self.c_x, self.c_y, self.c_d0, self.c_d1, self.c_s):
                c(z0).wait_send()
            @pl.when((z < NZ - 1) & (z0 <= z))
            def _(): self.c_up(z0).wait_send()
            @pl.when((z > 0) & (z0 >= z))
            def _(): self.c_down(z0).wait_send()


class GatherPlane:
    def __init__(self, pc, buf, send, recv):
        self.pc, self.buf, self.send, self.recv = pc, buf, send, recv
        R = buf.shape[-2]
        self.h = (pl.ds(0, R // 2), pl.ds(R // 2, R // 2))
    def cp(self, idx, dev, s, r):
        ref = self.buf.at[idx]
        return pltpu.make_async_remote_copy(src_ref=ref, dst_ref=ref, send_sem=self.send.at[s], recv_sem=self.recv.at[r], device_id=dev, device_id_type=MESH)
    def yx(self, k):
        p = self.pc
        return (p.y if k < 2 else 1 - p.y), (p.x if k % 2 == 0 else 1 - p.x)
    def kk(self, y, x): return y * 2 + x
    def c_x(self): p = self.pc; return self.cp((p.z, p.y, p.x, p.core), p.xn(), (KX, 0), (KX, 0))
    def c_y(self): p = self.pc; return self.cp((p.z, p.y, p.x, p.core), p.yn(), (KY, 0), (KY, 0))
    def c_d0(self): p = self.pc; return self.cp((p.z, p.y, 1 - p.x, p.core, self.h[0]), p.yn(), (KD0, 0), (KD0, 0))
    def c_d1(self): p = self.pc; return self.cp((p.z, 1 - p.y, p.x, p.core, self.h[1]), p.xn(), (KD1, 0), (KD1, 0))
    def c_up(self, z0, k): p = self.pc; y, x = self.yx(k); return self.cp((z0, y, x, p.core), p.up(), (KZ + 10 + z0, k), (KZ + 10 + z0, k))
    def c_down(self, z0, k): p = self.pc; y, x = self.yx(k); return self.cp((z0, y, x, p.core), p.down(), (14 + z0, k), (KZ + 10 + z0, k))
    def c_s(self, z0): p = self.pc; return self.cp((z0, slice(None), slice(None), p.core), p.sn(), (KS, z0), (KS, z0))
    def z_send(self, k):
        z = self.pc.z
        @pl.when(z < NZ - 1)
        def _(): self.c_up(z, k).start()
        @pl.when(z > 0)
        def _(): self.c_down(z, k).start()
    def own(self):
        self.c_x().start(); self.c_y().start()
        self.z_send(0)
    def plane_event(self):
        self.c_x().wait_recv(); self.c_d0().start()
        self.z_send(1)
        self.c_y().wait_recv(); self.c_d1().start()
        self.z_send(2)
    def diag_event(self):
        self.c_d0().wait_recv(); self.c_d1().wait_recv()
        self.z_send(3)
        self.c_s(self.pc.z).start()
    def z_event(self, s, k):
        z = self.pc.z
        @pl.when(z - s >= 0)
        def _():
            c = self.c_up(z - s, k); c.wait_recv()
            @pl.when(z < NZ - 1)
            def _(): c.start()
        @pl.when(z + s < NZ)
        def _():
            c = self.c_down(z + s, k); c.wait_recv()
            @pl.when(z > 0)
            def _(): c.start()
    def core_event(self, s):
        z = self.pc.z
        @pl.when(z - s >= 0)
        def _(): self.c_s(z - s).start()
        @pl.when(z + s < NZ)
        def _(): self.c_s(z + s).start()
    def done_event(self, z0):
        self.c_s(z0).wait_recv()
    def finish(self):
        z = self.pc.z
        for c in (self.c_x, self.c_y, self.c_d0, self.c_d1): c().wait_send()
        for z0 in range(NZ):
            self.c_s(z0).wait_send()
            for k in range(4):
                @pl.when((z < NZ - 1) & (z0 <= z))
                def _(): self.c_up(z0, k).wait_send()
                @pl.when((z > 0) & (z0 >= z))
                def _(): self.c_down(z0, k).wait_send()

def near(z, i):
    return None

def ag_kernel(n, W, plane_first, *refs):
    ins, outs = refs[:n], refs[n:2 * n]
    send, recv, lsem = refs[2 * n:]
    pc = Place()
    loc = [pltpu.make_async_copy(i, o.at[pc.z, pc.y, pc.x, pc.core], lsem.at[k]) for k, (i, o) in enumerate(zip(ins, outs))]
    for l in loc: l.start()
    barrier(pc)
    for l in loc: l.wait()
    z = pc.z
    ev = []
    gs = []
    def both(fn, s):
        if s == 0:
            fn(z)
        else:
            @pl.when(z - s >= 0)
            def _(): fn(z - s)
            @pl.when(z + s < NZ)
            def _(): fn(z + s)
    for k, o in enumerate(outs):
        T = W[k]
        if k in plane_first:
            g = GatherPlane(pc, o, send.at[k], recv.at[k]); gs.append(g)
            ev.append((T, g.own))
            ev.append((T + 1, g.plane_event)); ev.append((T + 2, g.diag_event))
            for s in range(1, NZ):
                for j in range(4):
                    ev.append((T + s * 2 + j * 0.5, functools.partial(g.z_event, s, j)))
                ev.append((T + s * 2 + 2.1, functools.partial(g.core_event, s)))
        else:
            g = Gather(pc, o, send.at[k], recv.at[k]); gs.append(g)
            ev.append((T, g.own))
            for s in range(1, NZ):
                ev.append((T + ZT[s], functools.partial(g.z_event, s, True)))
                ev.append((T + ZT[s], functools.partial(g.z_event, s, False)))
            for s in range(NZ):
                ev.append((T + PT[s], functools.partial(both, g.plane_event, s)))
                ev.append((T + CT[s], functools.partial(both, g.core_event, s)))
    ev.sort(key=lambda e: e[0])
    for _, e in ev: e()
    for g in gs:
        for z0 in range(NZ): g.done_event(z0)
    for g in gs: g.finish()

def gather_all(shards, W=(0,0,0,0), plane_first=()):
    n = len(shards)
    outs = [jax.ShapeDtypeStruct((NZ, 2, 2, 2) + s.shape, s.dtype) for s in shards]
    res = pl.pallas_call(functools.partial(ag_kernel, n, W, plane_first), out_shape=outs,
        in_specs=[pl.BlockSpec(memory_space=pl.ANY)] * n, out_specs=[pl.BlockSpec(memory_space=pl.ANY)] * n,
        scratch_shapes=[pltpu.SemaphoreType.DMA((n, 18, NZ)), pltpu.SemaphoreType.DMA((n, 14, NZ)), pltpu.SemaphoreType.DMA((n,))],
        compiler_params=pltpu.CompilerParams(collective_id=0, has_side_effects=True), name="gather_weights")(*shards)
    return res

f32 = jnp.float32
bf16 = jnp.bfloat16

def far(z, i):
    m = z // 2
    zz = z + m * (3 - 2 * z)
    lo = 3 - i if i < 2 else (1 - zz if i == 2 else zz)
    return lo + m * (3 - 2 * lo)

SD0, SD1, SX0, SX1, SY0, SY1, SA, SB = range(8)

class Scatter:
    def __init__(self, pc, part, bufs, out, send, recv):
        self.pc, self.part, self.out, self.send, self.recv = pc, part, out, send, recv
        self.rd, self.rx, self.ry, self.za, self.zb, self.sm = bufs
        R = part.shape[-2]
        self.R = R
        self.h = (pl.ds(0, R // 2), pl.ds(R // 2, R // 2))
    def cp(self, src, dst, dev, k, zp):
        return pltpu.make_async_remote_copy(src_ref=src, dst_ref=dst, send_sem=self.send.at[k, zp], recv_sem=self.recv.at[k, zp], device_id=dev, device_id_type=MESH)
    def d0(self, zp): p = self.pc; return self.cp(self.part.at[zp, 1 - p.y, 1 - p.x, self.h[0]], self.rd.at[zp, 0], p.yn(), SD0, zp)
    def d1(self, zp): p = self.pc; return self.cp(self.part.at[zp, 1 - p.y, 1 - p.x, self.h[1]], self.rd.at[zp, 1], p.xn(), SD1, zp)
    def x1(self, zp): p = self.pc; return self.cp(self.part.at[zp, p.y, 1 - p.x, self.h[1]], self.rx.at[zp, 1], p.xn(), SX1, zp)
    def y0(self, zp): p = self.pc; return self.cp(self.part.at[zp, 1 - p.y, p.x, self.h[0]], self.ry.at[zp, 0], p.yn(), SY0, zp)
    def x0(self, zp): p = self.pc; return self.cp(self.rd.at[zp, 0], self.rx.at[zp, 0], p.xn(), SX0, zp)
    def y1(self, zp): p = self.pc; return self.cp(self.rd.at[zp, 1], self.ry.at[zp, 1], p.yn(), SY1, zp)
    def down(self, zp): p = self.pc; return self.cp(self.sm.at[zp], self.za.at[zp], p.down(), SA, zp)
    def up(self, zp): p = self.pc; return self.cp(self.sm.at[zp], self.zb.at[zp], p.up(), SB, zp)
    def first(self, i):
        zp = far(self.pc.z, i)
        for c in (self.d0, self.d1, self.x1, self.y0): c(zp).start()
    def d_event(self, i):
        p = self.pc; zp = far(p.z, i)
        self.d0(zp).wait_recv()
        self.rd[zp, 0] = self.rd[zp, 0] + self.part[zp, p.y, 1 - p.x, self.h[0]]
        self.x0(zp).start()
        self.d1(zp).wait_recv()
        self.rd[zp, 1] = self.rd[zp, 1] + self.part[zp, 1 - p.y, p.x, self.h[1]]
        self.y1(zp).start()
    def xy_event(self, i):
        p = self.pc; zp = far(p.z, i)
        for c in (self.x1, self.y0, self.x0, self.y1): c(zp).wait_recv()
        for k in range(2):
            self.sm[zp, self.h[k]] = (self.part[zp, p.y, p.x, self.h[k]].astype(f32) + self.rx[zp, k].astype(f32) + self.ry[zp, k].astype(f32)).astype(bf16)
    def z_event(self, i):
        z = self.pc.z; zp = far(z, i)
        @pl.when(zp < z)
        def _():
            @pl.when(z < NZ - 1)
            def _():
                self.down(zp).wait_recv()
                self.sm[zp] = self.sm[zp] + self.za[zp]
            self.down(zp).start()
        @pl.when(zp > z)
        def _():
            @pl.when(z > 0)
            def _():
                self.up(zp).wait_recv()
                self.sm[zp] = self.sm[zp] + self.zb[zp]
            self.up(zp).start()
    def final(self):
        p = self.pc; z = p.z
        for c in (self.x1, self.y0, self.x0, self.y1): c(z).wait_recv()
        for k in range(2):
            self.out[self.h[k], :] = self.part[z, p.y, p.x, self.h[k]].astype(f32) + self.rx[z, k].astype(f32) + self.ry[z, k].astype(f32)
        @pl.when(z < NZ - 1)
        def _():
            self.down(z).wait_recv()
            self.out[...] += self.za[z].astype(f32)
        @pl.when(z > 0)
        def _():
            self.up(z).wait_recv()
            self.out[...] += self.zb[z].astype(f32)
    def finish(self):
        z = self.pc.z
        for zp in range(NZ):
            for c in (self.d0, self.d1, self.x1, self.y0, self.x0, self.y1): c(zp).wait_send()
            @pl.when(zp < z)
            def _(): self.down(zp).wait_send()
            @pl.when(zp > z)
            def _(): self.up(zp).wait_send()
    @staticmethod
    def scratch(R, C):
        v = pltpu.VMEM
        return [v((NZ, 2, R // 2, C), bf16), v((NZ, 2, R // 2, C), bf16), v((NZ, 2, R // 2, C), bf16), v((NZ, R, C), bf16), v((NZ, R, C), bf16), v((NZ, R, C), bf16)]

class ScatterZ:
    def __init__(self, pc, part, bufs, out, send, recv):
        self.pc, self.part, self.out, self.send, self.recv = pc, part, out, send, recv
        self.rd, self.rx, self.ry, self.za, self.zb, self.sm = bufs
        R = part.shape[-2]
        self.h = (pl.ds(0, R // 2), pl.ds(R // 2, R // 2))
    def cp(self, src, dst, dev, k, s):
        return pltpu.make_async_remote_copy(src_ref=src, dst_ref=dst, send_sem=self.send.at[k, s], recv_sem=self.recv.at[k, s], device_id=dev, device_id_type=MESH)
    def yx(self, k): return k // 2, k % 2
    def down(self, zp, k, src): return self.cp(src, self.za.at[zp, k], self.pc.down(), 8 + zp, k)
    def up(self, zp, k, src): return self.cp(src, self.zb.at[zp, k], self.pc.up(), 12 + zp, k)
    def first(self, i):
        z = self.pc.z; zp = far(z, i)
        for k in range(4):
            y, x = self.yx(k)
            @pl.when((z == NZ - 1) & (zp < z))
            def _(): self.down(zp, k, self.part.at[zp, y, x]).start()
            @pl.when((z == 0) & (zp > z))
            def _(): self.up(zp, k, self.part.at[zp, y, x]).start()
    def z_event(self, i, k):
        z = self.pc.z; zp = far(z, i); y, x = self.yx(k)
        @pl.when((zp < z) & (z < NZ - 1))
        def _():
            self.down(zp, k, self.za.at[zp, k]).wait_recv()
            self.za[zp, k] = self.za[zp, k] + self.part[zp, y, x]
            self.down(zp, k, self.za.at[zp, k]).start()
        @pl.when((zp > z) & (z > 0))
        def _():
            self.up(zp, k, self.zb.at[zp, k]).wait_recv()
            self.zb[zp, k] = self.zb[zp, k] + self.part[zp, y, x]
            self.up(zp, k, self.zb.at[zp, k]).start()
    def own_event(self, k):
        z = self.pc.z; y, x = self.yx(k)
        @pl.when(z < NZ - 1)
        def _(): self.down(z, k, self.za.at[z, k]).wait_recv()
        @pl.when(z > 0)
        def _(): self.up(z, k, self.zb.at[z, k]).wait_recv()
        @pl.when(z == 0)
        def _(): self.sm[k] = self.part[z, y, x] + self.za[z, k]
        @pl.when(z == NZ - 1)
        def _(): self.sm[k] = self.part[z, y, x] + self.zb[z, k]
        @pl.when((z > 0) & (z < NZ - 1))
        def _(): self.sm[k] = (self.part[z, y, x].astype(f32) + self.za[z, k].astype(f32) + self.zb[z, k].astype(f32)).astype(bf16)
    def kk(self, y, x): return y * 2 + x
    def d0(self): p = self.pc; return self.cp(self.sm.at[self.kk(1 - p.y, 1 - p.x), self.h[0]], self.rd.at[0, 0], p.yn(), SD0, 0)
    def d1(self): p = self.pc; return self.cp(self.sm.at[self.kk(1 - p.y, 1 - p.x), self.h[1]], self.rd.at[0, 1], p.xn(), SD1, 0)
    def x1(self): p = self.pc; return self.cp(self.sm.at[self.kk(p.y, 1 - p.x), self.h[1]], self.rx.at[0, 1], p.xn(), SX1, 0)
    def y0(self): p = self.pc; return self.cp(self.sm.at[self.kk(1 - p.y, p.x), self.h[0]], self.ry.at[0, 0], p.yn(), SY0, 0)
    def x0(self): p = self.pc; return self.cp(self.rd.at[0, 0], self.rx.at[0, 0], p.xn(), SX0, 0)
    def y1(self): p = self.pc; return self.cp(self.rd.at[0, 1], self.ry.at[0, 1], p.yn(), SY1, 0)
    def plane_send(self):
        for c in (self.d0, self.d1, self.x1, self.y0): c().start()
    def plane_event(self):
        p = self.pc
        self.d0().wait_recv()
        self.rd[0, 0] = self.rd[0, 0] + self.sm[self.kk(p.y, 1 - p.x), self.h[0]]
        self.x0().start()
        self.d1().wait_recv()
        self.rd[0, 1] = self.rd[0, 1] + self.sm[self.kk(1 - p.y, p.x), self.h[1]]
        self.y1().start()
    def final(self):
        p = self.pc
        for c in (self.x1, self.y0, self.x0, self.y1): c().wait_recv()
        for k in range(2):
            self.out[self.h[k], :] = self.sm[self.kk(p.y, p.x), self.h[k]].astype(f32) + self.rx[0, k].astype(f32) + self.ry[0, k].astype(f32)
    def finish(self):
        z = self.pc.z
        for c in (self.d0, self.d1, self.x1, self.y0, self.x0, self.y1): c().wait_send()
        for zp in range(NZ):
            for k in range(4):
                @pl.when(zp < z)
                def _(): self.down(zp, k, self.za.at[zp, k]).wait_send()
                @pl.when(zp > z)
                def _(): self.up(zp, k, self.zb.at[zp, k]).wait_send()
    @staticmethod
    def scratch(R, C):
        v = pltpu.VMEM
        return [v((1, 2, R // 2, C), bf16), v((1, 2, R // 2, C), bf16), v((1, 2, R // 2, C), bf16), v((NZ, 4, R, C), bf16), v((NZ, 4, R, C), bf16), v((4, R, C), bf16)]

FT=[0,0,0,0]; DT=[1,2,3,4]; XT=[2.2,3.2,4.2,5.2]; RZT=[2.5,3.5,4.5]; FINAL=6
def rs_kernel(n, W, zfirst, *refs):
    ins, outs = refs[:n], refs[n:2 * n]
    send, recv = refs[2 * n:2 * n + 2]
    bufs = refs[2 * n + 2:]
    pc = Place()
    barrier(pc)
    ev = []; gs = []
    P_ = functools.partial
    for k in range(n):
        b = bufs[6 * k:6 * k + 6]; T = W[k]
        cls = ScatterZ if k in zfirst else Scatter
        g = cls(pc, ins[k], b, outs[k], send.at[k], recv.at[k]); gs.append(g)
        if k in zfirst:
            for i in range(3):
                ev.append((T, P_(g.first, i)))
                for j in range(4): ev.append((T + 0.5 + i + j * .25, P_(g.z_event, i, j)))
            for j in range(4): ev.append((T + 4 + j * .01, P_(g.own_event, j)))
            ev.append((T + 4.1, g.plane_send)); ev.append((T + 5, g.plane_event)); ev.append((T + 6.5, g.final))
        else:
            for i in range(4):
                ev.append((T + FT[i], P_(g.first, i)))
                ev.append((T + DT[i], P_(g.d_event, i)))
                if i < 3:
                    ev.append((T + XT[i], P_(g.xy_event, i)))
                    ev.append((T + RZT[i], P_(g.z_event, i)))
            ev.append((T + FINAL, g.final))
    ev.sort(key=lambda e: e[0])
    for _, e in ev: e()
    for g in gs: g.finish()

def scatter_all(parts, W=(0, 0, 0, 0), zfirst=()):
    n = len(parts)
    outs = [jax.ShapeDtypeStruct(s.shape[-2:], f32) for s in parts]
    scr = []
    for k, s in enumerate(parts):
        scr += (ScatterZ if k in zfirst else Scatter).scratch(*s.shape[-2:])
    V = pl.BlockSpec(memory_space=pltpu.VMEM)
    return pl.pallas_call(functools.partial(rs_kernel, n, W, zfirst), out_shape=outs,
        in_specs=[V] * n, out_specs=[V] * n,
        scratch_shapes=[pltpu.SemaphoreType.DMA((n, 16, NZ)), pltpu.SemaphoreType.DMA((n, 16, NZ))] + scr,
        compiler_params=pltpu.CompilerParams(collective_id=1, has_side_effects=True, vmem_limit_bytes=60 << 20), name="scatter_grads")(*parts)


HEADS = 16
GROUPS = 4
HEAD_DIM = 64
FF = 1024


epsilon = 1e-06


def norm_rows(values, gain_vec):
    return (
        values * lax.rsqrt(jnp.mean(values * values, axis=-1, keepdims=True) + epsilon) * gain_vec
    )


def rotate(values, positions):
    half_dim = values.shape[-1] // 2
    frequency = jnp.exp(
        jnp.arange(half_dim).astype(jnp.float32) * (-2.0 * math.log(10000.0) / values.shape[-1])
    )
    angles = positions.astype(jnp.float32)[:, None] * frequency[None, :]
    cosine = jnp.cos(angles)[:, None, :]
    sine = jnp.sin(angles)[:, None, :]
    first = values[..., :half_dim]
    second = values[..., half_dim:]
    return jnp.concatenate(
        [first * cosine - second * sine, second * cosine + first * sine], axis=-1
    )


def project_heads(qkv_all, positions, q_gain, k_gain):
    tok_rows = qkv_all.shape[0]
    q_cols = HEADS * HEAD_DIM
    k_cols = GROUPS * HEAD_DIM
    queries = qkv_all[:, :q_cols].reshape(tok_rows, HEADS, HEAD_DIM)
    keys_raw = qkv_all[:, q_cols : q_cols + k_cols].reshape(tok_rows, GROUPS, HEAD_DIM)
    values = qkv_all[:, q_cols + k_cols :].reshape(tok_rows, GROUPS, HEAD_DIM)
    return (
        rotate(norm_rows(queries, q_gain), positions),
        rotate(norm_rows(keys_raw, k_gain), positions),
        values,
    )


def gated(gate_up):
    return jax.nn.silu(gate_up[:, :FF]) * gate_up[:, FF:]


def per_device_plain(
    inputs, places, cotangent, attn_gain, w_qkv, q_gain, k_gain, w_out, ffn_gain, w_gateup, w_down
):
    tok_rows = inputs.shape[1]
    repeat = HEADS // GROUPS
    score_scale = HEAD_DIM ** (-0.5)
    here_f = inputs[0].astype(jnp.float32)
    own_places = places[0]
    qkv_w, out_w = (
        lax.all_gather(w_qkv, ("dp", "ctx"), axis=0, tiled=True),
        lax.all_gather(w_out, ("dp", "ctx"), axis=0, tiled=True),
    )
    h_attn_f, pull_attn = jax.vjp(norm_rows, here_f, attn_gain)
    h_attn = h_attn_f.astype(jnp.bfloat16)
    qkv_all = jnp.dot(h_attn, qkv_w, preferred_element_type=jnp.float32)

    def heads_of(qkv_in, gain_q, gain_k):
        return project_heads(qkv_in, own_places, gain_q, gain_k)

    (queries, keys_f, values), pull_heads = jax.vjp(heads_of, qkv_all, q_gain, k_gain)
    query_b = queries.astype(jnp.bfloat16).reshape(tok_rows, GROUPS, repeat, HEAD_DIM)
    key_b = keys_f.astype(jnp.bfloat16)
    value_b = values.astype(jnp.bfloat16)
    all_keys, all_values = (
        lax.all_gather(key_b, "ctx", axis=0, tiled=True),
        lax.all_gather(value_b, "ctx", axis=0, tiled=True),
    )
    all_places = lax.all_gather(own_places, "ctx", axis=0, tiled=True)
    blocks = lax.axis_size("ctx")
    key_blocks = all_keys.reshape(blocks, tok_rows, GROUPS, HEAD_DIM)
    value_blocks = all_values.reshape(blocks, tok_rows, GROUPS, HEAD_DIM)
    place_blocks = all_places.reshape(blocks, tok_rows)

    def score_block(key_blk, place_blk):
        scores = (
            jnp.einsum("igrd,jgd->grij", query_b, key_blk, preferred_element_type=jnp.float32)
            * score_scale
        )
        allowed = place_blk[None, :] <= own_places[:, None]
        return (scores, allowed)

    def max_step(state_pair, entries):
        row_top, row_total = state_pair
        scores, allowed = score_block(entries[0], entries[1])
        scores = jnp.where(allowed, scores, -1e30)
        new_top = jnp.maximum(row_top, jnp.max(scores, axis=-1))
        row_total = row_total * jnp.exp(row_top - new_top) + jnp.sum(
            jnp.where(allowed, jnp.exp(scores - new_top[..., None]), 0.0), axis=-1
        )
        return ((new_top, row_total), None)

    start_pair = (
        jnp.full((GROUPS, repeat, tok_rows), -1e30, jnp.float32),
        jnp.zeros((GROUPS, repeat, tok_rows), jnp.float32),
    )
    (row_top, row_total), _ = lax.scan(max_step, start_pair, (key_blocks, place_blocks))
    log_total = row_top + jnp.log(row_total)

    def out_step(accum, entries):
        scores, allowed = score_block(entries[0], entries[1])
        weights_b = jnp.where(allowed, jnp.exp(scores - log_total[..., None]), 0.0).astype(
            jnp.bfloat16
        )
        return (
            accum
            + jnp.einsum(
                "grij,jgd->igrd", weights_b, entries[2], preferred_element_type=jnp.float32
            ),
            None,
        )

    mixed_f, _ = lax.scan(
        out_step,
        jnp.zeros((tok_rows, GROUPS, repeat, HEAD_DIM), jnp.float32),
        (key_blocks, place_blocks, value_blocks),
    )
    mixed_b = mixed_f.reshape(tok_rows, HEADS * HEAD_DIM).astype(jnp.bfloat16)
    attn_out = jnp.dot(mixed_b, out_w, preferred_element_type=jnp.float32)
    residual = here_f + attn_out
    gateup_w, down_w = (
        lax.all_gather(w_gateup, ("dp", "ctx"), axis=0, tiled=True),
        lax.all_gather(w_down, ("dp", "ctx"), axis=0, tiled=True),
    )
    h_ffn_f, pull_ffn = jax.vjp(norm_rows, residual, ffn_gain)
    h_ffn = h_ffn_f.astype(jnp.bfloat16)
    gate_up = jnp.dot(h_ffn, gateup_w, preferred_element_type=jnp.float32)
    act_f, pull_gate = jax.vjp(gated, gate_up)
    act_b = act_f.astype(jnp.bfloat16)
    result = residual + jnp.dot(act_b, down_w, preferred_element_type=jnp.float32)
    layer_output = result.astype(jnp.bfloat16)[None]
    gateup_w, down_w = (
        lax.all_gather(w_gateup, ("dp", "ctx"), axis=0, tiled=True),
        lax.all_gather(w_down, ("dp", "ctx"), axis=0, tiled=True),
    )
    grad_out = cotangent[0]
    grad_act = jnp.dot(grad_out, down_w.T, preferred_element_type=jnp.float32)
    grad_down = jnp.dot(act_b.T, grad_out, preferred_element_type=jnp.float32)
    grad_gu_b = pull_gate(grad_act)[0].astype(jnp.bfloat16)
    grad_gateup = jnp.dot(h_ffn.T, grad_gu_b, preferred_element_type=jnp.float32)
    grad_h_ffn = jnp.dot(grad_gu_b, gateup_w.T, preferred_element_type=jnp.float32)
    grad_resid_part, grad_ffn_gain = pull_ffn(grad_h_ffn)
    grad_residual = grad_out.astype(jnp.float32) + grad_resid_part
    grad_gateup_own, grad_down_own = (
        lax.psum_scatter(grad_gateup, ("dp", "ctx"), scatter_dimension=0, tiled=True),
        lax.psum_scatter(grad_down, ("dp", "ctx"), scatter_dimension=0, tiled=True),
    )
    qkv_w, out_w = (
        lax.all_gather(w_qkv, ("dp", "ctx"), axis=0, tiled=True),
        lax.all_gather(w_out, ("dp", "ctx"), axis=0, tiled=True),
    )
    grad_attn_b = grad_residual.astype(jnp.bfloat16)
    grad_out_w = jnp.dot(mixed_b.T, grad_attn_b, preferred_element_type=jnp.float32)
    grad_mixed_b = (
        jnp.dot(grad_attn_b, out_w.T, preferred_element_type=jnp.float32)
        .astype(jnp.bfloat16)
        .reshape(tok_rows, GROUPS, repeat, HEAD_DIM)
    )
    row_delta = jnp.transpose(
        jnp.sum(grad_mixed_b.astype(jnp.float32) * mixed_f, axis=-1), (1, 2, 0)
    )

    def back_step(grad_query, entries):
        key_blk, place_blk, value_blk = entries
        scores, allowed = score_block(key_blk, place_blk)
        weights_f = jnp.where(allowed, jnp.exp(scores - log_total[..., None]), 0.0)
        weights_b = weights_f.astype(jnp.bfloat16)
        grad_value = jnp.einsum(
            "grij,igrd->jgd", weights_b, grad_mixed_b, preferred_element_type=jnp.float32
        )
        grad_prob = jnp.einsum(
            "igrd,jgd->grij", grad_mixed_b, value_blk, preferred_element_type=jnp.float32
        )
        grad_score = (weights_f * (grad_prob - row_delta[..., None])).astype(jnp.bfloat16)
        grad_query = grad_query + jnp.einsum(
            "grij,jgd->igrd", grad_score, key_blk, preferred_element_type=jnp.float32
        )
        grad_key = (
            jnp.einsum("grij,igrd->jgd", grad_score, query_b, preferred_element_type=jnp.float32)
            * score_scale
        )
        return (
            grad_query,
            jnp.concatenate(
                [
                    grad_key.reshape(tok_rows, GROUPS * HEAD_DIM),
                    grad_value.reshape(tok_rows, GROUPS * HEAD_DIM),
                ],
                axis=1,
            ),
        )

    grad_query, kv_terms = lax.scan(
        back_step,
        jnp.zeros((tok_rows, GROUPS, repeat, HEAD_DIM), jnp.float32),
        (key_blocks, place_blocks, value_blocks),
    )
    grad_query = grad_query * score_scale
    kv_own = lax.psum_scatter(
        kv_terms.reshape(blocks * tok_rows, 2 * GROUPS * HEAD_DIM).astype(jnp.bfloat16),
        "ctx",
        scatter_dimension=0,
        tiled=True,
    ).astype(jnp.float32)
    grad_key_own = kv_own[:, : GROUPS * HEAD_DIM].reshape(tok_rows, GROUPS, HEAD_DIM)
    grad_value_own = kv_own[:, GROUPS * HEAD_DIM :].reshape(tok_rows, GROUPS, HEAD_DIM)
    grad_qkv_f, grad_q_gain, grad_k_gain = pull_heads(
        (grad_query.reshape(tok_rows, HEADS, HEAD_DIM), grad_key_own, grad_value_own)
    )
    grad_qkv_b = grad_qkv_f.astype(jnp.bfloat16)
    grad_qkv_w = jnp.dot(h_attn.T, grad_qkv_b, preferred_element_type=jnp.float32)
    grad_h_attn = jnp.dot(grad_qkv_b, qkv_w.T, preferred_element_type=jnp.float32)
    grad_here_part, grad_attn_gain = pull_attn(grad_h_attn)
    grad_inputs = (grad_residual + grad_here_part).astype(jnp.bfloat16)[None]
    grad_qkv_own, grad_out_own = (
        lax.psum_scatter(grad_qkv_w, ("dp", "ctx"), scatter_dimension=0, tiled=True),
        lax.psum_scatter(grad_out_w, ("dp", "ctx"), scatter_dimension=0, tiled=True),
    )
    gain_attn, gain_query, gain_key, gain_ffn = lax.psum(
        (grad_attn_gain, grad_q_gain, grad_k_gain, grad_ffn_gain), ("dp", "ctx")
    )
    return (
        layer_output,
        grad_inputs,
        gain_attn,
        grad_qkv_own,
        gain_query,
        gain_key,
        grad_out_own,
        gain_ffn,
        grad_gateup_own,
        grad_down_own,
    )


def per_device_fast(
    inputs, places, cotangent, attn_gain, w_qkv, q_gain, k_gain, w_out, ffn_gain, w_gateup, w_down
):
    tok_rows = inputs.shape[1]
    repeat = HEADS // GROUPS
    score_scale = HEAD_DIM ** (-0.5)
    here_f = inputs[0].astype(jnp.float32)
    own_places = places[0]
    qkv_w, out_w, gateup_w, down_w = [
        w.reshape(-1, w.shape[-1])
        for w in gather_all((w_qkv, w_out, w_gateup, w_down), plane_first=(1,))
    ]
    core = lax.axis_index("ctx") % 2

    def both(array):
        other = lax.ppermute(array, "ctx", [(i, i ^ 1) for i in range(lax.axis_size("ctx"))])
        return jnp.concatenate([array, other], axis=0)

    def grad_half(left, right, rows):
        left = both(left).reshape(2 * tok_rows, -1, 2, rows)
        left = lax.dynamic_index_in_dim(left, core, 2, keepdims=False).reshape(2 * tok_rows, -1)
        grad = jnp.dot(left.T, both(right), preferred_element_type=jnp.float32)
        return grad.astype(jnp.bfloat16).reshape(NZ, 2, 2, rows, right.shape[-1])

    h_attn_f, pull_attn = jax.vjp(norm_rows, here_f, attn_gain)
    h_attn = h_attn_f.astype(jnp.bfloat16)
    qkv_all = jnp.dot(h_attn, qkv_w, preferred_element_type=jnp.float32)

    def heads_of(qkv_in, gain_q, gain_k):
        return project_heads(qkv_in, own_places, gain_q, gain_k)

    (queries, keys_f, values), pull_heads = jax.vjp(heads_of, qkv_all, q_gain, k_gain)
    query_b = queries.astype(jnp.bfloat16).reshape(tok_rows, GROUPS, repeat, HEAD_DIM)
    key_b = keys_f.astype(jnp.bfloat16)
    value_b = values.astype(jnp.bfloat16)
    all_keys, all_values = (
        lax.all_gather(key_b, "ctx", axis=0, tiled=True),
        lax.all_gather(value_b, "ctx", axis=0, tiled=True),
    )
    all_places = lax.all_gather(own_places, "ctx", axis=0, tiled=True)
    blocks = lax.axis_size("ctx")
    key_blocks = all_keys.reshape(blocks, tok_rows, GROUPS, HEAD_DIM)
    value_blocks = all_values.reshape(blocks, tok_rows, GROUPS, HEAD_DIM)
    place_blocks = all_places.reshape(blocks, tok_rows)

    def score_block(key_blk, place_blk):
        scores = (
            jnp.einsum("igrd,jgd->grij", query_b, key_blk, preferred_element_type=jnp.float32)
            * score_scale
        )
        allowed = place_blk[None, :] <= own_places[:, None]
        return (scores, allowed)

    def max_step(state_pair, entries):
        row_top, row_total = state_pair
        scores, allowed = score_block(entries[0], entries[1])
        scores = jnp.where(allowed, scores, -1e30)
        new_top = jnp.maximum(row_top, jnp.max(scores, axis=-1))
        row_total = row_total * jnp.exp(row_top - new_top) + jnp.sum(
            jnp.where(allowed, jnp.exp(scores - new_top[..., None]), 0.0), axis=-1
        )
        return ((new_top, row_total), None)

    start_pair = (
        jnp.full((GROUPS, repeat, tok_rows), -1e30, jnp.float32),
        jnp.zeros((GROUPS, repeat, tok_rows), jnp.float32),
    )
    (row_top, row_total), _ = lax.scan(max_step, start_pair, (key_blocks, place_blocks))
    log_total = row_top + jnp.log(row_total)

    def out_step(accum, entries):
        scores, allowed = score_block(entries[0], entries[1])
        weights_b = jnp.where(allowed, jnp.exp(scores - log_total[..., None]), 0.0).astype(
            jnp.bfloat16
        )
        return (
            accum
            + jnp.einsum(
                "grij,jgd->igrd", weights_b, entries[2], preferred_element_type=jnp.float32
            ),
            None,
        )

    mixed_f, _ = lax.scan(
        out_step,
        jnp.zeros((tok_rows, GROUPS, repeat, HEAD_DIM), jnp.float32),
        (key_blocks, place_blocks, value_blocks),
    )
    mixed_b = mixed_f.reshape(tok_rows, HEADS * HEAD_DIM).astype(jnp.bfloat16)
    attn_out = jnp.dot(mixed_b, out_w, preferred_element_type=jnp.float32)
    residual = here_f + attn_out
    h_ffn_f, pull_ffn = jax.vjp(norm_rows, residual, ffn_gain)
    h_ffn = h_ffn_f.astype(jnp.bfloat16)
    gate_up = jnp.dot(h_ffn, gateup_w, preferred_element_type=jnp.float32)
    act_f, pull_gate = jax.vjp(gated, gate_up)
    act_b = act_f.astype(jnp.bfloat16)
    result = residual + jnp.dot(act_b, down_w, preferred_element_type=jnp.float32)
    layer_output = result.astype(jnp.bfloat16)[None]
    grad_out = cotangent[0]
    grad_act = jnp.dot(grad_out, down_w.T, preferred_element_type=jnp.float32)
    grad_down = grad_half(act_b, grad_out, w_down.shape[0])
    grad_gu_b = pull_gate(grad_act)[0].astype(jnp.bfloat16)
    grad_gateup = grad_half(h_ffn, grad_gu_b, w_gateup.shape[0])
    grad_h_ffn = jnp.dot(grad_gu_b, gateup_w.T, preferred_element_type=jnp.float32)
    grad_resid_part, grad_ffn_gain = pull_ffn(grad_h_ffn)
    grad_residual = grad_out.astype(jnp.float32) + grad_resid_part
    grad_attn_b = grad_residual.astype(jnp.bfloat16)
    grad_out_w = grad_half(mixed_b, grad_attn_b, w_out.shape[0])
    grad_mixed_b = (
        jnp.dot(grad_attn_b, out_w.T, preferred_element_type=jnp.float32)
        .astype(jnp.bfloat16)
        .reshape(tok_rows, GROUPS, repeat, HEAD_DIM)
    )
    row_delta = jnp.transpose(
        jnp.sum(grad_mixed_b.astype(jnp.float32) * mixed_f, axis=-1), (1, 2, 0)
    )

    def back_step(grad_query, entries):
        key_blk, place_blk, value_blk = entries
        scores, allowed = score_block(key_blk, place_blk)
        weights_f = jnp.where(allowed, jnp.exp(scores - log_total[..., None]), 0.0)
        weights_b = weights_f.astype(jnp.bfloat16)
        grad_value = jnp.einsum(
            "grij,igrd->jgd", weights_b, grad_mixed_b, preferred_element_type=jnp.float32
        )
        grad_prob = jnp.einsum(
            "igrd,jgd->grij", grad_mixed_b, value_blk, preferred_element_type=jnp.float32
        )
        grad_score = (weights_f * (grad_prob - row_delta[..., None])).astype(jnp.bfloat16)
        grad_query = grad_query + jnp.einsum(
            "grij,jgd->igrd", grad_score, key_blk, preferred_element_type=jnp.float32
        )
        grad_key = (
            jnp.einsum("grij,igrd->jgd", grad_score, query_b, preferred_element_type=jnp.float32)
            * score_scale
        )
        return (
            grad_query,
            jnp.concatenate(
                [
                    grad_key.reshape(tok_rows, GROUPS * HEAD_DIM),
                    grad_value.reshape(tok_rows, GROUPS * HEAD_DIM),
                ],
                axis=1,
            ),
        )

    grad_query, kv_terms = lax.scan(
        back_step,
        jnp.zeros((tok_rows, GROUPS, repeat, HEAD_DIM), jnp.float32),
        (key_blocks, place_blocks, value_blocks),
    )
    grad_query = grad_query * score_scale
    kv_own = lax.psum_scatter(
        kv_terms.reshape(blocks * tok_rows, 2 * GROUPS * HEAD_DIM).astype(jnp.bfloat16),
        "ctx",
        scatter_dimension=0,
        tiled=True,
    ).astype(jnp.float32)
    grad_key_own = kv_own[:, : GROUPS * HEAD_DIM].reshape(tok_rows, GROUPS, HEAD_DIM)
    grad_value_own = kv_own[:, GROUPS * HEAD_DIM :].reshape(tok_rows, GROUPS, HEAD_DIM)
    grad_qkv_f, grad_q_gain, grad_k_gain = pull_heads(
        (grad_query.reshape(tok_rows, HEADS, HEAD_DIM), grad_key_own, grad_value_own)
    )
    grad_qkv_b = grad_qkv_f.astype(jnp.bfloat16)
    grad_qkv_w = grad_half(h_attn, grad_qkv_b, w_qkv.shape[0])
    grad_h_attn = jnp.dot(grad_qkv_b, qkv_w.T, preferred_element_type=jnp.float32)
    grad_here_part, grad_attn_gain = pull_attn(grad_h_attn)
    grad_inputs = (grad_residual + grad_here_part).astype(jnp.bfloat16)[None]
    grad_qkv_own, grad_out_own, grad_gateup_own, grad_down_own = scatter_all(
        (grad_qkv_w, grad_out_w, grad_gateup, grad_down), zfirst=(1,)
    )
    gain_attn, gain_query, gain_key, gain_ffn = lax.psum(
        (grad_attn_gain, grad_q_gain, grad_k_gain, grad_ffn_gain), ("dp", "ctx")
    )
    return (
        layer_output,
        grad_inputs,
        gain_attn,
        grad_qkv_own,
        gain_query,
        gain_key,
        grad_out_own,
        gain_ffn,
        grad_gateup_own,
        grad_down_own,
    )


def solution(mesh):
    in_specs = (
        P("dp", "ctx", None),
        P("dp", "ctx"),
        P("dp", "ctx", None),
        P(),
        P(("dp", "ctx"), None),
        P(),
        P(),
        P(("dp", "ctx"), None),
        P(),
        P(("dp", "ctx"), None),
        P(("dp", "ctx"), None),
    )
    out_specs = (
        P("dp", "ctx", None),
        P("dp", "ctx", None),
        P(),
        P(("dp", "ctx"), None),
        P(),
        P(),
        P(("dp", "ctx"), None),
        P(),
        P(("dp", "ctx"), None),
        P(("dp", "ctx"), None),
    )
    fast = dict(mesh.shape) == {"dp": 4, "ctx": 8}
    per_device = per_device_fast if fast else per_device_plain
    return jax.shard_map(
        per_device, mesh=mesh, in_specs=in_specs, out_specs=out_specs, check_vma=False
    )
```

```python
import functools
import math

import jax
import jax.numpy as jnp
from jax import lax
from jax.experimental import pallas as pl
from jax.experimental.pallas import tpu as pltpu
from jax.sharding import PartitionSpec as P

HEADS = 16
GROUPS = 4
HEAD_DIM = 64
FF = 1024
f32 = jnp.float32
bf16 = jnp.bfloat16
MESH = pl.DeviceIdType.MESH
NZ = 4
EPS = 1e-06


class Place:
    def __init__(self):
        self.z = lax.axis_index("dp")
        spot = lax.axis_index("ctx")
        self.core = spot % 2
        self.x = (spot // 2) % 2
        self.y = spot // 4

    def at(self, z=None, y=None, x=None, core=None):
        z = self.z if z is None else z
        y = self.y if y is None else y
        x = self.x if x is None else x
        core = self.core if core is None else core
        return (z, y * 4 + x * 2 + core)

    def xn(self):
        return self.at(x=1 - self.x)

    def yn(self):
        return self.at(y=1 - self.y)

    def sn(self):
        return self.at(core=1 - self.core)

    def up(self):
        return self.at(z=self.z + 1)

    def down(self):
        return self.at(z=self.z - 1)


def barrier(pc):
    bar = pltpu.get_barrier_semaphore()

    def greet(device):
        pl.semaphore_signal(bar, inc=1, device_id=device, device_id_type=MESH)

    for device in (pc.xn(), pc.yn(), pc.sn()):
        greet(device)

    @pl.when(pc.z < NZ - 1)
    def _():
        greet(pc.up())

    @pl.when(pc.z > 0)
    def _():
        greet(pc.down())

    pl.semaphore_wait(bar, 3 + (1 - pc.z // (NZ - 1)) + (pc.z + NZ - 1) // NZ)


def far(z, i):
    m = z // 2
    zz = z + m * (3 - 2 * z)
    lo = 3 - i if i < 2 else (1 - zz if i == 2 else zz)
    return lo + m * (3 - 2 * lo)


def near(z, i):
    return far(z, NZ - 1 - i)


def remote(src, dst, dev, send, recv):
    return pltpu.make_async_remote_copy(
        src_ref=src, dst_ref=dst, send_sem=send, recv_sem=recv, device_id=dev, device_id_type=MESH
    )


def halves(rows):
    return pl.ds(0, rows // 2), pl.ds(rows // 2, rows // 2)


KZ, KX, KY, KD0, KD1, KS, KU = range(7)


class Gather:
    def __init__(self, pc, buf, send, recv):
        self.pc, self.buf, self.send, self.recv = pc, buf, send, recv
        self.h = halves(buf.shape[-2])

    def cp(self, idx, dev, ks, kr, slot):
        ref = self.buf.at[idx]
        return remote(ref, ref, dev, self.send.at[ks, slot], self.recv.at[kr, slot])

    def c_up(self, z0):
        p = self.pc
        return self.cp((z0, p.y, p.x, p.core), p.up(), KU, KZ, z0)

    def c_down(self, z0):
        p = self.pc
        return self.cp((z0, p.y, p.x, p.core), p.down(), KZ, KZ, z0)

    def c_x(self, z0):
        p = self.pc
        return self.cp((z0, p.y, p.x, p.core), p.xn(), KX, KX, z0)

    def c_y(self, z0):
        p = self.pc
        return self.cp((z0, p.y, p.x, p.core), p.yn(), KY, KY, z0)

    def c_d0(self, z0):
        p = self.pc
        return self.cp((z0, p.y, 1 - p.x, p.core, self.h[0]), p.yn(), KD0, KD0, z0)

    def c_d1(self, z0):
        p = self.pc
        return self.cp((z0, 1 - p.y, p.x, p.core, self.h[1]), p.xn(), KD1, KD1, z0)

    def c_s(self, z0):
        p = self.pc
        return self.cp((z0, slice(None), slice(None), p.core), p.sn(), KS, KS, z0)

    def plane_send(self, i):
        z0 = near(self.pc.z, i)
        self.c_x(z0).start()
        self.c_y(z0).start()

    def own_z(self):
        z = self.pc.z

        @pl.when(z < NZ - 1)
        def _():
            self.c_up(z).start()

        @pl.when(z > 0)
        def _():
            self.c_down(z).start()

    def z_event(self, i, plane=True):
        z = self.pc.z
        z0 = near(z, i)

        @pl.when(z0 < z)
        def _():
            self.c_up(z0).wait_recv()

            @pl.when(z < NZ - 1)
            def _():
                self.c_up(z0).start()

        @pl.when(z0 > z)
        def _():
            self.c_down(z0).wait_recv()

            @pl.when(z > 0)
            def _():
                self.c_down(z0).start()

        if plane:
            self.plane_send(i)

    def plane_event(self, i):
        z0 = near(self.pc.z, i)
        self.c_x(z0).wait_recv()
        self.c_d0(z0).start()
        self.c_y(z0).wait_recv()
        self.c_d1(z0).start()

    def core_event(self, i):
        z0 = near(self.pc.z, i)
        self.c_d0(z0).wait_recv()
        self.c_d1(z0).wait_recv()
        self.c_s(z0).start()

    def done_event(self, i):
        self.c_s(near(self.pc.z, i)).wait_recv()

    def finish(self):
        z = self.pc.z
        for z0 in range(NZ):
            for c in (self.c_x, self.c_y, self.c_d0, self.c_d1, self.c_s):
                c(z0).wait_send()

            @pl.when((z < NZ - 1) & (z0 <= z))
            def _():
                self.c_up(z0).wait_send()

            @pl.when((z > 0) & (z0 >= z))
            def _():
                self.c_down(z0).wait_send()


class GatherPlane:
    def __init__(self, pc, buf, send, recv):
        self.pc, self.buf, self.send, self.recv = pc, buf, send, recv
        self.h = halves(buf.shape[-2])

    def cp(self, idx, dev, s, r):
        ref = self.buf.at[idx]
        return remote(ref, ref, dev, self.send.at[s], self.recv.at[r])

    def yx(self, k):
        p = self.pc
        return (p.y if k < 2 else 1 - p.y), (p.x if k % 2 == 0 else 1 - p.x)

    def c_x(self):
        p = self.pc
        return self.cp((p.z, p.y, p.x, p.core), p.xn(), (KX, 0), (KX, 0))

    def c_y(self):
        p = self.pc
        return self.cp((p.z, p.y, p.x, p.core), p.yn(), (KY, 0), (KY, 0))

    def c_d0(self):
        p = self.pc
        return self.cp((p.z, p.y, 1 - p.x, p.core, self.h[0]), p.yn(), (KD0, 0), (KD0, 0))

    def c_d1(self):
        p = self.pc
        return self.cp((p.z, 1 - p.y, p.x, p.core, self.h[1]), p.xn(), (KD1, 0), (KD1, 0))

    def c_up(self, z0, k):
        p = self.pc
        y, x = self.yx(k)
        return self.cp((z0, y, x, p.core), p.up(), (10 + z0, k), (10 + z0, k))

    def c_down(self, z0, k):
        p = self.pc
        y, x = self.yx(k)
        return self.cp((z0, y, x, p.core), p.down(), (14 + z0, k), (10 + z0, k))

    def c_s(self, z0):
        p = self.pc
        return self.cp((z0, slice(None), slice(None), p.core), p.sn(), (KS, z0), (KS, z0))

    def z_send(self, k):
        z = self.pc.z

        @pl.when(z < NZ - 1)
        def _():
            self.c_up(z, k).start()

        @pl.when(z > 0)
        def _():
            self.c_down(z, k).start()

    def own_plane(self):
        self.c_x().start()
        self.c_y().start()

    def own_z(self):
        self.z_send(0)

    def plane_event(self):
        self.c_x().wait_recv()
        self.c_d0().start()
        self.z_send(1)
        self.c_y().wait_recv()
        self.c_d1().start()
        self.z_send(2)

    def diag_event(self):
        self.c_d0().wait_recv()
        self.c_d1().wait_recv()
        self.z_send(3)
        self.c_s(self.pc.z).start()

    def z_event(self, i, k):
        z = self.pc.z
        z0 = near(z, i)

        @pl.when(z0 < z)
        def _():
            self.c_up(z0, k).wait_recv()

            @pl.when(z < NZ - 1)
            def _():
                self.c_up(z0, k).start()

        @pl.when(z0 > z)
        def _():
            self.c_down(z0, k).wait_recv()

            @pl.when(z > 0)
            def _():
                self.c_down(z0, k).start()

    def core_event(self, i):
        self.c_s(near(self.pc.z, i)).start()

    def done_event(self, i):
        self.c_s(near(self.pc.z, i)).wait_recv()

    def finish(self):
        z = self.pc.z
        for c in (self.c_x, self.c_y, self.c_d0, self.c_d1):
            c().wait_send()
        for z0 in range(NZ):
            self.c_s(z0).wait_send()
            for k in range(4):

                @pl.when((z < NZ - 1) & (z0 <= z))
                def _():
                    self.c_up(z0, k).wait_send()

                @pl.when((z > 0) & (z0 >= z))
                def _():
                    self.c_down(z0, k).wait_send()


class GatherSequence:
    def __init__(self, pc, buf, send, recv):
        self.pc, self.buf, self.send, self.recv = pc, buf, send, recv
        rows = buf.shape[-2]
        self.h = (pl.ds(0, 128), pl.ds(128, rows - 128))

    def cp(self, idx, dev, k):
        ref = self.buf.at[idx]
        return remote(ref, ref, dev, self.send.at[k], self.recv.at[k])

    def c_x(self):
        p = self.pc
        return self.cp((p.y, p.x, p.core), p.xn(), 0)

    def c_y(self):
        p = self.pc
        return self.cp((p.y, p.x, p.core), p.yn(), 1)

    def c_d0(self):
        p = self.pc
        return self.cp((p.y, 1 - p.x, p.core, self.h[0]), p.yn(), 2)

    def c_d1(self):
        p = self.pc
        return self.cp((1 - p.y, p.x, p.core, self.h[1]), p.xn(), 3)

    def c_s(self, k):
        p = self.pc
        y, x = (p.y if k < 2 else 1 - p.y), (p.x if k % 2 == 0 else 1 - p.x)
        return self.cp((y, x, p.core), p.sn(), 4 + k)

    def own(self):
        for c in (self.c_x(), self.c_y(), self.c_s(0)):
            c.start()

    def plane_event(self):
        self.c_x().wait_recv()
        self.c_d0().start()
        self.c_s(1).start()
        self.c_y().wait_recv()
        self.c_d1().start()
        self.c_s(2).start()

    def core_event(self):
        self.c_d0().wait_recv()
        self.c_d1().wait_recv()
        self.c_s(3).start()

    def done_event(self):
        for k in range(4):
            self.c_s(k).wait_recv()

    def finish(self):
        for c in (self.c_x(), self.c_y(), self.c_d0(), self.c_d1()):
            c.wait_send()
        for k in range(4):
            self.c_s(k).wait_send()


LOG2E = math.log2(math.e)
VMEM = pltpu.VMEM


def dot(a, b):
    return jnp.dot(a, b, preferred_element_type=f32)


def dot_t(a, b):
    return lax.dot_general(a, b, (((1,), (1,)), ((), ())), preferred_element_type=f32)


def lanes(shape):
    return lax.broadcasted_iota(jnp.int32, shape, 1)


def roll_half(v):
    return pltpu.roll(v, 64, 1)


def swap_rot(v):
    first = lanes(v.shape) % 64 < 32
    return jnp.where(first, pltpu.roll(v, 96, 1), pltpu.roll(v, 32, 1))


def head_sums(v):
    row = lax.broadcasted_iota(jnp.int32, (128, 128), 0) // 64
    col = lax.broadcasted_iota(jnp.int32, (128, 128), 1) // 64
    ones = jnp.where(row == col, 1.0, 0.0).astype(bf16)
    high = v.astype(bf16)
    low = (v - high.astype(f32)).astype(bf16)
    return dot(high, ones) + dot(low, ones)


def cols(i, width):
    return pl.ds(pl.multiple_of(i * width, width), width)


def norm_into(src, gain, dst):
    def body(i, _):
        rows = pl.ds(pl.multiple_of(i * 32, 32), 32)
        v = src[rows, :].astype(f32)
        scale = lax.rsqrt(jnp.mean(v * v, axis=-1, keepdims=True) + EPS)
        dst[rows, :] = (v * scale * gain[...]).astype(dst.dtype)
        return 0

    lax.fori_loop(0, src.shape[0] // 32, body, 0)


def ticked(tick, first, events):
    for k, event in enumerate(events):
        if event is not None:

            @pl.when(tick == first + k)
            def _(event=event):
                event()


def forward_kernel(dims, *refs):
    (tok, width, n_dev, heads_w, kv_w, ff) = dims
    (
        x_ref, cot_ref, hi_ref, cos_ref, sin_ref, g_attn, g_q, g_k, g_ffn,
        s_qkv, s_out, s_down, s_gu,
        y_ref, hattn_ref, qkv_ref, q2_ref, kvb, linv_ref, mixf_ref, mixb_ref, res_ref, hffn_ref,
        act_ref, ggu_ref, o_qkv, o_out, o_gu,
        w_qkv, w_out, w_down, w_gu, kk, va, mask, o2, gu, gact,
        send, recv, kv_send, kv_recv, lsem, osem,
    ) = refs
    pc = Place()
    shards = (s_qkv, s_out, s_down, s_gu)
    bufs = (w_qkv, w_out, w_down, w_gu)
    local = [
        pltpu.make_async_copy(s, b.at[pc.z, pc.y, pc.x, pc.core], lsem.at[k])
        for k, (s, b) in enumerate(zip(shards, bufs))
    ]
    for c in local:
        c.start()
    barrier(pc)
    for c in local:
        c.wait()
    qkv = Gather(pc, w_qkv, send.at[0], recv.at[0])
    out = GatherPlane(pc, w_out, send.at[1], recv.at[1])
    down = Gather(pc, w_down, send.at[2], recv.at[2])
    gateup = Gather(pc, w_gu, send.at[3], recv.at[3])
    seq = GatherSequence(pc, kvb, kv_send, kv_recv)
    part = functools.partial
    z = pc.z

    qkv.own_z()
    qkv.plane_send(0)
    norm_into(x_ref, g_attn, hattn_ref)
    qkv.z_event(1)
    qkv.plane_event(0)
    qkv.z_event(2)
    out.own_plane()
    out.own_z()
    down.own_z()
    gateup.own_z()
    qkv.z_event(3)
    qkv.plane_event(1)
    qkv.core_event(0)
    down.plane_send(0)
    gateup.plane_send(0)
    qkv.plane_event(2)
    qkv.core_event(1)
    down.z_event(1)
    gateup.z_event(1)
    qkv.plane_event(3)
    out.plane_event()
    later = []

    def qkv_step(i):
        qkv.done_event(i)
        z0 = near(z, i)
        depth = width // NZ

        def body(n, _):
            c = cols(n, 256)
            w = w_qkv[z0, :, :, :, :, c].reshape(depth, 256)
            prod = dot(hattn_ref[:, cols(z0, depth)], w)
            if i == 0:
                qkv_ref[:, c] = prod
            else:
                qkv_ref[:, c] += prod
            return 0

        lax.fori_loop(0, qkv_ref.shape[1] // 256, body, 0)

    qkv_step(0)
    qkv.core_event(2)
    qkv_step(1)
    qkv.core_event(3)
    down.plane_event(0)
    gateup.plane_event(0)
    qkv_step(2)
    qkv_step(3)

    low = lanes((tok, 128)) < 64

    def head_tile(t, gain):
        u = qkv_ref[:, cols(t, 128)]
        n = u * lax.rsqrt(head_sums(u * u) * (1.0 / 64) + EPS) * gain[...]
        return n * cos_ref[...] + swap_rot(n) * sin_ref[...]

    for t in range(kv_w // 128):
        kvb[pc.y, pc.x, pc.core, pl.ds(0, tok), pl.ds(t * 128, 128)] = head_tile(
            heads_w // 128 + t, g_k
        ).astype(bf16)
    kvb[pc.y, pc.x, pc.core, pl.ds(0, tok), pl.ds(kv_w, kv_w)] = qkv_ref[
        :, pl.ds(heads_w + kv_w, kv_w)
    ].astype(bf16)
    blocks_row = jnp.broadcast_to(hi_ref[...], (16, tok)).astype(bf16)
    kvb[pc.y, pc.x, pc.core, pl.ds(tok, 16), pl.ds(0, tok)] = blocks_row
    kvb[pc.y, pc.x, pc.core, pl.ds(tok, 16), pl.ds(tok, tok)] = blocks_row
    seq.own()

    def query_tile(t, _):
        q = (head_tile(t, g_q) * 0.125).astype(bf16)
        zero = jnp.zeros_like(q)
        q2_ref[t, pl.ds(0, tok), :] = jnp.where(low, q, zero)
        q2_ref[t, pl.ds(tok, tok), :] = jnp.where(low, zero, q)
        return 0

    lax.fori_loop(0, heads_w // 128, query_tile, 0)

    down.z_event(2)
    gateup.z_event(2)
    out.diag_event()
    down.plane_event(1)
    gateup.plane_event(1)
    seq.plane_event()
    down.z_event(3)
    for j in range(4):
        out.z_event(1, j)
    gateup.z_event(3)
    down.core_event(0)
    gateup.core_event(0)
    seq.core_event()
    seq.done_event()

    def unpack(b, _):
        y, x, c = b // 4, (b // 2) % 2, b % 2
        rows = pl.ds(pl.multiple_of(b * tok, tok), tok)
        for t in range(kv_w // 128):
            k = kvb[y, x, c, pl.ds(0, tok), pl.ds(t * 128, 128)].astype(f32)
            v = kvb[y, x, c, pl.ds(0, tok), pl.ds(kv_w + t * 128, 128)].astype(f32)
            k_r, v_r = roll_half(k), roll_half(v)
            kk[2 * t, rows, :] = jnp.where(low, k, k_r).astype(bf16)
            kk[2 * t + 1, rows, :] = jnp.where(low, k_r, k).astype(bf16)
            va[2 * t, rows, :] = jnp.where(low, v, 1.0).astype(bf16)
            va[2 * t + 1, rows, :] = jnp.where(low, v_r, 1.0).astype(bf16)
        step = tok // 2
        key_hi = kvb[y, x, c, pl.ds(tok, 16), pl.ds(0, tok)].astype(f32)[:1, :]
        for a in range(2):
            own = hi_ref[:, a * step : (a + 1) * step].astype(f32)
            row = lax.broadcasted_iota(jnp.int32, (step, step), 0).astype(f32)
            col = lanes((step, step)).astype(f32)
            for d in range(2):
                theirs = key_hi[:, d * step : (d + 1) * step]
                gap = (own - theirs) * float(step) + row - col
                mask[pl.ds(a * step, step), pl.ds(pl.multiple_of(b * tok + d * step, step), step)] = (
                    jnp.where(gap >= 0, 1.0, 0.0).astype(bf16)
                )
        return 0

    lax.fori_loop(0, n_dev, unpack, 0)

    events = [part(out.z_event, 2, j) for j in range(4)] + [
        part(out.core_event, 1), part(down.plane_event, 2), part(gateup.plane_event, 2),
        part(down.core_event, 1), part(gateup.core_event, 1),
    ] + [part(out.z_event, 3, j) for j in range(4)] + [
        part(out.core_event, 2),
        part(down.plane_event, 3), part(gateup.plane_event, 3),
        part(down.core_event, 2), part(gateup.core_event, 2), part(out.core_event, 3),
    ]
    chunk = 512
    n_chunk = n_dev * tok // chunk

    def attend(tick, _):
        t, kc = tick // n_chunk, tick % n_chunk
        g = t // 2
        rows = pl.ds(pl.multiple_of(kc * chunk, chunk), chunk)
        s = dot_t(q2_ref[t], kk[g, rows, :])
        e = jnp.exp2(s * LOG2E).astype(bf16).reshape(2, tok, chunk) * mask[:, rows][None]
        o = dot(e.reshape(2 * tok, chunk), va[g, rows, :])

        @pl.when(kc == 0)
        def _():
            o2[...] = o

        @pl.when(kc > 0)
        def _():
            o2[...] += o

        @pl.when(kc == n_chunk - 1)
        def _():
            even, odd = o2[pl.ds(0, tok), :], o2[pl.ds(tok, tok), :]
            total = jnp.where(low, roll_half(even), odd)
            inv = 1.0 / total
            mixed = jnp.where(low, even, roll_half(odd)) * inv
            linv_ref[:, cols(t, 128)] = inv
            mixf_ref[:, cols(t, 128)] = mixed
            mixb_ref[:, cols(t, 128)] = mixed.astype(bf16)

        ticked(tick, 2, events)
        return 0

    lax.fori_loop(0, heads_w // 128 * n_chunk, attend, 0)

    for i in range(NZ):
        out.done_event(i)

    def residual_step(n, _):
        c = cols(n, 256)
        w = w_out[:, :, :, :, :, c].reshape(heads_w, 256)
        res_ref[:, c] = x_ref[:, c].astype(f32) + dot(mixb_ref[...], w)
        return 0

    lax.fori_loop(0, width // 256, residual_step, 0)
    norm_into(res_ref, g_ffn, hffn_ref)

    def gateup_step(i):
        gateup.done_event(i)
        z0 = near(z, i)
        depth = width // NZ

        def body(n, _):
            c = cols(n, 256)
            w = w_gu[z0, :, :, :, :, c].reshape(depth, 256)
            prod = dot(hffn_ref[:, cols(z0, depth)], w)
            if i == 0:
                gu[:, c] = prod
            else:
                gu[:, c] += prod
            return 0

        lax.fori_loop(0, 2 * ff // 256, body, 0)

    def grad_act_step(i):
        down.done_event(i)
        z0 = near(z, i)
        depth = ff // NZ
        gact[:, cols(z0, depth)] = dot_t(cot_ref[...], w_down[z0].reshape(depth, width))

    gateup_step(0)
    grad_act_step(0)
    gateup_step(1)
    grad_act_step(1)
    down.core_event(3)
    gateup_step(2)
    grad_act_step(2)
    gateup.core_event(3)
    grad_act_step(3)
    gateup_step(3)

    def gate_step(n, _):
        c = cols(n, 256)
        c2 = cols(n + ff // 256, 256)
        gate, up, grad = gu[:, c], gu[:, c2], gact[:, c]
        sig = 1.0 / (1.0 + jnp.exp(-gate))
        silu = gate * sig
        act_ref[:, c] = (silu * up).astype(bf16)
        ggu_ref[:, c] = (grad * up * (sig * (1.0 + gate * (1.0 - sig)))).astype(bf16)
        ggu_ref[:, c2] = (grad * silu).astype(bf16)
        return 0

    lax.fori_loop(0, ff // 256, gate_step, 0)
    outs = [
        pltpu.make_async_copy(b, o, osem.at[k])
        for k, (b, o) in enumerate(((w_qkv, o_qkv), (w_out, o_out), (w_gu, o_gu)))
    ]
    for c in outs:
        c.start()

    def output_step(n, _):
        c = cols(n, 256)
        w = w_down[:, :, :, :, :, c].reshape(ff, 256)
        y_ref[:, c] = (res_ref[:, c] + dot(act_ref[...], w)).astype(bf16)
        return 0

    lax.fori_loop(0, width // 256, output_step, 0)
    for g in (qkv, out, down, gateup, seq):
        g.finish()
    for c in outs:
        c.wait()


def forward(x, cot, blocks, cosine, sine, g_attn, g_q, g_k, g_ffn, s_qkv, s_out, s_down, s_gu, n_dev):
    tok, width = x.shape
    heads_w, kv_w = HEADS * HEAD_DIM, GROUPS * HEAD_DIM
    ff = s_down.shape[0] * n_dev * NZ
    length = n_dev * tok
    tiles = heads_w // 128
    shape = jax.ShapeDtypeStruct
    seven = [(NZ, 2, 2, 2) + s.shape for s in (s_qkv, s_out, s_down, s_gu)]
    outs = [
        shape((tok, width), bf16),
        shape((tok, width), bf16),
        shape((tok, s_qkv.shape[1]), f32),
        shape((tiles, 2 * tok, 128), bf16),
        shape((2, 2, 2, tok + 16, 2 * kv_w), bf16),
        shape((tok, heads_w), f32),
        shape((tok, heads_w), f32),
        shape((tok, heads_w), bf16),
        shape((tok, width), f32),
        shape((tok, width), bf16),
        shape((tok, ff), bf16),
        shape((tok, 2 * ff), bf16),
        shape(seven[0], bf16),
        shape(seven[1], bf16),
        shape(seven[3], bf16),
    ]
    vm = pl.BlockSpec(memory_space=VMEM)
    anyw = pl.BlockSpec(memory_space=pl.ANY)
    dma = pltpu.SemaphoreType.DMA
    flops = 2 * tok * (width * (s_qkv.shape[1] + heads_w + 2 * ff + 2 * ff) + 2 * heads_w * length)
    return pl.pallas_call(
        functools.partial(forward_kernel, (tok, width, n_dev, heads_w, kv_w, ff)),
        out_shape=outs,
        in_specs=[vm] * 9 + [anyw] * 4,
        out_specs=[vm] * 12 + [anyw] * 3,
        scratch_shapes=[VMEM(s, bf16) for s in seven]
        + [
            VMEM((GROUPS, length, 128), bf16),
            VMEM((GROUPS, length, 128), bf16),
            VMEM((tok, length), bf16),
            VMEM((2 * tok, 128), f32),
            VMEM((tok, 2 * ff), f32),
            VMEM((tok, ff), f32),
            dma((4, 18, NZ)),
            dma((4, 14, NZ)),
            dma((8,)),
            dma((8,)),
            dma((4,)),
            dma((3,)),
        ],
        compiler_params=pltpu.CompilerParams(
            collective_id=0, has_side_effects=True, vmem_limit_bytes=60 << 20
        ),
        cost_estimate=pl.CostEstimate(flops=flops, bytes_accessed=50 << 20, transcendentals=0),
        name="forward",
    )(x, cot, blocks, cosine, sine, g_attn, g_q, g_k, g_ffn, s_qkv, s_out, s_down, s_gu)


SD0, SD1, SX0, SX1, SY0, SY1, SA, SB = range(8)

class Scatter:
    def __init__(self, pc, part, bufs, out, send, recv):
        self.pc, self.part, self.out, self.send, self.recv = pc, part, out, send, recv
        self.rd, self.rx, self.ry, self.za, self.zb, self.sm = bufs
        R = part.shape[-2]
        self.R = R
        self.h = (pl.ds(0, R // 2), pl.ds(R // 2, R // 2))
    def cp(self, src, dst, dev, k, zp):
        return pltpu.make_async_remote_copy(src_ref=src, dst_ref=dst, send_sem=self.send.at[k, zp], recv_sem=self.recv.at[k, zp], device_id=dev, device_id_type=MESH)
    def d0(self, zp): p = self.pc; return self.cp(self.part.at[zp, 1 - p.y, 1 - p.x, self.h[0]], self.rd.at[zp, 0], p.yn(), SD0, zp)
    def d1(self, zp): p = self.pc; return self.cp(self.part.at[zp, 1 - p.y, 1 - p.x, self.h[1]], self.rd.at[zp, 1], p.xn(), SD1, zp)
    def x1(self, zp): p = self.pc; return self.cp(self.part.at[zp, p.y, 1 - p.x, self.h[1]], self.rx.at[zp, 1], p.xn(), SX1, zp)
    def y0(self, zp): p = self.pc; return self.cp(self.part.at[zp, 1 - p.y, p.x, self.h[0]], self.ry.at[zp, 0], p.yn(), SY0, zp)
    def x0(self, zp): p = self.pc; return self.cp(self.rd.at[zp, 0], self.rx.at[zp, 0], p.xn(), SX0, zp)
    def y1(self, zp): p = self.pc; return self.cp(self.rd.at[zp, 1], self.ry.at[zp, 1], p.yn(), SY1, zp)
    def down(self, zp): p = self.pc; return self.cp(self.sm.at[zp], self.za.at[zp], p.down(), SA, zp)
    def up(self, zp): p = self.pc; return self.cp(self.sm.at[zp], self.zb.at[zp], p.up(), SB, zp)
    def first(self, i):
        zp = far(self.pc.z, i)
        for c in (self.d0, self.d1, self.x1, self.y0): c(zp).start()
    def d_event(self, i):
        p = self.pc; zp = far(p.z, i)
        self.d0(zp).wait_recv()
        self.rd[zp, 0] = self.rd[zp, 0] + self.part[zp, p.y, 1 - p.x, self.h[0]]
        self.x0(zp).start()
        self.d1(zp).wait_recv()
        self.rd[zp, 1] = self.rd[zp, 1] + self.part[zp, 1 - p.y, p.x, self.h[1]]
        self.y1(zp).start()
    def xy_event(self, i):
        p = self.pc; zp = far(p.z, i)
        for c in (self.x1, self.y0, self.x0, self.y1): c(zp).wait_recv()
        for k in range(2):
            self.sm[zp, self.h[k]] = (self.part[zp, p.y, p.x, self.h[k]].astype(f32) + self.rx[zp, k].astype(f32) + self.ry[zp, k].astype(f32)).astype(bf16)
    def z_event(self, i):
        z = self.pc.z; zp = far(z, i)
        @pl.when(zp < z)
        def _():
            @pl.when(z < NZ - 1)
            def _():
                self.down(zp).wait_recv()
                self.sm[zp] = self.sm[zp] + self.za[zp]
            self.down(zp).start()
        @pl.when(zp > z)
        def _():
            @pl.when(z > 0)
            def _():
                self.up(zp).wait_recv()
                self.sm[zp] = self.sm[zp] + self.zb[zp]
            self.up(zp).start()
    def final(self):
        p = self.pc; z = p.z
        for c in (self.x1, self.y0, self.x0, self.y1): c(z).wait_recv()
        for k in range(2):
            self.out[self.h[k], :] = self.part[z, p.y, p.x, self.h[k]].astype(f32) + self.rx[z, k].astype(f32) + self.ry[z, k].astype(f32)
        @pl.when(z < NZ - 1)
        def _():
            self.down(z).wait_recv()
            self.out[...] += self.za[z].astype(f32)
        @pl.when(z > 0)
        def _():
            self.up(z).wait_recv()
            self.out[...] += self.zb[z].astype(f32)
    def finish(self):
        z = self.pc.z
        for zp in range(NZ):
            for c in (self.d0, self.d1, self.x1, self.y0, self.x0, self.y1): c(zp).wait_send()
            @pl.when(zp < z)
            def _(): self.down(zp).wait_send()
            @pl.when(zp > z)
            def _(): self.up(zp).wait_send()
    @staticmethod
    def scratch(R, C):
        v = pltpu.VMEM
        return [v((NZ, 2, R // 2, C), bf16), v((NZ, 2, R // 2, C), bf16), v((NZ, 2, R // 2, C), bf16), v((NZ, R, C), bf16), v((NZ, R, C), bf16), v((NZ, R, C), bf16)]

class ScatterZ:
    def __init__(self, pc, part, bufs, out, send, recv):
        self.pc, self.part, self.out, self.send, self.recv = pc, part, out, send, recv
        self.rd, self.rx, self.ry, self.za, self.zb, self.sm = bufs
        R = part.shape[-2]
        self.h = (pl.ds(0, R // 2), pl.ds(R // 2, R // 2))
    def cp(self, src, dst, dev, k, s):
        return pltpu.make_async_remote_copy(src_ref=src, dst_ref=dst, send_sem=self.send.at[k, s], recv_sem=self.recv.at[k, s], device_id=dev, device_id_type=MESH)
    def yx(self, k): return k // 2, k % 2
    def down(self, zp, k, src): return self.cp(src, self.za.at[zp, k], self.pc.down(), 8 + zp, k)
    def up(self, zp, k, src): return self.cp(src, self.zb.at[zp, k], self.pc.up(), 12 + zp, k)
    def first(self, i):
        z = self.pc.z; zp = far(z, i)
        for k in range(4):
            y, x = self.yx(k)
            @pl.when((z == NZ - 1) & (zp < z))
            def _(): self.down(zp, k, self.part.at[zp, y, x]).start()
            @pl.when((z == 0) & (zp > z))
            def _(): self.up(zp, k, self.part.at[zp, y, x]).start()
    def z_event(self, i, k):
        z = self.pc.z; zp = far(z, i); y, x = self.yx(k)
        @pl.when((zp < z) & (z < NZ - 1))
        def _():
            self.down(zp, k, self.za.at[zp, k]).wait_recv()
            self.za[zp, k] = self.za[zp, k] + self.part[zp, y, x]
            self.down(zp, k, self.za.at[zp, k]).start()
        @pl.when((zp > z) & (z > 0))
        def _():
            self.up(zp, k, self.zb.at[zp, k]).wait_recv()
            self.zb[zp, k] = self.zb[zp, k] + self.part[zp, y, x]
            self.up(zp, k, self.zb.at[zp, k]).start()
    def own_event(self, k):
        z = self.pc.z; y, x = self.yx(k)
        @pl.when(z < NZ - 1)
        def _(): self.down(z, k, self.za.at[z, k]).wait_recv()
        @pl.when(z > 0)
        def _(): self.up(z, k, self.zb.at[z, k]).wait_recv()
        @pl.when(z == 0)
        def _(): self.sm[k] = self.part[z, y, x] + self.za[z, k]
        @pl.when(z == NZ - 1)
        def _(): self.sm[k] = self.part[z, y, x] + self.zb[z, k]
        @pl.when((z > 0) & (z < NZ - 1))
        def _(): self.sm[k] = (self.part[z, y, x].astype(f32) + self.za[z, k].astype(f32) + self.zb[z, k].astype(f32)).astype(bf16)
    def kk(self, y, x): return y * 2 + x
    def d0(self): p = self.pc; return self.cp(self.sm.at[self.kk(1 - p.y, 1 - p.x), self.h[0]], self.rd.at[0, 0], p.yn(), SD0, 0)
    def d1(self): p = self.pc; return self.cp(self.sm.at[self.kk(1 - p.y, 1 - p.x), self.h[1]], self.rd.at[0, 1], p.xn(), SD1, 0)
    def x1(self): p = self.pc; return self.cp(self.sm.at[self.kk(p.y, 1 - p.x), self.h[1]], self.rx.at[0, 1], p.xn(), SX1, 0)
    def y0(self): p = self.pc; return self.cp(self.sm.at[self.kk(1 - p.y, p.x), self.h[0]], self.ry.at[0, 0], p.yn(), SY0, 0)
    def x0(self): p = self.pc; return self.cp(self.rd.at[0, 0], self.rx.at[0, 0], p.xn(), SX0, 0)
    def y1(self): p = self.pc; return self.cp(self.rd.at[0, 1], self.ry.at[0, 1], p.yn(), SY1, 0)
    def plane_send(self):
        for c in (self.d0, self.d1, self.x1, self.y0): c().start()
    def plane_event(self):
        p = self.pc
        self.d0().wait_recv()
        self.rd[0, 0] = self.rd[0, 0] + self.sm[self.kk(p.y, 1 - p.x), self.h[0]]
        self.x0().start()
        self.d1().wait_recv()
        self.rd[0, 1] = self.rd[0, 1] + self.sm[self.kk(1 - p.y, p.x), self.h[1]]
        self.y1().start()
    def final(self):
        p = self.pc
        for c in (self.x1, self.y0, self.x0, self.y1): c().wait_recv()
        for k in range(2):
            self.out[self.h[k], :] = self.sm[self.kk(p.y, p.x), self.h[k]].astype(f32) + self.rx[0, k].astype(f32) + self.ry[0, k].astype(f32)
    def finish(self):
        z = self.pc.z
        for c in (self.d0, self.d1, self.x1, self.y0, self.x0, self.y1): c().wait_send()
        for zp in range(NZ):
            for k in range(4):
                @pl.when(zp < z)
                def _(): self.down(zp, k, self.za.at[zp, k]).wait_send()
                @pl.when(zp > z)
                def _(): self.up(zp, k, self.zb.at[zp, k]).wait_send()
    @staticmethod
    def scratch(R, C):
        v = pltpu.VMEM
        return [v((1, 2, R // 2, C), bf16), v((1, 2, R // 2, C), bf16), v((1, 2, R // 2, C), bf16), v((NZ, 4, R, C), bf16), v((NZ, 4, R, C), bf16), v((4, R, C), bf16)]

FT=[0,0,0,0]; DT=[1,2,3,4]; XT=[2.2,3.2,4.2,5.2]; ZT=[2.5,3.5,4.5]; FINAL=6
def rs_kernel(n, W, zfirst, *refs):
    ins, outs = refs[:n], refs[n:2 * n]
    send, recv = refs[2 * n:2 * n + 2]
    bufs = refs[2 * n + 2:]
    pc = Place()
    barrier(pc)
    ev = []; gs = []
    P_ = functools.partial
    for k in range(n):
        b = bufs[6 * k:6 * k + 6]; T = W[k]
        cls = ScatterZ if k in zfirst else Scatter
        g = cls(pc, ins[k], b, outs[k], send.at[k], recv.at[k]); gs.append(g)
        if k in zfirst:
            for i in range(3):
                ev.append((T, P_(g.first, i)))
                for j in range(4): ev.append((T + 0.5 + i + j * .25, P_(g.z_event, i, j)))
            for j in range(4): ev.append((T + 4 + j * .01, P_(g.own_event, j)))
            ev.append((T + 4.1, g.plane_send)); ev.append((T + 5, g.plane_event)); ev.append((T + 6.5, g.final))
        else:
            for i in range(4):
                ev.append((T + FT[i], P_(g.first, i)))
                ev.append((T + DT[i], P_(g.d_event, i)))
                if i < 3:
                    ev.append((T + XT[i], P_(g.xy_event, i)))
                    ev.append((T + ZT[i], P_(g.z_event, i)))
            ev.append((T + FINAL, g.final))
    ev.sort(key=lambda e: e[0])
    for _, e in ev: e()
    for g in gs: g.finish()

def scatter_all(parts, W=(0, 0, 0, 0), zfirst=()):
    n = len(parts)
    outs = [jax.ShapeDtypeStruct(s.shape[-2:], f32) for s in parts]
    scr = []
    for k, s in enumerate(parts):
        scr += (ScatterZ if k in zfirst else Scatter).scratch(*s.shape[-2:])
    V = pl.BlockSpec(memory_space=pltpu.VMEM)
    return pl.pallas_call(functools.partial(rs_kernel, n, W, zfirst), out_shape=outs,
        in_specs=[V] * n, out_specs=[V] * n,
        scratch_shapes=[pltpu.SemaphoreType.DMA((n, 16, NZ)), pltpu.SemaphoreType.DMA((n, 16, NZ))] + scr,
        compiler_params=pltpu.CompilerParams(collective_id=1, has_side_effects=True, vmem_limit_bytes=60 << 20), name="scatter_grads")(*parts)


epsilon = 1e-06


def norm_rows(values, gain_vec):
    return (
        values * lax.rsqrt(jnp.mean(values * values, axis=-1, keepdims=True) + epsilon) * gain_vec
    )


def rotate(values, positions):
    half_dim = values.shape[-1] // 2
    frequency = jnp.exp(
        jnp.arange(half_dim).astype(jnp.float32) * (-2.0 * math.log(10000.0) / values.shape[-1])
    )
    angles = positions.astype(jnp.float32)[:, None] * frequency[None, :]
    cosine = jnp.cos(angles)[:, None, :]
    sine = jnp.sin(angles)[:, None, :]
    first = values[..., :half_dim]
    second = values[..., half_dim:]
    return jnp.concatenate(
        [first * cosine - second * sine, second * cosine + first * sine], axis=-1
    )


def project_heads(qkv_all, positions, q_gain, k_gain):
    tok_rows = qkv_all.shape[0]
    q_cols = HEADS * HEAD_DIM
    k_cols = GROUPS * HEAD_DIM
    queries = qkv_all[:, :q_cols].reshape(tok_rows, HEADS, HEAD_DIM)
    keys_raw = qkv_all[:, q_cols : q_cols + k_cols].reshape(tok_rows, GROUPS, HEAD_DIM)
    values = qkv_all[:, q_cols + k_cols :].reshape(tok_rows, GROUPS, HEAD_DIM)
    return (
        rotate(norm_rows(queries, q_gain), positions),
        rotate(norm_rows(keys_raw, k_gain), positions),
        values,
    )


def gated(gate_up):
    return jax.nn.silu(gate_up[:, :FF]) * gate_up[:, FF:]


def per_device_plain(
    inputs, places, cotangent, attn_gain, w_qkv, q_gain, k_gain, w_out, ffn_gain, w_gateup, w_down
):
    tok_rows = inputs.shape[1]
    repeat = HEADS // GROUPS
    score_scale = HEAD_DIM ** (-0.5)
    here_f = inputs[0].astype(jnp.float32)
    own_places = places[0]
    qkv_w, out_w = (
        lax.all_gather(w_qkv, ("dp", "ctx"), axis=0, tiled=True),
        lax.all_gather(w_out, ("dp", "ctx"), axis=0, tiled=True),
    )
    h_attn_f, pull_attn = jax.vjp(norm_rows, here_f, attn_gain)
    h_attn = h_attn_f.astype(jnp.bfloat16)
    qkv_all = jnp.dot(h_attn, qkv_w, preferred_element_type=jnp.float32)

    def heads_of(qkv_in, gain_q, gain_k):
        return project_heads(qkv_in, own_places, gain_q, gain_k)

    (queries, keys_f, values), pull_heads = jax.vjp(heads_of, qkv_all, q_gain, k_gain)
    query_b = queries.astype(jnp.bfloat16).reshape(tok_rows, GROUPS, repeat, HEAD_DIM)
    key_b = keys_f.astype(jnp.bfloat16)
    value_b = values.astype(jnp.bfloat16)
    all_keys, all_values = (
        lax.all_gather(key_b, "ctx", axis=0, tiled=True),
        lax.all_gather(value_b, "ctx", axis=0, tiled=True),
    )
    all_places = lax.all_gather(own_places, "ctx", axis=0, tiled=True)
    blocks = lax.axis_size("ctx")
    key_blocks = all_keys.reshape(blocks, tok_rows, GROUPS, HEAD_DIM)
    value_blocks = all_values.reshape(blocks, tok_rows, GROUPS, HEAD_DIM)
    place_blocks = all_places.reshape(blocks, tok_rows)

    def score_block(key_blk, place_blk):
        scores = (
            jnp.einsum("igrd,jgd->grij", query_b, key_blk, preferred_element_type=jnp.float32)
            * score_scale
        )
        allowed = place_blk[None, :] <= own_places[:, None]
        return (scores, allowed)

    def max_step(state_pair, entries):
        row_top, row_total = state_pair
        scores, allowed = score_block(entries[0], entries[1])
        scores = jnp.where(allowed, scores, -1e30)
        new_top = jnp.maximum(row_top, jnp.max(scores, axis=-1))
        row_total = row_total * jnp.exp(row_top - new_top) + jnp.sum(
            jnp.where(allowed, jnp.exp(scores - new_top[..., None]), 0.0), axis=-1
        )
        return ((new_top, row_total), None)

    start_pair = (
        jnp.full((GROUPS, repeat, tok_rows), -1e30, jnp.float32),
        jnp.zeros((GROUPS, repeat, tok_rows), jnp.float32),
    )
    (row_top, row_total), _ = lax.scan(max_step, start_pair, (key_blocks, place_blocks))
    log_total = row_top + jnp.log(row_total)

    def out_step(accum, entries):
        scores, allowed = score_block(entries[0], entries[1])
        weights_b = jnp.where(allowed, jnp.exp(scores - log_total[..., None]), 0.0).astype(
            jnp.bfloat16
        )
        return (
            accum
            + jnp.einsum(
                "grij,jgd->igrd", weights_b, entries[2], preferred_element_type=jnp.float32
            ),
            None,
        )

    mixed_f, _ = lax.scan(
        out_step,
        jnp.zeros((tok_rows, GROUPS, repeat, HEAD_DIM), jnp.float32),
        (key_blocks, place_blocks, value_blocks),
    )
    mixed_b = mixed_f.reshape(tok_rows, HEADS * HEAD_DIM).astype(jnp.bfloat16)
    attn_out = jnp.dot(mixed_b, out_w, preferred_element_type=jnp.float32)
    residual = here_f + attn_out
    gateup_w, down_w = (
        lax.all_gather(w_gateup, ("dp", "ctx"), axis=0, tiled=True),
        lax.all_gather(w_down, ("dp", "ctx"), axis=0, tiled=True),
    )
    h_ffn_f, pull_ffn = jax.vjp(norm_rows, residual, ffn_gain)
    h_ffn = h_ffn_f.astype(jnp.bfloat16)
    gate_up = jnp.dot(h_ffn, gateup_w, preferred_element_type=jnp.float32)
    act_f, pull_gate = jax.vjp(gated, gate_up)
    act_b = act_f.astype(jnp.bfloat16)
    result = residual + jnp.dot(act_b, down_w, preferred_element_type=jnp.float32)
    layer_output = result.astype(jnp.bfloat16)[None]
    gateup_w, down_w = (
        lax.all_gather(w_gateup, ("dp", "ctx"), axis=0, tiled=True),
        lax.all_gather(w_down, ("dp", "ctx"), axis=0, tiled=True),
    )
    grad_out = cotangent[0]
    grad_act = jnp.dot(grad_out, down_w.T, preferred_element_type=jnp.float32)
    grad_down = jnp.dot(act_b.T, grad_out, preferred_element_type=jnp.float32)
    grad_gu_b = pull_gate(grad_act)[0].astype(jnp.bfloat16)
    grad_gateup = jnp.dot(h_ffn.T, grad_gu_b, preferred_element_type=jnp.float32)
    grad_h_ffn = jnp.dot(grad_gu_b, gateup_w.T, preferred_element_type=jnp.float32)
    grad_resid_part, grad_ffn_gain = pull_ffn(grad_h_ffn)
    grad_residual = grad_out.astype(jnp.float32) + grad_resid_part
    grad_gateup_own, grad_down_own = (
        lax.psum_scatter(grad_gateup, ("dp", "ctx"), scatter_dimension=0, tiled=True),
        lax.psum_scatter(grad_down, ("dp", "ctx"), scatter_dimension=0, tiled=True),
    )
    qkv_w, out_w = (
        lax.all_gather(w_qkv, ("dp", "ctx"), axis=0, tiled=True),
        lax.all_gather(w_out, ("dp", "ctx"), axis=0, tiled=True),
    )
    grad_attn_b = grad_residual.astype(jnp.bfloat16)
    grad_out_w = jnp.dot(mixed_b.T, grad_attn_b, preferred_element_type=jnp.float32)
    grad_mixed_b = (
        jnp.dot(grad_attn_b, out_w.T, preferred_element_type=jnp.float32)
        .astype(jnp.bfloat16)
        .reshape(tok_rows, GROUPS, repeat, HEAD_DIM)
    )
    row_delta = jnp.transpose(
        jnp.sum(grad_mixed_b.astype(jnp.float32) * mixed_f, axis=-1), (1, 2, 0)
    )

    def back_step(grad_query, entries):
        key_blk, place_blk, value_blk = entries
        scores, allowed = score_block(key_blk, place_blk)
        weights_f = jnp.where(allowed, jnp.exp(scores - log_total[..., None]), 0.0)
        weights_b = weights_f.astype(jnp.bfloat16)
        grad_value = jnp.einsum(
            "grij,igrd->jgd", weights_b, grad_mixed_b, preferred_element_type=jnp.float32
        )
        grad_prob = jnp.einsum(
            "igrd,jgd->grij", grad_mixed_b, value_blk, preferred_element_type=jnp.float32
        )
        grad_score = (weights_f * (grad_prob - row_delta[..., None])).astype(jnp.bfloat16)
        grad_query = grad_query + jnp.einsum(
            "grij,jgd->igrd", grad_score, key_blk, preferred_element_type=jnp.float32
        )
        grad_key = (
            jnp.einsum("grij,igrd->jgd", grad_score, query_b, preferred_element_type=jnp.float32)
            * score_scale
        )
        return (
            grad_query,
            jnp.concatenate(
                [
                    grad_key.reshape(tok_rows, GROUPS * HEAD_DIM),
                    grad_value.reshape(tok_rows, GROUPS * HEAD_DIM),
                ],
                axis=1,
            ),
        )

    grad_query, kv_terms = lax.scan(
        back_step,
        jnp.zeros((tok_rows, GROUPS, repeat, HEAD_DIM), jnp.float32),
        (key_blocks, place_blocks, value_blocks),
    )
    grad_query = grad_query * score_scale
    kv_own = lax.psum_scatter(
        kv_terms.reshape(blocks * tok_rows, 2 * GROUPS * HEAD_DIM).astype(jnp.bfloat16),
        "ctx",
        scatter_dimension=0,
        tiled=True,
    ).astype(jnp.float32)
    grad_key_own = kv_own[:, : GROUPS * HEAD_DIM].reshape(tok_rows, GROUPS, HEAD_DIM)
    grad_value_own = kv_own[:, GROUPS * HEAD_DIM :].reshape(tok_rows, GROUPS, HEAD_DIM)
    grad_qkv_f, grad_q_gain, grad_k_gain = pull_heads(
        (grad_query.reshape(tok_rows, HEADS, HEAD_DIM), grad_key_own, grad_value_own)
    )
    grad_qkv_b = grad_qkv_f.astype(jnp.bfloat16)
    grad_qkv_w = jnp.dot(h_attn.T, grad_qkv_b, preferred_element_type=jnp.float32)
    grad_h_attn = jnp.dot(grad_qkv_b, qkv_w.T, preferred_element_type=jnp.float32)
    grad_here_part, grad_attn_gain = pull_attn(grad_h_attn)
    grad_inputs = (grad_residual + grad_here_part).astype(jnp.bfloat16)[None]
    grad_qkv_own, grad_out_own = (
        lax.psum_scatter(grad_qkv_w, ("dp", "ctx"), scatter_dimension=0, tiled=True),
        lax.psum_scatter(grad_out_w, ("dp", "ctx"), scatter_dimension=0, tiled=True),
    )
    gain_attn, gain_query, gain_key, gain_ffn = lax.psum(
        (grad_attn_gain, grad_q_gain, grad_k_gain, grad_ffn_gain), ("dp", "ctx")
    )
    return (
        layer_output,
        grad_inputs,
        gain_attn,
        grad_qkv_own,
        gain_query,
        gain_key,
        grad_out_own,
        gain_ffn,
        grad_gateup_own,
        grad_down_own,
    )


def per_device_fast(
    inputs, places, cotangent, attn_gain, w_qkv, q_gain, k_gain, w_out, ffn_gain, w_gateup, w_down
):
    tok_rows, width = inputs.shape[1:]
    repeat = HEADS // GROUPS
    score_scale = HEAD_DIM ** (-0.5)
    blocks = lax.axis_size("ctx")
    own_places = places[0]
    half = HEAD_DIM // 2
    spot = jnp.arange(128)
    frequency = jnp.exp((spot % half).astype(f32) * (-2.0 * math.log(10000.0) / HEAD_DIM))
    angles = own_places.astype(f32)[:, None] * frequency[None, :]
    cosine = jnp.cos(angles)
    sine = jnp.where(spot % HEAD_DIM < half, -1.0, 1.0) * jnp.sin(angles)
    block_row = (own_places // 128)[None, :]
    (layer_output, h_attn, qkv_all, q2, kvb, linv, mixed_f, mixed_b, residual, h_ffn, act_b, grad_gu_b, qkv_w, out_w, gateup_w) = forward(
        inputs[0], cotangent[0], block_row, cosine, sine, attn_gain[None], jnp.tile(q_gain, 2)[None], jnp.tile(k_gain, 2)[None], ffn_gain[None],
        w_qkv, w_out, w_down, w_gateup, blocks)
    qkv_w, out_w, gateup_w = [w.reshape(-1, w.shape[-1]) for w in (qkv_w, out_w, gateup_w)]
    layer_output = layer_output[None]
    core = lax.axis_index("ctx") % 2

    def both(array):
        other = lax.ppermute(array, "ctx", [(i, i ^ 1) for i in range(lax.axis_size("ctx"))])
        return jnp.concatenate([array, other], axis=0)

    def grad_half(left, right, rows):
        left = both(left).reshape(2 * tok_rows, -1, 2, rows)
        left = lax.dynamic_index_in_dim(left, core, 2, keepdims=False).reshape(2 * tok_rows, -1)
        grad = jnp.dot(left.T, both(right), preferred_element_type=jnp.float32)
        return grad.astype(jnp.bfloat16).reshape(NZ, 2, 2, rows, right.shape[-1])

    here_f = inputs[0].astype(f32)
    _, pull_attn = jax.vjp(norm_rows, here_f, attn_gain)
    _, pull_ffn = jax.vjp(norm_rows, residual, ffn_gain)
    _, pull_heads = jax.vjp(lambda a, b, c: project_heads(a, own_places, b, c), qkv_all, q_gain, k_gain)
    query_b = jnp.transpose((q2[:, :tok_rows] + q2[:, tok_rows:]) * 8, (1, 0, 2)).reshape(tok_rows, GROUPS, repeat, HEAD_DIM)
    kvf = kvb.reshape(blocks, tok_rows + 16, 512)
    key_blocks = kvf[:, :tok_rows, :256].reshape(blocks, tok_rows, GROUPS, HEAD_DIM)
    value_blocks = kvf[:, :tok_rows, 256:].reshape(blocks, tok_rows, GROUPS, HEAD_DIM)
    place_blocks = kvf[:, tok_rows, :256].astype(jnp.int32) * 128 + jnp.arange(256)[None] % 128
    log_total = -jnp.log(jnp.transpose(linv.reshape(tok_rows, GROUPS, repeat, HEAD_DIM)[..., 0], (1, 2, 0)))
    mixed_f = mixed_f.reshape(tok_rows, GROUPS, repeat, HEAD_DIM)

    def score_block(key_blk, place_blk):
        scores = (
            jnp.einsum("igrd,jgd->grij", query_b, key_blk, preferred_element_type=jnp.float32)
            * score_scale
        )
        allowed = place_blk[None, :] <= own_places[:, None]
        return (scores, allowed)

    grad_out = cotangent[0]
    grad_down = grad_half(act_b, grad_out, w_down.shape[0])
    grad_gateup = grad_half(h_ffn, grad_gu_b, w_gateup.shape[0])
    grad_h_ffn = jnp.dot(grad_gu_b, gateup_w.T, preferred_element_type=jnp.float32)
    grad_resid_part, grad_ffn_gain = pull_ffn(grad_h_ffn)
    grad_residual = grad_out.astype(jnp.float32) + grad_resid_part
    grad_attn_b = grad_residual.astype(jnp.bfloat16)
    grad_out_w = grad_half(mixed_b, grad_attn_b, w_out.shape[0])
    grad_mixed_b = (
        jnp.dot(grad_attn_b, out_w.T, preferred_element_type=jnp.float32)
        .astype(jnp.bfloat16)
        .reshape(tok_rows, GROUPS, repeat, HEAD_DIM)
    )
    row_delta = jnp.transpose(
        jnp.sum(grad_mixed_b.astype(jnp.float32) * mixed_f, axis=-1), (1, 2, 0)
    )

    def back_step(grad_query, entries):
        key_blk, place_blk, value_blk = entries
        scores, allowed = score_block(key_blk, place_blk)
        weights_f = jnp.where(allowed, jnp.exp(scores - log_total[..., None]), 0.0)
        weights_b = weights_f.astype(jnp.bfloat16)
        grad_value = jnp.einsum(
            "grij,igrd->jgd", weights_b, grad_mixed_b, preferred_element_type=jnp.float32
        )
        grad_prob = jnp.einsum(
            "igrd,jgd->grij", grad_mixed_b, value_blk, preferred_element_type=jnp.float32
        )
        grad_score = (weights_f * (grad_prob - row_delta[..., None])).astype(jnp.bfloat16)
        grad_query = grad_query + jnp.einsum(
            "grij,jgd->igrd", grad_score, key_blk, preferred_element_type=jnp.float32
        )
        grad_key = (
            jnp.einsum("grij,igrd->jgd", grad_score, query_b, preferred_element_type=jnp.float32)
            * score_scale
        )
        return (
            grad_query,
            jnp.concatenate(
                [
                    grad_key.reshape(tok_rows, GROUPS * HEAD_DIM),
                    grad_value.reshape(tok_rows, GROUPS * HEAD_DIM),
                ],
                axis=1,
            ),
        )

    grad_query, kv_terms = lax.scan(
        back_step,
        jnp.zeros((tok_rows, GROUPS, repeat, HEAD_DIM), jnp.float32),
        (key_blocks, place_blocks, value_blocks),
    )
    grad_query = grad_query * score_scale
    kv_own = lax.psum_scatter(
        kv_terms.reshape(blocks * tok_rows, 2 * GROUPS * HEAD_DIM).astype(jnp.bfloat16),
        "ctx",
        scatter_dimension=0,
        tiled=True,
    ).astype(jnp.float32)
    grad_key_own = kv_own[:, : GROUPS * HEAD_DIM].reshape(tok_rows, GROUPS, HEAD_DIM)
    grad_value_own = kv_own[:, GROUPS * HEAD_DIM :].reshape(tok_rows, GROUPS, HEAD_DIM)
    grad_qkv_f, grad_q_gain, grad_k_gain = pull_heads(
        (grad_query.reshape(tok_rows, HEADS, HEAD_DIM), grad_key_own, grad_value_own)
    )
    grad_qkv_b = grad_qkv_f.astype(jnp.bfloat16)
    grad_qkv_w = grad_half(h_attn, grad_qkv_b, w_qkv.shape[0])
    grad_h_attn = jnp.dot(grad_qkv_b, qkv_w.T, preferred_element_type=jnp.float32)
    grad_here_part, grad_attn_gain = pull_attn(grad_h_attn)
    grad_inputs = (grad_residual + grad_here_part).astype(jnp.bfloat16)[None]
    grad_qkv_own, grad_out_own, grad_gateup_own, grad_down_own = scatter_all(
        (grad_qkv_w, grad_out_w, grad_gateup, grad_down), zfirst=(1,)
    )
    gain_attn, gain_query, gain_key, gain_ffn = lax.psum(
        (grad_attn_gain, grad_q_gain, grad_k_gain, grad_ffn_gain), ("dp", "ctx")
    )
    return (
        layer_output,
        grad_inputs,
        gain_attn,
        grad_qkv_own,
        gain_query,
        gain_key,
        grad_out_own,
        gain_ffn,
        grad_gateup_own,
        grad_down_own,
    )


def solution(mesh):
    in_specs = (
        P("dp", "ctx", None),
        P("dp", "ctx"),
        P("dp", "ctx", None),
        P(),
        P(("dp", "ctx"), None),
        P(),
        P(),
        P(("dp", "ctx"), None),
        P(),
        P(("dp", "ctx"), None),
        P(("dp", "ctx"), None),
    )
    out_specs = (
        P("dp", "ctx", None),
        P("dp", "ctx", None),
        P(),
        P(("dp", "ctx"), None),
        P(),
        P(),
        P(("dp", "ctx"), None),
        P(),
        P(("dp", "ctx"), None),
        P(("dp", "ctx"), None),
    )
    fast = dict(mesh.shape) == {"dp": 4, "ctx": 8}
    per_device = per_device_fast if fast else per_device_plain
    return jax.shard_map(
        per_device, mesh=mesh, in_specs=in_specs, out_specs=out_specs, check_vma=False
    )
```

```python
import functools
import math

import jax
import jax.numpy as jnp
from jax import lax
from jax.experimental import pallas as pl
from jax.experimental.pallas import tpu as pltpu
from jax.sharding import PartitionSpec as P

HEADS = 16
GROUPS = 4
HEAD_DIM = 64
FF = 1024
f32 = jnp.float32
bf16 = jnp.bfloat16
MESH = pl.DeviceIdType.MESH
NZ = 4
EPS = 1e-06


class Place:
    def __init__(self):
        self.z = lax.axis_index("dp")
        spot = lax.axis_index("ctx")
        self.core = spot % 2
        self.x = (spot // 2) % 2
        self.y = spot // 4

    def at(self, z=None, y=None, x=None, core=None):
        z = self.z if z is None else z
        y = self.y if y is None else y
        x = self.x if x is None else x
        core = self.core if core is None else core
        return (z, y * 4 + x * 2 + core)

    def xn(self):
        return self.at(x=1 - self.x)

    def yn(self):
        return self.at(y=1 - self.y)

    def sn(self):
        return self.at(core=1 - self.core)

    def up(self):
        return self.at(z=self.z + 1)

    def down(self):
        return self.at(z=self.z - 1)


def barrier(pc):
    bar = pltpu.get_barrier_semaphore()

    def greet(device):
        pl.semaphore_signal(bar, inc=1, device_id=device, device_id_type=MESH)

    for device in (pc.xn(), pc.yn(), pc.sn()):
        greet(device)

    @pl.when(pc.z < NZ - 1)
    def _():
        greet(pc.up())

    @pl.when(pc.z > 0)
    def _():
        greet(pc.down())

    pl.semaphore_wait(bar, 3 + (1 - pc.z // (NZ - 1)) + (pc.z + NZ - 1) // NZ)


def far(z, i):
    m = z // 2
    zz = z + m * (3 - 2 * z)
    lo = 3 - i if i < 2 else (1 - zz if i == 2 else zz)
    return lo + m * (3 - 2 * lo)


def near(z, i):
    return far(z, NZ - 1 - i)


def remote(src, dst, dev, send, recv):
    return pltpu.make_async_remote_copy(
        src_ref=src, dst_ref=dst, send_sem=send, recv_sem=recv, device_id=dev, device_id_type=MESH
    )


def halves(rows):
    return pl.ds(0, rows // 2), pl.ds(rows // 2, rows // 2)


KZ, KX, KY, KD0, KD1, KS, KU = range(7)


class Gather:
    def __init__(self, pc, buf, send, recv):
        self.pc, self.buf, self.send, self.recv = pc, buf, send, recv
        self.h = halves(buf.shape[-2])

    def cp(self, idx, dev, ks, kr, slot):
        ref = self.buf.at[idx]
        return remote(ref, ref, dev, self.send.at[ks, slot], self.recv.at[kr, slot])

    def c_up(self, z0):
        p = self.pc
        return self.cp((z0, p.y, p.x, p.core), p.up(), KU, KZ, z0)

    def c_down(self, z0):
        p = self.pc
        return self.cp((z0, p.y, p.x, p.core), p.down(), KZ, KZ, z0)

    def c_x(self, z0):
        p = self.pc
        return self.cp((z0, p.y, p.x, p.core), p.xn(), KX, KX, z0)

    def c_y(self, z0):
        p = self.pc
        return self.cp((z0, p.y, p.x, p.core), p.yn(), KY, KY, z0)

    def c_d0(self, z0):
        p = self.pc
        return self.cp((z0, p.y, 1 - p.x, p.core, self.h[0]), p.yn(), KD0, KD0, z0)

    def c_d1(self, z0):
        p = self.pc
        return self.cp((z0, 1 - p.y, p.x, p.core, self.h[1]), p.xn(), KD1, KD1, z0)

    def c_s(self, z0):
        p = self.pc
        return self.cp((z0, slice(None), slice(None), p.core), p.sn(), KS, KS, z0)

    def plane_send(self, i):
        z0 = near(self.pc.z, i)
        self.c_x(z0).start()
        self.c_y(z0).start()

    def own_z(self):
        z = self.pc.z

        @pl.when(z < NZ - 1)
        def _():
            self.c_up(z).start()

        @pl.when(z > 0)
        def _():
            self.c_down(z).start()

    def z_event(self, i, plane=True):
        z = self.pc.z
        z0 = near(z, i)

        @pl.when(z0 < z)
        def _():
            self.c_up(z0).wait_recv()

            @pl.when(z < NZ - 1)
            def _():
                self.c_up(z0).start()

        @pl.when(z0 > z)
        def _():
            self.c_down(z0).wait_recv()

            @pl.when(z > 0)
            def _():
                self.c_down(z0).start()

        if plane:
            self.plane_send(i)

    def plane_event(self, i):
        z0 = near(self.pc.z, i)
        self.c_x(z0).wait_recv()
        self.c_d0(z0).start()
        self.c_y(z0).wait_recv()
        self.c_d1(z0).start()

    def core_event(self, i):
        z0 = near(self.pc.z, i)
        self.c_d0(z0).wait_recv()
        self.c_d1(z0).wait_recv()
        self.c_s(z0).start()

    def done_event(self, i):
        self.c_s(near(self.pc.z, i)).wait_recv()

    def finish(self):
        z = self.pc.z
        for z0 in range(NZ):
            for c in (self.c_x, self.c_y, self.c_d0, self.c_d1, self.c_s):
                c(z0).wait_send()

            @pl.when((z < NZ - 1) & (z0 <= z))
            def _():
                self.c_up(z0).wait_send()

            @pl.when((z > 0) & (z0 >= z))
            def _():
                self.c_down(z0).wait_send()


class GatherPlane:
    def __init__(self, pc, buf, send, recv):
        self.pc, self.buf, self.send, self.recv = pc, buf, send, recv
        self.h = halves(buf.shape[-2])

    def cp(self, idx, dev, s, r):
        ref = self.buf.at[idx]
        return remote(ref, ref, dev, self.send.at[s], self.recv.at[r])

    def yx(self, k):
        p = self.pc
        return (p.y if k < 2 else 1 - p.y), (p.x if k % 2 == 0 else 1 - p.x)

    def c_x(self):
        p = self.pc
        return self.cp((p.z, p.y, p.x, p.core), p.xn(), (KX, 0), (KX, 0))

    def c_y(self):
        p = self.pc
        return self.cp((p.z, p.y, p.x, p.core), p.yn(), (KY, 0), (KY, 0))

    def c_d0(self):
        p = self.pc
        return self.cp((p.z, p.y, 1 - p.x, p.core, self.h[0]), p.yn(), (KD0, 0), (KD0, 0))

    def c_d1(self):
        p = self.pc
        return self.cp((p.z, 1 - p.y, p.x, p.core, self.h[1]), p.xn(), (KD1, 0), (KD1, 0))

    def c_up(self, z0, k):
        p = self.pc
        y, x = self.yx(k)
        return self.cp((z0, y, x, p.core), p.up(), (10 + z0, k), (10 + z0, k))

    def c_down(self, z0, k):
        p = self.pc
        y, x = self.yx(k)
        return self.cp((z0, y, x, p.core), p.down(), (14 + z0, k), (10 + z0, k))

    def c_s(self, z0):
        p = self.pc
        return self.cp((z0, slice(None), slice(None), p.core), p.sn(), (KS, z0), (KS, z0))

    def z_send(self, k):
        z = self.pc.z

        @pl.when(z < NZ - 1)
        def _():
            self.c_up(z, k).start()

        @pl.when(z > 0)
        def _():
            self.c_down(z, k).start()

    def own_plane(self):
        self.c_x().start()
        self.c_y().start()

    def own_z(self):
        self.z_send(0)

    def plane_event(self):
        self.c_x().wait_recv()
        self.c_d0().start()
        self.z_send(1)
        self.c_y().wait_recv()
        self.c_d1().start()
        self.z_send(2)

    def diag_event(self):
        self.c_d0().wait_recv()
        self.c_d1().wait_recv()
        self.z_send(3)
        self.c_s(self.pc.z).start()

    def z_event(self, i, k):
        z = self.pc.z
        z0 = near(z, i)

        @pl.when(z0 < z)
        def _():
            self.c_up(z0, k).wait_recv()

            @pl.when(z < NZ - 1)
            def _():
                self.c_up(z0, k).start()

        @pl.when(z0 > z)
        def _():
            self.c_down(z0, k).wait_recv()

            @pl.when(z > 0)
            def _():
                self.c_down(z0, k).start()

    def core_event(self, i):
        self.c_s(near(self.pc.z, i)).start()

    def done_event(self, i):
        self.c_s(near(self.pc.z, i)).wait_recv()

    def finish(self):
        z = self.pc.z
        for c in (self.c_x, self.c_y, self.c_d0, self.c_d1):
            c().wait_send()
        for z0 in range(NZ):
            self.c_s(z0).wait_send()
            for k in range(4):

                @pl.when((z < NZ - 1) & (z0 <= z))
                def _():
                    self.c_up(z0, k).wait_send()

                @pl.when((z > 0) & (z0 >= z))
                def _():
                    self.c_down(z0, k).wait_send()


class GatherSequence:
    def __init__(self, pc, buf, send, recv):
        self.pc, self.buf, self.send, self.recv = pc, buf, send, recv
        rows = buf.shape[-2]
        self.h = (pl.ds(0, 128), pl.ds(128, rows - 128))

    def cp(self, idx, dev, k):
        ref = self.buf.at[idx]
        return remote(ref, ref, dev, self.send.at[k], self.recv.at[k])

    def c_x(self):
        p = self.pc
        return self.cp((p.y, p.x, p.core), p.xn(), 0)

    def c_y(self):
        p = self.pc
        return self.cp((p.y, p.x, p.core), p.yn(), 1)

    def c_d0(self):
        p = self.pc
        return self.cp((p.y, 1 - p.x, p.core, self.h[0]), p.yn(), 2)

    def c_d1(self):
        p = self.pc
        return self.cp((1 - p.y, p.x, p.core, self.h[1]), p.xn(), 3)

    def c_s(self, k):
        p = self.pc
        y, x = (p.y if k < 2 else 1 - p.y), (p.x if k % 2 == 0 else 1 - p.x)
        return self.cp((y, x, p.core), p.sn(), 4 + k)

    def own(self):
        for c in (self.c_x(), self.c_y(), self.c_s(0)):
            c.start()

    def plane_event(self):
        self.c_x().wait_recv()
        self.c_d0().start()
        self.c_s(1).start()
        self.c_y().wait_recv()
        self.c_d1().start()
        self.c_s(2).start()

    def core_event(self):
        self.c_d0().wait_recv()
        self.c_d1().wait_recv()
        self.c_s(3).start()

    def done_event(self):
        for k in range(4):
            self.c_s(k).wait_recv()

    def finish(self):
        for c in (self.c_x(), self.c_y(), self.c_d0(), self.c_d1()):
            c.wait_send()
        for k in range(4):
            self.c_s(k).wait_send()


LOG2E = math.log2(math.e)
VMEM = pltpu.VMEM


def dot(a, b):
    return jnp.dot(a, b, preferred_element_type=f32)


def dot_t(a, b):
    return lax.dot_general(a, b, (((1,), (1,)), ((), ())), preferred_element_type=f32)


def lanes(shape):
    return lax.broadcasted_iota(jnp.int32, shape, 1)


def roll_half(v):
    return pltpu.roll(v, 64, 1)


def swap_rot(v):
    first = lanes(v.shape) % 64 < 32
    return jnp.where(first, pltpu.roll(v, 96, 1), pltpu.roll(v, 32, 1))


def head_sums(v):
    row = lax.broadcasted_iota(jnp.int32, (128, 128), 0) // 64
    col = lax.broadcasted_iota(jnp.int32, (128, 128), 1) // 64
    ones = jnp.where(row == col, 1.0, 0.0).astype(bf16)
    high = v.astype(bf16)
    low = (v - high.astype(f32)).astype(bf16)
    return dot(high, ones) + dot(low, ones)


def cols(i, width):
    return pl.ds(pl.multiple_of(i * width, width), width)


def norm_into(src, gain, dst):
    def body(i, _):
        rows = pl.ds(pl.multiple_of(i * 32, 32), 32)
        v = src[rows, :].astype(f32)
        scale = lax.rsqrt(jnp.mean(v * v, axis=-1, keepdims=True) + EPS)
        dst[rows, :] = (v * scale * gain[...]).astype(dst.dtype)
        return 0

    lax.fori_loop(0, src.shape[0] // 32, body, 0)


def ticked(tick, first, events):
    for k, event in enumerate(events):
        if event is not None:

            @pl.when(tick == first + k)
            def _(event=event):
                event()


def turn(src, rows, core, mine, theirs):
    def body(t, _):
        v = jnp.transpose(src[:, cols(t, 128)])
        for k in range(64 // rows):
            a, b = v[2 * k * rows : (2 * k + 1) * rows], v[(2 * k + 1) * rows : (2 * k + 2) * rows]
            own, other = jnp.where(core == 0, a, b), jnp.where(core == 0, b, a)
            spot = t * (64 // rows) + k
            mine[spot, :, pl.ds(0, v.shape[1])] = own
            theirs[spot, pl.ds(0, rows), :] = other
        return 0

    lax.fori_loop(0, src.shape[1] // 128, body, 0)


def forward_kernel(dims, *refs):
    (tok, width, n_dev, heads_w, kv_w, ff) = dims
    (
        x_ref, cot_ref, hi_ref, cos_ref, sin_ref, g_attn, g_q, g_k, g_ffn,
        s_qkv, s_out, s_down, s_gu,
        o_y, o_tattn, o_tmix, o_tffn, o_tact, o_cot, o_ggu, o_kv, o_q2, o_linv, o_mixf, o_res,
        o_kk, o_va, o_mask, o_wqkv, o_wout, o_wgu,
        w_qkv, w_out, w_down, w_gu, kk, va, mask, mask_t, o2, gu, gact,
        y_ref, hattn_ref, qkv_ref, q2_ref, kvb, linv_ref, mixf_ref, mixb_ref, res_ref, hffn_ref,
        act_ref, cot2, ggu2, t_attn, t_mix, t_ffn, t_act, turn_a, turn_b,
        send, recv, kv_send, kv_recv, lsem, osem, ex_send, ex_recv,
    ) = refs
    pc = Place()
    shards = (s_qkv, s_out, s_down, s_gu)
    bufs = (w_qkv, w_out, w_down, w_gu)
    local = [
        pltpu.make_async_copy(s, b.at[pc.z, pc.y, pc.x, pc.core], lsem.at[k])
        for k, (s, b) in enumerate(zip(shards, bufs))
    ]
    for c in local:
        c.start()
    barrier(pc)
    for c in local:
        c.wait()
    qkv = Gather(pc, w_qkv, send.at[0], recv.at[0])
    out = GatherPlane(pc, w_out, send.at[1], recv.at[1])
    down = Gather(pc, w_down, send.at[2], recv.at[2])
    gateup = Gather(pc, w_gu, send.at[3], recv.at[3])
    seq = GatherSequence(pc, kvb, kv_send, kv_recv)
    part = functools.partial
    z = pc.z
    emitted = []

    def emit(src, dst):
        c = pltpu.make_async_copy(src, dst, osem.at[len(emitted)])
        emitted.append(c)
        c.start()

    def exchange(k, src, dst):
        return remote(src, dst, pc.sn(), ex_send.at[k], ex_recv.at[k])

    back = pl.ds(tok, tok)
    sent_cot = exchange(0, cot_ref, cot2.at[back, :])
    sent_attn = exchange(1, turn_a, t_attn.at[:, :, back])
    sent_mix = exchange(2, turn_b.at[:, pl.ds(0, s_out.shape[0]), :], t_mix.at[:, :, back])
    sent_ffn = exchange(3, turn_a, t_ffn.at[:, :, back])
    sent_act = exchange(4, turn_b.at[:, pl.ds(0, s_down.shape[0]), :], t_act.at[:, :, back])
    sent_ggu = exchange(5, ggu2.at[pl.ds(0, tok), :], ggu2.at[back, :])

    qkv.own_z()
    qkv.plane_send(0)
    norm_into(x_ref, g_attn, hattn_ref)
    qkv.z_event(1)
    sent_cot.start()
    cot2[pl.ds(0, tok), :] = cot_ref[...]
    turn(hattn_ref, s_qkv.shape[0], pc.core, t_attn, turn_a)
    sent_attn.start()
    qkv.plane_event(0)
    qkv.z_event(2)
    out.own_plane()
    out.own_z()
    down.own_z()
    gateup.own_z()
    qkv.z_event(3)
    qkv.plane_event(1)
    qkv.core_event(0)
    down.plane_send(0)
    gateup.plane_send(0)
    qkv.plane_event(2)
    qkv.core_event(1)
    down.z_event(1)
    gateup.z_event(1)
    qkv.plane_event(3)
    out.plane_event()

    def qkv_step(i):
        qkv.done_event(i)
        z0 = near(z, i)
        depth = width // NZ

        def body(n, _):
            c = cols(n, 256)
            w = w_qkv[z0, :, :, :, :, c].reshape(depth, 256)
            prod = dot(hattn_ref[:, cols(z0, depth)], w)
            if i == 0:
                qkv_ref[:, c] = prod
            else:
                qkv_ref[:, c] += prod
            return 0

        lax.fori_loop(0, qkv_ref.shape[1] // 256, body, 0)

    qkv_step(0)
    qkv.core_event(2)
    qkv_step(1)
    qkv.core_event(3)
    down.plane_event(0)
    gateup.plane_event(0)
    qkv_step(2)
    qkv_step(3)

    low = lanes((tok, 128)) < 64

    def head_tile(t, gain):
        u = qkv_ref[:, cols(t, 128)]
        n = u * lax.rsqrt(head_sums(u * u) * (1.0 / 64) + EPS) * gain[...]
        return n * cos_ref[...] + swap_rot(n) * sin_ref[...]

    for t in range(kv_w // 128):
        kvb[pc.y, pc.x, pc.core, pl.ds(0, tok), pl.ds(t * 128, 128)] = head_tile(
            heads_w // 128 + t, g_k
        ).astype(bf16)
    kvb[pc.y, pc.x, pc.core, pl.ds(0, tok), pl.ds(kv_w, kv_w)] = qkv_ref[
        :, pl.ds(heads_w + kv_w, kv_w)
    ].astype(bf16)
    blocks_row = jnp.broadcast_to(hi_ref[...], (16, tok)).astype(bf16)
    kvb[pc.y, pc.x, pc.core, pl.ds(tok, 16), pl.ds(0, tok)] = blocks_row
    kvb[pc.y, pc.x, pc.core, pl.ds(tok, 16), pl.ds(tok, tok)] = blocks_row
    seq.own()

    def query_tile(t, _):
        q = (head_tile(t, g_q) * 0.125).astype(bf16)
        zero = jnp.zeros_like(q)
        q2_ref[t, pl.ds(0, tok), :] = jnp.where(low, q, zero)
        q2_ref[t, pl.ds(tok, tok), :] = jnp.where(low, zero, q)
        return 0

    lax.fori_loop(0, heads_w // 128, query_tile, 0)
    emit(qkv_ref, o_kv)
    emit(q2_ref, o_q2)
    emit(w_qkv, o_wqkv)
    sent_cot.wait_recv()
    emit(cot2, o_cot)
    sent_attn.wait_recv()
    emit(t_attn, o_tattn)

    down.z_event(2)
    gateup.z_event(2)
    out.diag_event()
    down.plane_event(1)
    gateup.plane_event(1)
    seq.plane_event()
    down.z_event(3)
    for j in range(4):
        out.z_event(1, j)
    gateup.z_event(3)
    down.core_event(0)
    gateup.core_event(0)
    seq.core_event()
    seq.done_event()

    def unpack(b, _):
        y, x, c = b // 4, (b // 2) % 2, b % 2
        rows = pl.ds(pl.multiple_of(b * tok, tok), tok)
        for t in range(kv_w // 128):
            k = kvb[y, x, c, pl.ds(0, tok), pl.ds(t * 128, 128)].astype(f32)
            v = kvb[y, x, c, pl.ds(0, tok), pl.ds(kv_w + t * 128, 128)].astype(f32)
            k_r, v_r = roll_half(k), roll_half(v)
            kk[2 * t, rows, :] = jnp.where(low, k, k_r).astype(bf16)
            kk[2 * t + 1, rows, :] = jnp.where(low, k_r, k).astype(bf16)
            va[2 * t, rows, :] = jnp.where(low, v, 1.0).astype(bf16)
            va[2 * t + 1, rows, :] = jnp.where(low, v_r, 1.0).astype(bf16)
        step = tok // 2
        key_hi = kvb[y, x, c, pl.ds(tok, 16), pl.ds(0, tok)].astype(f32)[:1, :]
        for a in range(2):
            own = hi_ref[:, a * step : (a + 1) * step].astype(f32)
            row = lax.broadcasted_iota(jnp.int32, (step, step), 0).astype(f32)
            col = lanes((step, step)).astype(f32)
            for d in range(2):
                theirs = key_hi[:, d * step : (d + 1) * step]
                gap = (own - theirs) * float(step) + row - col
                place = pl.ds(pl.multiple_of(b * tok + d * step, step), step)
                mask[pl.ds(a * step, step), place] = jnp.where(gap >= 0, 1.0, 0.0).astype(bf16)
                gap = (own - theirs) * float(step) + col - row
                mask_t[place, pl.ds(a * step, step)] = jnp.where(gap >= 0, 1.0, 0.0).astype(bf16)
        return 0

    lax.fori_loop(0, n_dev, unpack, 0)
    emit(kk, o_kk)
    emit(va, o_va)
    emit(mask_t, o_mask)

    events = [part(out.z_event, 2, j) for j in range(4)] + [
        part(out.core_event, 1), part(down.plane_event, 2), part(gateup.plane_event, 2),
        part(down.core_event, 1), part(gateup.core_event, 1),
    ] + [part(out.z_event, 3, j) for j in range(4)] + [
        part(out.core_event, 2),
        part(down.plane_event, 3), part(gateup.plane_event, 3),
        part(down.core_event, 2), part(gateup.core_event, 2), part(out.core_event, 3),
    ]
    chunk = 512
    n_chunk = n_dev * tok // chunk

    def attend(tick, _):
        t, kc = tick // n_chunk, tick % n_chunk
        g = t // 2
        rows = pl.ds(pl.multiple_of(kc * chunk, chunk), chunk)
        s = dot_t(q2_ref[t], kk[g, rows, :])
        e = jnp.exp2(s * LOG2E).astype(bf16).reshape(2, tok, chunk) * mask[:, rows][None]
        o = dot(e.reshape(2 * tok, chunk), va[g, rows, :])

        @pl.when(kc == 0)
        def _():
            o2[...] = o

        @pl.when(kc > 0)
        def _():
            o2[...] += o

        @pl.when(kc == n_chunk - 1)
        def _():
            even, odd = o2[pl.ds(0, tok), :], o2[pl.ds(tok, tok), :]
            total = jnp.where(low, roll_half(even), odd)
            inv = 1.0 / total
            mixed = jnp.where(low, even, roll_half(odd)) * inv
            linv_ref[:, cols(t, 128)] = inv
            mixf_ref[:, cols(t, 128)] = mixed
            mixb_ref[:, cols(t, 128)] = mixed.astype(bf16)

        ticked(tick, 2, events)
        return 0

    lax.fori_loop(0, heads_w // 128 * n_chunk, attend, 0)

    emit(linv_ref, o_linv)
    emit(mixf_ref, o_mixf)
    turn(mixb_ref, s_out.shape[0], pc.core, t_mix, turn_b)
    sent_mix.start()
    for i in range(NZ):
        out.done_event(i)
    emit(w_out, o_wout)

    def residual_step(n, _):
        c = cols(n, 256)
        w = w_out[:, :, :, :, :, c].reshape(heads_w, 256)
        res_ref[:, c] = x_ref[:, c].astype(f32) + dot(mixb_ref[...], w)
        return 0

    lax.fori_loop(0, width // 256, residual_step, 0)
    norm_into(res_ref, g_ffn, hffn_ref)
    emit(res_ref, o_res)
    sent_mix.wait_recv()
    emit(t_mix, o_tmix)
    sent_attn.wait_send()
    turn(hffn_ref, s_gu.shape[0], pc.core, t_ffn, turn_a)
    sent_ffn.start()

    def gateup_step(i):
        gateup.done_event(i)
        z0 = near(z, i)
        depth = width // NZ

        def body(n, _):
            c = cols(n, 256)
            w = w_gu[z0, :, :, :, :, c].reshape(depth, 256)
            prod = dot(hffn_ref[:, cols(z0, depth)], w)
            if i == 0:
                gu[:, c] = prod
            else:
                gu[:, c] += prod
            return 0

        lax.fori_loop(0, 2 * ff // 256, body, 0)

    def grad_act_step(i):
        down.done_event(i)
        z0 = near(z, i)
        depth = ff // NZ
        gact[:, cols(z0, depth)] = dot_t(cot_ref[...], w_down[z0].reshape(depth, width))

    gateup_step(0)
    grad_act_step(0)
    gateup_step(1)
    grad_act_step(1)
    down.core_event(3)
    gateup_step(2)
    grad_act_step(2)
    gateup.core_event(3)
    grad_act_step(3)
    gateup_step(3)

    def gate_step(n, _):
        c = cols(n, 256)
        c2 = cols(n + ff // 256, 256)
        gate, up, grad = gu[:, c], gu[:, c2], gact[:, c]
        sig = 1.0 / (1.0 + jnp.exp(-gate))
        silu = gate * sig
        act_ref[:, c] = (silu * up).astype(bf16)
        ggu2[pl.ds(0, tok), c] = (grad * up * (sig * (1.0 + gate * (1.0 - sig)))).astype(bf16)
        ggu2[pl.ds(0, tok), c2] = (grad * silu).astype(bf16)
        return 0

    lax.fori_loop(0, ff // 256, gate_step, 0)
    sent_ggu.start()
    sent_mix.wait_send()
    turn(act_ref, s_down.shape[0], pc.core, t_act, turn_b)
    sent_act.start()
    emit(w_gu, o_wgu)
    sent_ffn.wait_recv()
    emit(t_ffn, o_tffn)

    def output_step(n, _):
        c = cols(n, 256)
        w = w_down[:, :, :, :, :, c].reshape(ff, 256)
        y_ref[:, c] = (res_ref[:, c] + dot(act_ref[...], w)).astype(bf16)
        return 0

    lax.fori_loop(0, width // 256, output_step, 0)
    emit(y_ref, o_y)
    sent_ggu.wait_recv()
    emit(ggu2, o_ggu)
    sent_act.wait_recv()
    emit(t_act, o_tact)
    for g in (qkv, out, down, gateup, seq):
        g.finish()
    for c in (sent_cot, sent_ffn, sent_act, sent_ggu):
        c.wait_send()
    for c in emitted:
        c.wait()


def forward(x, cot, blocks, cosine, sine, g_attn, g_q, g_k, g_ffn, s_qkv, s_out, s_down, s_gu, n_dev):
    tok, width = x.shape
    heads_w, kv_w = HEADS * HEAD_DIM, GROUPS * HEAD_DIM
    ff = s_down.shape[0] * n_dev * NZ
    length = n_dev * tok
    tiles = heads_w // 128
    shape = jax.ShapeDtypeStruct
    seven = [(NZ, 2, 2, 2) + s.shape for s in (s_qkv, s_out, s_down, s_gu)]
    qkv_rows, out_rows, down_rows, gu_rows = [s.shape[0] for s in (s_qkv, s_out, s_down, s_gu)]
    spots = n_dev * NZ // 2
    kv_buf = ((2, 2, 2, tok + 16, 2 * kv_w), bf16)
    turned = [((spots, r, 2 * tok), bf16) for r in (qkv_rows, out_rows, gu_rows, down_rows)]
    keep = [
        ((tok, width), bf16),
        *turned,
        ((2 * tok, width), bf16),
        ((2 * tok, 2 * ff), bf16),
        ((tok, s_qkv.shape[1]), f32),
        ((tiles, 2 * tok, 128), bf16),
        ((tok, heads_w), f32),
        ((tok, heads_w), f32),
        ((tok, width), f32),
        ((GROUPS, length, 128), bf16),
        ((GROUPS, length, 128), bf16),
        ((length, tok), bf16),
        (seven[0], bf16),
        (seven[1], bf16),
        (seven[3], bf16),
    ]
    outs = [shape(*k) for k in keep]
    vm = pl.BlockSpec(memory_space=VMEM)
    anyw = pl.BlockSpec(memory_space=pl.ANY)
    dma = pltpu.SemaphoreType.DMA
    flops = 2 * tok * (width * (s_qkv.shape[1] + heads_w + 2 * ff + 2 * ff) + 2 * heads_w * length)
    return pl.pallas_call(
        functools.partial(forward_kernel, (tok, width, n_dev, heads_w, kv_w, ff)),
        out_shape=outs,
        in_specs=[vm] * 9 + [anyw] * 4,
        out_specs=[anyw] * len(outs),
        scratch_shapes=[VMEM(s, bf16) for s in seven]
        + [
            VMEM((GROUPS, length, 128), bf16),
            VMEM((GROUPS, length, 128), bf16),
            VMEM((tok, length), bf16),
            VMEM((length, tok), bf16),
            VMEM((2 * tok, 128), f32),
            VMEM((tok, 2 * ff), f32),
            VMEM((tok, ff), f32),
            VMEM((tok, width), bf16),
            VMEM((tok, width), bf16),
            VMEM((tok, s_qkv.shape[1]), f32),
            VMEM((tiles, 2 * tok, 128), bf16),
            VMEM(*kv_buf),
            VMEM((tok, heads_w), f32),
            VMEM((tok, heads_w), f32),
            VMEM((tok, heads_w), bf16),
            VMEM((tok, width), f32),
            VMEM((tok, width), bf16),
            VMEM((tok, ff), bf16),
            VMEM((2 * tok, width), bf16),
            VMEM((2 * tok, 2 * ff), bf16),
            *[VMEM(*t) for t in turned],
            VMEM((spots, qkv_rows, tok), bf16),
            VMEM((spots, out_rows, tok), bf16),
            dma((4, 18, NZ)),
            dma((4, 14, NZ)),
            dma((8,)),
            dma((8,)),
            dma((4,)),
            dma((len(outs),)),
            dma((6,)),
            dma((6,)),
        ],
        compiler_params=pltpu.CompilerParams(
            collective_id=0, has_side_effects=True, vmem_limit_bytes=60 << 20
        ),
        cost_estimate=pl.CostEstimate(flops=flops, bytes_accessed=50 << 20, transcendentals=0),
        name="forward",
    )(x, cot, blocks, cosine, sine, g_attn, g_q, g_k, g_ffn, s_qkv, s_out, s_down, s_gu)


SD0, SD1, SX0, SX1, SY0, SY1, SA, SB = range(8)


class PlaneSum:
    def plane_setup(self, pc, rd, rx, ry, send, recv):
        self.pc, self.rd, self.rx, self.ry, self.send, self.recv = pc, rd, rx, ry, send, recv

    def cp(self, src, dst, dev, k, s):
        return remote(src, dst, dev, self.send.at[k, s], self.recv.at[k, s])

    def d0(self, s):
        p = self.pc
        return self.cp(self.piece(s, 1 - p.y, 1 - p.x, 0), self.rd.at[s, 0], p.yn(), SD0, s)

    def d1(self, s):
        p = self.pc
        return self.cp(self.piece(s, 1 - p.y, 1 - p.x, 1), self.rd.at[s, 1], p.xn(), SD1, s)

    def x1(self, s):
        p = self.pc
        return self.cp(self.piece(s, p.y, 1 - p.x, 1), self.rx.at[s, 1], p.xn(), SX1, s)

    def y0(self, s):
        p = self.pc
        return self.cp(self.piece(s, 1 - p.y, p.x, 0), self.ry.at[s, 0], p.yn(), SY0, s)

    def x0(self, s):
        return self.cp(self.rd.at[s, 0], self.rx.at[s, 0], self.pc.xn(), SX0, s)

    def y1(self, s):
        return self.cp(self.rd.at[s, 1], self.ry.at[s, 1], self.pc.yn(), SY1, s)

    def plane_first(self, s):
        for c in (self.d0, self.d1, self.x1, self.y0):
            c(s).start()

    def plane_second(self, s):
        p = self.pc
        self.d0(s).wait_recv()
        self.rd[s, 0] = self.rd[s, 0] + self.piece(s, p.y, 1 - p.x, 0)[...]
        self.x0(s).start()
        self.d1(s).wait_recv()
        self.rd[s, 1] = self.rd[s, 1] + self.piece(s, 1 - p.y, p.x, 1)[...]
        self.y1(s).start()

    def plane_arrived(self, s):
        for c in (self.x1, self.y0, self.x0, self.y1):
            c(s).wait_recv()

    def plane_total(self, s, k):
        p = self.pc
        own = self.piece(s, p.y, p.x, k)[...].astype(f32)
        return own + self.rx[s, k].astype(f32) + self.ry[s, k].astype(f32)

    def plane_finish(self, s):
        for c in (self.d0, self.d1, self.x1, self.y0, self.x0, self.y1):
            c(s).wait_send()


class Scatter(PlaneSum):
    def __init__(self, pc, part, bufs, out, send, recv):
        rd, rx, ry, self.zz = bufs
        self.plane_setup(pc, rd, rx, ry, send, recv)
        self.part, self.out = part, out
        self.h = halves(part.shape[-2])

    @staticmethod
    def scratch(rows, columns):
        half = VMEM((NZ, 2, rows // 2, columns), bf16)
        return [half, half, half, VMEM((NZ + 1, 2, rows // 2, columns), bf16)]

    def piece(self, s, y, x, k):
        return self.part.at[s, y, x, self.h[k]]

    def down(self, zp):
        return self.cp(self.rx.at[zp], self.zz.at[zp], self.pc.down(), SA, zp)

    def up(self, zp):
        gap = zp - (self.pc.z + 1)
        spot = zp + (1 - (gap + NZ - 1) // NZ) * (NZ - zp)
        return self.cp(self.rx.at[zp], self.zz.at[spot], self.pc.up(), SB, zp)

    def first(self, i):
        self.plane_first(far(self.pc.z, i))

    def d_event(self, i):
        self.plane_second(far(self.pc.z, i))

    def xy_event(self, i):
        zp = far(self.pc.z, i)
        self.plane_arrived(zp)
        for k in range(2):
            self.rx[zp, k] = self.plane_total(zp, k).astype(bf16)

    def z_event(self, i):
        z = self.pc.z
        zp = far(z, i)

        @pl.when(zp < z)
        def _():
            @pl.when(z < NZ - 1)
            def _():
                self.down(zp).wait_recv()
                self.rx[zp] = self.rx[zp] + self.zz[zp]

            self.down(zp).start()

        @pl.when(zp > z)
        def _():
            @pl.when(z > 0)
            def _():
                self.up(zp).wait_recv()
                self.rx[zp] = self.rx[zp] + self.zz[zp]

            self.up(zp).start()

    def final(self):
        z = self.pc.z
        self.plane_arrived(z)
        for k in range(2):
            self.out[self.h[k], :] = self.plane_total(z, k)

        @pl.when(z < NZ - 1)
        def _():
            self.down(z).wait_recv()
            for k in range(2):
                self.out[self.h[k], :] += self.zz[z, k].astype(f32)

        @pl.when(z > 0)
        def _():
            self.up(z).wait_recv()
            for k in range(2):
                self.out[self.h[k], :] += self.zz[NZ, k].astype(f32)

    def finish(self):
        z = self.pc.z
        for zp in range(NZ):
            self.plane_finish(zp)

            @pl.when(zp < z)
            def _():
                self.down(zp).wait_send()

            @pl.when(zp > z)
            def _():
                self.up(zp).wait_send()


class ScatterZ(PlaneSum):
    def __init__(self, pc, part, bufs, out, send, recv):
        rd, rx, ry, self.zz, self.sm = bufs
        self.plane_setup(pc, rd, rx, ry, send, recv)
        self.part, self.out = part, out
        self.h = halves(part.shape[-2])

    @staticmethod
    def scratch(rows, columns):
        half = VMEM((1, 2, rows // 2, columns), bf16)
        return [half, half, half, VMEM((NZ + 1, 4, rows, columns), bf16), VMEM((4, rows, columns), bf16)]

    def piece(self, s, y, x, k):
        return self.sm.at[y * 2 + x, self.h[k]]

    def down(self, zp, k, src):
        return self.cp(src, self.zz.at[zp, k], self.pc.down(), 8 + zp, k)

    def up(self, zp, k, src):
        gap = zp - (self.pc.z + 1)
        spot = zp + (1 - (gap + NZ - 1) // NZ) * (NZ - zp)
        return self.cp(src, self.zz.at[spot, k], self.pc.up(), 12 + zp, k)

    def first(self, i):
        z = self.pc.z
        zp = far(z, i)
        for k in range(4):
            src = self.part.at[zp, k // 2, k % 2]

            @pl.when((z == NZ - 1) & (zp < z))
            def _():
                self.down(zp, k, src).start()

            @pl.when((z == 0) & (zp > z))
            def _():
                self.up(zp, k, src).start()

    def z_event(self, i, k):
        z = self.pc.z
        zp = far(z, i)
        held = self.zz.at[zp, k]

        @pl.when((zp < z) & (z < NZ - 1))
        def _():
            self.down(zp, k, held).wait_recv()
            self.zz[zp, k] = self.zz[zp, k] + self.part[zp, k // 2, k % 2]
            self.down(zp, k, held).start()

        @pl.when((zp > z) & (z > 0))
        def _():
            self.up(zp, k, held).wait_recv()
            self.zz[zp, k] = self.zz[zp, k] + self.part[zp, k // 2, k % 2]
            self.up(zp, k, held).start()

    def own_event(self, k):
        z = self.pc.z

        @pl.when(z < NZ - 1)
        def _():
            self.down(z, k, self.zz.at[z, k]).wait_recv()

        @pl.when(z > 0)
        def _():
            self.up(z, k, self.zz.at[z, k]).wait_recv()

        own = self.part[z, k // 2, k % 2].astype(f32)

        @pl.when(z == 0)
        def _():
            self.sm[k] = (own + self.zz[z, k].astype(f32)).astype(bf16)

        @pl.when(z == NZ - 1)
        def _():
            self.sm[k] = (own + self.zz[NZ, k].astype(f32)).astype(bf16)

        @pl.when((z > 0) & (z < NZ - 1))
        def _():
            both = self.zz[z, k].astype(f32) + self.zz[NZ, k].astype(f32)
            self.sm[k] = (own + both).astype(bf16)

    def plane_send(self):
        self.plane_first(0)

    def plane_event(self):
        self.plane_second(0)

    def final(self):
        self.plane_arrived(0)
        for k in range(2):
            self.out[self.h[k], :] = self.plane_total(0, k)

    def finish(self):
        z = self.pc.z
        self.plane_finish(0)
        for zp in range(NZ):
            for k in range(4):

                @pl.when(zp < z)
                def _():
                    self.down(zp, k, self.zz.at[zp, k]).wait_send()

                @pl.when(zp > z)
                def _():
                    self.up(zp, k, self.zz.at[zp, k]).wait_send()


class SequenceSum(PlaneSum):
    def __init__(self, pc, terms, bufs, send, recv, core_send, core_recv):
        rd, rx, ry, self.theirs = bufs
        self.plane_setup(pc, rd, rx, ry, send, recv)
        self.terms, self.core_send, self.core_recv = terms, core_send, core_recv
        self.h = halves(terms.shape[-2])

    @staticmethod
    def scratch(rows, columns):
        half = VMEM((1, 2, rows // 2, columns), bf16)
        return [half, half, half, VMEM((2, 2, rows, columns), bf16)]

    def piece(self, s, y, x, k):
        return self.theirs.at[y, x, self.h[k]]

    def swap(self):
        p = self.pc
        return remote(
            self.terms.at[:, :, 1 - p.core], self.theirs, p.sn(), self.core_send, self.core_recv
        )

    def core_event(self):
        p = self.pc
        self.swap().wait_recv()
        for y in range(2):
            for x in range(2):
                self.theirs[y, x] = self.theirs[y, x] + self.terms[y, x, p.core]
        self.plane_first(0)

    def finish(self):
        self.swap().wait_send()
        self.plane_finish(0)


def norm_back(src, gain, grad, part_ref, part_row, emit):
    part_ref[pl.ds(part_row, 1), :] = jnp.zeros((1, part_ref.shape[1]), f32)

    def body(i, _):
        rows = pl.ds(pl.multiple_of(i * 32, 32), 32)
        v, g = src[rows, :].astype(f32), grad[rows, :]
        inv = lax.rsqrt(jnp.mean(v * v, axis=-1, keepdims=True) + EPS)
        unit = v * inv
        part_ref[pl.ds(part_row, 1), :] += jnp.sum(g * unit, axis=0, keepdims=True)
        gg = g * gain[...]
        emit(rows, inv * (gg - unit * jnp.mean(gg * unit, axis=-1, keepdims=True)))
        return 0

    lax.fori_loop(0, src.shape[0] // 32, body, 0)


def weight_grad(left, zp, right, part):
    rows, columns = part.shape[-2:]
    lhs = left[pl.ds(zp * 4, 4)].reshape(4 * rows, left.shape[-1])
    step = 512

    def body(n, _):
        c = cols(n, step)
        part[zp, :, :, :, c] = dot(lhs, right[:, c]).astype(bf16).reshape(2, 2, rows, step)
        return 0

    lax.fori_loop(0, columns // step, body, 0)


def backward_kernel(dims, *refs):
    (tok, width, n_dev, heads_w, kv_w, ff) = dims
    (
        cos_ref, sin_ref, g_q, g_k, g_ffn,
        i_tmix, i_tffn, i_tact, i_cot, i_ggu, i_qkv, i_q2, i_linv, i_mixf, i_res, i_kk, i_va,
        i_mask, i_wout, i_wgu,
        gqkv2, res, gains, out_wout, out_wgu, out_wdown,
        t_mix, t_ffn, t_act, cot2, ggu2, qkv, q2, linv, mixf, kk, va, mask_t, w_gu,
        part_out, part_gu, part_down, gh, gattn2, acc_k, acc_v, acc_q, aug, gm, terms,
        send, recv, kv_send, kv_recv, ex_send, ex_recv, lsem,
    ) = refs[:57]
    bufs = refs[57:]
    pc = Place()
    z = pc.z
    part = functools.partial
    loads = {}

    def load(name, src, dst):
        c = pltpu.make_async_copy(src, dst, lsem.at[len(loads)])
        loads[name] = c
        c.start()

    load("act", i_tact, t_act)
    load("cot", i_cot, cot2)
    load("ffn", i_tffn, t_ffn)
    load("ggu", i_ggu, ggu2)
    load("wgu", i_wgu, w_gu)
    load("res", i_res, res)
    load("mix", i_tmix, t_mix)
    load("mixf", i_mixf, mixf)
    load("linv", i_linv, linv)
    load("q2", i_q2, q2)
    load("kk", i_kk, kk)
    load("va", i_va, va)
    load("mask", i_mask, mask_t)
    load("qkv", i_qkv, qkv)
    barrier(pc)
    down = Scatter(pc, part_down, bufs[0:4], out_wdown, send.at[0], recv.at[0])
    gateup = Scatter(pc, part_gu, bufs[4:8], out_wgu, send.at[1], recv.at[1])
    out = ScatterZ(pc, part_out, bufs[8:13], out_wout, send.at[2], recv.at[2])
    seq = SequenceSum(pc, terms, bufs[13:17], kv_send, kv_recv, ex_send.at[2], ex_recv.at[2])

    loads["act"].wait()
    loads["cot"].wait()
    for i in range(NZ):
        weight_grad(t_act, far(z, i), cot2, part_down)
        down.first(i)
    loads["ffn"].wait()
    loads["ggu"].wait()
    for i in range(NZ):
        weight_grad(t_ffn, far(z, i), ggu2, part_gu)
        gateup.first(i)
        if i == 2:
            down.d_event(0)
    own = pl.ds(0, tok)
    back = pl.ds(tok, tok)
    loads["wgu"].wait()
    first_events = [part(gateup.d_event, 0), None, part(down.d_event, 1), None, part(down.xy_event, 0),
                    part(down.z_event, 0), None, None]

    def h_step(n, _):
        w = w_gu[n // 2, n % 2].reshape(width // 8, 2 * ff)
        gh[:, cols(n, width // 8)] = dot_t(ggu2[own, :], w)
        ticked(n, 0, first_events)
        return 0

    lax.fori_loop(0, 8, h_step, 0)
    load("wout", i_wout, w_gu.at[:, :, :, :, pl.ds(0, part_out.shape[-2]), :])
    loads["res"].wait()

    def keep_residual(rows, grad):
        total = cot2[rows, :].astype(f32) + grad
        res[rows, :] = total
        gattn2[rows, :] = total.astype(bf16)

    gains[...] = jnp.zeros_like(gains)
    norm_back(res, g_ffn, gh, gains, 1, keep_residual)
    sent_attn = remote(gattn2.at[own, :], gattn2.at[back, :], pc.sn(), ex_send.at[0], ex_recv.at[0])
    sent_attn.start()
    gateup.d_event(1)
    loads["wout"].wait()

    def m_step(n, _):
        w = w_gu[n, :, :, :, pl.ds(0, part_out.shape[-2]), :].reshape(heads_w // NZ, width)
        gm[:, cols(n, heads_w // NZ)] = dot_t(gattn2[own, :], w).astype(bf16)
        return 0

    lax.fori_loop(0, NZ, m_step, 0)
    sent_attn.wait_recv()
    loads["mix"].wait()
    for i in range(NZ):
        weight_grad(t_mix, far(z, i), gattn2, part_out)
        out.first(i)
    gateup.xy_event(0)
    gateup.z_event(0)
    down.d_event(2)
    down.xy_event(1)
    for name in ("mixf", "linv", "q2", "kk", "va", "mask", "qkv"):
        loads[name].wait()

    low = lanes((tok, 128)) < 64
    chunk = 512
    n_chunk = n_dev * tok // chunk
    events = [
        part(down.z_event, 1), part(gateup.d_event, 2), part(gateup.xy_event, 1),
        part(gateup.z_event, 1), part(down.d_event, 3), part(down.xy_event, 2),
        part(down.z_event, 2),
    ] + [part(out.z_event, 0, k) for k in range(4)] + [
        part(gateup.d_event, 3), part(gateup.xy_event, 2), part(gateup.z_event, 2),
    ] + [part(out.z_event, 1, k) for k in range(4)] + [part(out.z_event, 2, k) for k in range(4)]

    def attend(tick, _):
        t, kc = tick // n_chunk, tick % n_chunk
        g = t // 2
        rows = pl.ds(pl.multiple_of(kc * chunk, chunk), chunk)

        @pl.when(kc == 0)
        def _():
            c = cols(t, 128)
            grad = gm[:, c].astype(f32)
            delta = head_sums(grad * mixf[:, c]) * linv[:, c]
            grad = grad * linv[:, c]
            lane = lanes((tok, 128))
            for half in range(2):
                d = roll_half(delta) if half == 0 else delta
                v = grad if half == 0 else roll_half(grad)
                high = d.astype(bf16).astype(f32)
                rest = jnp.where(lane == 64, -high, jnp.where(lane == 65, high - d, 0.0))
                aug[pl.ds(half * tok, tok), :] = jnp.where(low, v, rest).astype(bf16)

        seen = mask_t[rows, :]
        e = jnp.exp2(dot_t(kk[g, rows, :], q2[t]) * LOG2E).astype(bf16)
        e = e * jnp.concatenate([seen, seen], axis=1)
        dv = dot(e, aug[...])
        ds = e * dot_t(va[g, rows, :], aug[...]).astype(bf16)
        dk = dot(ds, q2[t])
        dq = lax.dot_general(kk[g, rows, :], ds, (((0,), (0,)), ((), ())), preferred_element_type=f32)

        @pl.when(t % 2 == 0)
        def _():
            acc_k[rows, :] = dk
            acc_v[rows, :] = dv

        @pl.when(t % 2 == 1)
        def _():
            both_k = acc_k[rows, :] + dk
            both_v = acc_v[rows, :] + dv
            both_k = both_k + roll_half(both_k)
            lower = lanes((chunk, 128)) < 64
            both_v = jnp.where(lower, both_v, roll_half(both_v))
            mine = (lanes((chunk, 128)) // 64) == (g % 2)
            for b in range(chunk // tok):
                spot = kc * (chunk // tok) + b
                y, x, c = spot // 4, (spot // 2) % 2, spot % 2
                cut = slice(b * tok, (b + 1) * tok)
                for base, value in ((0, both_k), (kv_w, both_v)):
                    place = pl.ds(pl.multiple_of(base + (g // 2) * 128, 128), 128)
                    old = terms[y, x, c, :, place].astype(f32)
                    terms[y, x, c, :, place] = jnp.where(mine[cut], value[cut], old).astype(bf16)

        @pl.when(kc == 0)
        def _():
            acc_q[...] = dq

        @pl.when(kc > 0)
        def _():
            acc_q[...] += dq

        @pl.when(kc == n_chunk - 1)
        def _():
            turned = jnp.transpose(acc_q[...])
            gh[:, cols(t, 128)] = jnp.where(low, turned[:tok], turned[tok:]) * 0.125

        ticked(tick, 1, events)
        return 0

    lax.fori_loop(0, heads_w // 128 * n_chunk, attend, 0)
    seq.swap().start()

    def head_back(t, grad, gain, row):
        c = cols(t, 128)
        u = qkv[:, c]
        inv = lax.rsqrt(head_sums(u * u) * (1.0 / 64) + EPS)
        unit = u * inv
        grad = grad * cos_ref[...] - swap_rot(grad) * sin_ref[...]
        gains[pl.ds(row, 1), pl.ds(0, 128)] += jnp.sum(grad * unit, axis=0, keepdims=True)
        gg = grad * gain[...]
        gqkv2[own, c] = (inv * (gg - unit * head_sums(gg * unit) * (1.0 / 64))).astype(bf16)

    def query_back(t, _):
        head_back(t, gh[:, cols(t, 128)], g_q, 2)
        return 0

    lax.fori_loop(0, heads_w // 128 // 2, query_back, 0)
    seq.core_event()
    lax.fori_loop(heads_w // 128 // 2, heads_w // 128, query_back, 0)
    for k in range(4):
        out.own_event(k)
    seq.plane_second(0)
    out.plane_send()
    down.final()
    seq.plane_arrived(0)
    for k in range(2):
        rows = seq.h[k]
        gh[rows, pl.ds(0, 2 * kv_w)] = seq.plane_total(0, k)
    for t in range(kv_w // 128):
        head_back(heads_w // 128 + t, gh[:, pl.ds(t * 128, 128)], g_k, 3)
    gqkv2[own, pl.ds(heads_w + kv_w, kv_w)] = gh[:, pl.ds(kv_w, kv_w)].astype(bf16)
    sent_qkv = remote(gqkv2.at[own, :], gqkv2.at[back, :], pc.sn(), ex_send.at[1], ex_recv.at[1])
    sent_qkv.start()
    out.plane_event()
    gateup.final()
    out.final()
    sent_qkv.wait_recv()
    for g in (down, gateup, out, seq):
        g.finish()
    sent_attn.wait_send()
    sent_qkv.wait_send()


def last_kernel(dims, *refs):
    (tok, width, n_dev, heads_w, kv_w, ff) = dims
    (
        x_ref, g_attn, gqkv2, res, gains, i_tattn, i_wqkv,
        dx, o_attn, o_q, o_k, o_ffn, out_wqkv,
        t_attn, w_qkv, part_qkv, gh, held, came,
        send, recv, g_send, g_recv, lsem,
    ) = refs[:24]
    pc = Place()
    z = pc.z
    part = functools.partial
    load_t = pltpu.make_async_copy(i_tattn, t_attn, lsem.at[0])
    load_w = pltpu.make_async_copy(i_wqkv, w_qkv, lsem.at[1])
    load_t.start()
    load_w.start()
    bar = pltpu.get_barrier_semaphore()
    for device in (pc.xn(), pc.yn(), pc.sn()):
        pl.semaphore_signal(bar, inc=1, device_id=device, device_id_type=MESH)
    for k in range(1, NZ):
        there = pc.at(z=(z + k) % NZ)
        pl.semaphore_signal(bar, inc=1, device_id=there, device_id_type=MESH)
    pl.semaphore_wait(bar, 3 + NZ - 1)
    qkv = Scatter(pc, part_qkv, refs[24:28], out_wqkv, send, recv)
    load_t.wait()
    for i in range(NZ):
        weight_grad(t_attn, far(z, i), gqkv2, part_qkv)
        qkv.first(i)
    load_w.wait()
    columns = w_qkv.shape[-1]
    events = [None, None, part(qkv.d_event, 0), None, None, part(qkv.d_event, 1), part(qkv.xy_event, 0),
              part(qkv.z_event, 0)]

    def h_step(n, _):
        w = w_qkv[n // 2, n % 2].reshape(width // 8, columns)
        gh[:, cols(n, width // 8)] = dot_t(gqkv2[pl.ds(0, tok), :], w)
        ticked(n, 0, events)
        return 0

    lax.fori_loop(0, 8, h_step, 0)

    def keep_input(rows, grad):
        dx[rows, :] = (res[rows, :] + grad).astype(bf16)

    held[...] = gains[...]
    norm_back(x_ref, g_attn, gh, held, 0, keep_input)

    def hop(k, device):
        return remote(held, came.at[k], device, g_send.at[k], g_recv.at[k])

    hops = [hop(0, pc.sn()), hop(1, pc.xn()), hop(2, pc.yn())]
    between = [
        [part(qkv.d_event, 2), part(qkv.xy_event, 1), part(qkv.z_event, 1)],
        [part(qkv.d_event, 3), part(qkv.xy_event, 2), part(qkv.z_event, 2)],
        [],
    ]
    for k, c in enumerate(hops):
        c.start()
        for event in between[k]:
            event()
        c.wait()
        held[...] += came[k]
    came[3 + z] = held[...]
    ring = []
    for k in range(1, NZ):
        c = remote(held, came.at[3 + z], pc.at(z=(z + k) % NZ), g_send.at[2 + k], g_recv.at[3 + z])
        c.start()
        ring.append(c)
    qkv.final()
    for k in range(1, NZ):
        there = (z + k) % NZ
        remote(held, came.at[3 + there], pc.at(z=there), g_send.at[2 + k], g_recv.at[3 + there]).wait_recv()
    total = came[3]
    for k in range(1, NZ):
        total = total + came[3 + k]
    o_attn[...] = total[0:1]
    o_ffn[...] = total[1:2]
    for o, row in ((o_q, 2), (o_k, 3)):
        v = total[:, :128]
        o[...] = (v + roll_half(v))[row : row + 1, :64]
    for c in ring:
        c.wait_send()
    qkv.finish()


def backward(x, cosine, sine, g_attn, g_q, g_k, g_ffn, kept, rows, n_dev):
    (t_attn, t_mix, t_ffn, t_act, cot2, ggu2, qkv, q2, linv, mixf, res, kk, va, mask_t, w_qkv, w_out, w_gu) = kept
    tok, width = x.shape
    heads_w, kv_w = HEADS * HEAD_DIM, GROUPS * HEAD_DIM
    ff = ggu2.shape[1] // 2
    length = n_dev * tok
    columns = qkv.shape[1]
    dims = (tok, width, n_dev, heads_w, kv_w, ff)
    shape = jax.ShapeDtypeStruct
    vm = pl.BlockSpec(memory_space=VMEM)
    anyw = pl.BlockSpec(memory_space=pl.ANY)
    dma = pltpu.SemaphoreType.DMA
    r_qkv, r_out, r_gu, r_down = rows
    partial = [VMEM((NZ, 2, 2, r, width), bf16) for r in (r_out, r_gu, r_down)]
    like = [VMEM(v.shape, v.dtype) for v in (t_mix, t_ffn, t_act, cot2, ggu2, qkv, q2, linv, mixf, kk, va, mask_t, w_gu)]
    gqkv2, grad_res, gains, own_out, own_gu, own_down = pl.pallas_call(
        functools.partial(backward_kernel, dims),
        out_shape=[
            shape((2 * tok, columns), bf16),
            shape((tok, width), f32),
            shape((8, width), f32),
            shape((r_out, width), f32),
            shape((r_gu, width), f32),
            shape((r_down, width), f32),
        ],
        in_specs=[vm] * 5 + [anyw] * 15,
        out_specs=[vm] * 6,
        scratch_shapes=like
        + partial
        + [
            VMEM((tok, width), f32),
            VMEM((2 * tok, width), bf16),
            VMEM((length, 128), f32),
            VMEM((length, 128), f32),
            VMEM((128, 2 * tok), f32),
            VMEM((2 * tok, 128), bf16),
            VMEM((tok, heads_w), bf16),
            VMEM((2, 2, 2, tok, 2 * kv_w), bf16),
            dma((3, 16, NZ)),
            dma((3, 16, NZ)),
            dma((8, 1)),
            dma((8, 1)),
            dma((3,)),
            dma((3,)),
            dma((15,)),
        ]
        + Scatter.scratch(r_down, width)
        + Scatter.scratch(r_gu, width)
        + ScatterZ.scratch(r_out, width)
        + SequenceSum.scratch(tok, 2 * kv_w),
        compiler_params=pltpu.CompilerParams(
            collective_id=1, has_side_effects=True, vmem_limit_bytes=63 << 20
        ),
        cost_estimate=pl.CostEstimate(flops=20 * tok * width * width, bytes_accessed=60 << 20, transcendentals=0),
        name="backward",
    )(cosine, sine, g_q, g_k, g_ffn, t_mix, t_ffn, t_act, cot2, ggu2, qkv, q2, linv, mixf, res, kk, va, mask_t, w_out, w_gu)
    last = pl.pallas_call(
        functools.partial(last_kernel, dims),
        out_shape=[
            shape((tok, width), bf16),
            shape((1, width), f32),
            shape((1, 64), f32),
            shape((1, 64), f32),
            shape((1, width), f32),
            shape((r_qkv, columns), f32),
        ],
        in_specs=[vm] * 5 + [anyw] * 2,
        out_specs=[vm] * 6,
        scratch_shapes=[
            VMEM(t_attn.shape, bf16),
            VMEM(w_qkv.shape, bf16),
            VMEM((NZ, 2, 2, r_qkv, columns), bf16),
            VMEM((tok, width), f32),
            VMEM((8, width), f32),
            VMEM((3 + NZ, 8, width), f32),
            dma((8, NZ)),
            dma((8, NZ)),
            dma((3 + NZ,)),
            dma((3 + NZ,)),
            dma((2,)),
        ]
        + Scatter.scratch(r_qkv, columns),
        compiler_params=pltpu.CompilerParams(
            collective_id=2, has_side_effects=True, vmem_limit_bytes=60 << 20
        ),
        cost_estimate=pl.CostEstimate(flops=8 * tok * width * columns, bytes_accessed=20 << 20, transcendentals=0),
        name="last",
    )(x, g_attn, gqkv2, grad_res, gains, t_attn, w_qkv)
    dx, grad_attn, grad_q, grad_k, grad_ffn, own_qkv = last
    return dx, grad_attn[0], own_qkv, grad_q[0], grad_k[0], own_out, grad_ffn[0], own_gu, own_down


epsilon = 1e-06


def norm_rows(values, gain_vec):
    return (
        values * lax.rsqrt(jnp.mean(values * values, axis=-1, keepdims=True) + epsilon) * gain_vec
    )


def rotate(values, positions):
    half_dim = values.shape[-1] // 2
    frequency = jnp.exp(
        jnp.arange(half_dim).astype(jnp.float32) * (-2.0 * math.log(10000.0) / values.shape[-1])
    )
    angles = positions.astype(jnp.float32)[:, None] * frequency[None, :]
    cosine = jnp.cos(angles)[:, None, :]
    sine = jnp.sin(angles)[:, None, :]
    first = values[..., :half_dim]
    second = values[..., half_dim:]
    return jnp.concatenate(
        [first * cosine - second * sine, second * cosine + first * sine], axis=-1
    )


def project_heads(qkv_all, positions, q_gain, k_gain):
    tok_rows = qkv_all.shape[0]
    q_cols = HEADS * HEAD_DIM
    k_cols = GROUPS * HEAD_DIM
    queries = qkv_all[:, :q_cols].reshape(tok_rows, HEADS, HEAD_DIM)
    keys_raw = qkv_all[:, q_cols : q_cols + k_cols].reshape(tok_rows, GROUPS, HEAD_DIM)
    values = qkv_all[:, q_cols + k_cols :].reshape(tok_rows, GROUPS, HEAD_DIM)
    return (
        rotate(norm_rows(queries, q_gain), positions),
        rotate(norm_rows(keys_raw, k_gain), positions),
        values,
    )


def gated(gate_up):
    return jax.nn.silu(gate_up[:, :FF]) * gate_up[:, FF:]


def per_device_plain(
    inputs, places, cotangent, attn_gain, w_qkv, q_gain, k_gain, w_out, ffn_gain, w_gateup, w_down
):
    tok_rows = inputs.shape[1]
    repeat = HEADS // GROUPS
    score_scale = HEAD_DIM ** (-0.5)
    here_f = inputs[0].astype(jnp.float32)
    own_places = places[0]
    qkv_w, out_w = (
        lax.all_gather(w_qkv, ("dp", "ctx"), axis=0, tiled=True),
        lax.all_gather(w_out, ("dp", "ctx"), axis=0, tiled=True),
    )
    h_attn_f, pull_attn = jax.vjp(norm_rows, here_f, attn_gain)
    h_attn = h_attn_f.astype(jnp.bfloat16)
    qkv_all = jnp.dot(h_attn, qkv_w, preferred_element_type=jnp.float32)

    def heads_of(qkv_in, gain_q, gain_k):
        return project_heads(qkv_in, own_places, gain_q, gain_k)

    (queries, keys_f, values), pull_heads = jax.vjp(heads_of, qkv_all, q_gain, k_gain)
    query_b = queries.astype(jnp.bfloat16).reshape(tok_rows, GROUPS, repeat, HEAD_DIM)
    key_b = keys_f.astype(jnp.bfloat16)
    value_b = values.astype(jnp.bfloat16)
    all_keys, all_values = (
        lax.all_gather(key_b, "ctx", axis=0, tiled=True),
        lax.all_gather(value_b, "ctx", axis=0, tiled=True),
    )
    all_places = lax.all_gather(own_places, "ctx", axis=0, tiled=True)
    blocks = lax.axis_size("ctx")
    key_blocks = all_keys.reshape(blocks, tok_rows, GROUPS, HEAD_DIM)
    value_blocks = all_values.reshape(blocks, tok_rows, GROUPS, HEAD_DIM)
    place_blocks = all_places.reshape(blocks, tok_rows)

    def score_block(key_blk, place_blk):
        scores = (
            jnp.einsum("igrd,jgd->grij", query_b, key_blk, preferred_element_type=jnp.float32)
            * score_scale
        )
        allowed = place_blk[None, :] <= own_places[:, None]
        return (scores, allowed)

    def max_step(state_pair, entries):
        row_top, row_total = state_pair
        scores, allowed = score_block(entries[0], entries[1])
        scores = jnp.where(allowed, scores, -1e30)
        new_top = jnp.maximum(row_top, jnp.max(scores, axis=-1))
        row_total = row_total * jnp.exp(row_top - new_top) + jnp.sum(
            jnp.where(allowed, jnp.exp(scores - new_top[..., None]), 0.0), axis=-1
        )
        return ((new_top, row_total), None)

    start_pair = (
        jnp.full((GROUPS, repeat, tok_rows), -1e30, jnp.float32),
        jnp.zeros((GROUPS, repeat, tok_rows), jnp.float32),
    )
    (row_top, row_total), _ = lax.scan(max_step, start_pair, (key_blocks, place_blocks))
    log_total = row_top + jnp.log(row_total)

    def out_step(accum, entries):
        scores, allowed = score_block(entries[0], entries[1])
        weights_b = jnp.where(allowed, jnp.exp(scores - log_total[..., None]), 0.0).astype(
            jnp.bfloat16
        )
        return (
            accum
            + jnp.einsum(
                "grij,jgd->igrd", weights_b, entries[2], preferred_element_type=jnp.float32
            ),
            None,
        )

    mixed_f, _ = lax.scan(
        out_step,
        jnp.zeros((tok_rows, GROUPS, repeat, HEAD_DIM), jnp.float32),
        (key_blocks, place_blocks, value_blocks),
    )
    mixed_b = mixed_f.reshape(tok_rows, HEADS * HEAD_DIM).astype(jnp.bfloat16)
    attn_out = jnp.dot(mixed_b, out_w, preferred_element_type=jnp.float32)
    residual = here_f + attn_out
    gateup_w, down_w = (
        lax.all_gather(w_gateup, ("dp", "ctx"), axis=0, tiled=True),
        lax.all_gather(w_down, ("dp", "ctx"), axis=0, tiled=True),
    )
    h_ffn_f, pull_ffn = jax.vjp(norm_rows, residual, ffn_gain)
    h_ffn = h_ffn_f.astype(jnp.bfloat16)
    gate_up = jnp.dot(h_ffn, gateup_w, preferred_element_type=jnp.float32)
    act_f, pull_gate = jax.vjp(gated, gate_up)
    act_b = act_f.astype(jnp.bfloat16)
    result = residual + jnp.dot(act_b, down_w, preferred_element_type=jnp.float32)
    layer_output = result.astype(jnp.bfloat16)[None]
    gateup_w, down_w = (
        lax.all_gather(w_gateup, ("dp", "ctx"), axis=0, tiled=True),
        lax.all_gather(w_down, ("dp", "ctx"), axis=0, tiled=True),
    )
    grad_out = cotangent[0]
    grad_act = jnp.dot(grad_out, down_w.T, preferred_element_type=jnp.float32)
    grad_down = jnp.dot(act_b.T, grad_out, preferred_element_type=jnp.float32)
    grad_gu_b = pull_gate(grad_act)[0].astype(jnp.bfloat16)
    grad_gateup = jnp.dot(h_ffn.T, grad_gu_b, preferred_element_type=jnp.float32)
    grad_h_ffn = jnp.dot(grad_gu_b, gateup_w.T, preferred_element_type=jnp.float32)
    grad_resid_part, grad_ffn_gain = pull_ffn(grad_h_ffn)
    grad_residual = grad_out.astype(jnp.float32) + grad_resid_part
    grad_gateup_own, grad_down_own = (
        lax.psum_scatter(grad_gateup, ("dp", "ctx"), scatter_dimension=0, tiled=True),
        lax.psum_scatter(grad_down, ("dp", "ctx"), scatter_dimension=0, tiled=True),
    )
    qkv_w, out_w = (
        lax.all_gather(w_qkv, ("dp", "ctx"), axis=0, tiled=True),
        lax.all_gather(w_out, ("dp", "ctx"), axis=0, tiled=True),
    )
    grad_attn_b = grad_residual.astype(jnp.bfloat16)
    grad_out_w = jnp.dot(mixed_b.T, grad_attn_b, preferred_element_type=jnp.float32)
    grad_mixed_b = (
        jnp.dot(grad_attn_b, out_w.T, preferred_element_type=jnp.float32)
        .astype(jnp.bfloat16)
        .reshape(tok_rows, GROUPS, repeat, HEAD_DIM)
    )
    row_delta = jnp.transpose(
        jnp.sum(grad_mixed_b.astype(jnp.float32) * mixed_f, axis=-1), (1, 2, 0)
    )

    def back_step(grad_query, entries):
        key_blk, place_blk, value_blk = entries
        scores, allowed = score_block(key_blk, place_blk)
        weights_f = jnp.where(allowed, jnp.exp(scores - log_total[..., None]), 0.0)
        weights_b = weights_f.astype(jnp.bfloat16)
        grad_value = jnp.einsum(
            "grij,igrd->jgd", weights_b, grad_mixed_b, preferred_element_type=jnp.float32
        )
        grad_prob = jnp.einsum(
            "igrd,jgd->grij", grad_mixed_b, value_blk, preferred_element_type=jnp.float32
        )
        grad_score = (weights_f * (grad_prob - row_delta[..., None])).astype(jnp.bfloat16)
        grad_query = grad_query + jnp.einsum(
            "grij,jgd->igrd", grad_score, key_blk, preferred_element_type=jnp.float32
        )
        grad_key = (
            jnp.einsum("grij,igrd->jgd", grad_score, query_b, preferred_element_type=jnp.float32)
            * score_scale
        )
        return (
            grad_query,
            jnp.concatenate(
                [
                    grad_key.reshape(tok_rows, GROUPS * HEAD_DIM),
                    grad_value.reshape(tok_rows, GROUPS * HEAD_DIM),
                ],
                axis=1,
            ),
        )

    grad_query, kv_terms = lax.scan(
        back_step,
        jnp.zeros((tok_rows, GROUPS, repeat, HEAD_DIM), jnp.float32),
        (key_blocks, place_blocks, value_blocks),
    )
    grad_query = grad_query * score_scale
    kv_own = lax.psum_scatter(
        kv_terms.reshape(blocks * tok_rows, 2 * GROUPS * HEAD_DIM).astype(jnp.bfloat16),
        "ctx",
        scatter_dimension=0,
        tiled=True,
    ).astype(jnp.float32)
    grad_key_own = kv_own[:, : GROUPS * HEAD_DIM].reshape(tok_rows, GROUPS, HEAD_DIM)
    grad_value_own = kv_own[:, GROUPS * HEAD_DIM :].reshape(tok_rows, GROUPS, HEAD_DIM)
    grad_qkv_f, grad_q_gain, grad_k_gain = pull_heads(
        (grad_query.reshape(tok_rows, HEADS, HEAD_DIM), grad_key_own, grad_value_own)
    )
    grad_qkv_b = grad_qkv_f.astype(jnp.bfloat16)
    grad_qkv_w = jnp.dot(h_attn.T, grad_qkv_b, preferred_element_type=jnp.float32)
    grad_h_attn = jnp.dot(grad_qkv_b, qkv_w.T, preferred_element_type=jnp.float32)
    grad_here_part, grad_attn_gain = pull_attn(grad_h_attn)
    grad_inputs = (grad_residual + grad_here_part).astype(jnp.bfloat16)[None]
    grad_qkv_own, grad_out_own = (
        lax.psum_scatter(grad_qkv_w, ("dp", "ctx"), scatter_dimension=0, tiled=True),
        lax.psum_scatter(grad_out_w, ("dp", "ctx"), scatter_dimension=0, tiled=True),
    )
    gain_attn, gain_query, gain_key, gain_ffn = lax.psum(
        (grad_attn_gain, grad_q_gain, grad_k_gain, grad_ffn_gain), ("dp", "ctx")
    )
    return (
        layer_output,
        grad_inputs,
        gain_attn,
        grad_qkv_own,
        gain_query,
        gain_key,
        grad_out_own,
        gain_ffn,
        grad_gateup_own,
        grad_down_own,
    )


def per_device_fast(
    inputs, places, cotangent, attn_gain, w_qkv, q_gain, k_gain, w_out, ffn_gain, w_gateup, w_down
):
    n_dev = lax.axis_size("ctx")
    own_places = places[0]
    half = HEAD_DIM // 2
    spot = jnp.arange(128)
    frequency = jnp.exp((spot % half).astype(f32) * (-2.0 * math.log(10000.0) / HEAD_DIM))
    angles = own_places.astype(f32)[:, None] * frequency[None, :]
    cosine = jnp.cos(angles)
    sine = jnp.where(spot % HEAD_DIM < half, -1.0, 1.0) * jnp.sin(angles)
    block_row = (own_places // 128)[None, :]
    gain_q, gain_k = jnp.tile(q_gain, 2)[None], jnp.tile(k_gain, 2)[None]
    layer_output, *kept = forward(
        inputs[0], cotangent[0], block_row, cosine, sine, attn_gain[None], gain_q, gain_k,
        ffn_gain[None], w_qkv, w_out, w_down, w_gateup, n_dev,
    )
    rows = [w.shape[0] for w in (w_qkv, w_out, w_gateup, w_down)]
    grad_inputs, *grads = backward(
        inputs[0], cosine, sine, attn_gain[None], gain_q, gain_k, ffn_gain[None], kept, rows, n_dev
    )
    return (layer_output[None], grad_inputs[None], *grads)


def solution(mesh):
    in_specs = (
        P("dp", "ctx", None),
        P("dp", "ctx"),
        P("dp", "ctx", None),
        P(),
        P(("dp", "ctx"), None),
        P(),
        P(),
        P(("dp", "ctx"), None),
        P(),
        P(("dp", "ctx"), None),
        P(("dp", "ctx"), None),
    )
    out_specs = (
        P("dp", "ctx", None),
        P("dp", "ctx", None),
        P(),
        P(("dp", "ctx"), None),
        P(),
        P(),
        P(("dp", "ctx"), None),
        P(),
        P(("dp", "ctx"), None),
        P(("dp", "ctx"), None),
    )
    fast = dict(mesh.shape) == {"dp": 4, "ctx": 8}
    per_device = per_device_fast if fast else per_device_plain
    return jax.shard_map(
        per_device, mesh=mesh, in_specs=in_specs, out_specs=out_specs, check_vma=False
    )
```

```python
import functools
import math

import jax
import jax.numpy as jnp
from jax import lax
from jax.experimental import pallas as pl
from jax.experimental.pallas import tpu as pltpu
from jax.sharding import PartitionSpec as P

HEADS = 16
GROUPS = 4
HEAD_DIM = 64
FF = 1024


FORWARD_ORDER = [
    "qp0", "qZ", "norm", "dp0", "qz1", "qe0", "qp1", "qz2", "gZ", "qp2", "qc0", "qe1", "oP",
    "qz3", "qp3", "qe2", "gz1", "qs0", "gz2", "oZ", "qe3", "oe", "dZ", "qc1", "qc2", "gp2", "qc3",
    "qs1", "qs2", "oD", "qs3", "oz12", "keys", "de0", "turn", "oz22", "kve", "gp1", "gz3", "gp0",
    "dz1", "query", "kvc", "dp1", "oz32", "ge2", "unpack", "gp3", "oz10", "dz2", *["A"] * 3,
    "oz20", *["A"] * 4, "oz30", *["A"] * 5, "dp2", "oz11", "ge0", "dz3", *["A"] * 3, "dc0",
    "oz13", "ge1", "oz23", *["A"] * 5, "oz21", "de1", "A", "oc1", "gc2", *["A"] * 4, "oc2", "A",
    "dp3", "oz31", *["A"] * 3, "oz33", "oc3", *["A"] * 2, "gc0", "A", "mix", "de2", "dc1", "ds0",
    "res", "ge3", "de3", "gc1", "norm2", "dc2", "gc3", "gs0", "gs1", "dc3", "ds1", "ds2", "gs2",
    "turn2", "gs3", "ds3", "gate", "act", "y",
]

BACKWARD_ORDER = [
    "dw0", "dw1", "gw0", "gw1", "dw2", "dw3", "h", *["H"] * 6, "ga0", *["H"] * 2, "nb", "gw2",
    "db1", "gw3", "da1", "m", "att", "ow0", "ga2", "ga1", "oa0", "B", "ow1", "da2", "oa1", "dd1",
    "ow2", "gb0", "oa2", "da0", *["B"] * 2, "db2", "B", "oz00", *["B"] * 2, "dd2", *["B"] * 3,
    "gb1", *["B"] * 2, "gb2", "dd0", "dx1", *["B"] * 2, "oz02", "ga3", "oz10", "oz12", "db0", "B",
    "gd2", "oz22", *["B"] * 2, "gd1", "B", "gb3", "oz20", "B", "oz03", *["B"] * 2, "oz01", "B",
    "oz13", "dx0", *["B"] * 2, "oz23", "dz0", *["B"] * 2, "dx2", "gd0", "dz1", "B", "gd3",
    *["B"] * 2, "dz2", "gx2", "da3", "gx0", *["B"] * 4, "kvs", "db3", "oz11", "dd3", "gx1", "gz0",
    "Q", "kvc", "oz21", "ow3", "oa3", "oo0", "gz1", "kve", "oo3", "df", "gz2", "Q", "oo2", "Q",
    "oo1", *["Q"] * 2, "oS", *["Q"] * 3, "kvf", "oe", "of", "gf",
]

LAST_ORDER = [
    "qw0", "qa0", "qw1", "qa1", "qb0", "qw2", "h", *["H"] * 2, "qd0", "H", "qb1", "H", "qa2",
    *["H"] * 2, "qd1", "H", "qb2", "H", "nb", "qx0", "qz0", "qd2", "hs0", "qw3", "he0", "hs1",
    "qa3", "qx1", "qz1", "qx2", "qz2", "he1", "hs2", "qb3", "qd3", "he2", "rs", "qf", "re",
]

f32 = jnp.float32
bf16 = jnp.bfloat16
MESH = pl.DeviceIdType.MESH
NZ = 4
EPS = 1e-06


class Place:
    def __init__(self):
        self.z = lax.axis_index("dp")
        spot = lax.axis_index("ctx")
        self.core = spot % 2
        self.x = (spot // 2) % 2
        self.y = spot // 4

    def at(self, z=None, y=None, x=None, core=None):
        z = self.z if z is None else z
        y = self.y if y is None else y
        x = self.x if x is None else x
        core = self.core if core is None else core
        return (z, y * 4 + x * 2 + core)

    def xn(self):
        return self.at(x=1 - self.x)

    def yn(self):
        return self.at(y=1 - self.y)

    def sn(self):
        return self.at(core=1 - self.core)

    def up(self):
        return self.at(z=self.z + 1)

    def down(self):
        return self.at(z=self.z - 1)


def barrier(pc):
    bar = pltpu.get_barrier_semaphore()

    def greet(device):
        pl.semaphore_signal(bar, inc=1, device_id=device, device_id_type=MESH)

    for device in (pc.xn(), pc.yn(), pc.sn()):
        greet(device)

    @pl.when(pc.z < NZ - 1)
    def _():
        greet(pc.up())

    @pl.when(pc.z > 0)
    def _():
        greet(pc.down())

    pl.semaphore_wait(bar, 3 + (1 - pc.z // (NZ - 1)) + (pc.z + NZ - 1) // NZ)


def far(z, i):
    m = z // 2
    zz = z + m * (3 - 2 * z)
    lo = 3 - i if i < 2 else (1 - zz if i == 2 else zz)
    return lo + m * (3 - 2 * lo)


def near(z, i):
    return far(z, NZ - 1 - i)


def remote(src, dst, dev, send, recv):
    return pltpu.make_async_remote_copy(
        src_ref=src, dst_ref=dst, send_sem=send, recv_sem=recv, device_id=dev, device_id_type=MESH
    )


def halves(rows):
    return pl.ds(0, rows // 2), pl.ds(rows // 2, rows // 2)


KZ, KX, KY, KD0, KD1, KS, KU = range(7)


class Gather:
    def __init__(self, pc, buf, send, recv):
        self.pc, self.buf, self.send, self.recv = pc, buf, send, recv
        self.h = halves(buf.shape[-2])

    def cp(self, idx, dev, ks, kr, slot):
        ref = self.buf.at[idx]
        return remote(ref, ref, dev, self.send.at[ks, slot], self.recv.at[kr, slot])

    def c_up(self, z0):
        p = self.pc
        return self.cp((z0, p.y, p.x, p.core), p.up(), KU, KZ, z0)

    def c_down(self, z0):
        p = self.pc
        return self.cp((z0, p.y, p.x, p.core), p.down(), KZ, KZ, z0)

    def c_x(self, z0):
        p = self.pc
        return self.cp((z0, p.y, p.x, p.core), p.xn(), KX, KX, z0)

    def c_y(self, z0):
        p = self.pc
        return self.cp((z0, p.y, p.x, p.core), p.yn(), KY, KY, z0)

    def c_d0(self, z0):
        p = self.pc
        return self.cp((z0, p.y, 1 - p.x, p.core, self.h[0]), p.yn(), KD0, KD0, z0)

    def c_d1(self, z0):
        p = self.pc
        return self.cp((z0, 1 - p.y, p.x, p.core, self.h[1]), p.xn(), KD1, KD1, z0)

    def c_s(self, z0):
        p = self.pc
        return self.cp((z0, slice(None), slice(None), p.core), p.sn(), KS, KS, z0)

    def plane_send(self, i):
        z0 = near(self.pc.z, i)
        self.c_x(z0).start()
        self.c_y(z0).start()

    def own_z(self):
        z = self.pc.z

        @pl.when(z < NZ - 1)
        def _():
            self.c_up(z).start()

        @pl.when(z > 0)
        def _():
            self.c_down(z).start()

    def z_event(self, i, plane=True):
        z = self.pc.z
        z0 = near(z, i)

        @pl.when(z0 < z)
        def _():
            self.c_up(z0).wait_recv()

            @pl.when(z < NZ - 1)
            def _():
                self.c_up(z0).start()

        @pl.when(z0 > z)
        def _():
            self.c_down(z0).wait_recv()

            @pl.when(z > 0)
            def _():
                self.c_down(z0).start()

        if plane:
            self.plane_send(i)

    def plane_event(self, i):
        z0 = near(self.pc.z, i)
        self.c_x(z0).wait_recv()
        self.c_d0(z0).start()
        self.c_y(z0).wait_recv()
        self.c_d1(z0).start()

    def core_event(self, i):
        z0 = near(self.pc.z, i)
        self.c_d0(z0).wait_recv()
        self.c_d1(z0).wait_recv()
        self.c_s(z0).start()

    def done_event(self, i):
        self.c_s(near(self.pc.z, i)).wait_recv()

    def finish(self):
        z = self.pc.z
        for z0 in range(NZ):
            for c in (self.c_x, self.c_y, self.c_d0, self.c_d1, self.c_s):
                c(z0).wait_send()

            @pl.when((z < NZ - 1) & (z0 <= z))
            def _():
                self.c_up(z0).wait_send()

            @pl.when((z > 0) & (z0 >= z))
            def _():
                self.c_down(z0).wait_send()


class GatherPlane:
    def __init__(self, pc, buf, send, recv):
        self.pc, self.buf, self.send, self.recv = pc, buf, send, recv
        self.h = halves(buf.shape[-2])

    def cp(self, idx, dev, s, r):
        ref = self.buf.at[idx]
        return remote(ref, ref, dev, self.send.at[s], self.recv.at[r])

    def yx(self, k):
        p = self.pc
        return (p.y if k < 2 else 1 - p.y), (p.x if k % 2 == 0 else 1 - p.x)

    def c_x(self):
        p = self.pc
        return self.cp((p.z, p.y, p.x, p.core), p.xn(), (KX, 0), (KX, 0))

    def c_y(self):
        p = self.pc
        return self.cp((p.z, p.y, p.x, p.core), p.yn(), (KY, 0), (KY, 0))

    def c_d0(self):
        p = self.pc
        return self.cp((p.z, p.y, 1 - p.x, p.core, self.h[0]), p.yn(), (KD0, 0), (KD0, 0))

    def c_d1(self):
        p = self.pc
        return self.cp((p.z, 1 - p.y, p.x, p.core, self.h[1]), p.xn(), (KD1, 0), (KD1, 0))

    def c_up(self, z0, k):
        p = self.pc
        y, x = self.yx(k)
        return self.cp((z0, y, x, p.core), p.up(), (10 + z0, k), (10 + z0, k))

    def c_down(self, z0, k):
        p = self.pc
        y, x = self.yx(k)
        return self.cp((z0, y, x, p.core), p.down(), (14 + z0, k), (10 + z0, k))

    def c_s(self, z0):
        p = self.pc
        return self.cp((z0, slice(None), slice(None), p.core), p.sn(), (KS, z0), (KS, z0))

    def z_send(self, k):
        z = self.pc.z

        @pl.when(z < NZ - 1)
        def _():
            self.c_up(z, k).start()

        @pl.when(z > 0)
        def _():
            self.c_down(z, k).start()

    def own_plane(self):
        self.c_x().start()
        self.c_y().start()

    def own_z(self):
        self.z_send(0)

    def plane_event(self):
        self.c_x().wait_recv()
        self.c_d0().start()
        self.z_send(1)
        self.c_y().wait_recv()
        self.c_d1().start()
        self.z_send(2)

    def diag_event(self):
        self.c_d0().wait_recv()
        self.c_d1().wait_recv()
        self.z_send(3)
        self.c_s(self.pc.z).start()

    def z_event(self, i, k):
        z = self.pc.z
        z0 = near(z, i)

        @pl.when(z0 < z)
        def _():
            self.c_up(z0, k).wait_recv()

            @pl.when(z < NZ - 1)
            def _():
                self.c_up(z0, k).start()

        @pl.when(z0 > z)
        def _():
            self.c_down(z0, k).wait_recv()

            @pl.when(z > 0)
            def _():
                self.c_down(z0, k).start()

    def core_event(self, i):
        self.c_s(near(self.pc.z, i)).start()

    def done_event(self, i):
        self.c_s(near(self.pc.z, i)).wait_recv()

    def finish(self):
        z = self.pc.z
        for c in (self.c_x, self.c_y, self.c_d0, self.c_d1):
            c().wait_send()
        for z0 in range(NZ):
            self.c_s(z0).wait_send()
            for k in range(4):

                @pl.when((z < NZ - 1) & (z0 <= z))
                def _():
                    self.c_up(z0, k).wait_send()

                @pl.when((z > 0) & (z0 >= z))
                def _():
                    self.c_down(z0, k).wait_send()


class GatherSequence:
    def __init__(self, pc, buf, send, recv):
        self.pc, self.buf, self.send, self.recv = pc, buf, send, recv
        rows = buf.shape[-2]
        self.h = (pl.ds(0, 128), pl.ds(128, rows - 128))

    def cp(self, idx, dev, k):
        ref = self.buf.at[idx]
        return remote(ref, ref, dev, self.send.at[k], self.recv.at[k])

    def c_x(self):
        p = self.pc
        return self.cp((p.y, p.x, p.core), p.xn(), 0)

    def c_y(self):
        p = self.pc
        return self.cp((p.y, p.x, p.core), p.yn(), 1)

    def c_d0(self):
        p = self.pc
        return self.cp((p.y, 1 - p.x, p.core, self.h[0]), p.yn(), 2)

    def c_d1(self):
        p = self.pc
        return self.cp((1 - p.y, p.x, p.core, self.h[1]), p.xn(), 3)

    def c_s(self, k):
        p = self.pc
        y, x = (p.y if k < 2 else 1 - p.y), (p.x if k % 2 == 0 else 1 - p.x)
        return self.cp((y, x, p.core), p.sn(), 4 + k)

    def own(self):
        for c in (self.c_x(), self.c_y(), self.c_s(0)):
            c.start()

    def plane_event(self):
        self.c_x().wait_recv()
        self.c_d0().start()
        self.c_s(1).start()
        self.c_y().wait_recv()
        self.c_d1().start()
        self.c_s(2).start()

    def core_event(self):
        self.c_d0().wait_recv()
        self.c_d1().wait_recv()
        self.c_s(3).start()

    def done_event(self):
        for k in range(4):
            self.c_s(k).wait_recv()

    def finish(self):
        for c in (self.c_x(), self.c_y(), self.c_d0(), self.c_d1()):
            c.wait_send()
        for k in range(4):
            self.c_s(k).wait_send()


LOG2E = math.log2(math.e)
VMEM = pltpu.VMEM


def dot(a, b):
    return jnp.dot(a, b, preferred_element_type=f32)


def dot_t(a, b):
    return lax.dot_general(a, b, (((1,), (1,)), ((), ())), preferred_element_type=f32)


def lanes(shape):
    return lax.broadcasted_iota(jnp.int32, shape, 1)


def roll_half(v):
    return pltpu.roll(v, 64, 1)


def swap_rot(v):
    first = lanes(v.shape) % 64 < 32
    return jnp.where(first, pltpu.roll(v, 96, 1), pltpu.roll(v, 32, 1))


def head_sums(v):
    row = lax.broadcasted_iota(jnp.int32, (128, 128), 0) // 64
    col = lax.broadcasted_iota(jnp.int32, (128, 128), 1) // 64
    ones = jnp.where(row == col, 1.0, 0.0).astype(bf16)
    high = v.astype(bf16)
    low = (v - high.astype(f32)).astype(bf16)
    return dot(high, ones) + dot(low, ones)


def cols(i, width):
    return pl.ds(pl.multiple_of(i * width, width), width)


def norm_into(src, gain, dst):
    def body(i, _):
        rows = pl.ds(pl.multiple_of(i * 32, 32), 32)
        v = src[rows, :].astype(f32)
        scale = lax.rsqrt(jnp.mean(v * v, axis=-1, keepdims=True) + EPS)
        dst[rows, :] = (v * scale * gain[...]).astype(dst.dtype)
        return 0

    lax.fori_loop(0, src.shape[0] // 32, body, 0)


def run_steps(order, steps, loops):
    order = list(order)
    while order:
        name = order.pop(0)
        if name not in loops:
            steps[name]()
            continue
        count, body = loops[name]
        ticks, seen = {}, 1
        while seen < count:
            inner = order.pop(0)
            if inner == name:
                seen += 1
            else:
                ticks.setdefault(seen - 1, []).append(inner)

        def tick(i, _, body=body, ticks=ticks):
            body(i)
            for k, inner in ticks.items():

                @pl.when(i == k)
                def _(inner=inner):
                    for step in inner:
                        steps[step]()

            return 0

        lax.fori_loop(0, count, tick, 0)


def line_steps(letter, g):
    part = functools.partial
    steps = {letter + "Z": g.own_z}
    for i in range(NZ):
        steps[f"{letter}p{i}"] = part(g.plane_send, i)
        steps[f"{letter}e{i}"] = part(g.plane_event, i)
        steps[f"{letter}c{i}"] = part(g.core_event, i)
        if i:
            steps[f"{letter}z{i}"] = part(g.z_event, i, False)
    return steps


def turn(src, rows, core, mine, theirs):
    def body(t, _):
        v = jnp.transpose(src[:, cols(t, 128)])
        for k in range(64 // rows):
            a, b = v[2 * k * rows : (2 * k + 1) * rows], v[(2 * k + 1) * rows : (2 * k + 2) * rows]
            own, other = jnp.where(core == 0, a, b), jnp.where(core == 0, b, a)
            spot = t * (64 // rows) + k
            mine[spot, :, pl.ds(0, v.shape[1])] = own
            theirs[spot, pl.ds(0, rows), :] = other
        return 0

    lax.fori_loop(0, src.shape[1] // 128, body, 0)


def forward_kernel(dims, *refs):
    (tok, width, n_dev, heads_w, kv_w, ff) = dims
    (
        x_ref, cot_ref, hi_ref, cos_ref, sin_ref, g_attn, g_q, g_k, g_ffn,
        s_qkv, s_out, s_down, s_gu,
        o_y, o_tattn, o_tmix, o_tffn, o_tact, o_cot, o_ggu, o_kv, o_q2, o_linv, o_mixf, o_res,
        o_kk, o_va, o_mask, o_wqkv, o_wout, o_wgu,
        w_qkv, w_out, w_down, w_gu, kk, va, mask, mask_t, o2, gu, gact,
        y_ref, hattn_ref, qkv_ref, q2_ref, kvb, linv_ref, mixf_ref, mixb_ref, res_ref, hffn_ref,
        act_ref, cot2, ggu2, t_attn, t_mix, t_ffn, t_act, turn_a, turn_b,
        send, recv, kv_send, kv_recv, lsem, osem, ex_send, ex_recv,
    ) = refs
    pc = Place()
    shards = (s_qkv, s_out, s_down, s_gu)
    bufs = (w_qkv, w_out, w_down, w_gu)
    local = [
        pltpu.make_async_copy(s, b.at[pc.z, pc.y, pc.x, pc.core], lsem.at[k])
        for k, (s, b) in enumerate(zip(shards, bufs))
    ]
    for c in local:
        c.start()
    barrier(pc)
    for c in local:
        c.wait()
    qkv = Gather(pc, w_qkv, send.at[0], recv.at[0])
    out = GatherPlane(pc, w_out, send.at[1], recv.at[1])
    down = Gather(pc, w_down, send.at[2], recv.at[2])
    gateup = Gather(pc, w_gu, send.at[3], recv.at[3])
    seq = GatherSequence(pc, kvb, kv_send, kv_recv)
    part = functools.partial
    z = pc.z
    emitted = []

    def emit(src, dst):
        c = pltpu.make_async_copy(src, dst, osem.at[len(emitted)])
        emitted.append(c)
        c.start()

    def exchange(k, src, dst):
        return remote(src, dst, pc.sn(), ex_send.at[k], ex_recv.at[k])

    back = pl.ds(tok, tok)
    sent_cot = exchange(0, cot_ref, cot2.at[back, :])
    sent_attn = exchange(1, turn_a, t_attn.at[:, :, back])
    sent_mix = exchange(2, turn_b.at[:, pl.ds(0, s_out.shape[0]), :], t_mix.at[:, :, back])
    sent_ffn = exchange(3, turn_a, t_ffn.at[:, :, back])
    sent_act = exchange(4, turn_b.at[:, pl.ds(0, s_down.shape[0]), :], t_act.at[:, :, back])
    sent_ggu = exchange(5, ggu2.at[pl.ds(0, tok), :], ggu2.at[back, :])

    def first_norm():
        norm_into(x_ref, g_attn, hattn_ref)

    def first_turn():
        sent_cot.start()
        cot2[pl.ds(0, tok), :] = cot_ref[...]
        turn(hattn_ref, s_qkv.shape[0], pc.core, t_attn, turn_a)
        sent_attn.start()

    def columns_step(g, i, left, right, total, depth):
        g.done_event(i)
        z0 = near(z, i)

        def body(n, _):
            c = cols(n, 256)
            w = right[z0, :, :, :, :, c].reshape(depth, 256)
            prod = dot(left[:, cols(z0, depth)], w)
            if i == 0:
                total[:, c] = prod
            else:
                total[:, c] += prod
            return 0

        lax.fori_loop(0, total.shape[1] // 256, body, 0)

    def grad_act_step(i):
        down.done_event(i)
        z0 = near(z, i)
        depth = ff // NZ
        gact[:, cols(z0, depth)] = dot_t(cot_ref[...], w_down[z0].reshape(depth, width))

    low = lanes((tok, 128)) < 64

    def head_tile(t, gain):
        u = qkv_ref[:, cols(t, 128)]
        n = u * lax.rsqrt(head_sums(u * u) * (1.0 / 64) + EPS) * gain[...]
        return n * cos_ref[...] + swap_rot(n) * sin_ref[...]

    def keys_out():
        for t in range(kv_w // 128):
            kvb[pc.y, pc.x, pc.core, pl.ds(0, tok), pl.ds(t * 128, 128)] = head_tile(
                heads_w // 128 + t, g_k
            ).astype(bf16)
        kvb[pc.y, pc.x, pc.core, pl.ds(0, tok), pl.ds(kv_w, kv_w)] = qkv_ref[
            :, pl.ds(heads_w + kv_w, kv_w)
        ].astype(bf16)
        blocks_row = jnp.broadcast_to(hi_ref[...], (16, tok)).astype(bf16)
        kvb[pc.y, pc.x, pc.core, pl.ds(tok, 16), pl.ds(0, tok)] = blocks_row
        kvb[pc.y, pc.x, pc.core, pl.ds(tok, 16), pl.ds(tok, tok)] = blocks_row
        seq.own()

    def query_tile(t, _):
        q = (head_tile(t, g_q) * 0.125).astype(bf16)
        zero = jnp.zeros_like(q)
        q2_ref[t, pl.ds(0, tok), :] = jnp.where(low, q, zero)
        q2_ref[t, pl.ds(tok, tok), :] = jnp.where(low, zero, q)
        return 0

    def queries():
        lax.fori_loop(0, heads_w // 128, query_tile, 0)
        emit(qkv_ref, o_kv)
        emit(q2_ref, o_q2)
        emit(w_qkv, o_wqkv)
        sent_cot.wait_recv()
        emit(cot2, o_cot)
        sent_attn.wait_recv()
        emit(t_attn, o_tattn)

    def unpack(b, _):
        y, x, c = b // 4, (b // 2) % 2, b % 2
        rows = pl.ds(pl.multiple_of(b * tok, tok), tok)
        for t in range(kv_w // 128):
            k = kvb[y, x, c, pl.ds(0, tok), pl.ds(t * 128, 128)].astype(f32)
            v = kvb[y, x, c, pl.ds(0, tok), pl.ds(kv_w + t * 128, 128)].astype(f32)
            k_r, v_r = roll_half(k), roll_half(v)
            kk[2 * t, rows, :] = jnp.where(low, k, k_r).astype(bf16)
            kk[2 * t + 1, rows, :] = jnp.where(low, k_r, k).astype(bf16)
            va[2 * t, rows, :] = jnp.where(low, v, 1.0).astype(bf16)
            va[2 * t + 1, rows, :] = jnp.where(low, v_r, 1.0).astype(bf16)
        step = tok // 2
        key_hi = kvb[y, x, c, pl.ds(tok, 16), pl.ds(0, tok)].astype(f32)[:1, :]
        for a in range(2):
            own = hi_ref[:, a * step : (a + 1) * step].astype(f32)
            row = lax.broadcasted_iota(jnp.int32, (step, step), 0).astype(f32)
            col = lanes((step, step)).astype(f32)
            for d in range(2):
                theirs = key_hi[:, d * step : (d + 1) * step]
                gap = (own - theirs) * float(step) + row - col
                place = pl.ds(pl.multiple_of(b * tok + d * step, step), step)
                mask[pl.ds(a * step, step), place] = jnp.where(gap >= 0, 1.0, 0.0).astype(bf16)
                gap = (own - theirs) * float(step) + col - row
                mask_t[place, pl.ds(a * step, step)] = jnp.where(gap >= 0, 1.0, 0.0).astype(bf16)
        return 0

    def unpack_all():
        seq.done_event()
        lax.fori_loop(0, n_dev, unpack, 0)
        emit(kk, o_kk)
        emit(va, o_va)
        emit(mask_t, o_mask)

    chunk = 512
    n_chunk = n_dev * tok // chunk

    def attend(tick):
        t, kc = tick // n_chunk, tick % n_chunk
        g = t // 2
        rows = pl.ds(pl.multiple_of(kc * chunk, chunk), chunk)
        s = dot_t(q2_ref[t], kk[g, rows, :])
        e = jnp.exp2(s * LOG2E).astype(bf16).reshape(2, tok, chunk) * mask[:, rows][None]
        o = dot(e.reshape(2 * tok, chunk), va[g, rows, :])

        @pl.when(kc == 0)
        def _():
            o2[...] = o

        @pl.when(kc > 0)
        def _():
            o2[...] += o

        @pl.when(kc == n_chunk - 1)
        def _():
            even, odd = o2[pl.ds(0, tok), :], o2[pl.ds(tok, tok), :]
            total = jnp.where(low, roll_half(even), odd)
            inv = 1.0 / total
            mixed = jnp.where(low, even, roll_half(odd)) * inv
            linv_ref[:, cols(t, 128)] = inv
            mixf_ref[:, cols(t, 128)] = mixed
            mixb_ref[:, cols(t, 128)] = mixed.astype(bf16)

    def mix_out():
        emit(linv_ref, o_linv)
        emit(mixf_ref, o_mixf)
        turn(mixb_ref, s_out.shape[0], pc.core, t_mix, turn_b)
        sent_mix.start()

    def residual_step(n, _):
        c = cols(n, 256)
        w = w_out[:, :, :, :, :, c].reshape(heads_w, 256)
        res_ref[:, c] = x_ref[:, c].astype(f32) + dot(mixb_ref[...], w)
        return 0

    def residual():
        for i in range(NZ):
            out.done_event(i)
        emit(w_out, o_wout)
        lax.fori_loop(0, width // 256, residual_step, 0)

    def second_norm():
        norm_into(res_ref, g_ffn, hffn_ref)

    def second_turn():
        emit(res_ref, o_res)
        sent_mix.wait_recv()
        emit(t_mix, o_tmix)
        sent_attn.wait_send()
        turn(hffn_ref, s_gu.shape[0], pc.core, t_ffn, turn_a)
        sent_ffn.start()

    def gate_step(n, _):
        c = cols(n, 256)
        c2 = cols(n + ff // 256, 256)
        gate, up, grad = gu[:, c], gu[:, c2], gact[:, c]
        sig = 1.0 / (1.0 + jnp.exp(-gate))
        silu = gate * sig
        act_ref[:, c] = (silu * up).astype(bf16)
        ggu2[pl.ds(0, tok), c] = (grad * up * (sig * (1.0 + gate * (1.0 - sig)))).astype(bf16)
        ggu2[pl.ds(0, tok), c2] = (grad * silu).astype(bf16)
        return 0

    def gates():
        lax.fori_loop(0, ff // 256, gate_step, 0)
        sent_ggu.start()
        emit(w_gu, o_wgu)

    def act_out():
        sent_mix.wait_send()
        turn(act_ref, s_down.shape[0], pc.core, t_act, turn_b)
        sent_act.start()
        sent_ffn.wait_recv()
        emit(t_ffn, o_tffn)

    def output_step(n, _):
        c = cols(n, 256)
        w = w_down[:, :, :, :, :, c].reshape(ff, 256)
        y_ref[:, c] = (res_ref[:, c] + dot(act_ref[...], w)).astype(bf16)
        return 0

    def outputs():
        lax.fori_loop(0, width // 256, output_step, 0)
        emit(y_ref, o_y)
        sent_ggu.wait_recv()
        emit(ggu2, o_ggu)
        sent_act.wait_recv()
        emit(t_act, o_tact)

    steps = {
        "norm": first_norm, "turn": first_turn, "keys": keys_out, "query": queries,
        "kve": seq.plane_event, "kvc": seq.core_event, "unpack": unpack_all, "mix": mix_out,
        "res": residual, "norm2": second_norm, "turn2": second_turn, "gate": gates,
        "act": act_out, "y": outputs, "oP": out.own_plane, "oZ": out.own_z, "oe": out.plane_event,
        "oD": out.diag_event,
    }
    for letter, g in (("q", qkv), ("d", down), ("g", gateup)):
        steps.update(line_steps(letter, g))
    for i in range(NZ):
        steps[f"qs{i}"] = part(columns_step, qkv, i, hattn_ref, w_qkv, qkv_ref, width // NZ)
        steps[f"gs{i}"] = part(columns_step, gateup, i, hffn_ref, w_gu, gu, width // NZ)
        steps[f"ds{i}"] = part(grad_act_step, i)
        if i:
            steps[f"oc{i}"] = part(out.core_event, i)
            for k in range(4):
                steps[f"oz{i}{k}"] = part(out.z_event, i, k)
    run_steps(FORWARD_ORDER, steps, {"A": (heads_w // 128 * n_chunk, attend)})
    for g in (qkv, out, down, gateup, seq):
        g.finish()
    for c in (sent_cot, sent_ffn, sent_act, sent_ggu):
        c.wait_send()
    for c in emitted:
        c.wait()


def forward(x, cot, blocks, cosine, sine, g_attn, g_q, g_k, g_ffn, s_qkv, s_out, s_down, s_gu, n_dev):
    tok, width = x.shape
    heads_w, kv_w = HEADS * HEAD_DIM, GROUPS * HEAD_DIM
    ff = s_down.shape[0] * n_dev * NZ
    length = n_dev * tok
    tiles = heads_w // 128
    shape = jax.ShapeDtypeStruct
    seven = [(NZ, 2, 2, 2) + s.shape for s in (s_qkv, s_out, s_down, s_gu)]
    qkv_rows, out_rows, down_rows, gu_rows = [s.shape[0] for s in (s_qkv, s_out, s_down, s_gu)]
    spots = n_dev * NZ // 2
    kv_buf = ((2, 2, 2, tok + 16, 2 * kv_w), bf16)
    turned = [((spots, r, 2 * tok), bf16) for r in (qkv_rows, out_rows, gu_rows, down_rows)]
    keep = [
        ((tok, width), bf16),
        *turned,
        ((2 * tok, width), bf16),
        ((2 * tok, 2 * ff), bf16),
        ((tok, s_qkv.shape[1]), f32),
        ((tiles, 2 * tok, 128), bf16),
        ((tok, heads_w), f32),
        ((tok, heads_w), f32),
        ((tok, width), f32),
        ((GROUPS, length, 128), bf16),
        ((GROUPS, length, 128), bf16),
        ((length, tok), bf16),
        (seven[0], bf16),
        (seven[1], bf16),
        (seven[3], bf16),
    ]
    outs = [shape(*k) for k in keep]
    vm = pl.BlockSpec(memory_space=VMEM)
    anyw = pl.BlockSpec(memory_space=pl.ANY)
    dma = pltpu.SemaphoreType.DMA
    flops = 2 * tok * (width * (s_qkv.shape[1] + heads_w + 2 * ff + 2 * ff) + 2 * heads_w * length)
    return pl.pallas_call(
        functools.partial(forward_kernel, (tok, width, n_dev, heads_w, kv_w, ff)),
        out_shape=outs,
        in_specs=[vm] * 9 + [anyw] * 4,
        out_specs=[anyw] * len(outs),
        scratch_shapes=[VMEM(s, bf16) for s in seven]
        + [
            VMEM((GROUPS, length, 128), bf16),
            VMEM((GROUPS, length, 128), bf16),
            VMEM((tok, length), bf16),
            VMEM((length, tok), bf16),
            VMEM((2 * tok, 128), f32),
            VMEM((tok, 2 * ff), f32),
            VMEM((tok, ff), f32),
            VMEM((tok, width), bf16),
            VMEM((tok, width), bf16),
            VMEM((tok, s_qkv.shape[1]), f32),
            VMEM((tiles, 2 * tok, 128), bf16),
            VMEM(*kv_buf),
            VMEM((tok, heads_w), f32),
            VMEM((tok, heads_w), f32),
            VMEM((tok, heads_w), bf16),
            VMEM((tok, width), f32),
            VMEM((tok, width), bf16),
            VMEM((tok, ff), bf16),
            VMEM((2 * tok, width), bf16),
            VMEM((2 * tok, 2 * ff), bf16),
            *[VMEM(*t) for t in turned],
            VMEM((spots, qkv_rows, tok), bf16),
            VMEM((spots, out_rows, tok), bf16),
            dma((4, 18, NZ)),
            dma((4, 14, NZ)),
            dma((8,)),
            dma((8,)),
            dma((4,)),
            dma((len(outs),)),
            dma((6,)),
            dma((6,)),
        ],
        compiler_params=pltpu.CompilerParams(
            collective_id=0, has_side_effects=True, vmem_limit_bytes=60 << 20
        ),
        cost_estimate=pl.CostEstimate(flops=flops, bytes_accessed=50 << 20, transcendentals=0),
        name="forward",
    )(x, cot, blocks, cosine, sine, g_attn, g_q, g_k, g_ffn, s_qkv, s_out, s_down, s_gu)


SD0, SD1, SX0, SX1, SY0, SY1, SA, SB = range(8)


class PlaneSum:
    def plane_setup(self, pc, rd, rx, ry, send, recv):
        self.pc, self.rd, self.rx, self.ry, self.send, self.recv = pc, rd, rx, ry, send, recv

    def cp(self, src, dst, dev, k, s):
        return remote(src, dst, dev, self.send.at[k, s], self.recv.at[k, s])

    def d0(self, s):
        p = self.pc
        return self.cp(self.piece(s, 1 - p.y, 1 - p.x, 0), self.rd.at[s, 0], p.yn(), SD0, s)

    def d1(self, s):
        p = self.pc
        return self.cp(self.piece(s, 1 - p.y, 1 - p.x, 1), self.rd.at[s, 1], p.xn(), SD1, s)

    def x1(self, s):
        p = self.pc
        return self.cp(self.piece(s, p.y, 1 - p.x, 1), self.rx.at[s, 1], p.xn(), SX1, s)

    def y0(self, s):
        p = self.pc
        return self.cp(self.piece(s, 1 - p.y, p.x, 0), self.ry.at[s, 0], p.yn(), SY0, s)

    def x0(self, s):
        return self.cp(self.rd.at[s, 0], self.rx.at[s, 0], self.pc.xn(), SX0, s)

    def y1(self, s):
        return self.cp(self.rd.at[s, 1], self.ry.at[s, 1], self.pc.yn(), SY1, s)

    def plane_far(self, s):
        self.d0(s).start()
        self.d1(s).start()

    def plane_near(self, s):
        self.x1(s).start()
        self.y0(s).start()

    def plane_first(self, s):
        self.plane_far(s)
        self.plane_near(s)

    def plane_second(self, s):
        p = self.pc
        self.d0(s).wait_recv()
        self.rd[s, 0] = self.rd[s, 0] + self.piece(s, p.y, 1 - p.x, 0)[...]
        self.x0(s).start()
        self.d1(s).wait_recv()
        self.rd[s, 1] = self.rd[s, 1] + self.piece(s, 1 - p.y, p.x, 1)[...]
        self.y1(s).start()

    def plane_arrived(self, s):
        for c in (self.x1, self.y0, self.x0, self.y1):
            c(s).wait_recv()

    def plane_total(self, s, k):
        p = self.pc
        own = self.piece(s, p.y, p.x, k)[...].astype(f32)
        return own + self.rx[s, k].astype(f32) + self.ry[s, k].astype(f32)

    def plane_finish(self, s):
        for c in (self.d0, self.d1, self.x1, self.y0, self.x0, self.y1):
            c(s).wait_send()


class Scatter(PlaneSum):
    def __init__(self, pc, part, bufs, out, send, recv):
        rd, rx, ry, self.zz = bufs
        self.plane_setup(pc, rd, rx, ry, send, recv)
        self.part, self.out = part, out
        self.h = halves(part.shape[-2])

    @staticmethod
    def scratch(rows, columns):
        half = VMEM((NZ, 2, rows // 2, columns), bf16)
        return [half, half, half, VMEM((NZ + 1, 2, rows // 2, columns), bf16)]

    def piece(self, s, y, x, k):
        return self.part.at[s, y, x, self.h[k]]

    def down(self, zp):
        return self.cp(self.rx.at[zp], self.zz.at[zp], self.pc.down(), SA, zp)

    def up(self, zp):
        gap = zp - (self.pc.z + 1)
        spot = zp + (1 - (gap + NZ - 1) // NZ) * (NZ - zp)
        return self.cp(self.rx.at[zp], self.zz.at[spot], self.pc.up(), SB, zp)

    def far_event(self, i):
        self.plane_far(far(self.pc.z, i))

    def near_event(self, i):
        self.plane_near(far(self.pc.z, i))

    def d_event(self, i):
        self.plane_second(far(self.pc.z, i))

    def xy_event(self, i):
        zp = far(self.pc.z, i)
        self.plane_arrived(zp)
        for k in range(2):
            self.rx[zp, k] = self.plane_total(zp, k).astype(bf16)

    def z_event(self, i):
        z = self.pc.z
        zp = far(z, i)

        @pl.when(zp < z)
        def _():
            @pl.when(z < NZ - 1)
            def _():
                self.down(zp).wait_recv()
                self.rx[zp] = self.rx[zp] + self.zz[zp]

            self.down(zp).start()

        @pl.when(zp > z)
        def _():
            @pl.when(z > 0)
            def _():
                self.up(zp).wait_recv()
                self.rx[zp] = self.rx[zp] + self.zz[zp]

            self.up(zp).start()

    def final(self):
        z = self.pc.z
        self.plane_arrived(z)
        for k in range(2):
            self.out[self.h[k], :] = self.plane_total(z, k)

        @pl.when(z < NZ - 1)
        def _():
            self.down(z).wait_recv()
            for k in range(2):
                self.out[self.h[k], :] += self.zz[z, k].astype(f32)

        @pl.when(z > 0)
        def _():
            self.up(z).wait_recv()
            for k in range(2):
                self.out[self.h[k], :] += self.zz[NZ, k].astype(f32)

    def finish(self):
        z = self.pc.z
        for zp in range(NZ):
            self.plane_finish(zp)

            @pl.when(zp < z)
            def _():
                self.down(zp).wait_send()

            @pl.when(zp > z)
            def _():
                self.up(zp).wait_send()


class ScatterZ(PlaneSum):
    def __init__(self, pc, part, bufs, out, send, recv):
        rd, rx, ry, self.zz, self.sm = bufs
        self.plane_setup(pc, rd, rx, ry, send, recv)
        self.part, self.out = part, out
        self.h = halves(part.shape[-2])

    @staticmethod
    def scratch(rows, columns):
        half = VMEM((1, 2, rows // 2, columns), bf16)
        return [half, half, half, VMEM((NZ + 1, 4, rows, columns), bf16), VMEM((4, rows, columns), bf16)]

    def piece(self, s, y, x, k):
        return self.sm.at[y * 2 + x, self.h[k]]

    def down(self, zp, k, src):
        return self.cp(src, self.zz.at[zp, k], self.pc.down(), 8 + zp, k)

    def up(self, zp, k, src):
        gap = zp - (self.pc.z + 1)
        spot = zp + (1 - (gap + NZ - 1) // NZ) * (NZ - zp)
        return self.cp(src, self.zz.at[spot, k], self.pc.up(), 12 + zp, k)

    def first(self, i):
        z = self.pc.z
        zp = far(z, i)
        for k in range(4):
            src = self.part.at[zp, k // 2, k % 2]

            @pl.when((z == NZ - 1) & (zp < z))
            def _():
                self.down(zp, k, src).start()

            @pl.when((z == 0) & (zp > z))
            def _():
                self.up(zp, k, src).start()

    def z_event(self, i, k):
        z = self.pc.z
        zp = far(z, i)
        held = self.zz.at[zp, k]

        @pl.when((zp < z) & (z < NZ - 1))
        def _():
            self.down(zp, k, held).wait_recv()
            self.zz[zp, k] = self.zz[zp, k] + self.part[zp, k // 2, k % 2]
            self.down(zp, k, held).start()

        @pl.when((zp > z) & (z > 0))
        def _():
            self.up(zp, k, held).wait_recv()
            self.zz[zp, k] = self.zz[zp, k] + self.part[zp, k // 2, k % 2]
            self.up(zp, k, held).start()

    def own_event(self, k):
        z = self.pc.z

        @pl.when(z < NZ - 1)
        def _():
            self.down(z, k, self.zz.at[z, k]).wait_recv()

        @pl.when(z > 0)
        def _():
            self.up(z, k, self.zz.at[z, k]).wait_recv()

        own = self.part[z, k // 2, k % 2].astype(f32)

        @pl.when(z == 0)
        def _():
            self.sm[k] = (own + self.zz[z, k].astype(f32)).astype(bf16)

        @pl.when(z == NZ - 1)
        def _():
            self.sm[k] = (own + self.zz[NZ, k].astype(f32)).astype(bf16)

        @pl.when((z > 0) & (z < NZ - 1))
        def _():
            both = self.zz[z, k].astype(f32) + self.zz[NZ, k].astype(f32)
            self.sm[k] = (own + both).astype(bf16)

    def plane_send(self):
        self.plane_first(0)

    def plane_event(self):
        self.plane_second(0)

    def final(self):
        self.plane_arrived(0)
        for k in range(2):
            self.out[self.h[k], :] = self.plane_total(0, k)

    def finish(self):
        z = self.pc.z
        self.plane_finish(0)
        for zp in range(NZ):
            for k in range(4):

                @pl.when(zp < z)
                def _():
                    self.down(zp, k, self.zz.at[zp, k]).wait_send()

                @pl.when(zp > z)
                def _():
                    self.up(zp, k, self.zz.at[zp, k]).wait_send()


class SequenceSum(PlaneSum):
    def __init__(self, pc, terms, bufs, send, recv, core_send, core_recv):
        rd, rx, ry, self.theirs = bufs
        self.plane_setup(pc, rd, rx, ry, send, recv)
        self.terms, self.core_send, self.core_recv = terms, core_send, core_recv
        self.h = halves(terms.shape[-2])

    @staticmethod
    def scratch(rows, columns):
        half = VMEM((1, 2, rows // 2, columns), bf16)
        return [half, half, half, VMEM((2, 2, rows, columns), bf16)]

    def piece(self, s, y, x, k):
        return self.theirs.at[y, x, self.h[k]]

    def swap(self):
        p = self.pc
        return remote(
            self.terms.at[:, :, 1 - p.core], self.theirs, p.sn(), self.core_send, self.core_recv
        )

    def core_event(self):
        p = self.pc
        self.swap().wait_recv()
        for y in range(2):
            for x in range(2):
                self.theirs[y, x] = self.theirs[y, x] + self.terms[y, x, p.core]
        self.plane_first(0)

    def finish(self):
        self.swap().wait_send()
        self.plane_finish(0)


def norm_back(src, gain, grad, part_ref, part_row, emit):
    part_ref[pl.ds(part_row, 1), :] = jnp.zeros((1, part_ref.shape[1]), f32)

    def body(i, _):
        rows = pl.ds(pl.multiple_of(i * 32, 32), 32)
        v, g = src[rows, :].astype(f32), grad[rows, :]
        inv = lax.rsqrt(jnp.mean(v * v, axis=-1, keepdims=True) + EPS)
        unit = v * inv
        part_ref[pl.ds(part_row, 1), :] += jnp.sum(g * unit, axis=0, keepdims=True)
        gg = g * gain[...]
        emit(rows, inv * (gg - unit * jnp.mean(gg * unit, axis=-1, keepdims=True)))
        return 0

    lax.fori_loop(0, src.shape[0] // 32, body, 0)


def sum_steps(letter, g):
    part = functools.partial
    steps = {letter + "f": g.final}
    for i in range(NZ):
        steps[f"{letter}a{i}"] = part(g.far_event, i)
        steps[f"{letter}b{i}"] = part(g.near_event, i)
        steps[f"{letter}d{i}"] = part(g.d_event, i)
        if i < NZ - 1:
            steps[f"{letter}x{i}"] = part(g.xy_event, i)
            steps[f"{letter}z{i}"] = part(g.z_event, i)
    return steps


def weight_grad(left, zp, right, part):
    rows, columns = part.shape[-2:]
    lhs = left[pl.ds(zp * 4, 4)].reshape(4 * rows, left.shape[-1])
    step = 512

    def body(n, _):
        c = cols(n, step)
        part[zp, :, :, :, c] = dot(lhs, right[:, c]).astype(bf16).reshape(2, 2, rows, step)
        return 0

    lax.fori_loop(0, columns // step, body, 0)


LOADS = [
    "act", "cot", "ffn", "ggu", "wgu", "res", "mix", "mixf", "linv", "q2", "kk", "va", "mask",
    "qkv", "wout",
]


def backward_kernel(dims, *refs):
    (tok, width, n_dev, heads_w, kv_w, ff) = dims
    (
        cos_ref, sin_ref, g_q, g_k, g_ffn,
        i_tmix, i_tffn, i_tact, i_cot, i_ggu, i_qkv, i_q2, i_linv, i_mixf, i_res, i_kk, i_va,
        i_mask, i_wout, i_wgu,
        gqkv2, res, gains, out_wout, out_wgu, out_wdown,
        t_mix, t_ffn, t_act, cot2, ggu2, qkv, q2, linv, mixf, kk, va, mask_t, w_gu,
        part_out, part_gu, part_down, gh, gattn2, acc_k, acc_v, acc_q, aug, gm, terms,
        send, recv, kv_send, kv_recv, ex_send, ex_recv, lsem,
    ) = refs[:57]
    bufs = refs[57:]
    pc = Place()
    z = pc.z
    part = functools.partial
    loads = {}

    def load(name, src, dst):
        c = pltpu.make_async_copy(src, dst, lsem.at[LOADS.index(name)])
        loads[name] = c
        c.start()

    load("act", i_tact, t_act)
    load("cot", i_cot, cot2)
    load("ffn", i_tffn, t_ffn)
    load("ggu", i_ggu, ggu2)
    load("wgu", i_wgu, w_gu)
    load("res", i_res, res)
    load("mix", i_tmix, t_mix)
    load("mixf", i_mixf, mixf)
    load("linv", i_linv, linv)
    load("q2", i_q2, q2)
    load("kk", i_kk, kk)
    load("va", i_va, va)
    load("mask", i_mask, mask_t)
    load("qkv", i_qkv, qkv)
    barrier(pc)
    down = Scatter(pc, part_down, bufs[0:4], out_wdown, send.at[0], recv.at[0])
    gateup = Scatter(pc, part_gu, bufs[4:8], out_wgu, send.at[1], recv.at[1])
    out = ScatterZ(pc, part_out, bufs[8:13], out_wout, send.at[2], recv.at[2])
    seq = SequenceSum(pc, terms, bufs[13:17], kv_send, kv_recv, ex_send.at[2], ex_recv.at[2])

    own = pl.ds(0, tok)
    back = pl.ds(tok, tok)

    def rows_of(left, right, term, names, i):
        for name in names:
            if name in loads:
                loads.pop(name).wait()
        weight_grad(left, far(z, i), right, term)

    def h_step(n):
        w = w_gu[n // 2, n % 2].reshape(width // 8, 2 * ff)
        gh[:, cols(n, width // 8)] = dot_t(ggu2[own, :], w)

    def start_h():
        loads.pop("wgu").wait()
        loads.pop("res").wait()

    def keep_residual(rows, grad):
        total = cot2[rows, :].astype(f32) + grad
        res[rows, :] = total
        gattn2[rows, :] = total.astype(bf16)

    sent_attn = remote(gattn2.at[own, :], gattn2.at[back, :], pc.sn(), ex_send.at[0], ex_recv.at[0])

    def residual_back():
        load("wout", i_wout, w_gu.at[:, :, :, :, pl.ds(0, part_out.shape[-2]), :])
        gains[...] = jnp.zeros_like(gains)
        norm_back(res, g_ffn, gh, gains, 1, keep_residual)
        sent_attn.start()
        loads.pop("wout").wait()

    def m_step(n, _):
        w = w_gu[n, :, :, :, pl.ds(0, part_out.shape[-2]), :].reshape(heads_w // NZ, width)
        gm[:, cols(n, heads_w // NZ)] = dot_t(gattn2[own, :], w).astype(bf16)
        return 0

    def mixed_back():
        lax.fori_loop(0, NZ, m_step, 0)
        sent_attn.wait_recv()

    def start_attention():
        for name in ("mixf", "linv", "q2", "kk", "va", "mask", "qkv"):
            loads.pop(name).wait()

    low = lanes((tok, 128)) < 64
    chunk = 512
    n_chunk = n_dev * tok // chunk
    def attend(tick):
        t, kc = tick // n_chunk, tick % n_chunk
        g = t // 2
        rows = pl.ds(pl.multiple_of(kc * chunk, chunk), chunk)

        @pl.when(kc == 0)
        def _():
            c = cols(t, 128)
            grad = gm[:, c].astype(f32)
            delta = head_sums(grad * mixf[:, c]) * linv[:, c]
            grad = grad * linv[:, c]
            lane = lanes((tok, 128))
            for half in range(2):
                d = roll_half(delta) if half == 0 else delta
                v = grad if half == 0 else roll_half(grad)
                high = d.astype(bf16).astype(f32)
                rest = jnp.where(lane == 64, -high, jnp.where(lane == 65, high - d, 0.0))
                aug[pl.ds(half * tok, tok), :] = jnp.where(low, v, rest).astype(bf16)

        seen = mask_t[rows, :]
        e = jnp.exp2(dot_t(kk[g, rows, :], q2[t]) * LOG2E).astype(bf16)
        e = e * jnp.concatenate([seen, seen], axis=1)
        dv = dot(e, aug[...])
        ds = e * dot_t(va[g, rows, :], aug[...]).astype(bf16)
        dk = dot(ds, q2[t])
        dq = lax.dot_general(kk[g, rows, :], ds, (((0,), (0,)), ((), ())), preferred_element_type=f32)

        @pl.when(t % 2 == 0)
        def _():
            acc_k[rows, :] = dk
            acc_v[rows, :] = dv

        @pl.when(t % 2 == 1)
        def _():
            both_k = acc_k[rows, :] + dk
            both_v = acc_v[rows, :] + dv
            both_k = both_k + roll_half(both_k)
            lower = lanes((chunk, 128)) < 64
            both_v = jnp.where(lower, both_v, roll_half(both_v))
            mine = (lanes((chunk, 128)) // 64) == (g % 2)
            for b in range(chunk // tok):
                spot = kc * (chunk // tok) + b
                y, x, c = spot // 4, (spot // 2) % 2, spot % 2
                cut = slice(b * tok, (b + 1) * tok)
                for base, value in ((0, both_k), (kv_w, both_v)):
                    place = pl.ds(pl.multiple_of(base + (g // 2) * 128, 128), 128)
                    old = terms[y, x, c, :, place].astype(f32)
                    terms[y, x, c, :, place] = jnp.where(mine[cut], value[cut], old).astype(bf16)

        @pl.when(kc == 0)
        def _():
            acc_q[...] = dq

        @pl.when(kc > 0)
        def _():
            acc_q[...] += dq

        @pl.when(kc == n_chunk - 1)
        def _():
            turned = jnp.transpose(acc_q[...])
            gh[:, cols(t, 128)] = jnp.where(low, turned[:tok], turned[tok:]) * 0.125


    def head_back(t, grad, gain, row):
        c = cols(t, 128)
        u = qkv[:, c]
        inv = lax.rsqrt(head_sums(u * u) * (1.0 / 64) + EPS)
        unit = u * inv
        grad = grad * cos_ref[...] - swap_rot(grad) * sin_ref[...]
        gains[pl.ds(row, 1), pl.ds(0, 128)] += jnp.sum(grad * unit, axis=0, keepdims=True)
        gg = grad * gain[...]
        gqkv2[own, c] = (inv * (gg - unit * head_sums(gg * unit) * (1.0 / 64))).astype(bf16)

    def query_back(t):
        head_back(t, gh[:, cols(t, 128)], g_q, 2)

    sent_qkv = remote(gqkv2.at[own, :], gqkv2.at[back, :], pc.sn(), ex_send.at[1], ex_recv.at[1])

    def keys_back():
        seq.plane_arrived(0)
        for k in range(2):
            gh[seq.h[k], pl.ds(0, 2 * kv_w)] = seq.plane_total(0, k)
        for t in range(kv_w // 128):
            head_back(heads_w // 128 + t, gh[:, pl.ds(t * 128, 128)], g_k, 3)
        gqkv2[own, pl.ds(heads_w + kv_w, kv_w)] = gh[:, pl.ds(kv_w, kv_w)].astype(bf16)
        sent_qkv.start()

    steps = {
        "h": start_h, "nb": residual_back, "m": mixed_back, "att": start_attention,
        "kvs": seq.swap().start, "kvc": seq.core_event, "kve": part(seq.plane_second, 0),
        "kvf": keys_back, "oS": out.plane_send, "oe": out.plane_event, "of": out.final,
    }
    steps.update(sum_steps("d", down))
    steps.update(sum_steps("g", gateup))
    for i in range(NZ):
        steps[f"dw{i}"] = part(rows_of, t_act, cot2, part_down, ("act", "cot"), i)
        steps[f"gw{i}"] = part(rows_of, t_ffn, ggu2, part_gu, ("ffn", "ggu"), i)
        steps[f"ow{i}"] = part(rows_of, t_mix, gattn2, part_out, ("mix",), i)
        steps[f"oa{i}"] = part(out.first, i)
        steps[f"oo{i}"] = part(out.own_event, i)
        if i < NZ - 1:
            for k in range(4):
                steps[f"oz{i}{k}"] = part(out.z_event, i, k)
    loops = {
        "H": (8, h_step),
        "B": (heads_w // 128 * n_chunk, attend),
        "Q": (heads_w // 128, query_back),
    }
    run_steps(BACKWARD_ORDER, steps, loops)
    sent_qkv.wait_recv()
    for g in (down, gateup, out, seq):
        g.finish()
    sent_attn.wait_send()
    sent_qkv.wait_send()


def last_kernel(dims, *refs):
    (tok, width, n_dev, heads_w, kv_w, ff) = dims
    (
        x_ref, g_attn, gqkv2, res, gains, i_tattn, i_wqkv,
        dx, o_attn, o_q, o_k, o_ffn, out_wqkv,
        t_attn, w_qkv, part_qkv, gh, held, came,
        send, recv, g_send, g_recv, lsem,
    ) = refs[:24]
    pc = Place()
    z = pc.z
    part = functools.partial
    load_t = pltpu.make_async_copy(i_tattn, t_attn, lsem.at[0])
    load_w = pltpu.make_async_copy(i_wqkv, w_qkv, lsem.at[1])
    load_t.start()
    load_w.start()
    bar = pltpu.get_barrier_semaphore()
    for device in (pc.xn(), pc.yn(), pc.sn()):
        pl.semaphore_signal(bar, inc=1, device_id=device, device_id_type=MESH)
    for k in range(1, NZ):
        there = pc.at(z=(z + k) % NZ)
        pl.semaphore_signal(bar, inc=1, device_id=there, device_id_type=MESH)
    pl.semaphore_wait(bar, 3 + NZ - 1)
    qkv = Scatter(pc, part_qkv, refs[24:28], out_wqkv, send, recv)
    load_t.wait()
    columns = w_qkv.shape[-1]

    def h_step(n):
        w = w_qkv[n // 2, n % 2].reshape(width // 8, columns)
        gh[:, cols(n, width // 8)] = dot_t(gqkv2[pl.ds(0, tok), :], w)

    def keep_input(rows, grad):
        dx[rows, :] = (res[rows, :] + grad).astype(bf16)

    def input_back():
        held[...] = gains[...]
        norm_back(x_ref, g_attn, gh, held, 0, keep_input)

    def hop(k):
        device = (pc.sn(), pc.xn(), pc.yn())[k]
        return remote(held, came.at[k], device, g_send.at[k], g_recv.at[k])

    def hop_end(k):
        hop(k).wait()
        held[...] += came[k]

    def ring(k):
        there = pc.at(z=(z + k) % NZ)
        return remote(held, came.at[3 + z], there, g_send.at[2 + k], g_recv.at[3 + z])

    def ring_start():
        came[3 + z] = held[...]
        for k in range(1, NZ):
            ring(k).start()

    def ring_end():
        for k in range(1, NZ):
            there = (z + k) % NZ
            slot = came.at[3 + there]
            remote(held, slot, pc.at(z=there), g_send.at[2 + k], g_recv.at[3 + there]).wait_recv()
        total = came[3]
        for k in range(1, NZ):
            total = total + came[3 + k]
        o_attn[...] = total[0:1]
        o_ffn[...] = total[1:2]
        for o, row in ((o_q, 2), (o_k, 3)):
            v = total[:, :128]
            o[...] = (v + roll_half(v))[row : row + 1, :64]

    steps = {"h": load_w.wait, "nb": input_back, "rs": ring_start, "re": ring_end}
    steps.update(sum_steps("q", qkv))
    for i in range(NZ):
        steps[f"qw{i}"] = part(weight_grad, t_attn, far(z, i), gqkv2, part_qkv)
        if i < 3:
            steps[f"hs{i}"] = hop(i).start
            steps[f"he{i}"] = part(hop_end, i)
    run_steps(LAST_ORDER, steps, {"H": (8, h_step)})
    for k in range(1, NZ):
        ring(k).wait_send()
    qkv.finish()


def backward(x, cosine, sine, g_attn, g_q, g_k, g_ffn, kept, rows, n_dev):
    (t_attn, t_mix, t_ffn, t_act, cot2, ggu2, qkv, q2, linv, mixf, res, kk, va, mask_t, w_qkv, w_out, w_gu) = kept
    tok, width = x.shape
    heads_w, kv_w = HEADS * HEAD_DIM, GROUPS * HEAD_DIM
    ff = ggu2.shape[1] // 2
    length = n_dev * tok
    columns = qkv.shape[1]
    dims = (tok, width, n_dev, heads_w, kv_w, ff)
    shape = jax.ShapeDtypeStruct
    vm = pl.BlockSpec(memory_space=VMEM)
    anyw = pl.BlockSpec(memory_space=pl.ANY)
    dma = pltpu.SemaphoreType.DMA
    r_qkv, r_out, r_gu, r_down = rows
    partial = [VMEM((NZ, 2, 2, r, width), bf16) for r in (r_out, r_gu, r_down)]
    like = [VMEM(v.shape, v.dtype) for v in (t_mix, t_ffn, t_act, cot2, ggu2, qkv, q2, linv, mixf, kk, va, mask_t, w_gu)]
    gqkv2, grad_res, gains, own_out, own_gu, own_down = pl.pallas_call(
        functools.partial(backward_kernel, dims),
        out_shape=[
            shape((2 * tok, columns), bf16),
            shape((tok, width), f32),
            shape((8, width), f32),
            shape((r_out, width), f32),
            shape((r_gu, width), f32),
            shape((r_down, width), f32),
        ],
        in_specs=[vm] * 5 + [anyw] * 15,
        out_specs=[vm] * 6,
        scratch_shapes=like
        + partial
        + [
            VMEM((tok, width), f32),
            VMEM((2 * tok, width), bf16),
            VMEM((length, 128), f32),
            VMEM((length, 128), f32),
            VMEM((128, 2 * tok), f32),
            VMEM((2 * tok, 128), bf16),
            VMEM((tok, heads_w), bf16),
            VMEM((2, 2, 2, tok, 2 * kv_w), bf16),
            dma((3, 16, NZ)),
            dma((3, 16, NZ)),
            dma((8, 1)),
            dma((8, 1)),
            dma((3,)),
            dma((3,)),
            dma((15,)),
        ]
        + Scatter.scratch(r_down, width)
        + Scatter.scratch(r_gu, width)
        + ScatterZ.scratch(r_out, width)
        + SequenceSum.scratch(tok, 2 * kv_w),
        compiler_params=pltpu.CompilerParams(
            collective_id=1, has_side_effects=True, vmem_limit_bytes=63 << 20
        ),
        cost_estimate=pl.CostEstimate(flops=20 * tok * width * width, bytes_accessed=60 << 20, transcendentals=0),
        name="backward",
    )(cosine, sine, g_q, g_k, g_ffn, t_mix, t_ffn, t_act, cot2, ggu2, qkv, q2, linv, mixf, res, kk, va, mask_t, w_out, w_gu)
    last = pl.pallas_call(
        functools.partial(last_kernel, dims),
        out_shape=[
            shape((tok, width), bf16),
            shape((1, width), f32),
            shape((1, 64), f32),
            shape((1, 64), f32),
            shape((1, width), f32),
            shape((r_qkv, columns), f32),
        ],
        in_specs=[vm] * 5 + [anyw] * 2,
        out_specs=[vm] * 6,
        scratch_shapes=[
            VMEM(t_attn.shape, bf16),
            VMEM(w_qkv.shape, bf16),
            VMEM((NZ, 2, 2, r_qkv, columns), bf16),
            VMEM((tok, width), f32),
            VMEM((8, width), f32),
            VMEM((3 + NZ, 8, width), f32),
            dma((8, NZ)),
            dma((8, NZ)),
            dma((3 + NZ,)),
            dma((3 + NZ,)),
            dma((2,)),
        ]
        + Scatter.scratch(r_qkv, columns),
        compiler_params=pltpu.CompilerParams(
            collective_id=2, has_side_effects=True, vmem_limit_bytes=60 << 20
        ),
        cost_estimate=pl.CostEstimate(flops=8 * tok * width * columns, bytes_accessed=20 << 20, transcendentals=0),
        name="last",
    )(x, g_attn, gqkv2, grad_res, gains, t_attn, w_qkv)
    dx, grad_attn, grad_q, grad_k, grad_ffn, own_qkv = last
    return dx, grad_attn[0], own_qkv, grad_q[0], grad_k[0], own_out, grad_ffn[0], own_gu, own_down


epsilon = 1e-06


def norm_rows(values, gain_vec):
    return (
        values * lax.rsqrt(jnp.mean(values * values, axis=-1, keepdims=True) + epsilon) * gain_vec
    )


def rotate(values, positions):
    half_dim = values.shape[-1] // 2
    frequency = jnp.exp(
        jnp.arange(half_dim).astype(jnp.float32) * (-2.0 * math.log(10000.0) / values.shape[-1])
    )
    angles = positions.astype(jnp.float32)[:, None] * frequency[None, :]
    cosine = jnp.cos(angles)[:, None, :]
    sine = jnp.sin(angles)[:, None, :]
    first = values[..., :half_dim]
    second = values[..., half_dim:]
    return jnp.concatenate(
        [first * cosine - second * sine, second * cosine + first * sine], axis=-1
    )


def project_heads(qkv_all, positions, q_gain, k_gain):
    tok_rows = qkv_all.shape[0]
    q_cols = HEADS * HEAD_DIM
    k_cols = GROUPS * HEAD_DIM
    queries = qkv_all[:, :q_cols].reshape(tok_rows, HEADS, HEAD_DIM)
    keys_raw = qkv_all[:, q_cols : q_cols + k_cols].reshape(tok_rows, GROUPS, HEAD_DIM)
    values = qkv_all[:, q_cols + k_cols :].reshape(tok_rows, GROUPS, HEAD_DIM)
    return (
        rotate(norm_rows(queries, q_gain), positions),
        rotate(norm_rows(keys_raw, k_gain), positions),
        values,
    )


def gated(gate_up):
    return jax.nn.silu(gate_up[:, :FF]) * gate_up[:, FF:]


def per_device_plain(
    inputs, places, cotangent, attn_gain, w_qkv, q_gain, k_gain, w_out, ffn_gain, w_gateup, w_down
):
    tok_rows = inputs.shape[1]
    repeat = HEADS // GROUPS
    score_scale = HEAD_DIM ** (-0.5)
    here_f = inputs[0].astype(jnp.float32)
    own_places = places[0]
    qkv_w, out_w = (
        lax.all_gather(w_qkv, ("dp", "ctx"), axis=0, tiled=True),
        lax.all_gather(w_out, ("dp", "ctx"), axis=0, tiled=True),
    )
    h_attn_f, pull_attn = jax.vjp(norm_rows, here_f, attn_gain)
    h_attn = h_attn_f.astype(jnp.bfloat16)
    qkv_all = jnp.dot(h_attn, qkv_w, preferred_element_type=jnp.float32)

    def heads_of(qkv_in, gain_q, gain_k):
        return project_heads(qkv_in, own_places, gain_q, gain_k)

    (queries, keys_f, values), pull_heads = jax.vjp(heads_of, qkv_all, q_gain, k_gain)
    query_b = queries.astype(jnp.bfloat16).reshape(tok_rows, GROUPS, repeat, HEAD_DIM)
    key_b = keys_f.astype(jnp.bfloat16)
    value_b = values.astype(jnp.bfloat16)
    all_keys, all_values = (
        lax.all_gather(key_b, "ctx", axis=0, tiled=True),
        lax.all_gather(value_b, "ctx", axis=0, tiled=True),
    )
    all_places = lax.all_gather(own_places, "ctx", axis=0, tiled=True)
    blocks = lax.axis_size("ctx")
    key_blocks = all_keys.reshape(blocks, tok_rows, GROUPS, HEAD_DIM)
    value_blocks = all_values.reshape(blocks, tok_rows, GROUPS, HEAD_DIM)
    place_blocks = all_places.reshape(blocks, tok_rows)

    def score_block(key_blk, place_blk):
        scores = (
            jnp.einsum("igrd,jgd->grij", query_b, key_blk, preferred_element_type=jnp.float32)
            * score_scale
        )
        allowed = place_blk[None, :] <= own_places[:, None]
        return (scores, allowed)

    def max_step(state_pair, entries):
        row_top, row_total = state_pair
        scores, allowed = score_block(entries[0], entries[1])
        scores = jnp.where(allowed, scores, -1e30)
        new_top = jnp.maximum(row_top, jnp.max(scores, axis=-1))
        row_total = row_total * jnp.exp(row_top - new_top) + jnp.sum(
            jnp.where(allowed, jnp.exp(scores - new_top[..., None]), 0.0), axis=-1
        )
        return ((new_top, row_total), None)

    start_pair = (
        jnp.full((GROUPS, repeat, tok_rows), -1e30, jnp.float32),
        jnp.zeros((GROUPS, repeat, tok_rows), jnp.float32),
    )
    (row_top, row_total), _ = lax.scan(max_step, start_pair, (key_blocks, place_blocks))
    log_total = row_top + jnp.log(row_total)

    def out_step(accum, entries):
        scores, allowed = score_block(entries[0], entries[1])
        weights_b = jnp.where(allowed, jnp.exp(scores - log_total[..., None]), 0.0).astype(
            jnp.bfloat16
        )
        return (
            accum
            + jnp.einsum(
                "grij,jgd->igrd", weights_b, entries[2], preferred_element_type=jnp.float32
            ),
            None,
        )

    mixed_f, _ = lax.scan(
        out_step,
        jnp.zeros((tok_rows, GROUPS, repeat, HEAD_DIM), jnp.float32),
        (key_blocks, place_blocks, value_blocks),
    )
    mixed_b = mixed_f.reshape(tok_rows, HEADS * HEAD_DIM).astype(jnp.bfloat16)
    attn_out = jnp.dot(mixed_b, out_w, preferred_element_type=jnp.float32)
    residual = here_f + attn_out
    gateup_w, down_w = (
        lax.all_gather(w_gateup, ("dp", "ctx"), axis=0, tiled=True),
        lax.all_gather(w_down, ("dp", "ctx"), axis=0, tiled=True),
    )
    h_ffn_f, pull_ffn = jax.vjp(norm_rows, residual, ffn_gain)
    h_ffn = h_ffn_f.astype(jnp.bfloat16)
    gate_up = jnp.dot(h_ffn, gateup_w, preferred_element_type=jnp.float32)
    act_f, pull_gate = jax.vjp(gated, gate_up)
    act_b = act_f.astype(jnp.bfloat16)
    result = residual + jnp.dot(act_b, down_w, preferred_element_type=jnp.float32)
    layer_output = result.astype(jnp.bfloat16)[None]
    gateup_w, down_w = (
        lax.all_gather(w_gateup, ("dp", "ctx"), axis=0, tiled=True),
        lax.all_gather(w_down, ("dp", "ctx"), axis=0, tiled=True),
    )
    grad_out = cotangent[0]
    grad_act = jnp.dot(grad_out, down_w.T, preferred_element_type=jnp.float32)
    grad_down = jnp.dot(act_b.T, grad_out, preferred_element_type=jnp.float32)
    grad_gu_b = pull_gate(grad_act)[0].astype(jnp.bfloat16)
    grad_gateup = jnp.dot(h_ffn.T, grad_gu_b, preferred_element_type=jnp.float32)
    grad_h_ffn = jnp.dot(grad_gu_b, gateup_w.T, preferred_element_type=jnp.float32)
    grad_resid_part, grad_ffn_gain = pull_ffn(grad_h_ffn)
    grad_residual = grad_out.astype(jnp.float32) + grad_resid_part
    grad_gateup_own, grad_down_own = (
        lax.psum_scatter(grad_gateup, ("dp", "ctx"), scatter_dimension=0, tiled=True),
        lax.psum_scatter(grad_down, ("dp", "ctx"), scatter_dimension=0, tiled=True),
    )
    qkv_w, out_w = (
        lax.all_gather(w_qkv, ("dp", "ctx"), axis=0, tiled=True),
        lax.all_gather(w_out, ("dp", "ctx"), axis=0, tiled=True),
    )
    grad_attn_b = grad_residual.astype(jnp.bfloat16)
    grad_out_w = jnp.dot(mixed_b.T, grad_attn_b, preferred_element_type=jnp.float32)
    grad_mixed_b = (
        jnp.dot(grad_attn_b, out_w.T, preferred_element_type=jnp.float32)
        .astype(jnp.bfloat16)
        .reshape(tok_rows, GROUPS, repeat, HEAD_DIM)
    )
    row_delta = jnp.transpose(
        jnp.sum(grad_mixed_b.astype(jnp.float32) * mixed_f, axis=-1), (1, 2, 0)
    )

    def back_step(grad_query, entries):
        key_blk, place_blk, value_blk = entries
        scores, allowed = score_block(key_blk, place_blk)
        weights_f = jnp.where(allowed, jnp.exp(scores - log_total[..., None]), 0.0)
        weights_b = weights_f.astype(jnp.bfloat16)
        grad_value = jnp.einsum(
            "grij,igrd->jgd", weights_b, grad_mixed_b, preferred_element_type=jnp.float32
        )
        grad_prob = jnp.einsum(
            "igrd,jgd->grij", grad_mixed_b, value_blk, preferred_element_type=jnp.float32
        )
        grad_score = (weights_f * (grad_prob - row_delta[..., None])).astype(jnp.bfloat16)
        grad_query = grad_query + jnp.einsum(
            "grij,jgd->igrd", grad_score, key_blk, preferred_element_type=jnp.float32
        )
        grad_key = (
            jnp.einsum("grij,igrd->jgd", grad_score, query_b, preferred_element_type=jnp.float32)
            * score_scale
        )
        return (
            grad_query,
            jnp.concatenate(
                [
                    grad_key.reshape(tok_rows, GROUPS * HEAD_DIM),
                    grad_value.reshape(tok_rows, GROUPS * HEAD_DIM),
                ],
                axis=1,
            ),
        )

    grad_query, kv_terms = lax.scan(
        back_step,
        jnp.zeros((tok_rows, GROUPS, repeat, HEAD_DIM), jnp.float32),
        (key_blocks, place_blocks, value_blocks),
    )
    grad_query = grad_query * score_scale
    kv_own = lax.psum_scatter(
        kv_terms.reshape(blocks * tok_rows, 2 * GROUPS * HEAD_DIM).astype(jnp.bfloat16),
        "ctx",
        scatter_dimension=0,
        tiled=True,
    ).astype(jnp.float32)
    grad_key_own = kv_own[:, : GROUPS * HEAD_DIM].reshape(tok_rows, GROUPS, HEAD_DIM)
    grad_value_own = kv_own[:, GROUPS * HEAD_DIM :].reshape(tok_rows, GROUPS, HEAD_DIM)
    grad_qkv_f, grad_q_gain, grad_k_gain = pull_heads(
        (grad_query.reshape(tok_rows, HEADS, HEAD_DIM), grad_key_own, grad_value_own)
    )
    grad_qkv_b = grad_qkv_f.astype(jnp.bfloat16)
    grad_qkv_w = jnp.dot(h_attn.T, grad_qkv_b, preferred_element_type=jnp.float32)
    grad_h_attn = jnp.dot(grad_qkv_b, qkv_w.T, preferred_element_type=jnp.float32)
    grad_here_part, grad_attn_gain = pull_attn(grad_h_attn)
    grad_inputs = (grad_residual + grad_here_part).astype(jnp.bfloat16)[None]
    grad_qkv_own, grad_out_own = (
        lax.psum_scatter(grad_qkv_w, ("dp", "ctx"), scatter_dimension=0, tiled=True),
        lax.psum_scatter(grad_out_w, ("dp", "ctx"), scatter_dimension=0, tiled=True),
    )
    gain_attn, gain_query, gain_key, gain_ffn = lax.psum(
        (grad_attn_gain, grad_q_gain, grad_k_gain, grad_ffn_gain), ("dp", "ctx")
    )
    return (
        layer_output,
        grad_inputs,
        gain_attn,
        grad_qkv_own,
        gain_query,
        gain_key,
        grad_out_own,
        gain_ffn,
        grad_gateup_own,
        grad_down_own,
    )


def per_device_fast(
    inputs, places, cotangent, attn_gain, w_qkv, q_gain, k_gain, w_out, ffn_gain, w_gateup, w_down
):
    n_dev = lax.axis_size("ctx")
    own_places = places[0]
    half = HEAD_DIM // 2
    spot = jnp.arange(128)
    frequency = jnp.exp((spot % half).astype(f32) * (-2.0 * math.log(10000.0) / HEAD_DIM))
    angles = own_places.astype(f32)[:, None] * frequency[None, :]
    cosine = jnp.cos(angles)
    sine = jnp.where(spot % HEAD_DIM < half, -1.0, 1.0) * jnp.sin(angles)
    block_row = (own_places // 128)[None, :]
    gain_q, gain_k = jnp.tile(q_gain, 2)[None], jnp.tile(k_gain, 2)[None]
    layer_output, *kept = forward(
        inputs[0], cotangent[0], block_row, cosine, sine, attn_gain[None], gain_q, gain_k,
        ffn_gain[None], w_qkv, w_out, w_down, w_gateup, n_dev,
    )
    rows = [w.shape[0] for w in (w_qkv, w_out, w_gateup, w_down)]
    grad_inputs, *grads = backward(
        inputs[0], cosine, sine, attn_gain[None], gain_q, gain_k, ffn_gain[None], kept, rows, n_dev
    )
    return (layer_output[None], grad_inputs[None], *grads)


def solution(mesh):
    in_specs = (
        P("dp", "ctx", None),
        P("dp", "ctx"),
        P("dp", "ctx", None),
        P(),
        P(("dp", "ctx"), None),
        P(),
        P(),
        P(("dp", "ctx"), None),
        P(),
        P(("dp", "ctx"), None),
        P(("dp", "ctx"), None),
    )
    out_specs = (
        P("dp", "ctx", None),
        P("dp", "ctx", None),
        P(),
        P(("dp", "ctx"), None),
        P(),
        P(),
        P(("dp", "ctx"), None),
        P(),
        P(("dp", "ctx"), None),
        P(("dp", "ctx"), None),
    )
    fast = dict(mesh.shape) == {"dp": 4, "ctx": 8}
    per_device = per_device_fast if fast else per_device_plain
    return jax.shard_map(
        per_device, mesh=mesh, in_specs=in_specs, out_specs=out_specs, check_vma=False
    )
```

```python
import functools
import math

import jax
import jax.numpy as jnp
from jax import lax
from jax.experimental import pallas as pl
from jax.experimental.pallas import tpu as pltpu
from jax.sharding import PartitionSpec as P

HEADS = 16
GROUPS = 4
HEAD_DIM = 64
FF = 1024


FORWARD_ORDER = [
    "qp0", "qZ", "norm", "dp0", "qz1", "qe0", "qp1", "qz2", "gZ", "qp2", "qc0", "qe1", "oP",
    "qz3", "qp3", "qe2", "gz1", "qs0", "gz2", "oZ", "qe3", "oe", "dZ", "qc1", "qc2", "gp2", "qc3",
    "qs1", "qs2", "oD", "qs3", "oz12", "keys", "de0", "turn", "oz22", "kve", "gp1", "gz3", "gp0",
    "dz1", "query", "kvc", "dp1", "oz32", "ge2", "unpack", "gp3", "oz10", "dz2", *["A"] * 3,
    "oz20", *["A"] * 4, "oz30", *["A"] * 5, "dp2", "oz11", "ge0", "dz3", *["A"] * 3, "dc0",
    "oz13", "ge1", "oz23", *["A"] * 5, "oz21", "de1", "A", "oc1", "gc2", *["A"] * 4, "oc2", "A",
    "dp3", "oz31", *["A"] * 3, "oz33", "oc3", *["A"] * 2, "gc0", "A", "mix", "de2", "dc1", "ds0",
    "res", "ge3", "de3", "gc1", "norm2", "dc2", "gc3", "gs0", "gs1", "dc3", "ds1", "ds2", "gs2",
    "turn2", "gs3", "ds3", "gate", "act", "y",
]

BACKWARD_ORDER = [
    "dw0", "dw1", "gw0", "dw2", "ga0", "gb0", "da0", "gw1", "gw2", "h", *["H"] * 5, "ga1",
    *["H"] * 3, "nb", "gw3", "dw3", "m", "lm", "att", *["B"] * 4, "gd0", "ga3", "ow0", "ow1",
    "oa0", "B", "dd0", *["B"] * 4, "da2", "db0", "da3", *["B"] * 2, "oa1", "B", "ow2", "B", "ow3",
    "B", "gx0", "ga2", "da1", "oz00", "B", "oz02", "ll", "gd3", "B", "db2", "oa2", "B", "oz10",
    "dx0", "B", "gb1", "B", "gb3", *["B"] * 2, "oz03", *["B"] * 3, "gd2", "B", "oz12", "B",
    "oz01", "gd1", *["B"] * 3, "oz13", "B", "oz23", "oz11", "db1", "dd3", *["B"] * 2, "kvs",
    "dd1", "Q", "dd2", "Q", "dz0", "dx1", "Q", "kvc", "dz1", *["Q"] * 2, "oz20", *["Q"] * 3,
    "dx2", "gx1", "kve", "gb2", "gz0", "kvf", "dz2", "db3", "oo0", "qe", "qw0", "qb0", "qa0",
    "oa3", "qw1", "qa1", "g", "G", "qw2", "gx2", "oz21", "oz22", "qb1", "gz1", "qw3", "qa3",
    *["G"] * 2, "qd0", "oo3", *["G"] * 2, "qa2", "oo1", "qd1", "qb2", "gz2", *["G"] * 3, "nb2",
    "hs0", "qx0", "qz0", "oo2", "he0", "hs1", "qd2", "qx1", "qd3", "qz1", "he1", "hs2", "qb3",
    "qx2", "qz2", "oS", "he2", "rs", "oe", "gf", "qf", "re", "of", "df",
]

f32 = jnp.float32
bf16 = jnp.bfloat16
MESH = pl.DeviceIdType.MESH
NZ = 4
EPS = 1e-06


class Place:
    def __init__(self):
        self.z = lax.axis_index("dp")
        spot = lax.axis_index("ctx")
        self.core = spot % 2
        self.x = (spot // 2) % 2
        self.y = spot // 4

    def at(self, z=None, y=None, x=None, core=None):
        z = self.z if z is None else z
        y = self.y if y is None else y
        x = self.x if x is None else x
        core = self.core if core is None else core
        return (z, y * 4 + x * 2 + core)

    def xn(self):
        return self.at(x=1 - self.x)

    def yn(self):
        return self.at(y=1 - self.y)

    def sn(self):
        return self.at(core=1 - self.core)

    def up(self):
        return self.at(z=self.z + 1)

    def down(self):
        return self.at(z=self.z - 1)


def barrier(pc):
    bar = pltpu.get_barrier_semaphore()

    def greet(device):
        pl.semaphore_signal(bar, inc=1, device_id=device, device_id_type=MESH)

    for device in (pc.xn(), pc.yn(), pc.sn()):
        greet(device)

    @pl.when(pc.z < NZ - 1)
    def _():
        greet(pc.up())

    @pl.when(pc.z > 0)
    def _():
        greet(pc.down())

    pl.semaphore_wait(bar, 3 + (1 - pc.z // (NZ - 1)) + (pc.z + NZ - 1) // NZ)


def far(z, i):
    m = z // 2
    zz = z + m * (3 - 2 * z)
    lo = 3 - i if i < 2 else (1 - zz if i == 2 else zz)
    return lo + m * (3 - 2 * lo)


def near(z, i):
    return far(z, NZ - 1 - i)


def remote(src, dst, dev, send, recv):
    return pltpu.make_async_remote_copy(
        src_ref=src, dst_ref=dst, send_sem=send, recv_sem=recv, device_id=dev, device_id_type=MESH
    )


def halves(rows):
    return pl.ds(0, rows // 2), pl.ds(rows // 2, rows // 2)


KZ, KX, KY, KD0, KD1, KS, KU = range(7)


class Gather:
    def __init__(self, pc, buf, send, recv):
        self.pc, self.buf, self.send, self.recv = pc, buf, send, recv
        self.h = halves(buf.shape[-2])

    def cp(self, idx, dev, ks, kr, slot):
        ref = self.buf.at[idx]
        return remote(ref, ref, dev, self.send.at[ks, slot], self.recv.at[kr, slot])

    def c_up(self, z0):
        p = self.pc
        return self.cp((z0, p.y, p.x, p.core), p.up(), KU, KZ, z0)

    def c_down(self, z0):
        p = self.pc
        return self.cp((z0, p.y, p.x, p.core), p.down(), KZ, KZ, z0)

    def c_x(self, z0):
        p = self.pc
        return self.cp((z0, p.y, p.x, p.core), p.xn(), KX, KX, z0)

    def c_y(self, z0):
        p = self.pc
        return self.cp((z0, p.y, p.x, p.core), p.yn(), KY, KY, z0)

    def c_d0(self, z0):
        p = self.pc
        return self.cp((z0, p.y, 1 - p.x, p.core, self.h[0]), p.yn(), KD0, KD0, z0)

    def c_d1(self, z0):
        p = self.pc
        return self.cp((z0, 1 - p.y, p.x, p.core, self.h[1]), p.xn(), KD1, KD1, z0)

    def c_s(self, z0):
        p = self.pc
        return self.cp((z0, slice(None), slice(None), p.core), p.sn(), KS, KS, z0)

    def plane_send(self, i):
        z0 = near(self.pc.z, i)
        self.c_x(z0).start()
        self.c_y(z0).start()

    def own_z(self):
        z = self.pc.z

        @pl.when(z < NZ - 1)
        def _():
            self.c_up(z).start()

        @pl.when(z > 0)
        def _():
            self.c_down(z).start()

    def z_event(self, i, plane=True):
        z = self.pc.z
        z0 = near(z, i)

        @pl.when(z0 < z)
        def _():
            self.c_up(z0).wait_recv()

            @pl.when(z < NZ - 1)
            def _():
                self.c_up(z0).start()

        @pl.when(z0 > z)
        def _():
            self.c_down(z0).wait_recv()

            @pl.when(z > 0)
            def _():
                self.c_down(z0).start()

        if plane:
            self.plane_send(i)

    def plane_event(self, i):
        z0 = near(self.pc.z, i)
        self.c_x(z0).wait_recv()
        self.c_d0(z0).start()
        self.c_y(z0).wait_recv()
        self.c_d1(z0).start()

    def core_event(self, i):
        z0 = near(self.pc.z, i)
        self.c_d0(z0).wait_recv()
        self.c_d1(z0).wait_recv()
        self.c_s(z0).start()

    def done_event(self, i):
        self.c_s(near(self.pc.z, i)).wait_recv()

    def finish(self):
        z = self.pc.z
        for z0 in range(NZ):
            for c in (self.c_x, self.c_y, self.c_d0, self.c_d1, self.c_s):
                c(z0).wait_send()

            @pl.when((z < NZ - 1) & (z0 <= z))
            def _():
                self.c_up(z0).wait_send()

            @pl.when((z > 0) & (z0 >= z))
            def _():
                self.c_down(z0).wait_send()


class GatherPlane:
    def __init__(self, pc, buf, send, recv):
        self.pc, self.buf, self.send, self.recv = pc, buf, send, recv
        self.h = halves(buf.shape[-2])

    def cp(self, idx, dev, s, r):
        ref = self.buf.at[idx]
        return remote(ref, ref, dev, self.send.at[s], self.recv.at[r])

    def yx(self, k):
        p = self.pc
        return (p.y if k < 2 else 1 - p.y), (p.x if k % 2 == 0 else 1 - p.x)

    def c_x(self):
        p = self.pc
        return self.cp((p.z, p.y, p.x, p.core), p.xn(), (KX, 0), (KX, 0))

    def c_y(self):
        p = self.pc
        return self.cp((p.z, p.y, p.x, p.core), p.yn(), (KY, 0), (KY, 0))

    def c_d0(self):
        p = self.pc
        return self.cp((p.z, p.y, 1 - p.x, p.core, self.h[0]), p.yn(), (KD0, 0), (KD0, 0))

    def c_d1(self):
        p = self.pc
        return self.cp((p.z, 1 - p.y, p.x, p.core, self.h[1]), p.xn(), (KD1, 0), (KD1, 0))

    def c_up(self, z0, k):
        p = self.pc
        y, x = self.yx(k)
        return self.cp((z0, y, x, p.core), p.up(), (10 + z0, k), (10 + z0, k))

    def c_down(self, z0, k):
        p = self.pc
        y, x = self.yx(k)
        return self.cp((z0, y, x, p.core), p.down(), (14 + z0, k), (10 + z0, k))

    def c_s(self, z0):
        p = self.pc
        return self.cp((z0, slice(None), slice(None), p.core), p.sn(), (KS, z0), (KS, z0))

    def z_send(self, k):
        z = self.pc.z

        @pl.when(z < NZ - 1)
        def _():
            self.c_up(z, k).start()

        @pl.when(z > 0)
        def _():
            self.c_down(z, k).start()

    def own_plane(self):
        self.c_x().start()
        self.c_y().start()

    def own_z(self):
        self.z_send(0)

    def plane_event(self):
        self.c_x().wait_recv()
        self.c_d0().start()
        self.z_send(1)
        self.c_y().wait_recv()
        self.c_d1().start()
        self.z_send(2)

    def diag_event(self):
        self.c_d0().wait_recv()
        self.c_d1().wait_recv()
        self.z_send(3)
        self.c_s(self.pc.z).start()

    def z_event(self, i, k):
        z = self.pc.z
        z0 = near(z, i)

        @pl.when(z0 < z)
        def _():
            self.c_up(z0, k).wait_recv()

            @pl.when(z < NZ - 1)
            def _():
                self.c_up(z0, k).start()

        @pl.when(z0 > z)
        def _():
            self.c_down(z0, k).wait_recv()

            @pl.when(z > 0)
            def _():
                self.c_down(z0, k).start()

    def core_event(self, i):
        self.c_s(near(self.pc.z, i)).start()

    def done_event(self, i):
        self.c_s(near(self.pc.z, i)).wait_recv()

    def finish(self):
        z = self.pc.z
        for c in (self.c_x, self.c_y, self.c_d0, self.c_d1):
            c().wait_send()
        for z0 in range(NZ):
            self.c_s(z0).wait_send()
            for k in range(4):

                @pl.when((z < NZ - 1) & (z0 <= z))
                def _():
                    self.c_up(z0, k).wait_send()

                @pl.when((z > 0) & (z0 >= z))
                def _():
                    self.c_down(z0, k).wait_send()


class GatherSequence:
    def __init__(self, pc, buf, send, recv):
        self.pc, self.buf, self.send, self.recv = pc, buf, send, recv
        rows = buf.shape[-2]
        self.h = (pl.ds(0, 128), pl.ds(128, rows - 128))

    def cp(self, idx, dev, k):
        ref = self.buf.at[idx]
        return remote(ref, ref, dev, self.send.at[k], self.recv.at[k])

    def c_x(self):
        p = self.pc
        return self.cp((p.y, p.x, p.core), p.xn(), 0)

    def c_y(self):
        p = self.pc
        return self.cp((p.y, p.x, p.core), p.yn(), 1)

    def c_d0(self):
        p = self.pc
        return self.cp((p.y, 1 - p.x, p.core, self.h[0]), p.yn(), 2)

    def c_d1(self):
        p = self.pc
        return self.cp((1 - p.y, p.x, p.core, self.h[1]), p.xn(), 3)

    def c_s(self, k):
        p = self.pc
        y, x = (p.y if k < 2 else 1 - p.y), (p.x if k % 2 == 0 else 1 - p.x)
        return self.cp((y, x, p.core), p.sn(), 4 + k)

    def own(self):
        for c in (self.c_x(), self.c_y(), self.c_s(0)):
            c.start()

    def plane_event(self):
        self.c_x().wait_recv()
        self.c_d0().start()
        self.c_s(1).start()
        self.c_y().wait_recv()
        self.c_d1().start()
        self.c_s(2).start()

    def core_event(self):
        self.c_d0().wait_recv()
        self.c_d1().wait_recv()
        self.c_s(3).start()

    def done_event(self):
        for k in range(4):
            self.c_s(k).wait_recv()

    def finish(self):
        for c in (self.c_x(), self.c_y(), self.c_d0(), self.c_d1()):
            c.wait_send()
        for k in range(4):
            self.c_s(k).wait_send()


LOG2E = math.log2(math.e)
VMEM = pltpu.VMEM


def dot(a, b):
    return jnp.dot(a, b, preferred_element_type=f32)


def dot_t(a, b):
    return lax.dot_general(a, b, (((1,), (1,)), ((), ())), preferred_element_type=f32)


def lanes(shape):
    return lax.broadcasted_iota(jnp.int32, shape, 1)


def roll_half(v):
    return pltpu.roll(v, 64, 1)


def swap_rot(v):
    first = lanes(v.shape) % 64 < 32
    return jnp.where(first, pltpu.roll(v, 96, 1), pltpu.roll(v, 32, 1))


def head_sums(v):
    row = lax.broadcasted_iota(jnp.int32, (128, 128), 0) // 64
    col = lax.broadcasted_iota(jnp.int32, (128, 128), 1) // 64
    ones = jnp.where(row == col, 1.0, 0.0).astype(bf16)
    high = v.astype(bf16)
    low = (v - high.astype(f32)).astype(bf16)
    return dot(high, ones) + dot(low, ones)


def cols(i, width):
    return pl.ds(pl.multiple_of(i * width, width), width)


def norm_into(src, gain, dst):
    def body(i, _):
        rows = pl.ds(pl.multiple_of(i * 32, 32), 32)
        v = src[rows, :].astype(f32)
        scale = lax.rsqrt(jnp.mean(v * v, axis=-1, keepdims=True) + EPS)
        dst[rows, :] = (v * scale * gain[...]).astype(dst.dtype)
        return 0

    lax.fori_loop(0, src.shape[0] // 32, body, 0)


def run_steps(order, steps, loops):
    order = list(order)
    while order:
        name = order.pop(0)
        if name not in loops:
            steps[name]()
            continue
        count, body = loops[name]
        ticks, seen = {}, 1
        while seen < count:
            inner = order.pop(0)
            if inner == name:
                seen += 1
            else:
                ticks.setdefault(seen - 1, []).append(inner)

        def tick(i, _, body=body, ticks=ticks):
            body(i)
            for k, inner in ticks.items():

                @pl.when(i == k)
                def _(inner=inner):
                    for step in inner:
                        steps[step]()

            return 0

        lax.fori_loop(0, count, tick, 0)


def line_steps(letter, g):
    part = functools.partial
    steps = {letter + "Z": g.own_z}
    for i in range(NZ):
        steps[f"{letter}p{i}"] = part(g.plane_send, i)
        steps[f"{letter}e{i}"] = part(g.plane_event, i)
        steps[f"{letter}c{i}"] = part(g.core_event, i)
        if i:
            steps[f"{letter}z{i}"] = part(g.z_event, i, False)
    return steps


def turn(src, rows, core, mine, theirs):
    def body(t, _):
        v = jnp.transpose(src[:, cols(t, 128)])
        for k in range(64 // rows):
            a, b = v[2 * k * rows : (2 * k + 1) * rows], v[(2 * k + 1) * rows : (2 * k + 2) * rows]
            own, other = jnp.where(core == 0, a, b), jnp.where(core == 0, b, a)
            spot = t * (64 // rows) + k
            mine[spot, :, pl.ds(0, v.shape[1])] = own
            theirs[spot, pl.ds(0, rows), :] = other
        return 0

    lax.fori_loop(0, src.shape[1] // 128, body, 0)


def forward_kernel(dims, *refs):
    (tok, width, n_dev, heads_w, kv_w, ff) = dims
    (
        x_ref, cot_ref, hi_ref, cos_ref, sin_ref, g_attn, g_q, g_k, g_ffn,
        s_qkv, s_out, s_down, s_gu,
        o_y, o_tattn, o_tmix, o_tffn, o_tact, o_cot, o_ggu, o_kv, o_q2, o_linv, o_mixf, o_res,
        o_kk, o_va, o_mask, o_wqkv, o_wout, o_wgu,
        w_qkv, w_out, w_down, w_gu, kk, va, mask, mask_t, o2, gu, gact,
        y_ref, hattn_ref, qkv_ref, q2_ref, kvb, linv_ref, mixf_ref, mixb_ref, res_ref, hffn_ref,
        act_ref, cot2, ggu2, t_attn, t_mix, t_ffn, t_act, turn_a, turn_b,
        send, recv, kv_send, kv_recv, lsem, osem, ex_send, ex_recv,
    ) = refs
    pc = Place()
    shards = (s_qkv, s_out, s_down, s_gu)
    bufs = (w_qkv, w_out, w_down, w_gu)
    local = [
        pltpu.make_async_copy(s, b.at[pc.z, pc.y, pc.x, pc.core], lsem.at[k])
        for k, (s, b) in enumerate(zip(shards, bufs))
    ]
    for c in local:
        c.start()
    barrier(pc)
    for c in local:
        c.wait()
    qkv = Gather(pc, w_qkv, send.at[0], recv.at[0])
    out = GatherPlane(pc, w_out, send.at[1], recv.at[1])
    down = Gather(pc, w_down, send.at[2], recv.at[2])
    gateup = Gather(pc, w_gu, send.at[3], recv.at[3])
    seq = GatherSequence(pc, kvb, kv_send, kv_recv)
    part = functools.partial
    z = pc.z
    emitted = []

    def emit(src, dst):
        c = pltpu.make_async_copy(src, dst, osem.at[len(emitted)])
        emitted.append(c)
        c.start()

    def exchange(k, src, dst):
        return remote(src, dst, pc.sn(), ex_send.at[k], ex_recv.at[k])

    back = pl.ds(tok, tok)
    sent_cot = exchange(0, cot_ref, cot2.at[back, :])
    sent_attn = exchange(1, turn_a, t_attn.at[:, :, back])
    sent_mix = exchange(2, turn_b.at[:, pl.ds(0, s_out.shape[0]), :], t_mix.at[:, :, back])
    sent_ffn = exchange(3, turn_a, t_ffn.at[:, :, back])
    sent_act = exchange(4, turn_b.at[:, pl.ds(0, s_down.shape[0]), :], t_act.at[:, :, back])
    sent_ggu = exchange(5, ggu2.at[pl.ds(0, tok), :], ggu2.at[back, :])

    def first_norm():
        norm_into(x_ref, g_attn, hattn_ref)

    def first_turn():
        sent_cot.start()
        cot2[pl.ds(0, tok), :] = cot_ref[...]
        turn(hattn_ref, s_qkv.shape[0], pc.core, t_attn, turn_a)
        sent_attn.start()

    def columns_step(g, i, left, right, total, depth):
        g.done_event(i)
        z0 = near(z, i)

        def body(n, _):
            c = cols(n, 256)
            w = right[z0, :, :, :, :, c].reshape(depth, 256)
            prod = dot(left[:, cols(z0, depth)], w)
            if i == 0:
                total[:, c] = prod
            else:
                total[:, c] += prod
            return 0

        lax.fori_loop(0, total.shape[1] // 256, body, 0)

    def grad_act_step(i):
        down.done_event(i)
        z0 = near(z, i)
        depth = ff // NZ
        gact[:, cols(z0, depth)] = dot_t(cot_ref[...], w_down[z0].reshape(depth, width))

    low = lanes((tok, 128)) < 64

    def head_tile(t, gain):
        u = qkv_ref[:, cols(t, 128)]
        n = u * lax.rsqrt(head_sums(u * u) * (1.0 / 64) + EPS) * gain[...]
        return n * cos_ref[...] + swap_rot(n) * sin_ref[...]

    def keys_out():
        for t in range(kv_w // 128):
            kvb[pc.y, pc.x, pc.core, pl.ds(0, tok), pl.ds(t * 128, 128)] = head_tile(
                heads_w // 128 + t, g_k
            ).astype(bf16)
        kvb[pc.y, pc.x, pc.core, pl.ds(0, tok), pl.ds(kv_w, kv_w)] = qkv_ref[
            :, pl.ds(heads_w + kv_w, kv_w)
        ].astype(bf16)
        blocks_row = jnp.broadcast_to(hi_ref[...], (16, tok)).astype(bf16)
        kvb[pc.y, pc.x, pc.core, pl.ds(tok, 16), pl.ds(0, tok)] = blocks_row
        kvb[pc.y, pc.x, pc.core, pl.ds(tok, 16), pl.ds(tok, tok)] = blocks_row
        seq.own()

    def query_tile(t, _):
        q = (head_tile(t, g_q) * 0.125).astype(bf16)
        zero = jnp.zeros_like(q)
        q2_ref[t, pl.ds(0, tok), :] = jnp.where(low, q, zero)
        q2_ref[t, pl.ds(tok, tok), :] = jnp.where(low, zero, q)
        return 0

    def queries():
        lax.fori_loop(0, heads_w // 128, query_tile, 0)
        emit(qkv_ref, o_kv)
        emit(q2_ref, o_q2)
        emit(w_qkv, o_wqkv)
        sent_cot.wait_recv()
        emit(cot2, o_cot)
        sent_attn.wait_recv()
        emit(t_attn, o_tattn)

    def unpack(b, _):
        y, x, c = b // 4, (b // 2) % 2, b % 2
        rows = pl.ds(pl.multiple_of(b * tok, tok), tok)
        for t in range(kv_w // 128):
            k = kvb[y, x, c, pl.ds(0, tok), pl.ds(t * 128, 128)].astype(f32)
            v = kvb[y, x, c, pl.ds(0, tok), pl.ds(kv_w + t * 128, 128)].astype(f32)
            k_r, v_r = roll_half(k), roll_half(v)
            kk[2 * t, rows, :] = jnp.where(low, k, k_r).astype(bf16)
            kk[2 * t + 1, rows, :] = jnp.where(low, k_r, k).astype(bf16)
            va[2 * t, rows, :] = jnp.where(low, v, 1.0).astype(bf16)
            va[2 * t + 1, rows, :] = jnp.where(low, v_r, 1.0).astype(bf16)
        step = tok // 2
        key_hi = kvb[y, x, c, pl.ds(tok, 16), pl.ds(0, tok)].astype(f32)[:1, :]
        for a in range(2):
            own = hi_ref[:, a * step : (a + 1) * step].astype(f32)
            row = lax.broadcasted_iota(jnp.int32, (step, step), 0).astype(f32)
            col = lanes((step, step)).astype(f32)
            for d in range(2):
                theirs = key_hi[:, d * step : (d + 1) * step]
                gap = (own - theirs) * float(step) + row - col
                place = pl.ds(pl.multiple_of(b * tok + d * step, step), step)
                mask[pl.ds(a * step, step), place] = jnp.where(gap >= 0, 1.0, 0.0).astype(bf16)
                gap = (own - theirs) * float(step) + col - row
                mask_t[place, pl.ds(a * step, step)] = jnp.where(gap >= 0, 1.0, 0.0).astype(bf16)
        return 0

    def unpack_all():
        seq.done_event()
        lax.fori_loop(0, n_dev, unpack, 0)
        emit(kk, o_kk)
        emit(va, o_va)
        emit(mask_t, o_mask)

    chunk = 512
    n_chunk = n_dev * tok // chunk

    def attend(tick):
        t, kc = tick // n_chunk, tick % n_chunk
        g = t // 2
        rows = pl.ds(pl.multiple_of(kc * chunk, chunk), chunk)
        s = dot_t(q2_ref[t], kk[g, rows, :])
        e = jnp.exp2(s * LOG2E).astype(bf16).reshape(2, tok, chunk) * mask[:, rows][None]
        o = dot(e.reshape(2 * tok, chunk), va[g, rows, :])

        @pl.when(kc == 0)
        def _():
            o2[...] = o

        @pl.when(kc > 0)
        def _():
            o2[...] += o

        @pl.when(kc == n_chunk - 1)
        def _():
            even, odd = o2[pl.ds(0, tok), :], o2[pl.ds(tok, tok), :]
            total = jnp.where(low, roll_half(even), odd)
            inv = 1.0 / total
            mixed = jnp.where(low, even, roll_half(odd)) * inv
            linv_ref[:, cols(t, 128)] = inv
            mixf_ref[:, cols(t, 128)] = mixed
            mixb_ref[:, cols(t, 128)] = mixed.astype(bf16)

    def mix_out():
        emit(linv_ref, o_linv)
        emit(mixf_ref, o_mixf)
        turn(mixb_ref, s_out.shape[0], pc.core, t_mix, turn_b)
        sent_mix.start()

    def residual_step(n, _):
        c = cols(n, 256)
        w = w_out[:, :, :, :, :, c].reshape(heads_w, 256)
        res_ref[:, c] = x_ref[:, c].astype(f32) + dot(mixb_ref[...], w)
        return 0

    def residual():
        for i in range(NZ):
            out.done_event(i)
        emit(w_out, o_wout)
        lax.fori_loop(0, width // 256, residual_step, 0)

    def second_norm():
        norm_into(res_ref, g_ffn, hffn_ref)

    def second_turn():
        emit(res_ref, o_res)
        sent_mix.wait_recv()
        emit(t_mix, o_tmix)
        sent_attn.wait_send()
        turn(hffn_ref, s_gu.shape[0], pc.core, t_ffn, turn_a)
        sent_ffn.start()

    def gate_step(n, _):
        c = cols(n, 256)
        c2 = cols(n + ff // 256, 256)
        gate, up, grad = gu[:, c], gu[:, c2], gact[:, c]
        sig = 1.0 / (1.0 + jnp.exp(-gate))
        silu = gate * sig
        act_ref[:, c] = (silu * up).astype(bf16)
        ggu2[pl.ds(0, tok), c] = (grad * up * (sig * (1.0 + gate * (1.0 - sig)))).astype(bf16)
        ggu2[pl.ds(0, tok), c2] = (grad * silu).astype(bf16)
        return 0

    def gates():
        lax.fori_loop(0, ff // 256, gate_step, 0)
        sent_ggu.start()
        emit(w_gu, o_wgu)

    def act_out():
        sent_mix.wait_send()
        turn(act_ref, s_down.shape[0], pc.core, t_act, turn_b)
        sent_act.start()
        sent_ffn.wait_recv()
        emit(t_ffn, o_tffn)

    def output_step(n, _):
        c = cols(n, 256)
        w = w_down[:, :, :, :, :, c].reshape(ff, 256)
        y_ref[:, c] = (res_ref[:, c] + dot(act_ref[...], w)).astype(bf16)
        return 0

    def outputs():
        lax.fori_loop(0, width // 256, output_step, 0)
        emit(y_ref, o_y)
        sent_ggu.wait_recv()
        emit(ggu2, o_ggu)
        sent_act.wait_recv()
        emit(t_act, o_tact)

    steps = {
        "norm": first_norm, "turn": first_turn, "keys": keys_out, "query": queries,
        "kve": seq.plane_event, "kvc": seq.core_event, "unpack": unpack_all, "mix": mix_out,
        "res": residual, "norm2": second_norm, "turn2": second_turn, "gate": gates,
        "act": act_out, "y": outputs, "oP": out.own_plane, "oZ": out.own_z, "oe": out.plane_event,
        "oD": out.diag_event,
    }
    for letter, g in (("q", qkv), ("d", down), ("g", gateup)):
        steps.update(line_steps(letter, g))
    for i in range(NZ):
        steps[f"qs{i}"] = part(columns_step, qkv, i, hattn_ref, w_qkv, qkv_ref, width // NZ)
        steps[f"gs{i}"] = part(columns_step, gateup, i, hffn_ref, w_gu, gu, width // NZ)
        steps[f"ds{i}"] = part(grad_act_step, i)
        if i:
            steps[f"oc{i}"] = part(out.core_event, i)
            for k in range(4):
                steps[f"oz{i}{k}"] = part(out.z_event, i, k)
    run_steps(FORWARD_ORDER, steps, {"A": (heads_w // 128 * n_chunk, attend)})
    for g in (qkv, out, down, gateup, seq):
        g.finish()
    for c in (sent_cot, sent_ffn, sent_act, sent_ggu):
        c.wait_send()
    for c in emitted:
        c.wait()


def forward(x, cot, blocks, cosine, sine, g_attn, g_q, g_k, g_ffn, s_qkv, s_out, s_down, s_gu, n_dev):
    tok, width = x.shape
    heads_w, kv_w = HEADS * HEAD_DIM, GROUPS * HEAD_DIM
    ff = s_down.shape[0] * n_dev * NZ
    length = n_dev * tok
    tiles = heads_w // 128
    shape = jax.ShapeDtypeStruct
    seven = [(NZ, 2, 2, 2) + s.shape for s in (s_qkv, s_out, s_down, s_gu)]
    qkv_rows, out_rows, down_rows, gu_rows = [s.shape[0] for s in (s_qkv, s_out, s_down, s_gu)]
    spots = n_dev * NZ // 2
    kv_buf = ((2, 2, 2, tok + 16, 2 * kv_w), bf16)
    turned = [((spots, r, 2 * tok), bf16) for r in (qkv_rows, out_rows, gu_rows, down_rows)]
    keep = [
        ((tok, width), bf16),
        *turned,
        ((2 * tok, width), bf16),
        ((2 * tok, 2 * ff), bf16),
        ((tok, s_qkv.shape[1]), f32),
        ((tiles, 2 * tok, 128), bf16),
        ((tok, heads_w), f32),
        ((tok, heads_w), f32),
        ((tok, width), f32),
        ((GROUPS, length, 128), bf16),
        ((GROUPS, length, 128), bf16),
        ((length, tok), bf16),
        (seven[0], bf16),
        (seven[1], bf16),
        (seven[3], bf16),
    ]
    outs = [shape(*k) for k in keep]
    vm = pl.BlockSpec(memory_space=VMEM)
    anyw = pl.BlockSpec(memory_space=pl.ANY)
    dma = pltpu.SemaphoreType.DMA
    flops = 2 * tok * (width * (s_qkv.shape[1] + heads_w + 2 * ff + 2 * ff) + 2 * heads_w * length)
    return pl.pallas_call(
        functools.partial(forward_kernel, (tok, width, n_dev, heads_w, kv_w, ff)),
        out_shape=outs,
        in_specs=[vm] * 9 + [anyw] * 4,
        out_specs=[anyw] * len(outs),
        scratch_shapes=[VMEM(s, bf16) for s in seven]
        + [
            VMEM((GROUPS, length, 128), bf16),
            VMEM((GROUPS, length, 128), bf16),
            VMEM((tok, length), bf16),
            VMEM((length, tok), bf16),
            VMEM((2 * tok, 128), f32),
            VMEM((tok, 2 * ff), f32),
            VMEM((tok, ff), f32),
            VMEM((tok, width), bf16),
            VMEM((tok, width), bf16),
            VMEM((tok, s_qkv.shape[1]), f32),
            VMEM((tiles, 2 * tok, 128), bf16),
            VMEM(*kv_buf),
            VMEM((tok, heads_w), f32),
            VMEM((tok, heads_w), f32),
            VMEM((tok, heads_w), bf16),
            VMEM((tok, width), f32),
            VMEM((tok, width), bf16),
            VMEM((tok, ff), bf16),
            VMEM((2 * tok, width), bf16),
            VMEM((2 * tok, 2 * ff), bf16),
            *[VMEM(*t) for t in turned],
            VMEM((spots, qkv_rows, tok), bf16),
            VMEM((spots, out_rows, tok), bf16),
            dma((4, 18, NZ)),
            dma((4, 14, NZ)),
            dma((8,)),
            dma((8,)),
            dma((4,)),
            dma((len(outs),)),
            dma((6,)),
            dma((6,)),
        ],
        compiler_params=pltpu.CompilerParams(
            collective_id=0, has_side_effects=True, vmem_limit_bytes=60 << 20
        ),
        cost_estimate=pl.CostEstimate(flops=flops, bytes_accessed=50 << 20, transcendentals=0),
        name="forward",
    )(x, cot, blocks, cosine, sine, g_attn, g_q, g_k, g_ffn, s_qkv, s_out, s_down, s_gu)


SD0, SD1, SX0, SX1, SY0, SY1, SA, SB = range(8)


class PlaneSum:
    def plane_setup(self, pc, rd, rx, ry, send, recv):
        self.pc, self.rd, self.rx, self.ry, self.send, self.recv = pc, rd, rx, ry, send, recv

    def cp(self, src, dst, dev, k, s):
        return remote(src, dst, dev, self.send.at[k, s], self.recv.at[k, s])

    def d0(self, s):
        p = self.pc
        return self.cp(self.piece(s, 1 - p.y, 1 - p.x, 0), self.rd.at[s, 0], p.yn(), SD0, s)

    def d1(self, s):
        p = self.pc
        return self.cp(self.piece(s, 1 - p.y, 1 - p.x, 1), self.rd.at[s, 1], p.xn(), SD1, s)

    def x1(self, s):
        p = self.pc
        return self.cp(self.piece(s, p.y, 1 - p.x, 1), self.rx.at[s, 1], p.xn(), SX1, s)

    def y0(self, s):
        p = self.pc
        return self.cp(self.piece(s, 1 - p.y, p.x, 0), self.ry.at[s, 0], p.yn(), SY0, s)

    def x0(self, s):
        return self.cp(self.rd.at[s, 0], self.rx.at[s, 0], self.pc.xn(), SX0, s)

    def y1(self, s):
        return self.cp(self.rd.at[s, 1], self.ry.at[s, 1], self.pc.yn(), SY1, s)

    def plane_far(self, s):
        self.d0(s).start()
        self.d1(s).start()

    def plane_near(self, s):
        self.x1(s).start()
        self.y0(s).start()

    def plane_first(self, s):
        self.plane_far(s)
        self.plane_near(s)

    def plane_second(self, s):
        p = self.pc
        self.d0(s).wait_recv()
        self.rd[s, 0] = self.rd[s, 0] + self.piece(s, p.y, 1 - p.x, 0)[...]
        self.x0(s).start()
        self.d1(s).wait_recv()
        self.rd[s, 1] = self.rd[s, 1] + self.piece(s, 1 - p.y, p.x, 1)[...]
        self.y1(s).start()

    def plane_arrived(self, s):
        for c in (self.x1, self.y0, self.x0, self.y1):
            c(s).wait_recv()

    def plane_total(self, s, k):
        p = self.pc
        own = self.piece(s, p.y, p.x, k)[...].astype(f32)
        return own + self.rx[s, k].astype(f32) + self.ry[s, k].astype(f32)

    def plane_finish(self, s):
        for c in (self.d0, self.d1, self.x1, self.y0, self.x0, self.y1):
            c(s).wait_send()


class Scatter(PlaneSum):
    def __init__(self, pc, part, bufs, out, send, recv):
        rd, rx, ry, self.zz = bufs
        self.plane_setup(pc, rd, rx, ry, send, recv)
        self.part, self.out = part, out
        self.h = halves(part.shape[-2])

    @staticmethod
    def scratch(rows, columns):
        half = VMEM((NZ, 2, rows // 2, columns), bf16)
        return [half, half, half, VMEM((NZ + 1, 2, rows // 2, columns), bf16)]

    def piece(self, s, y, x, k):
        return self.part.at[s, y, x, self.h[k]]

    def down(self, zp):
        return self.cp(self.rx.at[zp], self.zz.at[zp], self.pc.down(), SA, zp)

    def up(self, zp):
        gap = zp - (self.pc.z + 1)
        spot = zp + (1 - (gap + NZ - 1) // NZ) * (NZ - zp)
        return self.cp(self.rx.at[zp], self.zz.at[spot], self.pc.up(), SB, zp)

    def far_event(self, i):
        self.plane_far(far(self.pc.z, i))

    def near_event(self, i):
        self.plane_near(far(self.pc.z, i))

    def d_event(self, i):
        self.plane_second(far(self.pc.z, i))

    def xy_event(self, i):
        zp = far(self.pc.z, i)
        self.plane_arrived(zp)
        for k in range(2):
            self.rx[zp, k] = self.plane_total(zp, k).astype(bf16)

    def z_event(self, i):
        z = self.pc.z
        zp = far(z, i)

        @pl.when(zp < z)
        def _():
            @pl.when(z < NZ - 1)
            def _():
                self.down(zp).wait_recv()
                self.rx[zp] = self.rx[zp] + self.zz[zp]

            self.down(zp).start()

        @pl.when(zp > z)
        def _():
            @pl.when(z > 0)
            def _():
                self.up(zp).wait_recv()
                self.rx[zp] = self.rx[zp] + self.zz[zp]

            self.up(zp).start()

    def final(self):
        z = self.pc.z
        self.plane_arrived(z)
        for k in range(2):
            self.out[self.h[k], :] = self.plane_total(z, k)

        @pl.when(z < NZ - 1)
        def _():
            self.down(z).wait_recv()
            for k in range(2):
                self.out[self.h[k], :] += self.zz[z, k].astype(f32)

        @pl.when(z > 0)
        def _():
            self.up(z).wait_recv()
            for k in range(2):
                self.out[self.h[k], :] += self.zz[NZ, k].astype(f32)

    def finish(self):
        z = self.pc.z
        for zp in range(NZ):
            self.plane_finish(zp)

            @pl.when(zp < z)
            def _():
                self.down(zp).wait_send()

            @pl.when(zp > z)
            def _():
                self.up(zp).wait_send()


class ScatterZ(PlaneSum):
    def __init__(self, pc, part, bufs, out, send, recv):
        rd, rx, ry, self.zz, self.sm = bufs
        self.plane_setup(pc, rd, rx, ry, send, recv)
        self.part, self.out = part, out
        self.h = halves(part.shape[-2])

    @staticmethod
    def scratch(rows, columns):
        half = VMEM((1, 2, rows // 2, columns), bf16)
        return [half, half, half, VMEM((NZ + 1, 4, rows, columns), bf16), VMEM((4, rows, columns), bf16)]

    def piece(self, s, y, x, k):
        return self.sm.at[y * 2 + x, self.h[k]]

    def down(self, zp, k, src):
        return self.cp(src, self.zz.at[zp, k], self.pc.down(), 8 + zp, k)

    def up(self, zp, k, src):
        gap = zp - (self.pc.z + 1)
        spot = zp + (1 - (gap + NZ - 1) // NZ) * (NZ - zp)
        return self.cp(src, self.zz.at[spot, k], self.pc.up(), 12 + zp, k)

    def first(self, i):
        z = self.pc.z
        zp = far(z, i)
        for k in range(4):
            src = self.part.at[zp, k // 2, k % 2]

            @pl.when((z == NZ - 1) & (zp < z))
            def _():
                self.down(zp, k, src).start()

            @pl.when((z == 0) & (zp > z))
            def _():
                self.up(zp, k, src).start()

    def z_event(self, i, k):
        z = self.pc.z
        zp = far(z, i)
        held = self.zz.at[zp, k]

        @pl.when((zp < z) & (z < NZ - 1))
        def _():
            self.down(zp, k, held).wait_recv()
            self.zz[zp, k] = self.zz[zp, k] + self.part[zp, k // 2, k % 2]
            self.down(zp, k, held).start()

        @pl.when((zp > z) & (z > 0))
        def _():
            self.up(zp, k, held).wait_recv()
            self.zz[zp, k] = self.zz[zp, k] + self.part[zp, k // 2, k % 2]
            self.up(zp, k, held).start()

    def own_event(self, k):
        z = self.pc.z

        @pl.when(z < NZ - 1)
        def _():
            self.down(z, k, self.zz.at[z, k]).wait_recv()

        @pl.when(z > 0)
        def _():
            self.up(z, k, self.zz.at[z, k]).wait_recv()

        own = self.part[z, k // 2, k % 2].astype(f32)

        @pl.when(z == 0)
        def _():
            self.sm[k] = (own + self.zz[z, k].astype(f32)).astype(bf16)

        @pl.when(z == NZ - 1)
        def _():
            self.sm[k] = (own + self.zz[NZ, k].astype(f32)).astype(bf16)

        @pl.when((z > 0) & (z < NZ - 1))
        def _():
            both = self.zz[z, k].astype(f32) + self.zz[NZ, k].astype(f32)
            self.sm[k] = (own + both).astype(bf16)

    def plane_send(self):
        self.plane_first(0)

    def plane_event(self):
        self.plane_second(0)

    def final(self):
        self.plane_arrived(0)
        for k in range(2):
            self.out[self.h[k], :] = self.plane_total(0, k)

    def finish(self):
        z = self.pc.z
        self.plane_finish(0)
        for zp in range(NZ):
            for k in range(4):

                @pl.when(zp < z)
                def _():
                    self.down(zp, k, self.zz.at[zp, k]).wait_send()

                @pl.when(zp > z)
                def _():
                    self.up(zp, k, self.zz.at[zp, k]).wait_send()


class SequenceSum(PlaneSum):
    def __init__(self, pc, terms, bufs, send, recv, core_send, core_recv):
        rd, rx, ry, self.theirs = bufs
        self.plane_setup(pc, rd, rx, ry, send, recv)
        self.terms, self.core_send, self.core_recv = terms, core_send, core_recv
        self.h = halves(terms.shape[-2])

    @staticmethod
    def scratch(rows, columns):
        half = VMEM((1, 2, rows // 2, columns), bf16)
        return [half, half, half, VMEM((2, 2, rows, columns), bf16)]

    def piece(self, s, y, x, k):
        return self.theirs.at[y, x, self.h[k]]

    def swap(self):
        p = self.pc
        return remote(
            self.terms.at[:, :, 1 - p.core], self.theirs, p.sn(), self.core_send, self.core_recv
        )

    def core_event(self):
        p = self.pc
        self.swap().wait_recv()
        for y in range(2):
            for x in range(2):
                self.theirs[y, x] = self.theirs[y, x] + self.terms[y, x, p.core]
        self.plane_first(0)

    def finish(self):
        self.swap().wait_send()
        self.plane_finish(0)


def norm_back(src, gain, grad, part_ref, part_row, emit):
    part_ref[pl.ds(part_row, 1), :] = jnp.zeros((1, part_ref.shape[1]), f32)

    def body(i, _):
        rows = pl.ds(pl.multiple_of(i * 32, 32), 32)
        v, g = src[rows, :].astype(f32), grad[rows, :]
        inv = lax.rsqrt(jnp.mean(v * v, axis=-1, keepdims=True) + EPS)
        unit = v * inv
        part_ref[pl.ds(part_row, 1), :] += jnp.sum(g * unit, axis=0, keepdims=True)
        gg = g * gain[...]
        emit(rows, inv * (gg - unit * jnp.mean(gg * unit, axis=-1, keepdims=True)))
        return 0

    lax.fori_loop(0, grad.shape[0] // 32, body, 0)


def sum_steps(letter, g):
    part = functools.partial
    steps = {letter + "f": g.final}
    for i in range(NZ):
        steps[f"{letter}a{i}"] = part(g.far_event, i)
        steps[f"{letter}b{i}"] = part(g.near_event, i)
        steps[f"{letter}d{i}"] = part(g.d_event, i)
        if i < NZ - 1:
            steps[f"{letter}x{i}"] = part(g.xy_event, i)
            steps[f"{letter}z{i}"] = part(g.z_event, i)
    return steps


def weight_grad(left, zp, right, part):
    rows, columns = part.shape[-2:]
    lhs = left[pl.ds(zp * 4, 4)].reshape(4 * rows, left.shape[-1])
    step = 512

    def body(n, _):
        c = cols(n, step)
        part[zp, :, :, :, c] = dot(lhs, right[:, c]).astype(bf16).reshape(2, 2, rows, step)
        return 0

    lax.fori_loop(0, columns // step, body, 0)


LOADS = [
    "act", "cot", "ffn", "ggu", "wgu", "res", "mix", "mixf", "linv", "q2", "kk", "va", "mask",
    "qkv", "wout", "attn", "wqkv", "x",
]


def backward_kernel(dims, *refs):
    (tok, width, n_dev, heads_w, kv_w, ff) = dims
    (
        cos_ref, sin_ref, g_attn, g_q, g_k, g_ffn,
        i_x, i_tattn, i_tmix, i_tffn, i_tact, i_cot, i_ggu, i_qkv, i_q2, i_linv, i_mixf, i_res,
        i_kk, i_va, i_mask, i_wqkv, i_wout, i_wgu,
        o_dx, o_attn, o_q, o_k, o_ffn, out_wqkv, out_wout, out_wgu, out_wdown,
        t_ffn, t_act, cot2, ggu2, qkv, q2, linv, mixf, kk, va, mask_t, w_gu,
        part_qkv, part_out, part_gu, part_down, res, gains, came, gh, gattn2, acc_k, acc_v, acc_q,
        aug, gm, terms,
        send, recv, kv_send, kv_recv, ex_send, ex_recv, g_send, g_recv, lsem,
    ) = refs[:69]
    bufs = refs[69:]
    pc = Place()
    z = pc.z
    part = functools.partial
    loads = {}

    def load(name, src, dst):
        def copy():
            return pltpu.make_async_copy(src(), dst(), lsem.at[LOADS.index(name)])

        loads[name] = lambda: copy().wait()
        copy().start()

    load("act", lambda: i_tact, lambda: t_act)
    load("cot", lambda: i_cot, lambda: cot2)
    load("ffn", lambda: i_tffn, lambda: t_ffn)
    load("ggu", lambda: i_ggu, lambda: ggu2)
    load("wgu", lambda: i_wgu, lambda: w_gu)
    load("res", lambda: i_res, lambda: res)
    load("mixf", lambda: i_mixf, lambda: mixf)
    load("linv", lambda: i_linv, lambda: linv)
    load("q2", lambda: i_q2, lambda: q2)
    load("kk", lambda: i_kk, lambda: kk)
    load("va", lambda: i_va, lambda: va)
    load("mask", lambda: i_mask, lambda: mask_t)
    load("qkv", lambda: i_qkv, lambda: qkv)
    bar = pltpu.get_barrier_semaphore()
    for device in (pc.xn(), pc.yn(), pc.sn()):
        pl.semaphore_signal(bar, inc=1, device_id=device, device_id_type=MESH)
    for k in range(1, NZ):
        there = pc.at(z=(z + k) % NZ)
        pl.semaphore_signal(bar, inc=1, device_id=there, device_id_type=MESH)
    pl.semaphore_wait(bar, 3 + NZ - 1)
    down = Scatter(pc, part_down, bufs[0:4], out_wdown, send.at[0], recv.at[0])
    gateup = Scatter(pc, part_gu, bufs[4:8], out_wgu, send.at[1], recv.at[1])
    out = ScatterZ(pc, part_out, bufs[8:13], out_wout, send.at[2], recv.at[2])
    last = Scatter(pc, part_qkv, bufs[17:21], out_wqkv, send.at[3], recv.at[3])
    seq = SequenceSum(pc, terms, bufs[13:17], kv_send, kv_recv, ex_send.at[2], ex_recv.at[2])

    own = pl.ds(0, tok)
    back = pl.ds(tok, tok)

    def rows_of(left, right, term, names, i):
        for name in names:
            if name in loads:
                loads.pop(name)()
        weight_grad(left, far(z, i), right, term)

    def h_step(n):
        w = w_gu[n // 2, n % 2].reshape(width // 8, 2 * ff)
        gh[:, cols(n, width // 8)] = dot_t(ggu2[own, :], w)

    def start_h():
        loads.pop("wgu")()
        loads.pop("res")()

    def keep_residual(rows, grad):
        total = cot2[rows, :].astype(f32) + grad
        res[rows, :] = total
        gattn2[rows, :] = total.astype(bf16)

    sent_attn = remote(gattn2.at[own, :], gattn2.at[back, :], pc.sn(), ex_send.at[0], ex_recv.at[0])

    def residual_back():
        load("wout", lambda: i_wout, lambda: w_gu.at[:, :, :, :, pl.ds(0, part_out.shape[-2]), :])
        gains[...] = jnp.zeros_like(gains)
        norm_back(res, g_ffn, gh, gains, 1, keep_residual)
        sent_attn.start()
        loads.pop("wout")()

    columns = part_qkv.shape[-1]
    some = pl.ds(0, columns)

    def load_mix():
        load("mix", lambda: i_tmix, lambda: t_act)

    def load_last():
        load("attn", lambda: i_tattn, lambda: t_ffn)
        load("wqkv", lambda: i_wqkv, lambda: w_gu.at[:, :, :, :, :, some])
        load("x", lambda: i_x, lambda: cot2.at[own, :])

    def m_step(n, _):
        w = w_gu[n, :, :, :, pl.ds(0, part_out.shape[-2]), :].reshape(heads_w // NZ, width)
        gm[:, cols(n, heads_w // NZ)] = dot_t(gattn2[own, :], w).astype(bf16)
        return 0

    def mixed_back():
        lax.fori_loop(0, NZ, m_step, 0)
        sent_attn.wait()

    def start_attention():
        for name in ("mixf", "linv", "q2", "kk", "va", "mask", "qkv"):
            loads.pop(name)()

    low = lanes((tok, 128)) < 64
    chunk = 512
    n_chunk = n_dev * tok // chunk
    def attend(tick):
        t, kc = tick // n_chunk, tick % n_chunk
        g = t // 2
        rows = pl.ds(pl.multiple_of(kc * chunk, chunk), chunk)

        @pl.when(kc == 0)
        def _():
            c = cols(t, 128)
            grad = gm[:, c].astype(f32)
            delta = head_sums(grad * mixf[:, c]) * linv[:, c]
            grad = grad * linv[:, c]
            lane = lanes((tok, 128))
            for half in range(2):
                d = roll_half(delta) if half == 0 else delta
                v = grad if half == 0 else roll_half(grad)
                high = d.astype(bf16).astype(f32)
                rest = jnp.where(lane == 64, -high, jnp.where(lane == 65, high - d, 0.0))
                aug[pl.ds(half * tok, tok), :] = jnp.where(low, v, rest).astype(bf16)

        seen = mask_t[rows, :]
        e = jnp.exp2(dot_t(kk[g, rows, :], q2[t]) * LOG2E).astype(bf16)
        e = e * jnp.concatenate([seen, seen], axis=1)
        dv = dot(e, aug[...])
        ds = e * dot_t(va[g, rows, :], aug[...]).astype(bf16)
        dk = dot(ds, q2[t])
        dq = lax.dot_general(kk[g, rows, :], ds, (((0,), (0,)), ((), ())), preferred_element_type=f32)

        @pl.when(t % 2 == 0)
        def _():
            acc_k[rows, :] = dk
            acc_v[rows, :] = dv

        @pl.when(t % 2 == 1)
        def _():
            both_k = acc_k[rows, :] + dk
            both_v = acc_v[rows, :] + dv
            both_k = both_k + roll_half(both_k)
            lower = lanes((chunk, 128)) < 64
            both_v = jnp.where(lower, both_v, roll_half(both_v))
            mine = (lanes((chunk, 128)) // 64) == (g % 2)
            for b in range(chunk // tok):
                spot = kc * (chunk // tok) + b
                y, x, c = spot // 4, (spot // 2) % 2, spot % 2
                cut = slice(b * tok, (b + 1) * tok)
                for base, value in ((0, both_k), (kv_w, both_v)):
                    place = pl.ds(pl.multiple_of(base + (g // 2) * 128, 128), 128)
                    old = terms[y, x, c, :, place].astype(f32)
                    terms[y, x, c, :, place] = jnp.where(mine[cut], value[cut], old).astype(bf16)

        @pl.when(kc == 0)
        def _():
            acc_q[...] = dq

        @pl.when(kc > 0)
        def _():
            acc_q[...] += dq

        @pl.when(kc == n_chunk - 1)
        def _():
            turned = jnp.transpose(acc_q[...])
            gh[:, cols(t, 128)] = jnp.where(low, turned[:tok], turned[tok:]) * 0.125


    def head_back(t, grad, gain, row):
        c = cols(t, 128)
        u = qkv[:, c]
        inv = lax.rsqrt(head_sums(u * u) * (1.0 / 64) + EPS)
        unit = u * inv
        grad = grad * cos_ref[...] - swap_rot(grad) * sin_ref[...]
        gains[pl.ds(row, 1), pl.ds(0, 128)] += jnp.sum(grad * unit, axis=0, keepdims=True)
        gg = grad * gain[...]
        gattn2[own, c] = (inv * (gg - unit * head_sums(gg * unit) * (1.0 / 64))).astype(bf16)

    def query_back(t):
        head_back(t, gh[:, cols(t, 128)], g_q, 2)

    sent_qkv = remote(gattn2.at[own, some], gattn2.at[back, some], pc.sn(), ex_send.at[1], ex_recv.at[1])

    def keys_back():
        seq.plane_arrived(0)
        for k in range(2):
            gh[seq.h[k], pl.ds(0, 2 * kv_w)] = seq.plane_total(0, k)
        for t in range(kv_w // 128):
            head_back(heads_w // 128 + t, gh[:, pl.ds(t * 128, 128)], g_k, 3)
        gattn2[own, pl.ds(heads_w + kv_w, kv_w)] = gh[:, pl.ds(kv_w, kv_w)].astype(bf16)
        sent_qkv.start()

    def g_step(n):
        w = w_gu[n // 2, n % 2, :, :, :, some].reshape(width // 8, columns)
        gh[:, cols(n, width // 8)] = dot_t(gattn2[own, some], w)

    def keep_input(rows, grad):
        cot2[pl.ds(rows.start + tok, rows.size), :] = (res[rows, :] + grad).astype(bf16)

    sent_dx = pltpu.make_async_copy(cot2.at[back, :], o_dx, lsem.at[len(LOADS)])

    def input_back():
        loads.pop("x")()
        norm_back(cot2, g_attn, gh, gains, 0, keep_input)
        sent_dx.start()

    def start_g():
        loads.pop("wqkv")()

    def hop(k):
        device = (pc.sn(), pc.xn(), pc.yn())[k]
        return remote(gains, came.at[k], device, g_send.at[k], g_recv.at[k])

    def hop_end(k):
        hop(k).wait()
        gains[...] += came[k]

    def ring(k):
        there = pc.at(z=(z + k) % NZ)
        return remote(gains, came.at[3 + z], there, g_send.at[2 + k], g_recv.at[3 + z])

    def ring_start():
        came[3 + z] = gains[...]
        for k in range(1, NZ):
            ring(k).start()

    def ring_end():
        for k in range(1, NZ):
            there = (z + k) % NZ
            slot = came.at[3 + there]
            remote(gains, slot, pc.at(z=there), g_send.at[2 + k], g_recv.at[3 + there]).wait_recv()
        total = came[3]
        for k in range(1, NZ):
            total = total + came[3 + k]
        o_attn[...] = total[0:1]
        o_ffn[...] = total[1:2]
        for o, row in ((o_q, 2), (o_k, 3)):
            v = total[:, :128]
            o[...] = (v + roll_half(v))[row : row + 1, :64]

    steps = {
        "h": start_h, "nb": residual_back, "m": mixed_back, "att": start_attention,
        "kvs": seq.swap().start, "kvc": seq.core_event, "kve": part(seq.plane_second, 0),
        "kvf": keys_back, "oS": out.plane_send, "oe": out.plane_event, "of": out.final,
        "lm": load_mix, "ll": load_last, "qe": sent_qkv.wait_recv, "g": start_g,
        "nb2": input_back, "rs": ring_start, "re": ring_end,
    }
    steps.update(sum_steps("q", last))
    steps.update(sum_steps("d", down))
    steps.update(sum_steps("g", gateup))
    for i in range(NZ):
        steps[f"dw{i}"] = part(rows_of, t_act, cot2, part_down, ("act", "cot"), i)
        steps[f"gw{i}"] = part(rows_of, t_ffn, ggu2, part_gu, ("ffn", "ggu"), i)
        steps[f"ow{i}"] = part(rows_of, t_act, gattn2, part_out, ("mix",), i)
        steps[f"qw{i}"] = part(rows_of, t_ffn, gattn2, part_qkv, ("attn",), i)
        steps[f"oa{i}"] = part(out.first, i)
        steps[f"oo{i}"] = part(out.own_event, i)
        if i < NZ - 1:
            for k in range(4):
                steps[f"oz{i}{k}"] = part(out.z_event, i, k)
            steps[f"hs{i}"] = hop(i).start
            steps[f"he{i}"] = part(hop_end, i)
    loops = {
        "H": (8, h_step),
        "B": (heads_w // 128 * n_chunk, attend),
        "Q": (heads_w // 128, query_back),
        "G": (8, g_step),
    }
    run_steps(BACKWARD_ORDER, steps, loops)
    for g in (down, gateup, out, seq, last):
        g.finish()
    sent_qkv.wait_send()
    for k in range(1, NZ):
        ring(k).wait_send()
    sent_dx.wait()


def backward(x, cosine, sine, g_attn, g_q, g_k, g_ffn, kept, rows, n_dev):
    (t_attn, t_mix, t_ffn, t_act, cot2, ggu2, qkv, q2, linv, mixf, res, kk, va, mask_t, w_qkv, w_out, w_gu) = kept
    tok, width = x.shape
    heads_w, kv_w = HEADS * HEAD_DIM, GROUPS * HEAD_DIM
    ff = ggu2.shape[1] // 2
    length = n_dev * tok
    columns = qkv.shape[1]
    dims = (tok, width, n_dev, heads_w, kv_w, ff)
    shape = jax.ShapeDtypeStruct
    vm = pl.BlockSpec(memory_space=VMEM)
    anyw = pl.BlockSpec(memory_space=pl.ANY)
    dma = pltpu.SemaphoreType.DMA
    r_qkv, r_out, r_gu, r_down = rows
    partial = [
        VMEM((NZ, 2, 2, r, c), bf16)
        for r, c in ((r_qkv, columns), (r_out, width), (r_gu, width), (r_down, width))
    ]
    like = [
        VMEM(v.shape, v.dtype)
        for v in (t_ffn, t_act, cot2, ggu2, qkv, q2, linv, mixf, kk, va, mask_t, w_gu)
    ]
    dx, grad_attn, grad_q, grad_k, grad_ffn, own_qkv, own_out, own_gu, own_down = pl.pallas_call(
        functools.partial(backward_kernel, dims),
        out_shape=[
            shape((tok, width), bf16),
            shape((1, width), f32),
            shape((1, 64), f32),
            shape((1, 64), f32),
            shape((1, width), f32),
            shape((r_qkv, columns), f32),
            shape((r_out, width), f32),
            shape((r_gu, width), f32),
            shape((r_down, width), f32),
        ],
        in_specs=[vm] * 6 + [anyw] * 18,
        out_specs=[anyw] + [vm] * 8,
        scratch_shapes=like
        + partial
        + [
            VMEM((tok, width), f32),
            VMEM((8, width), f32),
            VMEM((3 + NZ, 8, width), f32),
            VMEM((tok, width), f32),
            VMEM((2 * tok, width), bf16),
            VMEM((length, 128), f32),
            VMEM((length, 128), f32),
            VMEM((128, 2 * tok), f32),
            VMEM((2 * tok, 128), bf16),
            VMEM((tok, heads_w), bf16),
            VMEM((2, 2, 2, tok, 2 * kv_w), bf16),
            dma((4, 16, NZ)),
            dma((4, 16, NZ)),
            dma((8, 1)),
            dma((8, 1)),
            dma((3,)),
            dma((3,)),
            dma((3 + NZ,)),
            dma((3 + NZ,)),
            dma((len(LOADS) + 1,)),
        ]
        + Scatter.scratch(r_down, width)
        + Scatter.scratch(r_gu, width)
        + ScatterZ.scratch(r_out, width)
        + SequenceSum.scratch(tok, 2 * kv_w)
        + Scatter.scratch(r_qkv, columns),
        compiler_params=pltpu.CompilerParams(
            collective_id=1, has_side_effects=True, vmem_limit_bytes=64 << 20
        ),
        cost_estimate=pl.CostEstimate(
            flops=20 * tok * width * width, bytes_accessed=60 << 20, transcendentals=0
        ),
        name="backward",
    )(
        cosine, sine, g_attn, g_q, g_k, g_ffn, x, t_attn, t_mix, t_ffn, t_act, cot2, ggu2, qkv, q2,
        linv, mixf, res, kk, va, mask_t, w_qkv, w_out, w_gu,
    )
    return dx, grad_attn[0], own_qkv, grad_q[0], grad_k[0], own_out, grad_ffn[0], own_gu, own_down


epsilon = 1e-06


def norm_rows(values, gain_vec):
    return (
        values * lax.rsqrt(jnp.mean(values * values, axis=-1, keepdims=True) + epsilon) * gain_vec
    )


def rotate(values, positions):
    half_dim = values.shape[-1] // 2
    frequency = jnp.exp(
        jnp.arange(half_dim).astype(jnp.float32) * (-2.0 * math.log(10000.0) / values.shape[-1])
    )
    angles = positions.astype(jnp.float32)[:, None] * frequency[None, :]
    cosine = jnp.cos(angles)[:, None, :]
    sine = jnp.sin(angles)[:, None, :]
    first = values[..., :half_dim]
    second = values[..., half_dim:]
    return jnp.concatenate(
        [first * cosine - second * sine, second * cosine + first * sine], axis=-1
    )


def project_heads(qkv_all, positions, q_gain, k_gain):
    tok_rows = qkv_all.shape[0]
    q_cols = HEADS * HEAD_DIM
    k_cols = GROUPS * HEAD_DIM
    queries = qkv_all[:, :q_cols].reshape(tok_rows, HEADS, HEAD_DIM)
    keys_raw = qkv_all[:, q_cols : q_cols + k_cols].reshape(tok_rows, GROUPS, HEAD_DIM)
    values = qkv_all[:, q_cols + k_cols :].reshape(tok_rows, GROUPS, HEAD_DIM)
    return (
        rotate(norm_rows(queries, q_gain), positions),
        rotate(norm_rows(keys_raw, k_gain), positions),
        values,
    )


def gated(gate_up):
    return jax.nn.silu(gate_up[:, :FF]) * gate_up[:, FF:]


def per_device_plain(
    inputs, places, cotangent, attn_gain, w_qkv, q_gain, k_gain, w_out, ffn_gain, w_gateup, w_down
):
    tok_rows = inputs.shape[1]
    repeat = HEADS // GROUPS
    score_scale = HEAD_DIM ** (-0.5)
    here_f = inputs[0].astype(jnp.float32)
    own_places = places[0]
    qkv_w, out_w = (
        lax.all_gather(w_qkv, ("dp", "ctx"), axis=0, tiled=True),
        lax.all_gather(w_out, ("dp", "ctx"), axis=0, tiled=True),
    )
    h_attn_f, pull_attn = jax.vjp(norm_rows, here_f, attn_gain)
    h_attn = h_attn_f.astype(jnp.bfloat16)
    qkv_all = jnp.dot(h_attn, qkv_w, preferred_element_type=jnp.float32)

    def heads_of(qkv_in, gain_q, gain_k):
        return project_heads(qkv_in, own_places, gain_q, gain_k)

    (queries, keys_f, values), pull_heads = jax.vjp(heads_of, qkv_all, q_gain, k_gain)
    query_b = queries.astype(jnp.bfloat16).reshape(tok_rows, GROUPS, repeat, HEAD_DIM)
    key_b = keys_f.astype(jnp.bfloat16)
    value_b = values.astype(jnp.bfloat16)
    all_keys, all_values = (
        lax.all_gather(key_b, "ctx", axis=0, tiled=True),
        lax.all_gather(value_b, "ctx", axis=0, tiled=True),
    )
    all_places = lax.all_gather(own_places, "ctx", axis=0, tiled=True)
    blocks = lax.axis_size("ctx")
    key_blocks = all_keys.reshape(blocks, tok_rows, GROUPS, HEAD_DIM)
    value_blocks = all_values.reshape(blocks, tok_rows, GROUPS, HEAD_DIM)
    place_blocks = all_places.reshape(blocks, tok_rows)

    def score_block(key_blk, place_blk):
        scores = (
            jnp.einsum("igrd,jgd->grij", query_b, key_blk, preferred_element_type=jnp.float32)
            * score_scale
        )
        allowed = place_blk[None, :] <= own_places[:, None]
        return (scores, allowed)

    def max_step(state_pair, entries):
        row_top, row_total = state_pair
        scores, allowed = score_block(entries[0], entries[1])
        scores = jnp.where(allowed, scores, -1e30)
        new_top = jnp.maximum(row_top, jnp.max(scores, axis=-1))
        row_total = row_total * jnp.exp(row_top - new_top) + jnp.sum(
            jnp.where(allowed, jnp.exp(scores - new_top[..., None]), 0.0), axis=-1
        )
        return ((new_top, row_total), None)

    start_pair = (
        jnp.full((GROUPS, repeat, tok_rows), -1e30, jnp.float32),
        jnp.zeros((GROUPS, repeat, tok_rows), jnp.float32),
    )
    (row_top, row_total), _ = lax.scan(max_step, start_pair, (key_blocks, place_blocks))
    log_total = row_top + jnp.log(row_total)

    def out_step(accum, entries):
        scores, allowed = score_block(entries[0], entries[1])
        weights_b = jnp.where(allowed, jnp.exp(scores - log_total[..., None]), 0.0).astype(
            jnp.bfloat16
        )
        return (
            accum
            + jnp.einsum(
                "grij,jgd->igrd", weights_b, entries[2], preferred_element_type=jnp.float32
            ),
            None,
        )

    mixed_f, _ = lax.scan(
        out_step,
        jnp.zeros((tok_rows, GROUPS, repeat, HEAD_DIM), jnp.float32),
        (key_blocks, place_blocks, value_blocks),
    )
    mixed_b = mixed_f.reshape(tok_rows, HEADS * HEAD_DIM).astype(jnp.bfloat16)
    attn_out = jnp.dot(mixed_b, out_w, preferred_element_type=jnp.float32)
    residual = here_f + attn_out
    gateup_w, down_w = (
        lax.all_gather(w_gateup, ("dp", "ctx"), axis=0, tiled=True),
        lax.all_gather(w_down, ("dp", "ctx"), axis=0, tiled=True),
    )
    h_ffn_f, pull_ffn = jax.vjp(norm_rows, residual, ffn_gain)
    h_ffn = h_ffn_f.astype(jnp.bfloat16)
    gate_up = jnp.dot(h_ffn, gateup_w, preferred_element_type=jnp.float32)
    act_f, pull_gate = jax.vjp(gated, gate_up)
    act_b = act_f.astype(jnp.bfloat16)
    result = residual + jnp.dot(act_b, down_w, preferred_element_type=jnp.float32)
    layer_output = result.astype(jnp.bfloat16)[None]
    gateup_w, down_w = (
        lax.all_gather(w_gateup, ("dp", "ctx"), axis=0, tiled=True),
        lax.all_gather(w_down, ("dp", "ctx"), axis=0, tiled=True),
    )
    grad_out = cotangent[0]
    grad_act = jnp.dot(grad_out, down_w.T, preferred_element_type=jnp.float32)
    grad_down = jnp.dot(act_b.T, grad_out, preferred_element_type=jnp.float32)
    grad_gu_b = pull_gate(grad_act)[0].astype(jnp.bfloat16)
    grad_gateup = jnp.dot(h_ffn.T, grad_gu_b, preferred_element_type=jnp.float32)
    grad_h_ffn = jnp.dot(grad_gu_b, gateup_w.T, preferred_element_type=jnp.float32)
    grad_resid_part, grad_ffn_gain = pull_ffn(grad_h_ffn)
    grad_residual = grad_out.astype(jnp.float32) + grad_resid_part
    grad_gateup_own, grad_down_own = (
        lax.psum_scatter(grad_gateup, ("dp", "ctx"), scatter_dimension=0, tiled=True),
        lax.psum_scatter(grad_down, ("dp", "ctx"), scatter_dimension=0, tiled=True),
    )
    qkv_w, out_w = (
        lax.all_gather(w_qkv, ("dp", "ctx"), axis=0, tiled=True),
        lax.all_gather(w_out, ("dp", "ctx"), axis=0, tiled=True),
    )
    grad_attn_b = grad_residual.astype(jnp.bfloat16)
    grad_out_w = jnp.dot(mixed_b.T, grad_attn_b, preferred_element_type=jnp.float32)
    grad_mixed_b = (
        jnp.dot(grad_attn_b, out_w.T, preferred_element_type=jnp.float32)
        .astype(jnp.bfloat16)
        .reshape(tok_rows, GROUPS, repeat, HEAD_DIM)
    )
    row_delta = jnp.transpose(
        jnp.sum(grad_mixed_b.astype(jnp.float32) * mixed_f, axis=-1), (1, 2, 0)
    )

    def back_step(grad_query, entries):
        key_blk, place_blk, value_blk = entries
        scores, allowed = score_block(key_blk, place_blk)
        weights_f = jnp.where(allowed, jnp.exp(scores - log_total[..., None]), 0.0)
        weights_b = weights_f.astype(jnp.bfloat16)
        grad_value = jnp.einsum(
            "grij,igrd->jgd", weights_b, grad_mixed_b, preferred_element_type=jnp.float32
        )
        grad_prob = jnp.einsum(
            "igrd,jgd->grij", grad_mixed_b, value_blk, preferred_element_type=jnp.float32
        )
        grad_score = (weights_f * (grad_prob - row_delta[..., None])).astype(jnp.bfloat16)
        grad_query = grad_query + jnp.einsum(
            "grij,jgd->igrd", grad_score, key_blk, preferred_element_type=jnp.float32
        )
        grad_key = (
            jnp.einsum("grij,igrd->jgd", grad_score, query_b, preferred_element_type=jnp.float32)
            * score_scale
        )
        return (
            grad_query,
            jnp.concatenate(
                [
                    grad_key.reshape(tok_rows, GROUPS * HEAD_DIM),
                    grad_value.reshape(tok_rows, GROUPS * HEAD_DIM),
                ],
                axis=1,
            ),
        )

    grad_query, kv_terms = lax.scan(
        back_step,
        jnp.zeros((tok_rows, GROUPS, repeat, HEAD_DIM), jnp.float32),
        (key_blocks, place_blocks, value_blocks),
    )
    grad_query = grad_query * score_scale
    kv_own = lax.psum_scatter(
        kv_terms.reshape(blocks * tok_rows, 2 * GROUPS * HEAD_DIM).astype(jnp.bfloat16),
        "ctx",
        scatter_dimension=0,
        tiled=True,
    ).astype(jnp.float32)
    grad_key_own = kv_own[:, : GROUPS * HEAD_DIM].reshape(tok_rows, GROUPS, HEAD_DIM)
    grad_value_own = kv_own[:, GROUPS * HEAD_DIM :].reshape(tok_rows, GROUPS, HEAD_DIM)
    grad_qkv_f, grad_q_gain, grad_k_gain = pull_heads(
        (grad_query.reshape(tok_rows, HEADS, HEAD_DIM), grad_key_own, grad_value_own)
    )
    grad_qkv_b = grad_qkv_f.astype(jnp.bfloat16)
    grad_qkv_w = jnp.dot(h_attn.T, grad_qkv_b, preferred_element_type=jnp.float32)
    grad_h_attn = jnp.dot(grad_qkv_b, qkv_w.T, preferred_element_type=jnp.float32)
    grad_here_part, grad_attn_gain = pull_attn(grad_h_attn)
    grad_inputs = (grad_residual + grad_here_part).astype(jnp.bfloat16)[None]
    grad_qkv_own, grad_out_own = (
        lax.psum_scatter(grad_qkv_w, ("dp", "ctx"), scatter_dimension=0, tiled=True),
        lax.psum_scatter(grad_out_w, ("dp", "ctx"), scatter_dimension=0, tiled=True),
    )
    gain_attn, gain_query, gain_key, gain_ffn = lax.psum(
        (grad_attn_gain, grad_q_gain, grad_k_gain, grad_ffn_gain), ("dp", "ctx")
    )
    return (
        layer_output,
        grad_inputs,
        gain_attn,
        grad_qkv_own,
        gain_query,
        gain_key,
        grad_out_own,
        gain_ffn,
        grad_gateup_own,
        grad_down_own,
    )


def per_device_fast(
    inputs, places, cotangent, attn_gain, w_qkv, q_gain, k_gain, w_out, ffn_gain, w_gateup, w_down
):
    n_dev = lax.axis_size("ctx")
    own_places = places[0]
    half = HEAD_DIM // 2
    spot = jnp.arange(128)
    frequency = jnp.exp((spot % half).astype(f32) * (-2.0 * math.log(10000.0) / HEAD_DIM))
    angles = own_places.astype(f32)[:, None] * frequency[None, :]
    cosine = jnp.cos(angles)
    sine = jnp.where(spot % HEAD_DIM < half, -1.0, 1.0) * jnp.sin(angles)
    block_row = (own_places // 128)[None, :]
    gain_q, gain_k = jnp.tile(q_gain, 2)[None], jnp.tile(k_gain, 2)[None]
    layer_output, *kept = forward(
        inputs[0], cotangent[0], block_row, cosine, sine, attn_gain[None], gain_q, gain_k,
        ffn_gain[None], w_qkv, w_out, w_down, w_gateup, n_dev,
    )
    rows = [w.shape[0] for w in (w_qkv, w_out, w_gateup, w_down)]
    grad_inputs, *grads = backward(
        inputs[0], cosine, sine, attn_gain[None], gain_q, gain_k, ffn_gain[None], kept, rows, n_dev
    )
    return (layer_output[None], grad_inputs[None], *grads)


def solution(mesh):
    in_specs = (
        P("dp", "ctx", None),
        P("dp", "ctx"),
        P("dp", "ctx", None),
        P(),
        P(("dp", "ctx"), None),
        P(),
        P(),
        P(("dp", "ctx"), None),
        P(),
        P(("dp", "ctx"), None),
        P(("dp", "ctx"), None),
    )
    out_specs = (
        P("dp", "ctx", None),
        P("dp", "ctx", None),
        P(),
        P(("dp", "ctx"), None),
        P(),
        P(),
        P(("dp", "ctx"), None),
        P(),
        P(("dp", "ctx"), None),
        P(("dp", "ctx"), None),
    )
    fast = dict(mesh.shape) == {"dp": 4, "ctx": 8}
    per_device = per_device_fast if fast else per_device_plain
    return jax.shard_map(
        per_device, mesh=mesh, in_specs=in_specs, out_specs=out_specs, check_vma=False
    )
```

```python
import functools
import math

import jax
import jax.numpy as jnp
import numpy as np
from jax import lax
from jax.experimental import pallas as pl
from jax.experimental.pallas import tpu as pltpu
from jax.sharding import PartitionSpec as P

HEADS = 16
GROUPS = 4
HEAD_DIM = 64
FF = 1024


FORWARD_ORDER = [
    "qp0", "oP", "qZ", "dZ", "qz1", "qe0", "qp1", "dp0", "qz2", "gZ", "trig", "qp2", "norm",
    "qc0", "qe1", "turn", "qz3", "dz1", "qp3", "qe2", "gz1", "gz2", "oZ", "qc1", "qe3", "oe",
    "qc2", "gp2", "qs0", "qc3", "oz10", "oD", "qs1", "qs2", "qs3", "keys", "de0", "gz3", "oz11",
    "kve", "gp0", "oz12", "ge2", "dz2", "query", "oz22", "kvc", "gp1", "dc0", "oz13", "gp3",
    "oz21", "unpack", "oz32", "A", "dp2", *["A"] * 3, "oz31", *["A"] * 5, "oz20", *["A"] * 4,
    "ge0", "A", "oz30", "ge1", "A", "gc2", *["A"] * 4, "oz23", *["A"] * 5, "dp1", "oc1", "oz33",
    *["A"] * 2, "oc3", "ge3", "A", "oc2", "de2", "A", "dz3", *["A"] * 2, "gc1", "dp3", "A", "gc0",
    "A", "res", "norm2", "gc3", "de1", "gs0", "ds0", "mix", "gs1", "de3", "dc2", "gs2", "dc1",
    "gs3", "dc3", "turn2", "ds1", "ds2", "ds3", "gate", "act", "y",
]

BACKWARD_ORDER = [
    "dw0", "dw1", "gw0", "dw2", "gw1", "dw3", "h", "gb0", *["H"] * 8, "ga1", "nb", "lm", "db0",
    "db2", "ga0", "gw2", "db1", "da2", "da0", "m", "ow0", "ow1", "oa0", "gd1", "att", "B", "ga2",
    "gw3", "B", "oz00", "B", "dd0", "gd0", "oa1", "B", "da1", *["B"] * 2, "oz03", "B", "gb3",
    "oz01", "da3", "ow2", "dx0", "ga3", "oa2", "gb1", "ll", "B", "gd2", "ow3", *["B"] * 4, "oz13",
    "dd1", "B", "gx0", *["B"] * 2, "gb2", "oz02", "B", "kvs", "dx1", "Q", "dd3", "dd2", "Q",
    "dz0", "Q", "kvc", "Q", "dz1", "Q", "oz23", "Q", "oz10", "oz12", "Q", "oz22", "Q", "oz11",
    "kve", "dx2", "db3", "gd3", "oz21", "gz0", "kvf", "g", *["G"] * 2, "qe", "qw0", "qa0", "gx2",
    "qw1", "qw2", "qb0", "G", "dz2", "G", "oz20", "oa3", "qa1", "gx1", "qb1", "G", "qa2", "G",
    "qb2", *["G"] * 2, "gz1", "qd0", "nb2", "qw3", "gz2", "oo0", "hs0", "qd1", "he0", "oo3",
    "oo1", "hs1", "qb3", "qd2", "qx0", "oo2", "qz0", "df", "he1", "qx1", "hs2", "qa3", "qz1",
    "oS", "he2", "qx2", "rs", "qz2", "qd3", "oe", "of", "gf", "qf", "re",
]

f32 = jnp.float32
bf16 = jnp.bfloat16
MESH = pl.DeviceIdType.MESH
NZ = 4
EPS = 1e-06


class Place:
    def __init__(self):
        self.z = lax.axis_index("dp")
        spot = lax.axis_index("ctx")
        self.core = spot % 2
        self.x = (spot // 2) % 2
        self.y = spot // 4

    def at(self, z=None, y=None, x=None, core=None):
        z = self.z if z is None else z
        y = self.y if y is None else y
        x = self.x if x is None else x
        core = self.core if core is None else core
        return (z, y * 4 + x * 2 + core)

    def xn(self):
        return self.at(x=1 - self.x)

    def yn(self):
        return self.at(y=1 - self.y)

    def sn(self):
        return self.at(core=1 - self.core)

    def up(self):
        return self.at(z=self.z + 1)

    def down(self):
        return self.at(z=self.z - 1)


def barrier(pc):
    bar = pltpu.get_barrier_semaphore()

    def greet(device):
        pl.semaphore_signal(bar, inc=1, device_id=device, device_id_type=MESH)

    for device in (pc.xn(), pc.yn(), pc.sn()):
        greet(device)

    @pl.when(pc.z < NZ - 1)
    def _():
        greet(pc.up())

    @pl.when(pc.z > 0)
    def _():
        greet(pc.down())

    pl.semaphore_wait(bar, 3 + (1 - pc.z // (NZ - 1)) + (pc.z + NZ - 1) // NZ)


def far(z, i):
    m = z // 2
    zz = z + m * (3 - 2 * z)
    lo = 3 - i if i < 2 else (1 - zz if i == 2 else zz)
    return lo + m * (3 - 2 * lo)


def near(z, i):
    return far(z, NZ - 1 - i)


def remote(src, dst, dev, send, recv):
    return pltpu.make_async_remote_copy(
        src_ref=src, dst_ref=dst, send_sem=send, recv_sem=recv, device_id=dev, device_id_type=MESH
    )


def halves(rows):
    return pl.ds(0, rows // 2), pl.ds(rows // 2, rows // 2)


KZ, KX, KY, KD0, KD1, KS, KU = range(7)


class Gather:
    def __init__(self, pc, buf, send, recv):
        self.pc, self.buf, self.send, self.recv = pc, buf, send, recv
        self.h = halves(buf.shape[-2])

    def cp(self, idx, dev, ks, kr, slot):
        ref = self.buf.at[idx]
        return remote(ref, ref, dev, self.send.at[ks, slot], self.recv.at[kr, slot])

    def c_up(self, z0):
        p = self.pc
        return self.cp((z0, p.y, p.x, p.core), p.up(), KU, KZ, z0)

    def c_down(self, z0):
        p = self.pc
        return self.cp((z0, p.y, p.x, p.core), p.down(), KZ, KZ, z0)

    def c_x(self, z0):
        p = self.pc
        return self.cp((z0, p.y, p.x, p.core), p.xn(), KX, KX, z0)

    def c_y(self, z0):
        p = self.pc
        return self.cp((z0, p.y, p.x, p.core), p.yn(), KY, KY, z0)

    def c_d0(self, z0):
        p = self.pc
        return self.cp((z0, p.y, 1 - p.x, p.core, self.h[0]), p.yn(), KD0, KD0, z0)

    def c_d1(self, z0):
        p = self.pc
        return self.cp((z0, 1 - p.y, p.x, p.core, self.h[1]), p.xn(), KD1, KD1, z0)

    def c_s(self, z0):
        p = self.pc
        return self.cp((z0, slice(None), slice(None), p.core), p.sn(), KS, KS, z0)

    def plane_send(self, i):
        z0 = near(self.pc.z, i)
        self.c_x(z0).start()
        self.c_y(z0).start()

    def own_z(self):
        z = self.pc.z

        @pl.when(z < NZ - 1)
        def _():
            self.c_up(z).start()

        @pl.when(z > 0)
        def _():
            self.c_down(z).start()

    def z_event(self, i, plane=True):
        z = self.pc.z
        z0 = near(z, i)

        @pl.when(z0 < z)
        def _():
            self.c_up(z0).wait_recv()

            @pl.when(z < NZ - 1)
            def _():
                self.c_up(z0).start()

        @pl.when(z0 > z)
        def _():
            self.c_down(z0).wait_recv()

            @pl.when(z > 0)
            def _():
                self.c_down(z0).start()

        if plane:
            self.plane_send(i)

    def plane_event(self, i):
        z0 = near(self.pc.z, i)
        self.c_x(z0).wait_recv()
        self.c_d0(z0).start()
        self.c_y(z0).wait_recv()
        self.c_d1(z0).start()

    def core_event(self, i):
        z0 = near(self.pc.z, i)
        self.c_d0(z0).wait_recv()
        self.c_d1(z0).wait_recv()
        self.c_s(z0).start()

    def done_event(self, i):
        self.c_s(near(self.pc.z, i)).wait_recv()

    def finish(self):
        z = self.pc.z
        for z0 in range(NZ):
            for c in (self.c_x, self.c_y, self.c_d0, self.c_d1, self.c_s):
                c(z0).wait_send()

            @pl.when((z < NZ - 1) & (z0 <= z))
            def _():
                self.c_up(z0).wait_send()

            @pl.when((z > 0) & (z0 >= z))
            def _():
                self.c_down(z0).wait_send()


class GatherPlane:
    def __init__(self, pc, buf, send, recv):
        self.pc, self.buf, self.send, self.recv = pc, buf, send, recv
        self.h = halves(buf.shape[-2])

    def cp(self, idx, dev, s, r):
        ref = self.buf.at[idx]
        return remote(ref, ref, dev, self.send.at[s], self.recv.at[r])

    def yx(self, k):
        p = self.pc
        return (p.y if k < 2 else 1 - p.y), (p.x if k % 2 == 0 else 1 - p.x)

    def c_x(self):
        p = self.pc
        return self.cp((p.z, p.y, p.x, p.core), p.xn(), (KX, 0), (KX, 0))

    def c_y(self):
        p = self.pc
        return self.cp((p.z, p.y, p.x, p.core), p.yn(), (KY, 0), (KY, 0))

    def c_d0(self):
        p = self.pc
        return self.cp((p.z, p.y, 1 - p.x, p.core, self.h[0]), p.yn(), (KD0, 0), (KD0, 0))

    def c_d1(self):
        p = self.pc
        return self.cp((p.z, 1 - p.y, p.x, p.core, self.h[1]), p.xn(), (KD1, 0), (KD1, 0))

    def c_up(self, z0, k):
        p = self.pc
        y, x = self.yx(k)
        return self.cp((z0, y, x, p.core), p.up(), (10 + z0, k), (10 + z0, k))

    def c_down(self, z0, k):
        p = self.pc
        y, x = self.yx(k)
        return self.cp((z0, y, x, p.core), p.down(), (14 + z0, k), (10 + z0, k))

    def c_s(self, z0):
        p = self.pc
        return self.cp((z0, slice(None), slice(None), p.core), p.sn(), (KS, z0), (KS, z0))

    def z_send(self, k):
        z = self.pc.z

        @pl.when(z < NZ - 1)
        def _():
            self.c_up(z, k).start()

        @pl.when(z > 0)
        def _():
            self.c_down(z, k).start()

    def own_plane(self):
        self.c_x().start()
        self.c_y().start()

    def own_z(self):
        self.z_send(0)

    def plane_event(self):
        self.c_x().wait_recv()
        self.c_d0().start()
        self.z_send(1)
        self.c_y().wait_recv()
        self.c_d1().start()
        self.z_send(2)

    def diag_event(self):
        self.c_d0().wait_recv()
        self.c_d1().wait_recv()
        self.z_send(3)
        self.c_s(self.pc.z).start()

    def z_event(self, i, k):
        z = self.pc.z
        z0 = near(z, i)

        @pl.when(z0 < z)
        def _():
            self.c_up(z0, k).wait_recv()

            @pl.when(z < NZ - 1)
            def _():
                self.c_up(z0, k).start()

        @pl.when(z0 > z)
        def _():
            self.c_down(z0, k).wait_recv()

            @pl.when(z > 0)
            def _():
                self.c_down(z0, k).start()

    def core_event(self, i):
        self.c_s(near(self.pc.z, i)).start()

    def done_event(self, i):
        self.c_s(near(self.pc.z, i)).wait_recv()

    def finish(self):
        z = self.pc.z
        for c in (self.c_x, self.c_y, self.c_d0, self.c_d1):
            c().wait_send()
        for z0 in range(NZ):
            self.c_s(z0).wait_send()
            for k in range(4):

                @pl.when((z < NZ - 1) & (z0 <= z))
                def _():
                    self.c_up(z0, k).wait_send()

                @pl.when((z > 0) & (z0 >= z))
                def _():
                    self.c_down(z0, k).wait_send()


class GatherSequence:
    def __init__(self, pc, buf, send, recv):
        self.pc, self.buf, self.send, self.recv = pc, buf, send, recv
        rows = buf.shape[-2]
        self.h = (pl.ds(0, 128), pl.ds(128, rows - 128))

    def cp(self, idx, dev, k):
        ref = self.buf.at[idx]
        return remote(ref, ref, dev, self.send.at[k], self.recv.at[k])

    def c_x(self):
        p = self.pc
        return self.cp((p.y, p.x, p.core), p.xn(), 0)

    def c_y(self):
        p = self.pc
        return self.cp((p.y, p.x, p.core), p.yn(), 1)

    def c_d0(self):
        p = self.pc
        return self.cp((p.y, 1 - p.x, p.core, self.h[0]), p.yn(), 2)

    def c_d1(self):
        p = self.pc
        return self.cp((1 - p.y, p.x, p.core, self.h[1]), p.xn(), 3)

    def c_s(self, k):
        p = self.pc
        y, x = (p.y if k < 2 else 1 - p.y), (p.x if k % 2 == 0 else 1 - p.x)
        return self.cp((y, x, p.core), p.sn(), 4 + k)

    def own(self):
        for c in (self.c_x(), self.c_y(), self.c_s(0)):
            c.start()

    def plane_event(self):
        self.c_x().wait_recv()
        self.c_d0().start()
        self.c_s(1).start()
        self.c_y().wait_recv()
        self.c_d1().start()
        self.c_s(2).start()

    def core_event(self):
        self.c_d0().wait_recv()
        self.c_d1().wait_recv()
        self.c_s(3).start()

    def done_event(self):
        for k in range(4):
            self.c_s(k).wait_recv()

    def finish(self):
        for c in (self.c_x(), self.c_y(), self.c_d0(), self.c_d1()):
            c.wait_send()
        for k in range(4):
            self.c_s(k).wait_send()


LOG2E = math.log2(math.e)
VMEM = pltpu.VMEM


def dot(a, b):
    return jnp.dot(a, b, preferred_element_type=f32)


def dot_t(a, b):
    return lax.dot_general(a, b, (((1,), (1,)), ((), ())), preferred_element_type=f32)


def lanes(shape):
    return lax.broadcasted_iota(jnp.int32, shape, 1)


def roll_half(v):
    return pltpu.roll(v, 64, 1)


def swap_rot(v):
    first = lanes(v.shape) % 64 < 32
    return jnp.where(first, pltpu.roll(v, 96, 1), pltpu.roll(v, 32, 1))


def head_sums(v):
    row = lax.broadcasted_iota(jnp.int32, (128, 128), 0) // 64
    col = lax.broadcasted_iota(jnp.int32, (128, 128), 1) // 64
    ones = jnp.where(row == col, 1.0, 0.0).astype(bf16)
    high = v.astype(bf16)
    low = (v - high.astype(f32)).astype(bf16)
    return dot(high, ones) + dot(low, ones)


def twice(gain):
    return jnp.concatenate([gain[...], gain[...]], axis=1)


def cols(i, width):
    return pl.ds(pl.multiple_of(i * width, width), width)


def norm_into(src, gain, dst):
    def body(i, _):
        rows = pl.ds(pl.multiple_of(i * 32, 32), 32)
        v = src[rows, :].astype(f32)
        scale = lax.rsqrt(jnp.mean(v * v, axis=-1, keepdims=True) + EPS)
        dst[rows, :] = (v * scale * gain[...]).astype(dst.dtype)
        return 0

    lax.fori_loop(0, src.shape[0] // 32, body, 0)


def run_steps(order, steps, loops):
    order = list(order)
    while order:
        name = order.pop(0)
        if name not in loops:
            steps[name]()
            continue
        count, body = loops[name]
        ticks, seen = {}, 1
        while seen < count:
            inner = order.pop(0)
            if inner == name:
                seen += 1
            else:
                ticks.setdefault(seen - 1, []).append(inner)

        def tick(i, _, body=body, ticks=ticks):
            body(i)
            for k, inner in ticks.items():

                @pl.when(i == k)
                def _(inner=inner):
                    for step in inner:
                        steps[step]()

            return 0

        lax.fori_loop(0, count, tick, 0)


def line_steps(letter, g):
    part = functools.partial
    steps = {letter + "Z": g.own_z}
    for i in range(NZ):
        steps[f"{letter}p{i}"] = part(g.plane_send, i)
        steps[f"{letter}e{i}"] = part(g.plane_event, i)
        steps[f"{letter}c{i}"] = part(g.core_event, i)
        if i:
            steps[f"{letter}z{i}"] = part(g.z_event, i, False)
    return steps


def turn(src, rows, core, mine, theirs):
    def body(t, _):
        v = jnp.transpose(src[:, cols(t, 128)])
        for k in range(64 // rows):
            a, b = v[2 * k * rows : (2 * k + 1) * rows], v[(2 * k + 1) * rows : (2 * k + 2) * rows]
            own, other = jnp.where(core == 0, a, b), jnp.where(core == 0, b, a)
            spot = t * (64 // rows) + k
            mine[spot, :, pl.ds(0, v.shape[1])] = own
            theirs[spot, pl.ds(0, rows), :] = other
        return 0

    lax.fori_loop(0, src.shape[1] // 128, body, 0)


def forward_kernel(dims, *refs):
    (tok, width, n_dev, heads_w, kv_w, ff) = dims
    (
        x_ref, cot_ref, place_ref, freq_ref, g_attn, one_q, one_k, g_ffn,
        s_qkv, s_out, s_down, s_gu,
        o_y, o_tattn, o_tmix, o_tffn, o_tact, o_cot, o_ggu, o_kv, o_q2, o_linv, o_mixf, o_res,
        o_kk, o_va, o_mask, o_wqkv, o_wout, o_wgu, o_cos, o_sin,
        w_qkv, w_out, w_down, w_gu, kk, va, mask, mask_t, o2, gu, gact,
        y_ref, hattn_ref, qkv_ref, q2_ref, kvb, linv_ref, mixf_ref, mixb_ref, res_ref, hffn_ref,
        act_ref, cot2, ggu2, cos_ref, sin_ref, t_attn, t_mix, t_ffn, t_act, turn_a, turn_b,
        send, recv, kv_send, kv_recv, lsem, osem, ex_send, ex_recv,
    ) = refs
    pc = Place()
    shards = (s_qkv, s_out, s_down, s_gu)
    bufs = (w_qkv, w_out, w_down, w_gu)
    local = [
        pltpu.make_async_copy(s, b.at[pc.z, pc.y, pc.x, pc.core], lsem.at[k])
        for k, (s, b) in enumerate(zip(shards, bufs))
    ]
    for c in local:
        c.start()
    barrier(pc)
    for c in local:
        c.wait()
    qkv = Gather(pc, w_qkv, send.at[0], recv.at[0])
    out = GatherPlane(pc, w_out, send.at[1], recv.at[1])
    down = Gather(pc, w_down, send.at[2], recv.at[2])
    gateup = Gather(pc, w_gu, send.at[3], recv.at[3])
    seq = GatherSequence(pc, kvb, kv_send, kv_recv)
    part = functools.partial
    z = pc.z
    emitted = []

    def emit(src, dst):
        c = pltpu.make_async_copy(src, dst, osem.at[len(emitted)])
        emitted.append(c)
        c.start()

    def exchange(k, src, dst):
        return remote(src, dst, pc.sn(), ex_send.at[k], ex_recv.at[k])

    back = pl.ds(tok, tok)
    sent_cot = exchange(0, cot_ref, cot2.at[back, :])
    sent_attn = exchange(1, turn_a, t_attn.at[:, :, back])
    sent_mix = exchange(2, turn_b.at[:, pl.ds(0, s_out.shape[0]), :], t_mix.at[:, :, back])
    sent_ffn = exchange(3, turn_a, t_ffn.at[:, :, back])
    sent_act = exchange(4, turn_b.at[:, pl.ds(0, s_down.shape[0]), :], t_act.at[:, :, back])
    sent_ggu = exchange(5, ggu2.at[pl.ds(0, tok), :], ggu2.at[back, :])

    g_q, g_k = twice(one_q), twice(one_k)

    def block_row(a):
        return jnp.right_shift(place_ref[:, a * (tok // 2) : (a + 1) * (tok // 2)], 7).astype(f32)

    def tables():
        step = tok // 2
        sign = jnp.where(lanes((step, 128)) % 64 < 32, -1.0, 1.0)
        row = lax.broadcasted_iota(jnp.int32, (step, 128), 0).astype(f32)
        for a in range(2):
            angle = (block_row(a) * 128.0 + row) * freq_ref[...]
            cos_ref[pl.ds(a * step, step), :] = jnp.cos(angle)
            sin_ref[pl.ds(a * step, step), :] = sign * jnp.sin(angle)
        emit(cos_ref, o_cos)
        emit(sin_ref, o_sin)

    def first_norm():
        norm_into(x_ref, g_attn, hattn_ref)

    def first_turn():
        sent_cot.start()
        cot2[pl.ds(0, tok), :] = cot_ref[...]
        turn(hattn_ref, s_qkv.shape[0], pc.core, t_attn, turn_a)
        sent_attn.start()

    def columns_step(g, i, left, right, total, depth):
        g.done_event(i)
        z0 = near(z, i)

        def body(n, _):
            c = cols(n, 256)
            w = right[z0, :, :, :, :, c].reshape(depth, 256)
            prod = dot(left[:, cols(z0, depth)], w)
            if i == 0:
                total[:, c] = prod
            else:
                total[:, c] += prod
            return 0

        lax.fori_loop(0, total.shape[1] // 256, body, 0)

    def grad_act_step(i):
        down.done_event(i)
        z0 = near(z, i)
        depth = ff // NZ
        gact[:, cols(z0, depth)] = dot_t(cot_ref[...], w_down[z0].reshape(depth, width))

    low = lanes((tok, 128)) < 64

    def head_tile(t, gain):
        u = qkv_ref[:, cols(t, 128)]
        n = u * lax.rsqrt(head_sums(u * u) * (1.0 / 64) + EPS) * gain
        return n * cos_ref[...] + swap_rot(n) * sin_ref[...]

    def keys_out():
        for t in range(kv_w // 128):
            kvb[pc.y, pc.x, pc.core, pl.ds(0, tok), pl.ds(t * 128, 128)] = head_tile(
                heads_w // 128 + t, g_k
            ).astype(bf16)
        kvb[pc.y, pc.x, pc.core, pl.ds(0, tok), pl.ds(kv_w, kv_w)] = qkv_ref[
            :, pl.ds(heads_w + kv_w, kv_w)
        ].astype(bf16)
        both_rows = jnp.concatenate([block_row(0), block_row(1)], axis=1)
        blocks_row = jnp.broadcast_to(both_rows, (16, tok)).astype(bf16)
        kvb[pc.y, pc.x, pc.core, pl.ds(tok, 16), pl.ds(0, tok)] = blocks_row
        kvb[pc.y, pc.x, pc.core, pl.ds(tok, 16), pl.ds(tok, tok)] = blocks_row
        seq.own()

    def query_tile(t, _):
        q = (head_tile(t, g_q) * 0.125).astype(bf16)
        zero = jnp.zeros_like(q)
        q2_ref[t, pl.ds(0, tok), :] = jnp.where(low, q, zero)
        q2_ref[t, pl.ds(tok, tok), :] = jnp.where(low, zero, q)
        return 0

    def queries():
        lax.fori_loop(0, heads_w // 128, query_tile, 0)
        emit(qkv_ref, o_kv)
        emit(q2_ref, o_q2)
        emit(w_qkv, o_wqkv)
        sent_cot.wait_recv()
        emit(cot2, o_cot)
        sent_attn.wait_recv()
        emit(t_attn, o_tattn)

    def unpack(b, _):
        y, x, c = b // 4, (b // 2) % 2, b % 2
        rows = pl.ds(pl.multiple_of(b * tok, tok), tok)
        for t in range(kv_w // 128):
            k = kvb[y, x, c, pl.ds(0, tok), pl.ds(t * 128, 128)].astype(f32)
            v = kvb[y, x, c, pl.ds(0, tok), pl.ds(kv_w + t * 128, 128)].astype(f32)
            k_r, v_r = roll_half(k), roll_half(v)
            kk[2 * t, rows, :] = jnp.where(low, k, k_r).astype(bf16)
            kk[2 * t + 1, rows, :] = jnp.where(low, k_r, k).astype(bf16)
            va[2 * t, rows, :] = jnp.where(low, v, 1.0).astype(bf16)
            va[2 * t + 1, rows, :] = jnp.where(low, v_r, 1.0).astype(bf16)
        step = tok // 2
        key_hi = kvb[y, x, c, pl.ds(tok, 16), pl.ds(0, tok)].astype(f32)[:1, :]
        for a in range(2):
            own = block_row(a)
            row = lax.broadcasted_iota(jnp.int32, (step, step), 0).astype(f32)
            col = lanes((step, step)).astype(f32)
            for d in range(2):
                theirs = key_hi[:, d * step : (d + 1) * step]
                gap = (own - theirs) * float(step) + row - col
                place = pl.ds(pl.multiple_of(b * tok + d * step, step), step)
                mask[pl.ds(a * step, step), place] = jnp.where(gap >= 0, 1.0, 0.0).astype(bf16)
                gap = (own - theirs) * float(step) + col - row
                mask_t[place, pl.ds(a * step, step)] = jnp.where(gap >= 0, 1.0, 0.0).astype(bf16)
        return 0

    def unpack_all():
        seq.done_event()
        lax.fori_loop(0, n_dev, unpack, 0)
        emit(kk, o_kk)
        emit(va, o_va)
        emit(mask_t, o_mask)

    chunk = 512
    n_chunk = n_dev * tok // chunk

    def attend(tick):
        t, kc = tick // n_chunk, tick % n_chunk
        g = t // 2
        rows = pl.ds(pl.multiple_of(kc * chunk, chunk), chunk)
        s = dot_t(q2_ref[t], kk[g, rows, :])
        e = jnp.exp2(s * LOG2E).astype(bf16).reshape(2, tok, chunk) * mask[:, rows][None]
        o = dot(e.reshape(2 * tok, chunk), va[g, rows, :])

        @pl.when(kc == 0)
        def _():
            o2[...] = o

        @pl.when(kc > 0)
        def _():
            o2[...] += o

        @pl.when(kc == n_chunk - 1)
        def _():
            even, odd = o2[pl.ds(0, tok), :], o2[pl.ds(tok, tok), :]
            total = jnp.where(low, roll_half(even), odd)
            inv = 1.0 / total
            mixed = jnp.where(low, even, roll_half(odd)) * inv
            linv_ref[:, cols(t, 128)] = inv
            mixf_ref[:, cols(t, 128)] = mixed
            mixb_ref[:, cols(t, 128)] = mixed.astype(bf16)

    def mix_out():
        emit(linv_ref, o_linv)
        emit(mixf_ref, o_mixf)
        turn(mixb_ref, s_out.shape[0], pc.core, t_mix, turn_b)
        sent_mix.start()

    def residual_step(n, _):
        c = cols(n, 256)
        w = w_out[:, :, :, :, :, c].reshape(heads_w, 256)
        res_ref[:, c] = x_ref[:, c].astype(f32) + dot(mixb_ref[...], w)
        return 0

    def residual():
        for i in range(NZ):
            out.done_event(i)
        emit(w_out, o_wout)
        lax.fori_loop(0, width // 256, residual_step, 0)

    def second_norm():
        norm_into(res_ref, g_ffn, hffn_ref)

    def second_turn():
        emit(res_ref, o_res)
        sent_mix.wait_recv()
        emit(t_mix, o_tmix)
        sent_attn.wait_send()
        turn(hffn_ref, s_gu.shape[0], pc.core, t_ffn, turn_a)
        sent_ffn.start()

    def gate_step(n, _):
        c = cols(n, 256)
        c2 = cols(n + ff // 256, 256)
        gate, up, grad = gu[:, c], gu[:, c2], gact[:, c]
        sig = 1.0 / (1.0 + jnp.exp(-gate))
        silu = gate * sig
        act_ref[:, c] = (silu * up).astype(bf16)
        ggu2[pl.ds(0, tok), c] = (grad * up * (sig * (1.0 + gate * (1.0 - sig)))).astype(bf16)
        ggu2[pl.ds(0, tok), c2] = (grad * silu).astype(bf16)
        return 0

    def gates():
        lax.fori_loop(0, ff // 256, gate_step, 0)
        sent_ggu.start()
        emit(w_gu, o_wgu)

    def act_out():
        sent_mix.wait_send()
        turn(act_ref, s_down.shape[0], pc.core, t_act, turn_b)
        sent_act.start()
        sent_ffn.wait_recv()
        emit(t_ffn, o_tffn)

    def output_step(n, _):
        c = cols(n, 256)
        w = w_down[:, :, :, :, :, c].reshape(ff, 256)
        y_ref[:, c] = (res_ref[:, c] + dot(act_ref[...], w)).astype(bf16)
        return 0

    def outputs():
        lax.fori_loop(0, width // 256, output_step, 0)
        emit(y_ref, o_y)
        sent_ggu.wait_recv()
        emit(ggu2, o_ggu)
        sent_act.wait_recv()
        emit(t_act, o_tact)

    steps = {
        "norm": first_norm, "trig": tables, "turn": first_turn, "keys": keys_out, "query": queries,
        "kve": seq.plane_event, "kvc": seq.core_event, "unpack": unpack_all, "mix": mix_out,
        "res": residual, "norm2": second_norm, "turn2": second_turn, "gate": gates,
        "act": act_out, "y": outputs, "oP": out.own_plane, "oZ": out.own_z, "oe": out.plane_event,
        "oD": out.diag_event,
    }
    for letter, g in (("q", qkv), ("d", down), ("g", gateup)):
        steps.update(line_steps(letter, g))
    for i in range(NZ):
        steps[f"qs{i}"] = part(columns_step, qkv, i, hattn_ref, w_qkv, qkv_ref, width // NZ)
        steps[f"gs{i}"] = part(columns_step, gateup, i, hffn_ref, w_gu, gu, width // NZ)
        steps[f"ds{i}"] = part(grad_act_step, i)
        if i:
            steps[f"oc{i}"] = part(out.core_event, i)
            for k in range(4):
                steps[f"oz{i}{k}"] = part(out.z_event, i, k)
    run_steps(FORWARD_ORDER, steps, {"A": (heads_w // 128 * n_chunk, attend)})
    for g in (qkv, out, down, gateup, seq):
        g.finish()
    for c in (sent_cot, sent_ffn, sent_act, sent_ggu):
        c.wait_send()
    for c in emitted:
        c.wait()


def forward(x, cot, places, frequency, g_attn, g_q, g_k, g_ffn, s_qkv, s_out, s_down, s_gu, n_dev):
    tok, width = x.shape
    heads_w, kv_w = HEADS * HEAD_DIM, GROUPS * HEAD_DIM
    ff = s_down.shape[0] * n_dev * NZ
    length = n_dev * tok
    tiles = heads_w // 128
    shape = jax.ShapeDtypeStruct
    seven = [(NZ, 2, 2, 2) + s.shape for s in (s_qkv, s_out, s_down, s_gu)]
    qkv_rows, out_rows, down_rows, gu_rows = [s.shape[0] for s in (s_qkv, s_out, s_down, s_gu)]
    spots = n_dev * NZ // 2
    kv_buf = ((2, 2, 2, tok + 16, 2 * kv_w), bf16)
    turned = [((spots, r, 2 * tok), bf16) for r in (qkv_rows, out_rows, gu_rows, down_rows)]
    keep = [
        ((tok, width), bf16),
        *turned,
        ((2 * tok, width), bf16),
        ((2 * tok, 2 * ff), bf16),
        ((tok, s_qkv.shape[1]), f32),
        ((tiles, 2 * tok, 128), bf16),
        ((tok, heads_w), f32),
        ((tok, heads_w), f32),
        ((tok, width), f32),
        ((GROUPS, length, 128), bf16),
        ((GROUPS, length, 128), bf16),
        ((length, tok), bf16),
        (seven[0], bf16),
        (seven[1], bf16),
        (seven[3], bf16),
        ((tok, 128), f32),
        ((tok, 128), f32),
    ]
    outs = [shape(*k) for k in keep]
    vm = pl.BlockSpec(memory_space=VMEM)
    anyw = pl.BlockSpec(memory_space=pl.ANY)
    dma = pltpu.SemaphoreType.DMA
    flops = 2 * tok * (width * (s_qkv.shape[1] + heads_w + 2 * ff + 2 * ff) + 2 * heads_w * length)
    return pl.pallas_call(
        functools.partial(forward_kernel, (tok, width, n_dev, heads_w, kv_w, ff)),
        out_shape=outs,
        in_specs=[vm] * 8 + [anyw] * 4,
        out_specs=[anyw] * len(outs),
        scratch_shapes=[VMEM(s, bf16) for s in seven]
        + [
            VMEM((GROUPS, length, 128), bf16),
            VMEM((GROUPS, length, 128), bf16),
            VMEM((tok, length), bf16),
            VMEM((length, tok), bf16),
            VMEM((2 * tok, 128), f32),
            VMEM((tok, 2 * ff), f32),
            VMEM((tok, ff), f32),
            VMEM((tok, width), bf16),
            VMEM((tok, width), bf16),
            VMEM((tok, s_qkv.shape[1]), f32),
            VMEM((tiles, 2 * tok, 128), bf16),
            VMEM(*kv_buf),
            VMEM((tok, heads_w), f32),
            VMEM((tok, heads_w), f32),
            VMEM((tok, heads_w), bf16),
            VMEM((tok, width), f32),
            VMEM((tok, width), bf16),
            VMEM((tok, ff), bf16),
            VMEM((2 * tok, width), bf16),
            VMEM((2 * tok, 2 * ff), bf16),
            VMEM((tok, 128), f32),
            VMEM((tok, 128), f32),
            *[VMEM(*t) for t in turned],
            VMEM((spots, qkv_rows, tok), bf16),
            VMEM((spots, out_rows, tok), bf16),
            dma((4, 18, NZ)),
            dma((4, 14, NZ)),
            dma((8,)),
            dma((8,)),
            dma((4,)),
            dma((len(outs),)),
            dma((6,)),
            dma((6,)),
        ],
        compiler_params=pltpu.CompilerParams(
            collective_id=0, has_side_effects=True, vmem_limit_bytes=60 << 20
        ),
        cost_estimate=pl.CostEstimate(flops=flops, bytes_accessed=50 << 20, transcendentals=0),
        name="forward",
    )(x, cot, places, frequency, g_attn, g_q, g_k, g_ffn, s_qkv, s_out, s_down, s_gu)


SD0, SD1, SX0, SX1, SY0, SY1, SA, SB = range(8)


class PlaneSum:
    def plane_setup(self, pc, rd, rx, ry, send, recv):
        self.pc, self.rd, self.rx, self.ry, self.send, self.recv = pc, rd, rx, ry, send, recv

    def cp(self, src, dst, dev, k, s):
        return remote(src, dst, dev, self.send.at[k, s], self.recv.at[k, s])

    def d0(self, s):
        p = self.pc
        return self.cp(self.piece(s, 1 - p.y, 1 - p.x, 0), self.rd.at[s, 0], p.yn(), SD0, s)

    def d1(self, s):
        p = self.pc
        return self.cp(self.piece(s, 1 - p.y, 1 - p.x, 1), self.rd.at[s, 1], p.xn(), SD1, s)

    def x1(self, s):
        p = self.pc
        return self.cp(self.piece(s, p.y, 1 - p.x, 1), self.rx.at[s, 1], p.xn(), SX1, s)

    def y0(self, s):
        p = self.pc
        return self.cp(self.piece(s, 1 - p.y, p.x, 0), self.ry.at[s, 0], p.yn(), SY0, s)

    def x0(self, s):
        return self.cp(self.rd.at[s, 0], self.rx.at[s, 0], self.pc.xn(), SX0, s)

    def y1(self, s):
        return self.cp(self.rd.at[s, 1], self.ry.at[s, 1], self.pc.yn(), SY1, s)

    def plane_far(self, s):
        self.d0(s).start()
        self.d1(s).start()

    def plane_near(self, s):
        self.x1(s).start()
        self.y0(s).start()

    def plane_first(self, s):
        self.plane_far(s)
        self.plane_near(s)

    def plane_second(self, s):
        p = self.pc
        self.d0(s).wait_recv()
        self.rd[s, 0] = self.rd[s, 0] + self.piece(s, p.y, 1 - p.x, 0)[...]
        self.x0(s).start()
        self.d1(s).wait_recv()
        self.rd[s, 1] = self.rd[s, 1] + self.piece(s, 1 - p.y, p.x, 1)[...]
        self.y1(s).start()

    def plane_arrived(self, s):
        for c in (self.x1, self.y0, self.x0, self.y1):
            c(s).wait_recv()

    def plane_total(self, s, k):
        p = self.pc
        own = self.piece(s, p.y, p.x, k)[...].astype(f32)
        return own + self.rx[s, k].astype(f32) + self.ry[s, k].astype(f32)

    def plane_finish(self, s):
        for c in (self.d0, self.d1, self.x1, self.y0, self.x0, self.y1):
            c(s).wait_send()


class Scatter(PlaneSum):
    def __init__(self, pc, part, bufs, out, send, recv):
        rd, rx, ry, self.zz = bufs
        self.plane_setup(pc, rd, rx, ry, send, recv)
        self.part, self.out = part, out
        self.h = halves(part.shape[-2])

    @staticmethod
    def scratch(rows, columns):
        half = VMEM((NZ, 2, rows // 2, columns), bf16)
        return [half, half, half, VMEM((NZ + 1, 2, rows // 2, columns), bf16)]

    def piece(self, s, y, x, k):
        return self.part.at[s, y, x, self.h[k]]

    def down(self, zp):
        return self.cp(self.rx.at[zp], self.zz.at[zp], self.pc.down(), SA, zp)

    def up(self, zp):
        gap = zp - (self.pc.z + 1)
        spot = zp + (1 - (gap + NZ - 1) // NZ) * (NZ - zp)
        return self.cp(self.rx.at[zp], self.zz.at[spot], self.pc.up(), SB, zp)

    def far_event(self, i):
        self.plane_far(far(self.pc.z, i))

    def near_event(self, i):
        self.plane_near(far(self.pc.z, i))

    def d_event(self, i):
        self.plane_second(far(self.pc.z, i))

    def xy_event(self, i):
        zp = far(self.pc.z, i)
        self.plane_arrived(zp)
        for k in range(2):
            self.rx[zp, k] = self.plane_total(zp, k).astype(bf16)

    def z_event(self, i):
        z = self.pc.z
        zp = far(z, i)

        @pl.when(zp < z)
        def _():
            @pl.when(z < NZ - 1)
            def _():
                self.down(zp).wait_recv()
                self.rx[zp] = self.rx[zp] + self.zz[zp]

            self.down(zp).start()

        @pl.when(zp > z)
        def _():
            @pl.when(z > 0)
            def _():
                self.up(zp).wait_recv()
                self.rx[zp] = self.rx[zp] + self.zz[zp]

            self.up(zp).start()

    def final(self):
        z = self.pc.z
        self.plane_arrived(z)
        for k in range(2):
            self.out[self.h[k], :] = self.plane_total(z, k)

        @pl.when(z < NZ - 1)
        def _():
            self.down(z).wait_recv()
            for k in range(2):
                self.out[self.h[k], :] += self.zz[z, k].astype(f32)

        @pl.when(z > 0)
        def _():
            self.up(z).wait_recv()
            for k in range(2):
                self.out[self.h[k], :] += self.zz[NZ, k].astype(f32)

    def finish(self):
        z = self.pc.z
        for zp in range(NZ):
            self.plane_finish(zp)

            @pl.when(zp < z)
            def _():
                self.down(zp).wait_send()

            @pl.when(zp > z)
            def _():
                self.up(zp).wait_send()


class ScatterZ(PlaneSum):
    def __init__(self, pc, part, bufs, out, send, recv):
        rd, rx, ry, self.zz, self.sm = bufs
        self.plane_setup(pc, rd, rx, ry, send, recv)
        self.part, self.out = part, out
        self.h = halves(part.shape[-2])

    @staticmethod
    def scratch(rows, columns):
        half = VMEM((1, 2, rows // 2, columns), bf16)
        return [half, half, half, VMEM((NZ + 1, 4, rows, columns), bf16), VMEM((4, rows, columns), bf16)]

    def piece(self, s, y, x, k):
        return self.sm.at[y * 2 + x, self.h[k]]

    def down(self, zp, k, src):
        return self.cp(src, self.zz.at[zp, k], self.pc.down(), 8 + zp, k)

    def up(self, zp, k, src):
        gap = zp - (self.pc.z + 1)
        spot = zp + (1 - (gap + NZ - 1) // NZ) * (NZ - zp)
        return self.cp(src, self.zz.at[spot, k], self.pc.up(), 12 + zp, k)

    def first(self, i):
        z = self.pc.z
        zp = far(z, i)
        for k in range(4):
            src = self.part.at[zp, k // 2, k % 2]

            @pl.when((z == NZ - 1) & (zp < z))
            def _():
                self.down(zp, k, src).start()

            @pl.when((z == 0) & (zp > z))
            def _():
                self.up(zp, k, src).start()

    def z_event(self, i, k):
        z = self.pc.z
        zp = far(z, i)
        held = self.zz.at[zp, k]

        @pl.when((zp < z) & (z < NZ - 1))
        def _():
            self.down(zp, k, held).wait_recv()
            self.zz[zp, k] = self.zz[zp, k] + self.part[zp, k // 2, k % 2]
            self.down(zp, k, held).start()

        @pl.when((zp > z) & (z > 0))
        def _():
            self.up(zp, k, held).wait_recv()
            self.zz[zp, k] = self.zz[zp, k] + self.part[zp, k // 2, k % 2]
            self.up(zp, k, held).start()

    def own_event(self, k):
        z = self.pc.z

        @pl.when(z < NZ - 1)
        def _():
            self.down(z, k, self.zz.at[z, k]).wait_recv()

        @pl.when(z > 0)
        def _():
            self.up(z, k, self.zz.at[z, k]).wait_recv()

        own = self.part[z, k // 2, k % 2].astype(f32)

        @pl.when(z == 0)
        def _():
            self.sm[k] = (own + self.zz[z, k].astype(f32)).astype(bf16)

        @pl.when(z == NZ - 1)
        def _():
            self.sm[k] = (own + self.zz[NZ, k].astype(f32)).astype(bf16)

        @pl.when((z > 0) & (z < NZ - 1))
        def _():
            both = self.zz[z, k].astype(f32) + self.zz[NZ, k].astype(f32)
            self.sm[k] = (own + both).astype(bf16)

    def plane_send(self):
        self.plane_first(0)

    def plane_event(self):
        self.plane_second(0)

    def final(self):
        self.plane_arrived(0)
        for k in range(2):
            self.out[self.h[k], :] = self.plane_total(0, k)

    def finish(self):
        z = self.pc.z
        self.plane_finish(0)
        for zp in range(NZ):
            for k in range(4):

                @pl.when(zp < z)
                def _():
                    self.down(zp, k, self.zz.at[zp, k]).wait_send()

                @pl.when(zp > z)
                def _():
                    self.up(zp, k, self.zz.at[zp, k]).wait_send()


class SequenceSum(PlaneSum):
    def __init__(self, pc, terms, bufs, send, recv, core_send, core_recv):
        rd, rx, ry, self.theirs = bufs
        self.plane_setup(pc, rd, rx, ry, send, recv)
        self.terms, self.core_send, self.core_recv = terms, core_send, core_recv
        self.h = halves(terms.shape[-2])

    @staticmethod
    def scratch(rows, columns):
        half = VMEM((1, 2, rows // 2, columns), bf16)
        return [half, half, half, VMEM((2, 2, rows, columns), bf16)]

    def piece(self, s, y, x, k):
        return self.theirs.at[y, x, self.h[k]]

    def swap(self):
        p = self.pc
        return remote(
            self.terms.at[:, :, 1 - p.core], self.theirs, p.sn(), self.core_send, self.core_recv
        )

    def core_event(self):
        p = self.pc
        self.swap().wait_recv()
        for y in range(2):
            for x in range(2):
                self.theirs[y, x] = self.theirs[y, x] + self.terms[y, x, p.core]
        self.plane_first(0)

    def finish(self):
        self.swap().wait_send()
        self.plane_finish(0)


def norm_back(src, gain, grad, part_ref, part_row, emit):
    part_ref[pl.ds(part_row, 1), :] = jnp.zeros((1, part_ref.shape[1]), f32)

    def body(i, _):
        rows = pl.ds(pl.multiple_of(i * 32, 32), 32)
        v, g = src[rows, :].astype(f32), grad[rows, :]
        inv = lax.rsqrt(jnp.mean(v * v, axis=-1, keepdims=True) + EPS)
        unit = v * inv
        part_ref[pl.ds(part_row, 1), :] += jnp.sum(g * unit, axis=0, keepdims=True)
        gg = g * gain[...]
        emit(rows, inv * (gg - unit * jnp.mean(gg * unit, axis=-1, keepdims=True)))
        return 0

    lax.fori_loop(0, grad.shape[0] // 32, body, 0)


def sum_steps(letter, g):
    part = functools.partial
    steps = {letter + "f": g.final}
    for i in range(NZ):
        steps[f"{letter}a{i}"] = part(g.far_event, i)
        steps[f"{letter}b{i}"] = part(g.near_event, i)
        steps[f"{letter}d{i}"] = part(g.d_event, i)
        if i < NZ - 1:
            steps[f"{letter}x{i}"] = part(g.xy_event, i)
            steps[f"{letter}z{i}"] = part(g.z_event, i)
    return steps


def weight_grad(left, zp, right, part):
    rows, columns = part.shape[-2:]
    lhs = left[pl.ds(zp * 4, 4)].reshape(4 * rows, left.shape[-1])
    step = 512

    def body(n, _):
        c = cols(n, step)
        part[zp, :, :, :, c] = dot(lhs, right[:, c]).astype(bf16).reshape(2, 2, rows, step)
        return 0

    lax.fori_loop(0, columns // step, body, 0)


LOADS = [
    "act", "cot", "ffn", "ggu", "wgu", "res", "mix", "mixf", "linv", "q2", "kk", "va", "mask",
    "qkv", "wout", "attn", "wqkv", "x",
]


def backward_kernel(dims, *refs):
    (tok, width, n_dev, heads_w, kv_w, ff) = dims
    (
        cos_ref, sin_ref, g_attn, one_q, one_k, g_ffn,
        i_x, i_tattn, i_tmix, i_tffn, i_tact, i_cot, i_ggu, i_qkv, i_q2, i_linv, i_mixf, i_res,
        i_kk, i_va, i_mask, i_wqkv, i_wout, i_wgu,
        o_dx, o_attn, o_q, o_k, o_ffn, out_wqkv, out_wout, out_wgu, out_wdown,
        t_ffn, t_act, cot2, ggu2, qkv, q2, linv, mixf, kk, va, mask_t, w_gu,
        part_qkv, part_out, part_gu, part_down, res, gains, came, gh, gattn2, acc_q,
        aug, gm, terms,
        send, recv, kv_send, kv_recv, ex_send, ex_recv, g_send, g_recv, lsem,
    ) = refs[:67]
    bufs = refs[67:]
    g_q, g_k = twice(one_q), twice(one_k)
    pc = Place()
    z = pc.z
    part = functools.partial
    loads = {}

    def load(name, src, dst):
        def copy():
            return pltpu.make_async_copy(src(), dst(), lsem.at[LOADS.index(name)])

        loads[name] = lambda: copy().wait()
        copy().start()

    load("act", lambda: i_tact, lambda: t_act)
    load("cot", lambda: i_cot, lambda: cot2)
    load("ffn", lambda: i_tffn, lambda: t_ffn)
    load("ggu", lambda: i_ggu, lambda: ggu2)
    load("wgu", lambda: i_wgu, lambda: w_gu)
    load("res", lambda: i_res, lambda: res)
    load("mixf", lambda: i_mixf, lambda: mixf)
    load("linv", lambda: i_linv, lambda: linv)
    load("q2", lambda: i_q2, lambda: q2)
    load("kk", lambda: i_kk, lambda: kk)
    load("va", lambda: i_va, lambda: va)
    load("mask", lambda: i_mask, lambda: mask_t)
    load("qkv", lambda: i_qkv, lambda: qkv)
    bar = pltpu.get_barrier_semaphore()
    for device in (pc.xn(), pc.yn(), pc.sn()):
        pl.semaphore_signal(bar, inc=1, device_id=device, device_id_type=MESH)
    for k in range(1, NZ):
        there = pc.at(z=(z + k) % NZ)
        pl.semaphore_signal(bar, inc=1, device_id=there, device_id_type=MESH)
    pl.semaphore_wait(bar, 3 + NZ - 1)
    down = Scatter(pc, part_down, bufs[0:4], out_wdown, send.at[0], recv.at[0])
    gateup = Scatter(pc, part_gu, bufs[4:8], out_wgu, send.at[1], recv.at[1])
    out = ScatterZ(pc, part_out, bufs[8:13], out_wout, send.at[2], recv.at[2])
    last = Scatter(pc, part_qkv, bufs[17:21], out_wqkv, send.at[3], recv.at[3])
    seq = SequenceSum(pc, terms, bufs[13:17], kv_send, kv_recv, ex_send.at[2], ex_recv.at[2])

    own = pl.ds(0, tok)
    back = pl.ds(tok, tok)

    def rows_of(left, right, term, names, i):
        for name in names:
            if name in loads:
                loads.pop(name)()
        weight_grad(left, far(z, i), right, term)

    def h_step(n):
        w = w_gu[n // 2, n % 2].reshape(width // 8, 2 * ff)
        gh[:, cols(n, width // 8)] = dot_t(ggu2[own, :], w)

    def start_h():
        loads.pop("wgu")()
        loads.pop("res")()

    def keep_residual(rows, grad):
        total = cot2[rows, :].astype(f32) + grad
        res[rows, :] = total
        gattn2[rows, :] = total.astype(bf16)

    sent_attn = remote(gattn2.at[own, :], gattn2.at[back, :], pc.sn(), ex_send.at[0], ex_recv.at[0])

    def residual_back():
        load("wout", lambda: i_wout, lambda: w_gu.at[:, :, :, :, pl.ds(0, part_out.shape[-2]), :])
        gains[...] = jnp.zeros_like(gains)
        norm_back(res, g_ffn, gh, gains, 1, keep_residual)
        sent_attn.start()
        loads.pop("wout")()

    columns = part_qkv.shape[-1]
    some = pl.ds(0, columns)

    def load_mix():
        load("mix", lambda: i_tmix, lambda: t_act)

    def load_last():
        load("attn", lambda: i_tattn, lambda: t_ffn)
        load("wqkv", lambda: i_wqkv, lambda: w_gu.at[:, :, :, :, :, some])
        load("x", lambda: i_x, lambda: cot2.at[own, :])

    def m_step(n, _):
        w = w_gu[n, :, :, :, pl.ds(0, part_out.shape[-2]), :].reshape(heads_w // NZ, width)
        gm[:, cols(n, heads_w // NZ)] = dot_t(gattn2[own, :], w).astype(bf16)
        return 0

    def mixed_back():
        lax.fori_loop(0, NZ, m_step, 0)
        sent_attn.wait()

    def start_attention():
        for name in ("mixf", "linv", "q2", "kk", "va", "mask", "qkv"):
            loads.pop(name)()

    low = lanes((tok, 128)) < 64
    chunk = 512
    n_chunk = n_dev * tok // chunk
    def attend(tick):
        g, kc = tick // n_chunk, tick % n_chunk
        rows = pl.ds(pl.multiple_of(kc * chunk, chunk), chunk)

        @pl.when(kc == 0)
        def _():
            lane = lanes((tok, 128))
            for k in range(2):
                c = cols(2 * g + k, 128)
                grad = gm[:, c].astype(f32)
                delta = head_sums(grad * mixf[:, c]) * linv[:, c]
                grad = grad * linv[:, c]
                for half in range(2):
                    d = roll_half(delta) if half == 0 else delta
                    v = grad if half == 0 else roll_half(grad)
                    high = d.astype(bf16).astype(f32)
                    rest = jnp.where(lane == 64, -high, jnp.where(lane == 65, high - d, 0.0))
                    aug[pl.ds((2 * k + half) * tok, tok), :] = jnp.where(low, v, rest).astype(bf16)

        q = q2[pl.ds(2 * g, 2)].reshape(4 * tok, 128)
        seen = mask_t[rows, :]
        e = jnp.exp2(dot_t(kk[g, rows, :], q) * LOG2E).astype(bf16)
        e = e * jnp.concatenate([seen] * 4, axis=1)
        ds = e * dot_t(va[g, rows, :], aug[...]).astype(bf16)
        dv = dot(e, aug[...])
        dk = dot(ds, q)
        dq = lax.dot_general(kk[g, rows, :], ds, (((0,), (0,)), ((), ())), preferred_element_type=f32)
        dk = dk + roll_half(dk)
        lower = lanes((chunk, 128)) < 64
        dv = jnp.where(lower, dv, roll_half(dv))
        mine = (lanes((chunk, 128)) // 64) == (g % 2)
        for b in range(chunk // tok):
            spot = kc * (chunk // tok) + b
            y, x, c = spot // 4, (spot // 2) % 2, spot % 2
            cut = slice(b * tok, (b + 1) * tok)
            for base, value in ((0, dk), (kv_w, dv)):
                place = pl.ds(pl.multiple_of(base + (g // 2) * 128, 128), 128)
                old = terms[y, x, c, :, place].astype(f32)
                terms[y, x, c, :, place] = jnp.where(mine[cut], value[cut], old).astype(bf16)

        @pl.when(kc == 0)
        def _():
            acc_q[...] = dq

        @pl.when(kc > 0)
        def _():
            acc_q[...] += dq

        @pl.when(kc == n_chunk - 1)
        def _():
            turned = jnp.transpose(acc_q[...])
            for k in range(2):
                even, odd = [turned[(2 * k + h) * tok : (2 * k + h + 1) * tok] for h in range(2)]
                gh[:, cols(2 * g + k, 128)] = jnp.where(low, even, odd) * 0.125

    def head_back(t, grad, gain, row):
        c = cols(t, 128)
        u = qkv[:, c]
        inv = lax.rsqrt(head_sums(u * u) * (1.0 / 64) + EPS)
        unit = u * inv
        grad = grad * cos_ref[...] - swap_rot(grad) * sin_ref[...]
        gains[pl.ds(row, 1), pl.ds(0, 128)] += jnp.sum(grad * unit, axis=0, keepdims=True)
        gg = grad * gain
        gattn2[own, c] = (inv * (gg - unit * head_sums(gg * unit) * (1.0 / 64))).astype(bf16)

    def query_back(t):
        head_back(t, gh[:, cols(t, 128)], g_q, 2)

    sent_qkv = remote(gattn2.at[own, some], gattn2.at[back, some], pc.sn(), ex_send.at[1], ex_recv.at[1])

    def keys_back():
        seq.plane_arrived(0)
        for k in range(2):
            gh[seq.h[k], pl.ds(0, 2 * kv_w)] = seq.plane_total(0, k)
        for t in range(kv_w // 128):
            head_back(heads_w // 128 + t, gh[:, pl.ds(t * 128, 128)], g_k, 3)
        gattn2[own, pl.ds(heads_w + kv_w, kv_w)] = gh[:, pl.ds(kv_w, kv_w)].astype(bf16)
        sent_qkv.start()

    def g_step(n):
        w = w_gu[n // 2, n % 2, :, :, :, some].reshape(width // 8, columns)
        gh[:, cols(n, width // 8)] = dot_t(gattn2[own, some], w)

    def keep_input(rows, grad):
        cot2[pl.ds(rows.start + tok, rows.size), :] = (res[rows, :] + grad).astype(bf16)

    sent_dx = pltpu.make_async_copy(cot2.at[back, :], o_dx, lsem.at[len(LOADS)])

    def input_back():
        loads.pop("x")()
        norm_back(cot2, g_attn, gh, gains, 0, keep_input)
        sent_dx.start()

    def start_g():
        loads.pop("wqkv")()

    def hop(k):
        device = (pc.sn(), pc.xn(), pc.yn())[k]
        return remote(gains, came.at[k], device, g_send.at[k], g_recv.at[k])

    def hop_end(k):
        hop(k).wait()
        gains[...] += came[k]

    def ring(k):
        there = pc.at(z=(z + k) % NZ)
        return remote(gains, came.at[3 + z], there, g_send.at[2 + k], g_recv.at[3 + z])

    def ring_start():
        came[3 + z] = gains[...]
        for k in range(1, NZ):
            ring(k).start()

    def ring_end():
        for k in range(1, NZ):
            there = (z + k) % NZ
            slot = came.at[3 + there]
            remote(gains, slot, pc.at(z=there), g_send.at[2 + k], g_recv.at[3 + there]).wait_recv()
        total = came[3]
        for k in range(1, NZ):
            total = total + came[3 + k]
        o_attn[...] = total[0:1]
        o_ffn[...] = total[1:2]
        for o, row in ((o_q, 2), (o_k, 3)):
            v = total[:, :128]
            o[...] = (v + roll_half(v))[row : row + 1, :64]

    steps = {
        "h": start_h, "nb": residual_back, "m": mixed_back, "att": start_attention,
        "kvs": seq.swap().start, "kvc": seq.core_event, "kve": part(seq.plane_second, 0),
        "kvf": keys_back, "oS": out.plane_send, "oe": out.plane_event, "of": out.final,
        "lm": load_mix, "ll": load_last, "qe": sent_qkv.wait_recv, "g": start_g,
        "nb2": input_back, "rs": ring_start, "re": ring_end,
    }
    steps.update(sum_steps("q", last))
    steps.update(sum_steps("d", down))
    steps.update(sum_steps("g", gateup))
    for i in range(NZ):
        steps[f"dw{i}"] = part(rows_of, t_act, cot2, part_down, ("act", "cot"), i)
        steps[f"gw{i}"] = part(rows_of, t_ffn, ggu2, part_gu, ("ffn", "ggu"), i)
        steps[f"ow{i}"] = part(rows_of, t_act, gattn2, part_out, ("mix",), i)
        steps[f"qw{i}"] = part(rows_of, t_ffn, gattn2, part_qkv, ("attn",), i)
        steps[f"oa{i}"] = part(out.first, i)
        steps[f"oo{i}"] = part(out.own_event, i)
        if i < NZ - 1:
            for k in range(4):
                steps[f"oz{i}{k}"] = part(out.z_event, i, k)
            steps[f"hs{i}"] = hop(i).start
            steps[f"he{i}"] = part(hop_end, i)
    loops = {
        "H": (8, h_step),
        "B": (GROUPS * n_chunk, attend),
        "Q": (heads_w // 128, query_back),
        "G": (8, g_step),
    }
    run_steps(BACKWARD_ORDER, steps, loops)
    for g in (down, gateup, out, seq, last):
        g.finish()
    sent_qkv.wait_send()
    for k in range(1, NZ):
        ring(k).wait_send()
    sent_dx.wait()


def backward(x, g_attn, g_q, g_k, g_ffn, kept, rows, n_dev):
    (t_attn, t_mix, t_ffn, t_act, cot2, ggu2, qkv, q2, linv, mixf, res, kk, va, mask_t, w_qkv, w_out, w_gu, cosine, sine) = kept
    tok, width = x.shape
    heads_w, kv_w = HEADS * HEAD_DIM, GROUPS * HEAD_DIM
    ff = ggu2.shape[1] // 2
    length = n_dev * tok
    columns = qkv.shape[1]
    dims = (tok, width, n_dev, heads_w, kv_w, ff)
    shape = jax.ShapeDtypeStruct
    vm = pl.BlockSpec(memory_space=VMEM)
    anyw = pl.BlockSpec(memory_space=pl.ANY)
    dma = pltpu.SemaphoreType.DMA
    r_qkv, r_out, r_gu, r_down = rows
    partial = [
        VMEM((NZ, 2, 2, r, c), bf16)
        for r, c in ((r_qkv, columns), (r_out, width), (r_gu, width), (r_down, width))
    ]
    like = [
        VMEM(v.shape, v.dtype)
        for v in (t_ffn, t_act, cot2, ggu2, qkv, q2, linv, mixf, kk, va, mask_t, w_gu)
    ]
    return pl.pallas_call(
        functools.partial(backward_kernel, dims),
        out_shape=[
            shape((tok, width), bf16),
            shape((1, width), f32),
            shape((1, 64), f32),
            shape((1, 64), f32),
            shape((1, width), f32),
            shape((r_qkv, columns), f32),
            shape((r_out, width), f32),
            shape((r_gu, width), f32),
            shape((r_down, width), f32),
        ],
        in_specs=[vm] * 6 + [anyw] * 18,
        out_specs=[anyw] + [vm] * 8,
        scratch_shapes=like
        + partial
        + [
            VMEM((tok, width), f32),
            VMEM((8, width), f32),
            VMEM((3 + NZ, 8, width), f32),
            VMEM((tok, width), f32),
            VMEM((2 * tok, width), bf16),
            VMEM((128, 4 * tok), f32),
            VMEM((4 * tok, 128), bf16),
            VMEM((tok, heads_w), bf16),
            VMEM((2, 2, 2, tok, 2 * kv_w), bf16),
            dma((4, 16, NZ)),
            dma((4, 16, NZ)),
            dma((8, 1)),
            dma((8, 1)),
            dma((3,)),
            dma((3,)),
            dma((3 + NZ,)),
            dma((3 + NZ,)),
            dma((len(LOADS) + 1,)),
        ]
        + Scatter.scratch(r_down, width)
        + Scatter.scratch(r_gu, width)
        + ScatterZ.scratch(r_out, width)
        + SequenceSum.scratch(tok, 2 * kv_w)
        + Scatter.scratch(r_qkv, columns),
        compiler_params=pltpu.CompilerParams(
            collective_id=1, has_side_effects=True, vmem_limit_bytes=64 << 20
        ),
        cost_estimate=pl.CostEstimate(
            flops=20 * tok * width * width, bytes_accessed=60 << 20, transcendentals=0
        ),
        name="backward",
    )(
        cosine, sine, g_attn, g_q, g_k, g_ffn, x, t_attn, t_mix, t_ffn, t_act, cot2, ggu2, qkv, q2,
        linv, mixf, res, kk, va, mask_t, w_qkv, w_out, w_gu,
    )


def settle_kernel(count, *refs):
    copies = [
        pltpu.make_async_copy(a, b, refs[-1].at[k])
        for k, (a, b) in enumerate(zip(refs[:count], refs[count : 2 * count]))
    ]
    for c in copies:
        c.start()
    for c in copies:
        c.wait()


def settle(arrays):
    count = len(arrays)
    anyw = pl.BlockSpec(memory_space=pl.ANY)
    return pl.pallas_call(
        functools.partial(settle_kernel, count),
        out_shape=[jax.ShapeDtypeStruct(a.shape, a.dtype) for a in arrays],
        in_specs=[pl.BlockSpec(memory_space=VMEM)] * count,
        out_specs=[anyw] * count,
        scratch_shapes=[pltpu.SemaphoreType.DMA((count,))],
        name="settle",
    )(*arrays)


epsilon = 1e-06


def norm_rows(values, gain_vec):
    return (
        values * lax.rsqrt(jnp.mean(values * values, axis=-1, keepdims=True) + epsilon) * gain_vec
    )


def rotate(values, positions):
    half_dim = values.shape[-1] // 2
    frequency = jnp.exp(
        jnp.arange(half_dim).astype(jnp.float32) * (-2.0 * math.log(10000.0) / values.shape[-1])
    )
    angles = positions.astype(jnp.float32)[:, None] * frequency[None, :]
    cosine = jnp.cos(angles)[:, None, :]
    sine = jnp.sin(angles)[:, None, :]
    first = values[..., :half_dim]
    second = values[..., half_dim:]
    return jnp.concatenate(
        [first * cosine - second * sine, second * cosine + first * sine], axis=-1
    )


def project_heads(qkv_all, positions, q_gain, k_gain):
    tok_rows = qkv_all.shape[0]
    q_cols = HEADS * HEAD_DIM
    k_cols = GROUPS * HEAD_DIM
    queries = qkv_all[:, :q_cols].reshape(tok_rows, HEADS, HEAD_DIM)
    keys_raw = qkv_all[:, q_cols : q_cols + k_cols].reshape(tok_rows, GROUPS, HEAD_DIM)
    values = qkv_all[:, q_cols + k_cols :].reshape(tok_rows, GROUPS, HEAD_DIM)
    return (
        rotate(norm_rows(queries, q_gain), positions),
        rotate(norm_rows(keys_raw, k_gain), positions),
        values,
    )


def gated(gate_up):
    return jax.nn.silu(gate_up[:, :FF]) * gate_up[:, FF:]


def per_device_plain(
    inputs, places, cotangent, attn_gain, w_qkv, q_gain, k_gain, w_out, ffn_gain, w_gateup, w_down
):
    tok_rows = inputs.shape[1]
    repeat = HEADS // GROUPS
    score_scale = HEAD_DIM ** (-0.5)
    here_f = inputs[0].astype(jnp.float32)
    own_places = places[0]
    qkv_w, out_w = (
        lax.all_gather(w_qkv, ("dp", "ctx"), axis=0, tiled=True),
        lax.all_gather(w_out, ("dp", "ctx"), axis=0, tiled=True),
    )
    h_attn_f, pull_attn = jax.vjp(norm_rows, here_f, attn_gain)
    h_attn = h_attn_f.astype(jnp.bfloat16)
    qkv_all = jnp.dot(h_attn, qkv_w, preferred_element_type=jnp.float32)

    def heads_of(qkv_in, gain_q, gain_k):
        return project_heads(qkv_in, own_places, gain_q, gain_k)

    (queries, keys_f, values), pull_heads = jax.vjp(heads_of, qkv_all, q_gain, k_gain)
    query_b = queries.astype(jnp.bfloat16).reshape(tok_rows, GROUPS, repeat, HEAD_DIM)
    key_b = keys_f.astype(jnp.bfloat16)
    value_b = values.astype(jnp.bfloat16)
    all_keys, all_values = (
        lax.all_gather(key_b, "ctx", axis=0, tiled=True),
        lax.all_gather(value_b, "ctx", axis=0, tiled=True),
    )
    all_places = lax.all_gather(own_places, "ctx", axis=0, tiled=True)
    blocks = lax.axis_size("ctx")
    key_blocks = all_keys.reshape(blocks, tok_rows, GROUPS, HEAD_DIM)
    value_blocks = all_values.reshape(blocks, tok_rows, GROUPS, HEAD_DIM)
    place_blocks = all_places.reshape(blocks, tok_rows)

    def score_block(key_blk, place_blk):
        scores = (
            jnp.einsum("igrd,jgd->grij", query_b, key_blk, preferred_element_type=jnp.float32)
            * score_scale
        )
        allowed = place_blk[None, :] <= own_places[:, None]
        return (scores, allowed)

    def max_step(state_pair, entries):
        row_top, row_total = state_pair
        scores, allowed = score_block(entries[0], entries[1])
        scores = jnp.where(allowed, scores, -1e30)
        new_top = jnp.maximum(row_top, jnp.max(scores, axis=-1))
        row_total = row_total * jnp.exp(row_top - new_top) + jnp.sum(
            jnp.where(allowed, jnp.exp(scores - new_top[..., None]), 0.0), axis=-1
        )
        return ((new_top, row_total), None)

    start_pair = (
        jnp.full((GROUPS, repeat, tok_rows), -1e30, jnp.float32),
        jnp.zeros((GROUPS, repeat, tok_rows), jnp.float32),
    )
    (row_top, row_total), _ = lax.scan(max_step, start_pair, (key_blocks, place_blocks))
    log_total = row_top + jnp.log(row_total)

    def out_step(accum, entries):
        scores, allowed = score_block(entries[0], entries[1])
        weights_b = jnp.where(allowed, jnp.exp(scores - log_total[..., None]), 0.0).astype(
            jnp.bfloat16
        )
        return (
            accum
            + jnp.einsum(
                "grij,jgd->igrd", weights_b, entries[2], preferred_element_type=jnp.float32
            ),
            None,
        )

    mixed_f, _ = lax.scan(
        out_step,
        jnp.zeros((tok_rows, GROUPS, repeat, HEAD_DIM), jnp.float32),
        (key_blocks, place_blocks, value_blocks),
    )
    mixed_b = mixed_f.reshape(tok_rows, HEADS * HEAD_DIM).astype(jnp.bfloat16)
    attn_out = jnp.dot(mixed_b, out_w, preferred_element_type=jnp.float32)
    residual = here_f + attn_out
    gateup_w, down_w = (
        lax.all_gather(w_gateup, ("dp", "ctx"), axis=0, tiled=True),
        lax.all_gather(w_down, ("dp", "ctx"), axis=0, tiled=True),
    )
    h_ffn_f, pull_ffn = jax.vjp(norm_rows, residual, ffn_gain)
    h_ffn = h_ffn_f.astype(jnp.bfloat16)
    gate_up = jnp.dot(h_ffn, gateup_w, preferred_element_type=jnp.float32)
    act_f, pull_gate = jax.vjp(gated, gate_up)
    act_b = act_f.astype(jnp.bfloat16)
    result = residual + jnp.dot(act_b, down_w, preferred_element_type=jnp.float32)
    layer_output = result.astype(jnp.bfloat16)[None]
    gateup_w, down_w = (
        lax.all_gather(w_gateup, ("dp", "ctx"), axis=0, tiled=True),
        lax.all_gather(w_down, ("dp", "ctx"), axis=0, tiled=True),
    )
    grad_out = cotangent[0]
    grad_act = jnp.dot(grad_out, down_w.T, preferred_element_type=jnp.float32)
    grad_down = jnp.dot(act_b.T, grad_out, preferred_element_type=jnp.float32)
    grad_gu_b = pull_gate(grad_act)[0].astype(jnp.bfloat16)
    grad_gateup = jnp.dot(h_ffn.T, grad_gu_b, preferred_element_type=jnp.float32)
    grad_h_ffn = jnp.dot(grad_gu_b, gateup_w.T, preferred_element_type=jnp.float32)
    grad_resid_part, grad_ffn_gain = pull_ffn(grad_h_ffn)
    grad_residual = grad_out.astype(jnp.float32) + grad_resid_part
    grad_gateup_own, grad_down_own = (
        lax.psum_scatter(grad_gateup, ("dp", "ctx"), scatter_dimension=0, tiled=True),
        lax.psum_scatter(grad_down, ("dp", "ctx"), scatter_dimension=0, tiled=True),
    )
    qkv_w, out_w = (
        lax.all_gather(w_qkv, ("dp", "ctx"), axis=0, tiled=True),
        lax.all_gather(w_out, ("dp", "ctx"), axis=0, tiled=True),
    )
    grad_attn_b = grad_residual.astype(jnp.bfloat16)
    grad_out_w = jnp.dot(mixed_b.T, grad_attn_b, preferred_element_type=jnp.float32)
    grad_mixed_b = (
        jnp.dot(grad_attn_b, out_w.T, preferred_element_type=jnp.float32)
        .astype(jnp.bfloat16)
        .reshape(tok_rows, GROUPS, repeat, HEAD_DIM)
    )
    row_delta = jnp.transpose(
        jnp.sum(grad_mixed_b.astype(jnp.float32) * mixed_f, axis=-1), (1, 2, 0)
    )

    def back_step(grad_query, entries):
        key_blk, place_blk, value_blk = entries
        scores, allowed = score_block(key_blk, place_blk)
        weights_f = jnp.where(allowed, jnp.exp(scores - log_total[..., None]), 0.0)
        weights_b = weights_f.astype(jnp.bfloat16)
        grad_value = jnp.einsum(
            "grij,igrd->jgd", weights_b, grad_mixed_b, preferred_element_type=jnp.float32
        )
        grad_prob = jnp.einsum(
            "igrd,jgd->grij", grad_mixed_b, value_blk, preferred_element_type=jnp.float32
        )
        grad_score = (weights_f * (grad_prob - row_delta[..., None])).astype(jnp.bfloat16)
        grad_query = grad_query + jnp.einsum(
            "grij,jgd->igrd", grad_score, key_blk, preferred_element_type=jnp.float32
        )
        grad_key = (
            jnp.einsum("grij,igrd->jgd", grad_score, query_b, preferred_element_type=jnp.float32)
            * score_scale
        )
        return (
            grad_query,
            jnp.concatenate(
                [
                    grad_key.reshape(tok_rows, GROUPS * HEAD_DIM),
                    grad_value.reshape(tok_rows, GROUPS * HEAD_DIM),
                ],
                axis=1,
            ),
        )

    grad_query, kv_terms = lax.scan(
        back_step,
        jnp.zeros((tok_rows, GROUPS, repeat, HEAD_DIM), jnp.float32),
        (key_blocks, place_blocks, value_blocks),
    )
    grad_query = grad_query * score_scale
    kv_own = lax.psum_scatter(
        kv_terms.reshape(blocks * tok_rows, 2 * GROUPS * HEAD_DIM).astype(jnp.bfloat16),
        "ctx",
        scatter_dimension=0,
        tiled=True,
    ).astype(jnp.float32)
    grad_key_own = kv_own[:, : GROUPS * HEAD_DIM].reshape(tok_rows, GROUPS, HEAD_DIM)
    grad_value_own = kv_own[:, GROUPS * HEAD_DIM :].reshape(tok_rows, GROUPS, HEAD_DIM)
    grad_qkv_f, grad_q_gain, grad_k_gain = pull_heads(
        (grad_query.reshape(tok_rows, HEADS, HEAD_DIM), grad_key_own, grad_value_own)
    )
    grad_qkv_b = grad_qkv_f.astype(jnp.bfloat16)
    grad_qkv_w = jnp.dot(h_attn.T, grad_qkv_b, preferred_element_type=jnp.float32)
    grad_h_attn = jnp.dot(grad_qkv_b, qkv_w.T, preferred_element_type=jnp.float32)
    grad_here_part, grad_attn_gain = pull_attn(grad_h_attn)
    grad_inputs = (grad_residual + grad_here_part).astype(jnp.bfloat16)[None]
    grad_qkv_own, grad_out_own = (
        lax.psum_scatter(grad_qkv_w, ("dp", "ctx"), scatter_dimension=0, tiled=True),
        lax.psum_scatter(grad_out_w, ("dp", "ctx"), scatter_dimension=0, tiled=True),
    )
    gain_attn, gain_query, gain_key, gain_ffn = lax.psum(
        (grad_attn_gain, grad_q_gain, grad_k_gain, grad_ffn_gain), ("dp", "ctx")
    )
    return (
        layer_output,
        grad_inputs,
        gain_attn,
        grad_qkv_own,
        gain_query,
        gain_key,
        grad_out_own,
        gain_ffn,
        grad_gateup_own,
        grad_down_own,
    )


def per_device_fast(
    inputs, places, cotangent, attn_gain, w_qkv, q_gain, k_gain, w_out, ffn_gain, w_gateup, w_down
):
    n_dev = lax.axis_size("ctx")
    half = HEAD_DIM // 2
    spot = np.arange(128) % half
    step = np.float32(-2.0 * math.log(10000.0) / HEAD_DIM)
    frequency = np.exp(spot.astype(np.float32) * step).astype(np.float32)[None]
    gain_q, gain_k = q_gain[None], k_gain[None]
    layer_output, *kept = forward(
        inputs[0], cotangent[0], places, frequency, attn_gain[None], gain_q, gain_k,
        ffn_gain[None], w_qkv, w_out, w_down, w_gateup, n_dev,
    )
    rows = [w.shape[0] for w in (w_qkv, w_out, w_gateup, w_down)]
    grads = backward(inputs[0], attn_gain[None], gain_q, gain_k, ffn_gain[None], kept, rows, n_dev)
    layer_output, dx, g_attn, g_q, g_k, g_ffn, d_qkv, d_out, d_gu, d_down = settle(
        [layer_output, *grads]
    )
    return (
        layer_output[None], dx[None], g_attn[0], d_qkv, g_q[0], g_k[0], d_out, g_ffn[0], d_gu, d_down
    )


def solution(mesh):
    in_specs = (
        P("dp", "ctx", None),
        P("dp", "ctx"),
        P("dp", "ctx", None),
        P(),
        P(("dp", "ctx"), None),
        P(),
        P(),
        P(("dp", "ctx"), None),
        P(),
        P(("dp", "ctx"), None),
        P(("dp", "ctx"), None),
    )
    out_specs = (
        P("dp", "ctx", None),
        P("dp", "ctx", None),
        P(),
        P(("dp", "ctx"), None),
        P(),
        P(),
        P(("dp", "ctx"), None),
        P(),
        P(("dp", "ctx"), None),
        P(("dp", "ctx"), None),
    )
    fast = dict(mesh.shape) == {"dp": 4, "ctx": 8}
    per_device = per_device_fast if fast else per_device_plain
    return jax.shard_map(
        per_device, mesh=mesh, in_specs=in_specs, out_specs=out_specs, check_vma=False
    )
```

```python
import functools
import math

import jax
import jax.numpy as jnp
import numpy as np
from jax import lax
from jax.experimental import pallas as pl
from jax.experimental.pallas import tpu as pltpu
from jax.sharding import PartitionSpec as P

HEADS = 16
GROUPS = 4
HEAD_DIM = 64
FF = 1024


(
    f_qZ, f_qp0, f_qp1, f_qp2, f_qp3, f_qe0, f_qe1, f_qe2, f_qe3, f_qc0, f_qc1, f_qc2, f_qc3,
    f_qz0, f_qz1, f_qz2, f_qz3, f_dZ, f_dp0, f_dp1, f_dp2, f_dp3, f_de0, f_de1, f_de2, f_de3,
    f_dc0, f_dc1, f_dc2, f_dc3, f_dz0, f_dz1, f_dz2, f_dz3, f_gZ, f_gp0, f_gp1, f_gp2, f_gp3,
    f_ge0, f_ge1, f_ge2, f_ge3, f_gc0, f_gc1, f_gc2, f_gc3, f_gz0, f_gz1, f_gz2, f_gz3, f_qs0,
    f_qs1, f_qs2, f_qs3, f_gs0, f_gs1, f_gs2, f_gs3, f_ds0, f_ds1, f_ds2, f_ds3, f_oc0, f_oc1,
    f_oc2, f_oc3, f_oz00, f_oz01, f_oz02, f_oz03, f_oz10, f_oz11, f_oz12, f_oz13, f_oz20, f_oz21,
    f_oz22, f_oz23, f_oz30, f_oz31, f_oz32, f_oz33, f_kc0, f_kc1, f_kc2, f_kc3, f_kz00, f_kz01,
    f_kz02, f_kz03, f_kz10, f_kz11, f_kz12, f_kz13, f_kz20, f_kz21, f_kz22, f_kz23, f_kz30,
    f_kz31, f_kz32, f_kz33, f_kP, f_kZ, f_ke, f_kD, f_A, f_norm, f_trig, f_turn, f_keys, f_query,
    f_kve, f_kvc, f_unpack, f_mix, f_res, f_norm2, f_turn2, f_gate, f_act, f_y, f_oP, f_oZ, f_oe,
    f_oD,
) = range(127)

(
    b_df, b_da0, b_da1, b_da2, b_da3, b_db0, b_db1, b_db2, b_db3, b_dd0, b_dd1, b_dd2, b_dd3,
    b_dx0, b_dx1, b_dx2, b_dx3, b_dz0, b_dz1, b_dz2, b_dz3, b_gf, b_ga0, b_ga1, b_ga2, b_ga3,
    b_gb0, b_gb1, b_gb2, b_gb3, b_gd0, b_gd1, b_gd2, b_gd3, b_gx0, b_gx1, b_gx2, b_gx3, b_gz0,
    b_gz1, b_gz2, b_gz3, b_qf, b_qa0, b_qa1, b_qa2, b_qa3, b_qb0, b_qb1, b_qb2, b_qb3, b_qd0,
    b_qd1, b_qd2, b_qd3, b_qx0, b_qx1, b_qx2, b_qx3, b_qz0, b_qz1, b_qz2, b_qz3, b_dw0, b_dw1,
    b_dw2, b_dw3, b_gw0, b_gw1, b_gw2, b_gw3, b_ow0, b_ow1, b_ow2, b_ow3, b_qw0, b_qw1, b_qw2,
    b_qw3, b_oa0, b_oa1, b_oa2, b_oa3, b_oo0, b_oo1, b_oo2, b_oo3, b_hs0, b_hs1, b_hs2, b_he0,
    b_he1, b_he2, b_oz00, b_oz01, b_oz02, b_oz03, b_oz10, b_oz11, b_oz12, b_oz13, b_oz20, b_oz21,
    b_oz22, b_oz23, b_ka0, b_ka1, b_ka2, b_ka3, b_ko0, b_ko1, b_ko2, b_ko3, b_kz00, b_kz01,
    b_kz02, b_kz03, b_kz10, b_kz11, b_kz12, b_kz13, b_kz20, b_kz21, b_kz22, b_kz23, b_kS, b_ke,
    b_kf, b_H, b_B, b_Q, b_G, b_h, b_nb, b_m, b_att, b_kvs, b_kvc, b_kve, b_kvf, b_oS, b_oe, b_of,
    b_lm, b_ll, b_qe, b_g, b_nb2, b_rs, b_re,
) = range(150)

FORWARD_ORDER = [
    f_kP, f_qZ, f_qp0, f_oP, f_norm, f_oZ, f_qz1, f_qp1, f_qe0, f_qz2, f_trig, f_oz10, f_dZ,
    f_qp2, f_oz20, f_qz3, f_qe1, f_qp3, f_turn, f_gZ, f_qe2, f_ke, f_kZ, f_qc0, f_qe3, f_oe,
    f_qc1, f_qs0, f_gp0, f_qc2, f_qc3, f_qs1, f_qs2, f_oD, f_gz1, f_dz1, f_qs3, f_keys, f_dz2,
    f_dp2, f_gz2, f_dp1, f_kve, f_gp1, f_gz3, f_kz11, f_query, f_de1, f_gp2, f_dz3, f_oz12,
    f_kz10, f_oz11, f_oz13, f_kvc, f_dp0, f_oz22, f_kz12, f_ge0, f_kD, f_gp3, f_unpack, f_oz23,
    *[f_A] * 5, f_kz22, *[f_A] * 2, f_oz21, *[f_A] * 3, f_ge2, f_oc1, f_ge1, f_A, f_oz30,
    *[f_A] * 5, f_kz20, f_gc0, *[f_A] * 2, f_oz31, f_A, f_de2, *[f_A] * 3, f_oc2, f_dp3, f_oz32,
    *[f_A] * 6, f_oz33, f_oc3, f_dc1, *[f_A] * 2, f_kz13, f_ge3, f_kc1, f_gc2, f_kz32, *[f_A] * 2,
    f_gc1, f_de0, f_dc2, f_kz30, f_res, f_kz21, f_de3, f_mix, f_kz23, f_gc3, f_norm2, f_kz33,
    f_gs0, f_dc0, f_gs1, f_kz31, f_kc3, f_gs2, f_dc3, f_kc2, f_turn2, f_ds0, f_gs3, f_ds1, f_ds2,
    f_ds3, f_gate, f_act, f_y,
]

BACKWARD_ORDER = [
    b_dw0, b_dw1, b_dw2, b_da1, b_ka1, b_dw3, b_gw0, b_gw1, b_ka0, b_h, *[b_H] * 6, b_ga0,
    *[b_H] * 2, b_nb, b_lm, b_gw2, b_gw3, b_gb1, b_kz03, b_gb0, b_m, b_db1, b_att, b_gb2, b_kz02,
    b_da2, b_ow0, b_B, b_oa0, *[b_B] * 2, b_ow1, *[b_B] * 2, b_kz13, b_B, b_da0, b_ga2, b_ll, b_B,
    b_oa1, b_ga1, b_B, b_gd0, b_B, b_gd2, b_kz00, b_kz01, b_B, b_ow2, b_B, b_gb3, b_B, b_oa2,
    b_ga3, *[b_B] * 3, b_oz01, b_gd1, b_ow3, b_B, b_kvs, b_Q, b_da3, b_ka2, b_kz12, b_dd1, b_kz22,
    b_kz23, b_kz11, b_Q, b_dd0, b_db0, b_Q, b_db3, b_Q, b_oz00, b_gx0, b_dx1, b_oz10, b_oz11,
    b_kvc, b_kz10, b_oz03, *[b_Q] * 2, b_oz21, b_oz13, b_Q, b_kz21, b_Q, b_kve, b_gd3, b_gz0,
    b_kvf, b_kz20, b_ko3, b_dd2, b_g, b_db2, b_gx1, b_oz02, b_gx2, b_dd3, b_G, b_dx0, b_G, b_dz0,
    b_qe, b_ko1, b_qw0, b_qa0, b_qb0, b_oz20, b_dx2, b_oz23, b_oz12, b_qw1, b_qw2, b_dz1, b_qa1,
    b_qb1, b_G, b_oz22, b_qa2, b_dz2, *[b_G] * 2, b_qd0, b_gz1, b_ko0, b_qw3, b_qb2, *[b_G] * 2,
    b_ko2, b_gz2, b_G, b_qd1, b_nb2, b_oo3, b_hs0, b_kS, b_oo1, b_oo2, b_qd2, b_qx0, b_he0, b_oo0,
    b_qz0, b_hs1, b_qx1, b_oS, b_qa3, b_qz1, b_he1, b_hs2, b_qx2, b_df, b_gf, b_ka3, b_qz2, b_ke,
    b_oe, b_he2, b_rs, b_qb3, b_oa3, b_qd3, b_qf, b_kf, b_re, b_of,
]


f32 = jnp.float32
bf16 = jnp.bfloat16
MESH = pl.DeviceIdType.MESH
NZ = 4
EPS = 1e-06


class Place:
    def __init__(self):
        self.z = lax.axis_index("dp")
        spot = lax.axis_index("ctx")
        self.core = spot % 2
        self.x = (spot // 2) % 2
        self.y = spot // 4

    def at(self, z=None, y=None, x=None, core=None):
        z = self.z if z is None else z
        y = self.y if y is None else y
        x = self.x if x is None else x
        core = self.core if core is None else core
        return (z, y * 4 + x * 2 + core)

    def xn(self):
        return self.at(x=1 - self.x)

    def yn(self):
        return self.at(y=1 - self.y)

    def sn(self):
        return self.at(core=1 - self.core)

    def up(self):
        return self.at(z=self.z + 1)

    def down(self):
        return self.at(z=self.z - 1)


def barrier(pc):
    bar = pltpu.get_barrier_semaphore()

    def greet(device):
        pl.semaphore_signal(bar, inc=1, device_id=device, device_id_type=MESH)

    for device in (pc.xn(), pc.yn(), pc.sn()):
        greet(device)

    @pl.when(pc.z < NZ - 1)
    def _():
        greet(pc.up())

    @pl.when(pc.z > 0)
    def _():
        greet(pc.down())

    pl.semaphore_wait(bar, 3 + (1 - pc.z // (NZ - 1)) + (pc.z + NZ - 1) // NZ)


def far(z, i):
    m = z // 2
    zz = z + m * (3 - 2 * z)
    lo = 3 - i if i < 2 else (1 - zz if i == 2 else zz)
    return lo + m * (3 - 2 * lo)


def near(z, i):
    return far(z, NZ - 1 - i)


def remote(src, dst, dev, send, recv):
    return pltpu.make_async_remote_copy(
        src_ref=src, dst_ref=dst, send_sem=send, recv_sem=recv, device_id=dev, device_id_type=MESH
    )


def halves(rows):
    return pl.ds(0, rows // 2), pl.ds(rows // 2, rows // 2)


def cuts(shape, some=None):
    rows, columns = shape[-2:]
    if some is None:
        return (pl.ds(0, rows),), tuple((h,) for h in halves(rows))
    return (some,), tuple((some, h) for h in halves(columns))


KZ, KX, KY, KD0, KD1, KS, KU = range(7)


class Gather:
    def __init__(self, pc, buf, send, recv, some=None):
        self.pc, self.buf, self.send, self.recv = pc, buf, send, recv
        self.full, self.h = cuts(buf.shape, some)

    def cp(self, idx, dev, ks, kr, slot):
        ref = self.buf.at[idx]
        return remote(ref, ref, dev, self.send.at[ks, slot], self.recv.at[kr, slot])

    def c_up(self, z0):
        p = self.pc
        return self.cp((z0, p.y, p.x, p.core, *self.full), p.up(), KU, KZ, z0)

    def c_down(self, z0):
        p = self.pc
        return self.cp((z0, p.y, p.x, p.core, *self.full), p.down(), KZ, KZ, z0)

    def c_x(self, z0):
        p = self.pc
        return self.cp((z0, p.y, p.x, p.core, *self.full), p.xn(), KX, KX, z0)

    def c_y(self, z0):
        p = self.pc
        return self.cp((z0, p.y, p.x, p.core, *self.full), p.yn(), KY, KY, z0)

    def c_d0(self, z0):
        p = self.pc
        return self.cp((z0, p.y, 1 - p.x, p.core, *self.h[0]), p.yn(), KD0, KD0, z0)

    def c_d1(self, z0):
        p = self.pc
        return self.cp((z0, 1 - p.y, p.x, p.core, *self.h[1]), p.xn(), KD1, KD1, z0)

    def c_s(self, z0):
        p = self.pc
        return self.cp((z0, slice(None), slice(None), p.core, *self.full), p.sn(), KS, KS, z0)

    def plane_send(self, i):
        z0 = near(self.pc.z, i)
        self.c_x(z0).start()
        self.c_y(z0).start()

    def own_z(self):
        z = self.pc.z

        @pl.when(z < NZ - 1)
        def _():
            self.c_up(z).start()

        @pl.when(z > 0)
        def _():
            self.c_down(z).start()

    def z_event(self, i, plane=True):
        z = self.pc.z
        z0 = near(z, i)

        @pl.when(z0 < z)
        def _():
            self.c_up(z0).wait_recv()

            @pl.when(z < NZ - 1)
            def _():
                self.c_up(z0).start()

        @pl.when(z0 > z)
        def _():
            self.c_down(z0).wait_recv()

            @pl.when(z > 0)
            def _():
                self.c_down(z0).start()

        if plane:
            self.plane_send(i)

    def plane_event(self, i):
        z0 = near(self.pc.z, i)
        self.c_x(z0).wait_recv()
        self.c_d0(z0).start()
        self.c_y(z0).wait_recv()
        self.c_d1(z0).start()

    def core_event(self, i):
        z0 = near(self.pc.z, i)
        self.c_d0(z0).wait_recv()
        self.c_d1(z0).wait_recv()
        self.c_s(z0).start()

    def done_event(self, i):
        self.c_s(near(self.pc.z, i)).wait_recv()

    def finish(self):
        z = self.pc.z
        for z0 in range(NZ):
            for c in (self.c_x, self.c_y, self.c_d0, self.c_d1, self.c_s):
                c(z0).wait_send()

            @pl.when((z < NZ - 1) & (z0 <= z))
            def _():
                self.c_up(z0).wait_send()

            @pl.when((z > 0) & (z0 >= z))
            def _():
                self.c_down(z0).wait_send()


class GatherPlane:
    def __init__(self, pc, buf, send, recv, some=None):
        self.pc, self.buf, self.send, self.recv = pc, buf, send, recv
        self.full, self.h = cuts(buf.shape, some)

    def cp(self, idx, dev, s, r):
        ref = self.buf.at[idx]
        return remote(ref, ref, dev, self.send.at[s], self.recv.at[r])

    def yx(self, k):
        p = self.pc
        return (p.y if k < 2 else 1 - p.y), (p.x if k % 2 == 0 else 1 - p.x)

    def c_x(self):
        p = self.pc
        return self.cp((p.z, p.y, p.x, p.core, *self.full), p.xn(), (KX, 0), (KX, 0))

    def c_y(self):
        p = self.pc
        return self.cp((p.z, p.y, p.x, p.core, *self.full), p.yn(), (KY, 0), (KY, 0))

    def c_d0(self):
        p = self.pc
        return self.cp((p.z, p.y, 1 - p.x, p.core, *self.h[0]), p.yn(), (KD0, 0), (KD0, 0))

    def c_d1(self):
        p = self.pc
        return self.cp((p.z, 1 - p.y, p.x, p.core, *self.h[1]), p.xn(), (KD1, 0), (KD1, 0))

    def c_up(self, z0, k):
        p = self.pc
        y, x = self.yx(k)
        return self.cp((z0, y, x, p.core, *self.full), p.up(), (10 + z0, k), (10 + z0, k))

    def c_down(self, z0, k):
        p = self.pc
        y, x = self.yx(k)
        return self.cp((z0, y, x, p.core, *self.full), p.down(), (14 + z0, k), (10 + z0, k))

    def c_s(self, z0):
        p = self.pc
        return self.cp((z0, slice(None), slice(None), p.core, *self.full), p.sn(), (KS, z0), (KS, z0))

    def z_send(self, k):
        z = self.pc.z

        @pl.when(z < NZ - 1)
        def _():
            self.c_up(z, k).start()

        @pl.when(z > 0)
        def _():
            self.c_down(z, k).start()

    def own_plane(self):
        self.c_x().start()
        self.c_y().start()

    def own_z(self):
        self.z_send(0)

    def plane_event(self):
        self.c_x().wait_recv()
        self.c_d0().start()
        self.z_send(1)
        self.c_y().wait_recv()
        self.c_d1().start()
        self.z_send(2)

    def diag_event(self):
        self.c_d0().wait_recv()
        self.c_d1().wait_recv()
        self.z_send(3)
        self.c_s(self.pc.z).start()

    def z_event(self, i, k):
        z = self.pc.z
        z0 = near(z, i)

        @pl.when(z0 < z)
        def _():
            self.c_up(z0, k).wait_recv()

            @pl.when(z < NZ - 1)
            def _():
                self.c_up(z0, k).start()

        @pl.when(z0 > z)
        def _():
            self.c_down(z0, k).wait_recv()

            @pl.when(z > 0)
            def _():
                self.c_down(z0, k).start()

    def core_event(self, i):
        self.c_s(near(self.pc.z, i)).start()

    def done_event(self, i):
        self.c_s(near(self.pc.z, i)).wait_recv()

    def finish(self):
        z = self.pc.z
        for c in (self.c_x, self.c_y, self.c_d0, self.c_d1):
            c().wait_send()
        for z0 in range(NZ):
            self.c_s(z0).wait_send()
            for k in range(4):

                @pl.when((z < NZ - 1) & (z0 <= z))
                def _():
                    self.c_up(z0, k).wait_send()

                @pl.when((z > 0) & (z0 >= z))
                def _():
                    self.c_down(z0, k).wait_send()


class GatherSequence:
    def __init__(self, pc, buf, send, recv):
        self.pc, self.buf, self.send, self.recv = pc, buf, send, recv
        rows = buf.shape[-2]
        self.h = (pl.ds(0, 128), pl.ds(128, rows - 128))

    def cp(self, idx, dev, k):
        ref = self.buf.at[idx]
        return remote(ref, ref, dev, self.send.at[k], self.recv.at[k])

    def c_x(self):
        p = self.pc
        return self.cp((p.y, p.x, p.core), p.xn(), 0)

    def c_y(self):
        p = self.pc
        return self.cp((p.y, p.x, p.core), p.yn(), 1)

    def c_d0(self):
        p = self.pc
        return self.cp((p.y, 1 - p.x, p.core, self.h[0]), p.yn(), 2)

    def c_d1(self):
        p = self.pc
        return self.cp((1 - p.y, p.x, p.core, self.h[1]), p.xn(), 3)

    def c_s(self, k):
        p = self.pc
        y, x = (p.y if k < 2 else 1 - p.y), (p.x if k % 2 == 0 else 1 - p.x)
        return self.cp((y, x, p.core), p.sn(), 4 + k)

    def own(self):
        for c in (self.c_x(), self.c_y(), self.c_s(0)):
            c.start()

    def plane_event(self):
        self.c_x().wait_recv()
        self.c_d0().start()
        self.c_s(1).start()
        self.c_y().wait_recv()
        self.c_d1().start()
        self.c_s(2).start()

    def core_event(self):
        self.c_d0().wait_recv()
        self.c_d1().wait_recv()
        self.c_s(3).start()

    def done_event(self):
        for k in range(4):
            self.c_s(k).wait_recv()

    def finish(self):
        for c in (self.c_x(), self.c_y(), self.c_d0(), self.c_d1()):
            c.wait_send()
        for k in range(4):
            self.c_s(k).wait_send()


LOG2E = math.log2(math.e)
VMEM = pltpu.VMEM


def dot(a, b):
    return jnp.dot(a, b, preferred_element_type=f32)


def dot_t(a, b):
    return lax.dot_general(a, b, (((1,), (1,)), ((), ())), preferred_element_type=f32)


def lanes(shape):
    return lax.broadcasted_iota(jnp.int32, shape, 1)


def roll_half(v):
    return pltpu.roll(v, 64, 1)


def swap_rot(v):
    first = lanes(v.shape) % 64 < 32
    return jnp.where(first, pltpu.roll(v, 96, 1), pltpu.roll(v, 32, 1))


def head_sums(v):
    row = lax.broadcasted_iota(jnp.int32, (128, 128), 0) // 64
    col = lax.broadcasted_iota(jnp.int32, (128, 128), 1) // 64
    ones = jnp.where(row == col, 1.0, 0.0).astype(bf16)
    high = v.astype(bf16)
    low = (v - high.astype(f32)).astype(bf16)
    return dot(high, ones) + dot(low, ones)


def twice(gain):
    return jnp.concatenate([gain[...], gain[...]], axis=1)


def cols(i, width):
    return pl.ds(pl.multiple_of(i * width, width), width)


def norm_into(src, gain, dst):
    def body(i, _):
        rows = pl.ds(pl.multiple_of(i * 32, 32), 32)
        v = src[rows, :].astype(f32)
        scale = lax.rsqrt(jnp.mean(v * v, axis=-1, keepdims=True) + EPS)
        dst[rows, :] = (v * scale * gain[...]).astype(dst.dtype)
        return 0

    lax.fori_loop(0, src.shape[0] // 32, body, 0)


def run_steps(order, steps, loops):
    order = list(order)
    while order:
        name = order.pop(0)
        if name not in loops:
            steps[name]()
            continue
        count, body = loops[name]
        ticks, seen = {}, 1
        while seen < count:
            inner = order.pop(0)
            if inner == name:
                seen += 1
            else:
                ticks.setdefault(seen - 1, []).append(inner)

        def tick(i, _, body=body, ticks=ticks):
            body(i)
            for k, inner in ticks.items():

                @pl.when(i == k)
                def _(inner=inner):
                    for step in inner:
                        steps[step]()

            return 0

        lax.fori_loop(0, count, tick, 0)


def line_steps(first, g):
    part = functools.partial
    steps = {first: g.own_z}
    for i in range(NZ):
        steps[first + 1 + i] = part(g.plane_send, i)
        steps[first + 5 + i] = part(g.plane_event, i)
        steps[first + 9 + i] = part(g.core_event, i)
        if i:
            steps[first + 13 + i] = part(g.z_event, i, False)
    return steps


def turn(src, rows, core, mine, theirs):
    def body(t, _):
        v = jnp.transpose(src[:, cols(t, 128)])
        for k in range(64 // rows):
            a, b = v[2 * k * rows : (2 * k + 1) * rows], v[(2 * k + 1) * rows : (2 * k + 2) * rows]
            own, other = jnp.where(core == 0, a, b), jnp.where(core == 0, b, a)
            spot = t * (64 // rows) + k
            mine[spot, :, pl.ds(0, v.shape[1])] = own
            theirs[spot, pl.ds(0, rows), :] = other
        return 0

    lax.fori_loop(0, src.shape[1] // 128, body, 0)


def forward_kernel(dims, *refs):
    (tok, width, n_dev, heads_w, kv_w, ff) = dims
    (
        x_ref, cot_ref, place_ref, freq_ref, g_attn, one_q, one_k, g_ffn,
        s_qkv, s_out, s_down, s_gu,
        o_y, o_tattn, o_tmix, o_tffn, o_tact, o_cot, o_ggu, o_kv, o_q2, o_linv, o_mixf, o_res,
        o_kk, o_va, o_mask, o_wqkv, o_wout, o_wgu, o_cos, o_sin,
        w_qkv, w_out, w_down, w_gu, kk, va, mask, mask_t, o2, gu, gact,
        y_ref, hattn_ref, qkv_ref, q2_ref, kvb, linv_ref, mixf_ref, mixb_ref, res_ref, hffn_ref,
        act_ref, cot2, ggu2, cos_ref, sin_ref, t_attn, t_mix, t_ffn, t_act, turn_a, turn_b,
        send, recv, kv_send, kv_recv, lsem, osem, ex_send, ex_recv,
    ) = refs
    pc = Place()
    shards = (s_qkv, s_out, s_down, s_gu)
    bufs = (w_qkv, w_out, w_down, w_gu)
    local = [
        pltpu.make_async_copy(s, b.at[pc.z, pc.y, pc.x, pc.core], lsem.at[k])
        for k, (s, b) in enumerate(zip(shards, bufs))
    ]
    for c in local:
        c.start()
    barrier(pc)
    for c in local:
        c.wait()
    qkv = Gather(pc, w_qkv, send.at[0], recv.at[0])
    out = GatherPlane(pc, w_out, send.at[1], recv.at[1])
    half = s_down.shape[0] // 2
    down = Gather(pc, w_down, send.at[2], recv.at[2], pl.ds(0, half))
    rest = GatherPlane(pc, w_down, send.at[4], recv.at[4], pl.ds(half, half))
    gateup = Gather(pc, w_gu, send.at[3], recv.at[3])
    seq = GatherSequence(pc, kvb, kv_send, kv_recv)
    part = functools.partial
    z = pc.z
    emitted = []

    def emit(src, dst):
        c = pltpu.make_async_copy(src, dst, osem.at[len(emitted)])
        emitted.append(c)
        c.start()

    def exchange(k, src, dst):
        return remote(src, dst, pc.sn(), ex_send.at[k], ex_recv.at[k])

    back = pl.ds(tok, tok)
    sent_cot = exchange(0, cot_ref, cot2.at[back, :])
    sent_attn = exchange(1, turn_a, t_attn.at[:, :, back])
    sent_mix = exchange(2, turn_b.at[:, pl.ds(0, s_out.shape[0]), :], t_mix.at[:, :, back])
    sent_ffn = exchange(3, turn_a, t_ffn.at[:, :, back])
    sent_act = exchange(4, turn_b.at[:, pl.ds(0, s_down.shape[0]), :], t_act.at[:, :, back])
    sent_ggu = exchange(5, ggu2.at[pl.ds(0, tok), :], ggu2.at[back, :])

    g_q, g_k = twice(one_q), twice(one_k)

    def block_row(a):
        return jnp.right_shift(place_ref[:, a * (tok // 2) : (a + 1) * (tok // 2)], 7).astype(f32)

    def tables():
        step = tok // 2
        sign = jnp.where(lanes((step, 128)) % 64 < 32, -1.0, 1.0)
        row = lax.broadcasted_iota(jnp.int32, (step, 128), 0).astype(f32)
        for a in range(2):
            angle = (block_row(a) * 128.0 + row) * freq_ref[...]
            cos_ref[pl.ds(a * step, step), :] = jnp.cos(angle)
            sin_ref[pl.ds(a * step, step), :] = sign * jnp.sin(angle)
        emit(cos_ref, o_cos)
        emit(sin_ref, o_sin)

    def first_norm():
        norm_into(x_ref, g_attn, hattn_ref)

    def first_turn():
        sent_cot.start()
        cot2[pl.ds(0, tok), :] = cot_ref[...]
        turn(hattn_ref, s_qkv.shape[0], pc.core, t_attn, turn_a)
        sent_attn.start()

    def columns_step(g, i, left, right, total, depth):
        g.done_event(i)
        z0 = near(z, i)

        def body(n, _):
            c = cols(n, 256)
            w = right[z0, :, :, :, :, c].reshape(depth, 256)
            prod = dot(left[:, cols(z0, depth)], w)
            if i == 0:
                total[:, c] = prod
            else:
                total[:, c] += prod
            return 0

        lax.fori_loop(0, total.shape[1] // 256, body, 0)

    def grad_act_step(i):
        down.done_event(i)
        rest.done_event(i)
        z0 = near(z, i)
        depth = ff // NZ
        gact[:, cols(z0, depth)] = dot_t(cot_ref[...], w_down[z0].reshape(depth, width))

    low = lanes((tok, 128)) < 64

    def head_tile(t, gain):
        u = qkv_ref[:, cols(t, 128)]
        n = u * lax.rsqrt(head_sums(u * u) * (1.0 / 64) + EPS) * gain
        return n * cos_ref[...] + swap_rot(n) * sin_ref[...]

    def keys_out():
        for t in range(kv_w // 128):
            kvb[pc.y, pc.x, pc.core, pl.ds(0, tok), pl.ds(t * 128, 128)] = head_tile(
                heads_w // 128 + t, g_k
            ).astype(bf16)
        kvb[pc.y, pc.x, pc.core, pl.ds(0, tok), pl.ds(kv_w, kv_w)] = qkv_ref[
            :, pl.ds(heads_w + kv_w, kv_w)
        ].astype(bf16)
        both_rows = jnp.concatenate([block_row(0), block_row(1)], axis=1)
        blocks_row = jnp.broadcast_to(both_rows, (16, tok)).astype(bf16)
        kvb[pc.y, pc.x, pc.core, pl.ds(tok, 16), pl.ds(0, tok)] = blocks_row
        kvb[pc.y, pc.x, pc.core, pl.ds(tok, 16), pl.ds(tok, tok)] = blocks_row
        seq.own()

    def query_tile(t, _):
        q = (head_tile(t, g_q) * 0.125).astype(bf16)
        zero = jnp.zeros_like(q)
        q2_ref[t, pl.ds(0, tok), :] = jnp.where(low, q, zero)
        q2_ref[t, pl.ds(tok, tok), :] = jnp.where(low, zero, q)
        return 0

    def queries():
        lax.fori_loop(0, heads_w // 128, query_tile, 0)
        emit(qkv_ref, o_kv)
        emit(q2_ref, o_q2)
        emit(w_qkv, o_wqkv)
        sent_cot.wait_recv()
        emit(cot2, o_cot)
        sent_attn.wait_recv()
        emit(t_attn, o_tattn)

    def unpack(b, _):
        y, x, c = b // 4, (b // 2) % 2, b % 2
        rows = pl.ds(pl.multiple_of(b * tok, tok), tok)
        for t in range(kv_w // 128):
            k = kvb[y, x, c, pl.ds(0, tok), pl.ds(t * 128, 128)].astype(f32)
            v = kvb[y, x, c, pl.ds(0, tok), pl.ds(kv_w + t * 128, 128)].astype(f32)
            k_r, v_r = roll_half(k), roll_half(v)
            kk[2 * t, rows, :] = jnp.where(low, k, k_r).astype(bf16)
            kk[2 * t + 1, rows, :] = jnp.where(low, k_r, k).astype(bf16)
            va[2 * t, rows, :] = jnp.where(low, v, 1.0).astype(bf16)
            va[2 * t + 1, rows, :] = jnp.where(low, v_r, 1.0).astype(bf16)
        step = tok // 2
        key_hi = kvb[y, x, c, pl.ds(tok, 16), pl.ds(0, tok)].astype(f32)[:1, :]
        for a in range(2):
            own = block_row(a)
            row = lax.broadcasted_iota(jnp.int32, (step, step), 0).astype(f32)
            col = lanes((step, step)).astype(f32)
            for d in range(2):
                theirs = key_hi[:, d * step : (d + 1) * step]
                gap = (own - theirs) * float(step) + row - col
                place = pl.ds(pl.multiple_of(b * tok + d * step, step), step)
                mask[pl.ds(a * step, step), place] = jnp.where(gap >= 0, 1.0, 0.0).astype(bf16)
                gap = (own - theirs) * float(step) + col - row
                mask_t[place, pl.ds(a * step, step)] = jnp.where(gap >= 0, 1.0, 0.0).astype(bf16)
        return 0

    def unpack_all():
        seq.done_event()
        lax.fori_loop(0, n_dev, unpack, 0)
        emit(kk, o_kk)
        emit(va, o_va)
        emit(mask_t, o_mask)

    chunk = 512
    n_chunk = n_dev * tok // chunk

    def attend(tick):
        t, kc = tick // n_chunk, tick % n_chunk
        g = t // 2
        rows = pl.ds(pl.multiple_of(kc * chunk, chunk), chunk)
        s = dot_t(q2_ref[t], kk[g, rows, :])
        e = jnp.exp2(s * LOG2E).astype(bf16).reshape(2, tok, chunk) * mask[:, rows][None]
        o = dot(e.reshape(2 * tok, chunk), va[g, rows, :])

        @pl.when(kc == 0)
        def _():
            o2[...] = o

        @pl.when(kc > 0)
        def _():
            o2[...] += o

        @pl.when(kc == n_chunk - 1)
        def _():
            even, odd = o2[pl.ds(0, tok), :], o2[pl.ds(tok, tok), :]
            total = jnp.where(low, roll_half(even), odd)
            inv = 1.0 / total
            mixed = jnp.where(low, even, roll_half(odd)) * inv
            linv_ref[:, cols(t, 128)] = inv
            mixf_ref[:, cols(t, 128)] = mixed
            mixb_ref[:, cols(t, 128)] = mixed.astype(bf16)

    def mix_out():
        emit(linv_ref, o_linv)
        emit(mixf_ref, o_mixf)
        turn(mixb_ref, s_out.shape[0], pc.core, t_mix, turn_b)
        sent_mix.start()

    def residual_step(n, _):
        c = cols(n, 256)
        w = w_out[:, :, :, :, :, c].reshape(heads_w, 256)
        res_ref[:, c] = x_ref[:, c].astype(f32) + dot(mixb_ref[...], w)
        return 0

    def residual():
        for i in range(NZ):
            out.done_event(i)
        emit(w_out, o_wout)
        lax.fori_loop(0, width // 256, residual_step, 0)

    def second_norm():
        norm_into(res_ref, g_ffn, hffn_ref)

    def second_turn():
        emit(res_ref, o_res)
        sent_mix.wait_recv()
        emit(t_mix, o_tmix)
        sent_attn.wait_send()
        turn(hffn_ref, s_gu.shape[0], pc.core, t_ffn, turn_a)
        sent_ffn.start()

    def gate_step(n, _):
        c = cols(n, 256)
        c2 = cols(n + ff // 256, 256)
        gate, up, grad = gu[:, c], gu[:, c2], gact[:, c]
        sig = 1.0 / (1.0 + jnp.exp(-gate))
        silu = gate * sig
        act_ref[:, c] = (silu * up).astype(bf16)
        ggu2[pl.ds(0, tok), c] = (grad * up * (sig * (1.0 + gate * (1.0 - sig)))).astype(bf16)
        ggu2[pl.ds(0, tok), c2] = (grad * silu).astype(bf16)
        return 0

    def gates():
        lax.fori_loop(0, ff // 256, gate_step, 0)
        sent_ggu.start()
        emit(w_gu, o_wgu)

    def act_out():
        sent_mix.wait_send()
        turn(act_ref, s_down.shape[0], pc.core, t_act, turn_b)
        sent_act.start()
        sent_ffn.wait_recv()
        emit(t_ffn, o_tffn)

    def output_step(n, _):
        c = cols(n, 256)
        w = w_down[:, :, :, :, :, c].reshape(ff, 256)
        y_ref[:, c] = (res_ref[:, c] + dot(act_ref[...], w)).astype(bf16)
        return 0

    def outputs():
        lax.fori_loop(0, width // 256, output_step, 0)
        emit(y_ref, o_y)
        sent_ggu.wait_recv()
        emit(ggu2, o_ggu)
        sent_act.wait_recv()
        emit(t_act, o_tact)

    steps = {
        f_norm: first_norm, f_trig: tables, f_turn: first_turn, f_keys: keys_out, f_query: queries,
        f_kve: seq.plane_event, f_kvc: seq.core_event, f_unpack: unpack_all, f_mix: mix_out,
        f_res: residual, f_norm2: second_norm, f_turn2: second_turn, f_gate: gates,
        f_act: act_out, f_y: outputs, f_oP: out.own_plane, f_oZ: out.own_z, f_oe: out.plane_event,
        f_oD: out.diag_event, f_kP: rest.own_plane, f_kZ: rest.own_z, f_ke: rest.plane_event,
        f_kD: rest.diag_event,
    }
    for first, g in ((f_qZ, qkv), (f_dZ, down), (f_gZ, gateup)):
        steps.update(line_steps(first, g))
    for i in range(NZ):
        steps[f_qs0 + i] = part(columns_step, qkv, i, hattn_ref, w_qkv, qkv_ref, width // NZ)
        steps[f_gs0 + i] = part(columns_step, gateup, i, hffn_ref, w_gu, gu, width // NZ)
        steps[f_ds0 + i] = part(grad_act_step, i)
        if i:
            steps[f_oc0 + i] = part(out.core_event, i)
            steps[f_kc0 + i] = part(rest.core_event, i)
            for k in range(4):
                steps[f_oz00 + 4 * i + k] = part(out.z_event, i, k)
                steps[f_kz00 + 4 * i + k] = part(rest.z_event, i, k)
    run_steps(FORWARD_ORDER, steps, {f_A: (heads_w // 128 * n_chunk, attend)})
    for g in (qkv, out, down, rest, gateup, seq):
        g.finish()
    for c in (sent_cot, sent_ffn, sent_act, sent_ggu):
        c.wait_send()
    for c in emitted:
        c.wait()


def forward(x, cot, places, frequency, g_attn, g_q, g_k, g_ffn, s_qkv, s_out, s_down, s_gu, n_dev):
    tok, width = x.shape
    heads_w, kv_w = HEADS * HEAD_DIM, GROUPS * HEAD_DIM
    ff = s_down.shape[0] * n_dev * NZ
    length = n_dev * tok
    tiles = heads_w // 128
    shape = jax.ShapeDtypeStruct
    seven = [(NZ, 2, 2, 2) + s.shape for s in (s_qkv, s_out, s_down, s_gu)]
    qkv_rows, out_rows, down_rows, gu_rows = [s.shape[0] for s in (s_qkv, s_out, s_down, s_gu)]
    spots = n_dev * NZ // 2
    kv_buf = ((2, 2, 2, tok + 16, 2 * kv_w), bf16)
    turned = [((spots, r, 2 * tok), bf16) for r in (qkv_rows, out_rows, gu_rows, down_rows)]
    keep = [
        ((tok, width), bf16),
        *turned,
        ((2 * tok, width), bf16),
        ((2 * tok, 2 * ff), bf16),
        ((tok, s_qkv.shape[1]), f32),
        ((tiles, 2 * tok, 128), bf16),
        ((tok, heads_w), f32),
        ((tok, heads_w), f32),
        ((tok, width), f32),
        ((GROUPS, length, 128), bf16),
        ((GROUPS, length, 128), bf16),
        ((length, tok), bf16),
        (seven[0], bf16),
        (seven[1], bf16),
        (seven[3], bf16),
        ((tok, 128), f32),
        ((tok, 128), f32),
    ]
    outs = [shape(*k) for k in keep]
    vm = pl.BlockSpec(memory_space=VMEM)
    anyw = pl.BlockSpec(memory_space=pl.ANY)
    dma = pltpu.SemaphoreType.DMA
    flops = 2 * tok * (width * (s_qkv.shape[1] + heads_w + 2 * ff + 2 * ff) + 2 * heads_w * length)
    return pl.pallas_call(
        functools.partial(forward_kernel, (tok, width, n_dev, heads_w, kv_w, ff)),
        out_shape=outs,
        in_specs=[vm] * 8 + [anyw] * 4,
        out_specs=[anyw] * len(outs),
        scratch_shapes=[VMEM(s, bf16) for s in seven]
        + [
            VMEM((GROUPS, length, 128), bf16),
            VMEM((GROUPS, length, 128), bf16),
            VMEM((tok, length), bf16),
            VMEM((length, tok), bf16),
            VMEM((2 * tok, 128), f32),
            VMEM((tok, 2 * ff), f32),
            VMEM((tok, ff), f32),
            VMEM((tok, width), bf16),
            VMEM((tok, width), bf16),
            VMEM((tok, s_qkv.shape[1]), f32),
            VMEM((tiles, 2 * tok, 128), bf16),
            VMEM(*kv_buf),
            VMEM((tok, heads_w), f32),
            VMEM((tok, heads_w), f32),
            VMEM((tok, heads_w), bf16),
            VMEM((tok, width), f32),
            VMEM((tok, width), bf16),
            VMEM((tok, ff), bf16),
            VMEM((2 * tok, width), bf16),
            VMEM((2 * tok, 2 * ff), bf16),
            VMEM((tok, 128), f32),
            VMEM((tok, 128), f32),
            *[VMEM(*t) for t in turned],
            VMEM((spots, qkv_rows, tok), bf16),
            VMEM((spots, out_rows, tok), bf16),
            dma((5, 18, NZ)),
            dma((5, 14, NZ)),
            dma((8,)),
            dma((8,)),
            dma((4,)),
            dma((len(outs),)),
            dma((6,)),
            dma((6,)),
        ],
        compiler_params=pltpu.CompilerParams(
            collective_id=0, has_side_effects=True, vmem_limit_bytes=60 << 20
        ),
        cost_estimate=pl.CostEstimate(flops=flops, bytes_accessed=50 << 20, transcendentals=0),
        name="forward",
    )(x, cot, places, frequency, g_attn, g_q, g_k, g_ffn, s_qkv, s_out, s_down, s_gu)


SD0, SD1, SX0, SX1, SY0, SY1, SA, SB = range(8)


class PlaneSum:
    def plane_setup(self, pc, rd, rx, ry, send, recv):
        self.pc, self.rd, self.rx, self.ry, self.send, self.recv = pc, rd, rx, ry, send, recv

    def cp(self, src, dst, dev, k, s):
        return remote(src, dst, dev, self.send.at[k, s], self.recv.at[k, s])

    def d0(self, s):
        p = self.pc
        return self.cp(self.piece(s, 1 - p.y, 1 - p.x, 0), self.rd.at[s, 0], p.yn(), SD0, s)

    def d1(self, s):
        p = self.pc
        return self.cp(self.piece(s, 1 - p.y, 1 - p.x, 1), self.rd.at[s, 1], p.xn(), SD1, s)

    def x1(self, s):
        p = self.pc
        return self.cp(self.piece(s, p.y, 1 - p.x, 1), self.rx.at[s, 1], p.xn(), SX1, s)

    def y0(self, s):
        p = self.pc
        return self.cp(self.piece(s, 1 - p.y, p.x, 0), self.ry.at[s, 0], p.yn(), SY0, s)

    def x0(self, s):
        return self.cp(self.rd.at[s, 0], self.rx.at[s, 0], self.pc.xn(), SX0, s)

    def y1(self, s):
        return self.cp(self.rd.at[s, 1], self.ry.at[s, 1], self.pc.yn(), SY1, s)

    def plane_far(self, s):
        self.d0(s).start()
        self.d1(s).start()

    def plane_near(self, s):
        self.x1(s).start()
        self.y0(s).start()

    def plane_first(self, s):
        self.plane_far(s)
        self.plane_near(s)

    def plane_second(self, s):
        p = self.pc
        self.d0(s).wait_recv()
        self.rd[s, 0] = self.rd[s, 0] + self.piece(s, p.y, 1 - p.x, 0)[...]
        self.x0(s).start()
        self.d1(s).wait_recv()
        self.rd[s, 1] = self.rd[s, 1] + self.piece(s, 1 - p.y, p.x, 1)[...]
        self.y1(s).start()

    def plane_arrived(self, s):
        for c in (self.x1, self.y0, self.x0, self.y1):
            c(s).wait_recv()

    def plane_total(self, s, k):
        p = self.pc
        own = self.piece(s, p.y, p.x, k)[...].astype(f32)
        return own + self.rx[s, k].astype(f32) + self.ry[s, k].astype(f32)

    def plane_finish(self, s):
        for c in (self.d0, self.d1, self.x1, self.y0, self.x0, self.y1):
            c(s).wait_send()


class Scatter(PlaneSum):
    def __init__(self, pc, part, bufs, out, send, recv, some=None):
        rd, rx, ry, self.zz = bufs
        self.plane_setup(pc, rd, rx, ry, send, recv)
        self.part, self.out = part, out
        self.full, self.h = cuts(part.shape, some)

    @staticmethod
    def scratch(rows, columns, wide=True):
        shape = (2, rows // 2, columns) if wide else (2, rows, columns // 2)
        half = VMEM((NZ, *shape), bf16)
        return [half, half, half, VMEM((NZ + 1, *shape), bf16)]

    def piece(self, s, y, x, k):
        return self.part.at[(s, y, x, *self.h[k])]

    def down(self, zp):
        return self.cp(self.rx.at[zp], self.zz.at[zp], self.pc.down(), SA, zp)

    def up(self, zp):
        gap = zp - (self.pc.z + 1)
        spot = zp + (1 - (gap + NZ - 1) // NZ) * (NZ - zp)
        return self.cp(self.rx.at[zp], self.zz.at[spot], self.pc.up(), SB, zp)

    def far_event(self, i):
        self.plane_far(far(self.pc.z, i))

    def near_event(self, i):
        self.plane_near(far(self.pc.z, i))

    def d_event(self, i):
        self.plane_second(far(self.pc.z, i))

    def xy_event(self, i):
        zp = far(self.pc.z, i)
        self.plane_arrived(zp)
        for k in range(2):
            self.rx[zp, k] = self.plane_total(zp, k).astype(bf16)

    def z_event(self, i):
        z = self.pc.z
        zp = far(z, i)

        @pl.when(zp < z)
        def _():
            @pl.when(z < NZ - 1)
            def _():
                self.down(zp).wait_recv()
                self.rx[zp] = self.rx[zp] + self.zz[zp]

            self.down(zp).start()

        @pl.when(zp > z)
        def _():
            @pl.when(z > 0)
            def _():
                self.up(zp).wait_recv()
                self.rx[zp] = self.rx[zp] + self.zz[zp]

            self.up(zp).start()

    def final(self):
        z = self.pc.z
        self.plane_arrived(z)
        for k in range(2):
            self.out[self.h[k]] = self.plane_total(z, k)

        @pl.when(z < NZ - 1)
        def _():
            self.down(z).wait_recv()
            for k in range(2):
                self.out[self.h[k]] += self.zz[z, k].astype(f32)

        @pl.when(z > 0)
        def _():
            self.up(z).wait_recv()
            for k in range(2):
                self.out[self.h[k]] += self.zz[NZ, k].astype(f32)

    def finish(self):
        z = self.pc.z
        for zp in range(NZ):
            self.plane_finish(zp)

            @pl.when(zp < z)
            def _():
                self.down(zp).wait_send()

            @pl.when(zp > z)
            def _():
                self.up(zp).wait_send()


class ScatterZ(PlaneSum):
    def __init__(self, pc, part, bufs, out, send, recv, some=None):
        rd, rx, ry, self.zz, self.sm = bufs
        wide = some is None
        whole = pl.ds(0, self.sm.shape[-2])
        axis = self.sm.shape[-2 if wide else -1]
        self.inner = [(h,) if wide else (whole, h) for h in halves(axis)]
        self.plane_setup(pc, rd, rx, ry, send, recv)
        self.part, self.out = part, out
        self.full, self.h = cuts(part.shape, some)

    @staticmethod
    def scratch(rows, columns, wide=True):
        half = VMEM((1, 2, rows // 2, columns) if wide else (1, 2, rows, columns // 2), bf16)
        return [half, half, half, VMEM((NZ + 1, 4, rows, columns), bf16), VMEM((4, rows, columns), bf16)]

    def piece(self, s, y, x, k):
        return self.sm.at[(y * 2 + x, *self.inner[k])]

    def down(self, zp, k, src):
        return self.cp(src, self.zz.at[zp, k], self.pc.down(), 8 + zp, k)

    def up(self, zp, k, src):
        gap = zp - (self.pc.z + 1)
        spot = zp + (1 - (gap + NZ - 1) // NZ) * (NZ - zp)
        return self.cp(src, self.zz.at[spot, k], self.pc.up(), 12 + zp, k)

    def first(self, i):
        z = self.pc.z
        zp = far(z, i)
        for k in range(4):
            src = self.part.at[(zp, k // 2, k % 2, *self.full)]

            @pl.when((z == NZ - 1) & (zp < z))
            def _():
                self.down(zp, k, src).start()

            @pl.when((z == 0) & (zp > z))
            def _():
                self.up(zp, k, src).start()

    def z_event(self, i, k):
        z = self.pc.z
        zp = far(z, i)
        held = self.zz.at[zp, k]

        @pl.when((zp < z) & (z < NZ - 1))
        def _():
            self.down(zp, k, held).wait_recv()
            self.zz[zp, k] = self.zz[zp, k] + self.part[(zp, k // 2, k % 2, *self.full)]
            self.down(zp, k, held).start()

        @pl.when((zp > z) & (z > 0))
        def _():
            self.up(zp, k, held).wait_recv()
            self.zz[zp, k] = self.zz[zp, k] + self.part[(zp, k // 2, k % 2, *self.full)]
            self.up(zp, k, held).start()

    def own_event(self, k):
        z = self.pc.z

        @pl.when(z < NZ - 1)
        def _():
            self.down(z, k, self.zz.at[z, k]).wait_recv()

        @pl.when(z > 0)
        def _():
            self.up(z, k, self.zz.at[z, k]).wait_recv()

        own = self.part[(z, k // 2, k % 2, *self.full)].astype(f32)

        @pl.when(z == 0)
        def _():
            self.sm[k] = (own + self.zz[z, k].astype(f32)).astype(bf16)

        @pl.when(z == NZ - 1)
        def _():
            self.sm[k] = (own + self.zz[NZ, k].astype(f32)).astype(bf16)

        @pl.when((z > 0) & (z < NZ - 1))
        def _():
            both = self.zz[z, k].astype(f32) + self.zz[NZ, k].astype(f32)
            self.sm[k] = (own + both).astype(bf16)

    def plane_send(self):
        self.plane_first(0)

    def plane_event(self):
        self.plane_second(0)

    def final(self):
        self.plane_arrived(0)
        for k in range(2):
            self.out[self.h[k]] = self.plane_total(0, k)

    def finish(self):
        z = self.pc.z
        self.plane_finish(0)
        for zp in range(NZ):
            for k in range(4):

                @pl.when(zp < z)
                def _():
                    self.down(zp, k, self.zz.at[zp, k]).wait_send()

                @pl.when(zp > z)
                def _():
                    self.up(zp, k, self.zz.at[zp, k]).wait_send()


class SequenceSum(PlaneSum):
    def __init__(self, pc, terms, bufs, send, recv, core_send, core_recv):
        rd, rx, ry, self.theirs = bufs
        self.plane_setup(pc, rd, rx, ry, send, recv)
        self.terms, self.core_send, self.core_recv = terms, core_send, core_recv
        self.h = halves(terms.shape[-2])

    @staticmethod
    def scratch(rows, columns):
        half = VMEM((1, 2, rows // 2, columns), bf16)
        return [half, half, half, VMEM((2, 2, rows, columns), bf16)]

    def piece(self, s, y, x, k):
        return self.theirs.at[y, x, self.h[k]]

    def swap(self):
        p = self.pc
        return remote(
            self.terms.at[:, :, 1 - p.core], self.theirs, p.sn(), self.core_send, self.core_recv
        )

    def core_event(self):
        p = self.pc
        self.swap().wait_recv()
        for y in range(2):
            for x in range(2):
                self.theirs[y, x] = self.theirs[y, x] + self.terms[y, x, p.core]
        self.plane_first(0)

    def finish(self):
        self.swap().wait_send()
        self.plane_finish(0)


def norm_back(src, gain, grad, part_ref, part_row, emit):
    part_ref[pl.ds(part_row, 1), :] = jnp.zeros((1, part_ref.shape[1]), f32)

    def body(i, _):
        rows = pl.ds(pl.multiple_of(i * 32, 32), 32)
        v, g = src[rows, :].astype(f32), grad[rows, :]
        inv = lax.rsqrt(jnp.mean(v * v, axis=-1, keepdims=True) + EPS)
        unit = v * inv
        part_ref[pl.ds(part_row, 1), :] += jnp.sum(g * unit, axis=0, keepdims=True)
        gg = g * gain[...]
        emit(rows, inv * (gg - unit * jnp.mean(gg * unit, axis=-1, keepdims=True)))
        return 0

    lax.fori_loop(0, grad.shape[0] // 32, body, 0)


def sum_steps(first, g):
    part = functools.partial
    steps = {first: g.final}
    for i in range(NZ):
        steps[first + 1 + i] = part(g.far_event, i)
        steps[first + 5 + i] = part(g.near_event, i)
        steps[first + 9 + i] = part(g.d_event, i)
        if i < NZ - 1:
            steps[first + 13 + i] = part(g.xy_event, i)
            steps[first + 17 + i] = part(g.z_event, i)
    return steps


def weight_grad(left, zp, right, part):
    rows, columns = part.shape[-2:]
    lhs = left[pl.ds(zp * 4, 4)].reshape(4 * rows, left.shape[-1])
    step = 512

    def body(n, _):
        c = cols(n, step)
        part[zp, :, :, :, c] = dot(lhs, right[:, c]).astype(bf16).reshape(2, 2, rows, step)
        return 0

    lax.fori_loop(0, columns // step, body, 0)


LOADS = [
    "act", "cot", "ffn", "ggu", "wgu", "res", "mix", "mixf", "linv", "q2", "kk", "va", "mask",
    "qkv", "wout", "attn", "wqkv", "x",
]


def backward_kernel(dims, *refs):
    (tok, width, n_dev, heads_w, kv_w, ff) = dims
    (
        cos_ref, sin_ref, g_attn, one_q, one_k, g_ffn,
        i_x, i_tattn, i_tmix, i_tffn, i_tact, i_cot, i_ggu, i_qkv, i_q2, i_linv, i_mixf, i_res,
        i_kk, i_va, i_mask, i_wqkv, i_wout, i_wgu,
        o_dx, o_attn, o_q, o_k, o_ffn, out_wqkv, out_wout, out_wgu, out_wdown,
        t_ffn, t_act, cot2, ggu2, qkv, q2, linv, kk, va, mask_t, w_gu,
        part_qkv, part_out, part_gu, part_down, res, gains, came, gh, gattn2, acc_q,
        aug, gm, terms,
        send, recv, kv_send, kv_recv, ex_send, ex_recv, g_send, g_recv, lsem,
    ) = refs[:66]
    bufs = refs[66:]
    g_q, g_k = twice(one_q), twice(one_k)
    pc = Place()
    z = pc.z
    part = functools.partial
    loads = {}

    def load(name, src, dst):
        def copy():
            return pltpu.make_async_copy(src(), dst(), lsem.at[LOADS.index(name)])

        loads[name] = lambda: copy().wait()
        copy().start()

    load("act", lambda: i_tact, lambda: t_act)
    load("cot", lambda: i_cot, lambda: cot2)
    load("ffn", lambda: i_tffn, lambda: t_ffn)
    load("ggu", lambda: i_ggu, lambda: ggu2)
    load("wgu", lambda: i_wgu, lambda: w_gu)
    load("res", lambda: i_res, lambda: res)
    load("linv", lambda: i_linv, lambda: linv)
    load("q2", lambda: i_q2, lambda: q2)
    load("kk", lambda: i_kk, lambda: kk)
    load("va", lambda: i_va, lambda: va)
    load("mask", lambda: i_mask, lambda: mask_t)
    load("qkv", lambda: i_qkv, lambda: qkv)
    bar = pltpu.get_barrier_semaphore()
    for device in (pc.xn(), pc.yn(), pc.sn()):
        pl.semaphore_signal(bar, inc=1, device_id=device, device_id_type=MESH)
    for k in range(1, NZ):
        there = pc.at(z=(z + k) % NZ)
        pl.semaphore_signal(bar, inc=1, device_id=there, device_id_type=MESH)
    pl.semaphore_wait(bar, 3 + NZ - 1)
    cut = part_down.shape[-2] // 2
    down = Scatter(pc, part_down, bufs[0:4], out_wdown, send.at[0], recv.at[0], pl.ds(0, cut))
    rest = ScatterZ(pc, part_down, bufs[21:26], out_wdown, send.at[4], recv.at[4], pl.ds(cut, cut))
    gateup = Scatter(pc, part_gu, bufs[4:8], out_wgu, send.at[1], recv.at[1])
    out = ScatterZ(pc, part_out, bufs[8:13], out_wout, send.at[2], recv.at[2])
    last = Scatter(pc, part_qkv, bufs[17:21], out_wqkv, send.at[3], recv.at[3])
    seq = SequenceSum(pc, terms, bufs[13:17], kv_send, kv_recv, ex_send.at[2], ex_recv.at[2])

    own = pl.ds(0, tok)
    back = pl.ds(tok, tok)

    def rows_of(left, right, term, names, i):
        for name in names:
            if name in loads:
                loads.pop(name)()
        weight_grad(left, far(z, i), right, term)

    def h_step(n):
        w = w_gu[n // 2, n % 2].reshape(width // 8, 2 * ff)
        gh[:, cols(n, width // 8)] = dot_t(ggu2[own, :], w)

    def start_h():
        loads.pop("wgu")()
        loads.pop("res")()

    def keep_residual(rows, grad):
        total = cot2[rows, :].astype(f32) + grad
        res[rows, :] = total
        gattn2[rows, :] = total.astype(bf16)

    sent_attn = remote(gattn2.at[own, :], gattn2.at[back, :], pc.sn(), ex_send.at[0], ex_recv.at[0])

    def residual_back():
        load("wout", lambda: i_wout, lambda: w_gu.at[:, :, :, :, pl.ds(0, part_out.shape[-2]), :])
        gains[...] = jnp.zeros_like(gains)
        norm_back(res, g_ffn, gh, gains, 1, keep_residual)
        load("mixf", lambda: i_mixf, lambda: gh.at[:, pl.ds(heads_w, heads_w)])
        sent_attn.start()
        loads.pop("wout")()

    columns = part_qkv.shape[-1]
    some = pl.ds(0, columns)

    def load_mix():
        load("mix", lambda: i_tmix, lambda: t_act)

    def load_last():
        load("attn", lambda: i_tattn, lambda: t_ffn)
        load("wqkv", lambda: i_wqkv, lambda: w_gu.at[:, :, :, :, :, some])
        load("x", lambda: i_x, lambda: cot2.at[own, :])

    def m_step(n, _):
        w = w_gu[n, :, :, :, pl.ds(0, part_out.shape[-2]), :].reshape(heads_w // NZ, width)
        gm[:, cols(n, heads_w // NZ)] = dot_t(gattn2[own, :], w).astype(bf16)
        return 0

    def mixed_back():
        lax.fori_loop(0, NZ, m_step, 0)
        sent_attn.wait()

    def start_attention():
        for name in ("mixf", "linv", "q2", "kk", "va", "mask", "qkv"):
            loads.pop(name)()

    low = lanes((tok, 128)) < 64
    chunk = 512
    n_chunk = n_dev * tok // chunk
    def attend(tick):
        g, kc = tick // n_chunk, tick % n_chunk
        rows = pl.ds(pl.multiple_of(kc * chunk, chunk), chunk)

        @pl.when(kc == 0)
        def _():
            lane = lanes((tok, 128))
            for k in range(2):
                c = cols(2 * g + k, 128)
                grad = gm[:, c].astype(f32)
                mixed = gh[:, cols(2 * g + k + heads_w // 128, 128)]
                delta = head_sums(grad * mixed) * linv[:, c]
                grad = grad * linv[:, c]
                for half in range(2):
                    d = roll_half(delta) if half == 0 else delta
                    v = grad if half == 0 else roll_half(grad)
                    high = d.astype(bf16).astype(f32)
                    rest = jnp.where(lane == 64, -high, jnp.where(lane == 65, high - d, 0.0))
                    aug[pl.ds((2 * k + half) * tok, tok), :] = jnp.where(low, v, rest).astype(bf16)

        q = q2[pl.ds(2 * g, 2)].reshape(4 * tok, 128)
        seen = mask_t[rows, :]
        e = jnp.exp2(dot_t(kk[g, rows, :], q) * LOG2E).astype(bf16)
        e = e * jnp.concatenate([seen] * 4, axis=1)
        ds = e * dot_t(va[g, rows, :], aug[...]).astype(bf16)
        dv = dot(e, aug[...])
        dk = dot(ds, q)
        dq = lax.dot_general(kk[g, rows, :], ds, (((0,), (0,)), ((), ())), preferred_element_type=f32)
        dk = dk + roll_half(dk)
        lower = lanes((chunk, 128)) < 64
        dv = jnp.where(lower, dv, roll_half(dv))
        mine = (lanes((chunk, 128)) // 64) == (g % 2)
        for b in range(chunk // tok):
            spot = kc * (chunk // tok) + b
            y, x, c = spot // 4, (spot // 2) % 2, spot % 2
            cut = slice(b * tok, (b + 1) * tok)
            for base, value in ((0, dk), (kv_w, dv)):
                place = pl.ds(pl.multiple_of(base + (g // 2) * 128, 128), 128)
                old = terms[y, x, c, :, place].astype(f32)
                terms[y, x, c, :, place] = jnp.where(mine[cut], value[cut], old).astype(bf16)

        @pl.when(kc == 0)
        def _():
            acc_q[...] = dq

        @pl.when(kc > 0)
        def _():
            acc_q[...] += dq

        @pl.when(kc == n_chunk - 1)
        def _():
            turned = jnp.transpose(acc_q[...])
            for k in range(2):
                even, odd = [turned[(2 * k + h) * tok : (2 * k + h + 1) * tok] for h in range(2)]
                gh[:, cols(2 * g + k, 128)] = jnp.where(low, even, odd) * 0.125

    def head_back(t, grad, gain, row):
        c = cols(t, 128)
        u = qkv[:, c]
        inv = lax.rsqrt(head_sums(u * u) * (1.0 / 64) + EPS)
        unit = u * inv
        grad = grad * cos_ref[...] - swap_rot(grad) * sin_ref[...]
        gains[pl.ds(row, 1), pl.ds(0, 128)] += jnp.sum(grad * unit, axis=0, keepdims=True)
        gg = grad * gain
        gattn2[own, c] = (inv * (gg - unit * head_sums(gg * unit) * (1.0 / 64))).astype(bf16)

    def query_back(t):
        head_back(t, gh[:, cols(t, 128)], g_q, 2)

    sent_qkv = remote(gattn2.at[own, some], gattn2.at[back, some], pc.sn(), ex_send.at[1], ex_recv.at[1])

    def keys_back():
        seq.plane_arrived(0)
        for k in range(2):
            gh[seq.h[k], pl.ds(0, 2 * kv_w)] = seq.plane_total(0, k)
        for t in range(kv_w // 128):
            head_back(heads_w // 128 + t, gh[:, pl.ds(t * 128, 128)], g_k, 3)
        gattn2[own, pl.ds(heads_w + kv_w, kv_w)] = gh[:, pl.ds(kv_w, kv_w)].astype(bf16)
        sent_qkv.start()

    def g_step(n):
        w = w_gu[n // 2, n % 2, :, :, :, some].reshape(width // 8, columns)
        gh[:, cols(n, width // 8)] = dot_t(gattn2[own, some], w)

    def keep_input(rows, grad):
        cot2[pl.ds(rows.start + tok, rows.size), :] = (res[rows, :] + grad).astype(bf16)

    sent_dx = pltpu.make_async_copy(cot2.at[back, :], o_dx, lsem.at[len(LOADS)])

    def input_back():
        loads.pop("x")()
        norm_back(cot2, g_attn, gh, gains, 0, keep_input)
        sent_dx.start()

    def start_g():
        loads.pop("wqkv")()

    def hop(k):
        device = (pc.sn(), pc.xn(), pc.yn())[k]
        return remote(gains, came.at[k], device, g_send.at[k], g_recv.at[k])

    def hop_end(k):
        hop(k).wait()
        gains[...] += came[k]

    def ring(k):
        there = pc.at(z=(z + k) % NZ)
        return remote(gains, came.at[3 + z], there, g_send.at[2 + k], g_recv.at[3 + z])

    def ring_start():
        came[3 + z] = gains[...]
        for k in range(1, NZ):
            ring(k).start()

    def ring_end():
        for k in range(1, NZ):
            there = (z + k) % NZ
            slot = came.at[3 + there]
            remote(gains, slot, pc.at(z=there), g_send.at[2 + k], g_recv.at[3 + there]).wait_recv()
        total = came[3]
        for k in range(1, NZ):
            total = total + came[3 + k]
        o_attn[...] = total[0:1]
        o_ffn[...] = total[1:2]
        for o, row in ((o_q, 2), (o_k, 3)):
            v = total[:, :128]
            o[...] = (v + roll_half(v))[row : row + 1, :64]

    steps = {
        b_h: start_h, b_nb: residual_back, b_m: mixed_back, b_att: start_attention,
        b_kvs: seq.swap().start, b_kvc: seq.core_event, b_kve: part(seq.plane_second, 0),
        b_kvf: keys_back, b_oS: out.plane_send, b_oe: out.plane_event, b_of: out.final, b_kS: rest.plane_send,
        b_ke: rest.plane_event, b_kf: rest.final,
        b_lm: load_mix, b_ll: load_last, b_qe: sent_qkv.wait_recv, b_g: start_g,
        b_nb2: input_back, b_rs: ring_start, b_re: ring_end,
    }
    steps.update(sum_steps(b_qf, last))
    steps.update(sum_steps(b_df, down))
    steps.update(sum_steps(b_gf, gateup))
    for i in range(NZ):
        steps[b_dw0 + i] = part(rows_of, t_act, cot2, part_down, ("act", "cot"), i)
        steps[b_gw0 + i] = part(rows_of, t_ffn, ggu2, part_gu, ("ffn", "ggu"), i)
        steps[b_ow0 + i] = part(rows_of, t_act, gattn2, part_out, ("mix",), i)
        steps[b_qw0 + i] = part(rows_of, t_ffn, gattn2, part_qkv, ("attn",), i)
        steps[b_oa0 + i] = part(out.first, i)
        steps[b_oo0 + i] = part(out.own_event, i)
        steps[b_ka0 + i] = part(rest.first, i)
        steps[b_ko0 + i] = part(rest.own_event, i)
        if i < NZ - 1:
            for k in range(4):
                steps[b_oz00 + 4 * i + k] = part(out.z_event, i, k)
                steps[b_kz00 + 4 * i + k] = part(rest.z_event, i, k)
            steps[b_hs0 + i] = hop(i).start
            steps[b_he0 + i] = part(hop_end, i)
    loops = {
        b_H: (8, h_step),
        b_B: (GROUPS * n_chunk, attend),
        b_Q: (heads_w // 128, query_back),
        b_G: (8, g_step),
    }
    run_steps(BACKWARD_ORDER, steps, loops)
    for g in (down, rest, gateup, out, seq, last):
        g.finish()
    sent_qkv.wait_send()
    for k in range(1, NZ):
        ring(k).wait_send()
    sent_dx.wait()


def backward(x, g_attn, g_q, g_k, g_ffn, kept, rows, n_dev):
    (t_attn, t_mix, t_ffn, t_act, cot2, ggu2, qkv, q2, linv, mixf, res, kk, va, mask_t, w_qkv, w_out, w_gu, cosine, sine) = kept
    tok, width = x.shape
    heads_w, kv_w = HEADS * HEAD_DIM, GROUPS * HEAD_DIM
    ff = ggu2.shape[1] // 2
    length = n_dev * tok
    columns = qkv.shape[1]
    dims = (tok, width, n_dev, heads_w, kv_w, ff)
    shape = jax.ShapeDtypeStruct
    vm = pl.BlockSpec(memory_space=VMEM)
    anyw = pl.BlockSpec(memory_space=pl.ANY)
    dma = pltpu.SemaphoreType.DMA
    r_qkv, r_out, r_gu, r_down = rows
    partial = [
        VMEM((NZ, 2, 2, r, c), bf16)
        for r, c in ((r_qkv, columns), (r_out, width), (r_gu, width), (r_down, width))
    ]
    like = [
        VMEM(v.shape, v.dtype)
        for v in (t_ffn, t_act, cot2, ggu2, qkv, q2, linv, kk, va, mask_t, w_gu)
    ]
    return pl.pallas_call(
        functools.partial(backward_kernel, dims),
        out_shape=[
            shape((tok, width), bf16),
            shape((1, width), f32),
            shape((1, 64), f32),
            shape((1, 64), f32),
            shape((1, width), f32),
            shape((r_qkv, columns), f32),
            shape((r_out, width), f32),
            shape((r_gu, width), f32),
            shape((r_down, width), f32),
        ],
        in_specs=[vm] * 6 + [anyw] * 18,
        out_specs=[anyw] + [vm] * 8,
        scratch_shapes=like
        + partial
        + [
            VMEM((tok, width), f32),
            VMEM((8, width), f32),
            VMEM((3 + NZ, 8, width), f32),
            VMEM((tok, width), f32),
            VMEM((2 * tok, width), bf16),
            VMEM((128, 4 * tok), f32),
            VMEM((4 * tok, 128), bf16),
            VMEM((tok, heads_w), bf16),
            VMEM((2, 2, 2, tok, 2 * kv_w), bf16),
            dma((5, 16, NZ)),
            dma((5, 16, NZ)),
            dma((8, 1)),
            dma((8, 1)),
            dma((3,)),
            dma((3,)),
            dma((3 + NZ,)),
            dma((3 + NZ,)),
            dma((len(LOADS) + 1,)),
        ]
        + Scatter.scratch(r_down // 2, width, False)
        + Scatter.scratch(r_gu, width)
        + ScatterZ.scratch(r_out, width)
        + SequenceSum.scratch(tok, 2 * kv_w)
        + Scatter.scratch(r_qkv, columns)
        + ScatterZ.scratch(r_down // 2, width, False),
        compiler_params=pltpu.CompilerParams(
            collective_id=1, has_side_effects=True, vmem_limit_bytes=64 << 20
        ),
        cost_estimate=pl.CostEstimate(
            flops=20 * tok * width * width, bytes_accessed=60 << 20, transcendentals=0
        ),
        name="backward",
    )(
        cosine, sine, g_attn, g_q, g_k, g_ffn, x, t_attn, t_mix, t_ffn, t_act, cot2, ggu2, qkv, q2,
        linv, mixf, res, kk, va, mask_t, w_qkv, w_out, w_gu,
    )


def settle_kernel(count, *refs):
    copies = [
        pltpu.make_async_copy(a, b, refs[-1].at[k])
        for k, (a, b) in enumerate(zip(refs[:count], refs[count : 2 * count]))
    ]
    for c in copies:
        c.start()
    for c in copies:
        c.wait()


def settle(arrays):
    count = len(arrays)
    anyw = pl.BlockSpec(memory_space=pl.ANY)
    return pl.pallas_call(
        functools.partial(settle_kernel, count),
        out_shape=[jax.ShapeDtypeStruct(a.shape, a.dtype) for a in arrays],
        in_specs=[pl.BlockSpec(memory_space=VMEM)] * count,
        out_specs=[anyw] * count,
        scratch_shapes=[pltpu.SemaphoreType.DMA((count,))],
        name="settle",
    )(*arrays)


epsilon = 1e-06


def norm_rows(values, gain_vec):
    return (
        values * lax.rsqrt(jnp.mean(values * values, axis=-1, keepdims=True) + epsilon) * gain_vec
    )


def rotate(values, positions):
    half_dim = values.shape[-1] // 2
    frequency = jnp.exp(
        jnp.arange(half_dim).astype(jnp.float32) * (-2.0 * math.log(10000.0) / values.shape[-1])
    )
    angles = positions.astype(jnp.float32)[:, None] * frequency[None, :]
    cosine = jnp.cos(angles)[:, None, :]
    sine = jnp.sin(angles)[:, None, :]
    first = values[..., :half_dim]
    second = values[..., half_dim:]
    return jnp.concatenate(
        [first * cosine - second * sine, second * cosine + first * sine], axis=-1
    )


def project_heads(qkv_all, positions, q_gain, k_gain):
    tok_rows = qkv_all.shape[0]
    q_cols = HEADS * HEAD_DIM
    k_cols = GROUPS * HEAD_DIM
    queries = qkv_all[:, :q_cols].reshape(tok_rows, HEADS, HEAD_DIM)
    keys_raw = qkv_all[:, q_cols : q_cols + k_cols].reshape(tok_rows, GROUPS, HEAD_DIM)
    values = qkv_all[:, q_cols + k_cols :].reshape(tok_rows, GROUPS, HEAD_DIM)
    return (
        rotate(norm_rows(queries, q_gain), positions),
        rotate(norm_rows(keys_raw, k_gain), positions),
        values,
    )


def gated(gate_up):
    return jax.nn.silu(gate_up[:, :FF]) * gate_up[:, FF:]


def per_device_plain(
    inputs, places, cotangent, attn_gain, w_qkv, q_gain, k_gain, w_out, ffn_gain, w_gateup, w_down
):
    tok_rows = inputs.shape[1]
    repeat = HEADS // GROUPS
    score_scale = HEAD_DIM ** (-0.5)
    here_f = inputs[0].astype(jnp.float32)
    own_places = places[0]
    qkv_w, out_w = (
        lax.all_gather(w_qkv, ("dp", "ctx"), axis=0, tiled=True),
        lax.all_gather(w_out, ("dp", "ctx"), axis=0, tiled=True),
    )
    h_attn_f, pull_attn = jax.vjp(norm_rows, here_f, attn_gain)
    h_attn = h_attn_f.astype(jnp.bfloat16)
    qkv_all = jnp.dot(h_attn, qkv_w, preferred_element_type=jnp.float32)

    def heads_of(qkv_in, gain_q, gain_k):
        return project_heads(qkv_in, own_places, gain_q, gain_k)

    (queries, keys_f, values), pull_heads = jax.vjp(heads_of, qkv_all, q_gain, k_gain)
    query_b = queries.astype(jnp.bfloat16).reshape(tok_rows, GROUPS, repeat, HEAD_DIM)
    key_b = keys_f.astype(jnp.bfloat16)
    value_b = values.astype(jnp.bfloat16)
    all_keys, all_values = (
        lax.all_gather(key_b, "ctx", axis=0, tiled=True),
        lax.all_gather(value_b, "ctx", axis=0, tiled=True),
    )
    all_places = lax.all_gather(own_places, "ctx", axis=0, tiled=True)
    blocks = lax.axis_size("ctx")
    key_blocks = all_keys.reshape(blocks, tok_rows, GROUPS, HEAD_DIM)
    value_blocks = all_values.reshape(blocks, tok_rows, GROUPS, HEAD_DIM)
    place_blocks = all_places.reshape(blocks, tok_rows)

    def score_block(key_blk, place_blk):
        scores = (
            jnp.einsum("igrd,jgd->grij", query_b, key_blk, preferred_element_type=jnp.float32)
            * score_scale
        )
        allowed = place_blk[None, :] <= own_places[:, None]
        return (scores, allowed)

    def max_step(state_pair, entries):
        row_top, row_total = state_pair
        scores, allowed = score_block(entries[0], entries[1])
        scores = jnp.where(allowed, scores, -1e30)
        new_top = jnp.maximum(row_top, jnp.max(scores, axis=-1))
        row_total = row_total * jnp.exp(row_top - new_top) + jnp.sum(
            jnp.where(allowed, jnp.exp(scores - new_top[..., None]), 0.0), axis=-1
        )
        return ((new_top, row_total), None)

    start_pair = (
        jnp.full((GROUPS, repeat, tok_rows), -1e30, jnp.float32),
        jnp.zeros((GROUPS, repeat, tok_rows), jnp.float32),
    )
    (row_top, row_total), _ = lax.scan(max_step, start_pair, (key_blocks, place_blocks))
    log_total = row_top + jnp.log(row_total)

    def out_step(accum, entries):
        scores, allowed = score_block(entries[0], entries[1])
        weights_b = jnp.where(allowed, jnp.exp(scores - log_total[..., None]), 0.0).astype(
            jnp.bfloat16
        )
        return (
            accum
            + jnp.einsum(
                "grij,jgd->igrd", weights_b, entries[2], preferred_element_type=jnp.float32
            ),
            None,
        )

    mixed_f, _ = lax.scan(
        out_step,
        jnp.zeros((tok_rows, GROUPS, repeat, HEAD_DIM), jnp.float32),
        (key_blocks, place_blocks, value_blocks),
    )
    mixed_b = mixed_f.reshape(tok_rows, HEADS * HEAD_DIM).astype(jnp.bfloat16)
    attn_out = jnp.dot(mixed_b, out_w, preferred_element_type=jnp.float32)
    residual = here_f + attn_out
    gateup_w, down_w = (
        lax.all_gather(w_gateup, ("dp", "ctx"), axis=0, tiled=True),
        lax.all_gather(w_down, ("dp", "ctx"), axis=0, tiled=True),
    )
    h_ffn_f, pull_ffn = jax.vjp(norm_rows, residual, ffn_gain)
    h_ffn = h_ffn_f.astype(jnp.bfloat16)
    gate_up = jnp.dot(h_ffn, gateup_w, preferred_element_type=jnp.float32)
    act_f, pull_gate = jax.vjp(gated, gate_up)
    act_b = act_f.astype(jnp.bfloat16)
    result = residual + jnp.dot(act_b, down_w, preferred_element_type=jnp.float32)
    layer_output = result.astype(jnp.bfloat16)[None]
    gateup_w, down_w = (
        lax.all_gather(w_gateup, ("dp", "ctx"), axis=0, tiled=True),
        lax.all_gather(w_down, ("dp", "ctx"), axis=0, tiled=True),
    )
    grad_out = cotangent[0]
    grad_act = jnp.dot(grad_out, down_w.T, preferred_element_type=jnp.float32)
    grad_down = jnp.dot(act_b.T, grad_out, preferred_element_type=jnp.float32)
    grad_gu_b = pull_gate(grad_act)[0].astype(jnp.bfloat16)
    grad_gateup = jnp.dot(h_ffn.T, grad_gu_b, preferred_element_type=jnp.float32)
    grad_h_ffn = jnp.dot(grad_gu_b, gateup_w.T, preferred_element_type=jnp.float32)
    grad_resid_part, grad_ffn_gain = pull_ffn(grad_h_ffn)
    grad_residual = grad_out.astype(jnp.float32) + grad_resid_part
    grad_gateup_own, grad_down_own = (
        lax.psum_scatter(grad_gateup, ("dp", "ctx"), scatter_dimension=0, tiled=True),
        lax.psum_scatter(grad_down, ("dp", "ctx"), scatter_dimension=0, tiled=True),
    )
    qkv_w, out_w = (
        lax.all_gather(w_qkv, ("dp", "ctx"), axis=0, tiled=True),
        lax.all_gather(w_out, ("dp", "ctx"), axis=0, tiled=True),
    )
    grad_attn_b = grad_residual.astype(jnp.bfloat16)
    grad_out_w = jnp.dot(mixed_b.T, grad_attn_b, preferred_element_type=jnp.float32)
    grad_mixed_b = (
        jnp.dot(grad_attn_b, out_w.T, preferred_element_type=jnp.float32)
        .astype(jnp.bfloat16)
        .reshape(tok_rows, GROUPS, repeat, HEAD_DIM)
    )
    row_delta = jnp.transpose(
        jnp.sum(grad_mixed_b.astype(jnp.float32) * mixed_f, axis=-1), (1, 2, 0)
    )

    def back_step(grad_query, entries):
        key_blk, place_blk, value_blk = entries
        scores, allowed = score_block(key_blk, place_blk)
        weights_f = jnp.where(allowed, jnp.exp(scores - log_total[..., None]), 0.0)
        weights_b = weights_f.astype(jnp.bfloat16)
        grad_value = jnp.einsum(
            "grij,igrd->jgd", weights_b, grad_mixed_b, preferred_element_type=jnp.float32
        )
        grad_prob = jnp.einsum(
            "igrd,jgd->grij", grad_mixed_b, value_blk, preferred_element_type=jnp.float32
        )
        grad_score = (weights_f * (grad_prob - row_delta[..., None])).astype(jnp.bfloat16)
        grad_query = grad_query + jnp.einsum(
            "grij,jgd->igrd", grad_score, key_blk, preferred_element_type=jnp.float32
        )
        grad_key = (
            jnp.einsum("grij,igrd->jgd", grad_score, query_b, preferred_element_type=jnp.float32)
            * score_scale
        )
        return (
            grad_query,
            jnp.concatenate(
                [
                    grad_key.reshape(tok_rows, GROUPS * HEAD_DIM),
                    grad_value.reshape(tok_rows, GROUPS * HEAD_DIM),
                ],
                axis=1,
            ),
        )

    grad_query, kv_terms = lax.scan(
        back_step,
        jnp.zeros((tok_rows, GROUPS, repeat, HEAD_DIM), jnp.float32),
        (key_blocks, place_blocks, value_blocks),
    )
    grad_query = grad_query * score_scale
    kv_own = lax.psum_scatter(
        kv_terms.reshape(blocks * tok_rows, 2 * GROUPS * HEAD_DIM).astype(jnp.bfloat16),
        "ctx",
        scatter_dimension=0,
        tiled=True,
    ).astype(jnp.float32)
    grad_key_own = kv_own[:, : GROUPS * HEAD_DIM].reshape(tok_rows, GROUPS, HEAD_DIM)
    grad_value_own = kv_own[:, GROUPS * HEAD_DIM :].reshape(tok_rows, GROUPS, HEAD_DIM)
    grad_qkv_f, grad_q_gain, grad_k_gain = pull_heads(
        (grad_query.reshape(tok_rows, HEADS, HEAD_DIM), grad_key_own, grad_value_own)
    )
    grad_qkv_b = grad_qkv_f.astype(jnp.bfloat16)
    grad_qkv_w = jnp.dot(h_attn.T, grad_qkv_b, preferred_element_type=jnp.float32)
    grad_h_attn = jnp.dot(grad_qkv_b, qkv_w.T, preferred_element_type=jnp.float32)
    grad_here_part, grad_attn_gain = pull_attn(grad_h_attn)
    grad_inputs = (grad_residual + grad_here_part).astype(jnp.bfloat16)[None]
    grad_qkv_own, grad_out_own = (
        lax.psum_scatter(grad_qkv_w, ("dp", "ctx"), scatter_dimension=0, tiled=True),
        lax.psum_scatter(grad_out_w, ("dp", "ctx"), scatter_dimension=0, tiled=True),
    )
    gain_attn, gain_query, gain_key, gain_ffn = lax.psum(
        (grad_attn_gain, grad_q_gain, grad_k_gain, grad_ffn_gain), ("dp", "ctx")
    )
    return (
        layer_output,
        grad_inputs,
        gain_attn,
        grad_qkv_own,
        gain_query,
        gain_key,
        grad_out_own,
        gain_ffn,
        grad_gateup_own,
        grad_down_own,
    )


def per_device_fast(
    inputs, places, cotangent, attn_gain, w_qkv, q_gain, k_gain, w_out, ffn_gain, w_gateup, w_down
):
    n_dev = lax.axis_size("ctx")
    half = HEAD_DIM // 2
    spot = np.arange(128) % half
    step = np.float32(-2.0 * math.log(10000.0) / HEAD_DIM)
    frequency = np.exp(spot.astype(np.float32) * step).astype(np.float32)[None]
    gain_q, gain_k = q_gain[None], k_gain[None]
    layer_output, *kept = forward(
        inputs[0], cotangent[0], places, frequency, attn_gain[None], gain_q, gain_k,
        ffn_gain[None], w_qkv, w_out, w_down, w_gateup, n_dev,
    )
    rows = [w.shape[0] for w in (w_qkv, w_out, w_gateup, w_down)]
    grads = backward(inputs[0], attn_gain[None], gain_q, gain_k, ffn_gain[None], kept, rows, n_dev)
    layer_output, dx, g_attn, g_q, g_k, g_ffn, d_qkv, d_out, d_gu, d_down = settle(
        [layer_output, *grads]
    )
    return (
        layer_output[None], dx[None], g_attn[0], d_qkv, g_q[0], g_k[0], d_out, g_ffn[0], d_gu, d_down
    )


def solution(mesh):
    in_specs = (
        P("dp", "ctx", None),
        P("dp", "ctx"),
        P("dp", "ctx", None),
        P(),
        P(("dp", "ctx"), None),
        P(),
        P(),
        P(("dp", "ctx"), None),
        P(),
        P(("dp", "ctx"), None),
        P(("dp", "ctx"), None),
    )
    out_specs = (
        P("dp", "ctx", None),
        P("dp", "ctx", None),
        P(),
        P(("dp", "ctx"), None),
        P(),
        P(),
        P(("dp", "ctx"), None),
        P(),
        P(("dp", "ctx"), None),
        P(("dp", "ctx"), None),
    )
    fast = dict(mesh.shape) == {"dp": 4, "ctx": 8}
    per_device = per_device_fast if fast else per_device_plain
    return jax.shard_map(
        per_device, mesh=mesh, in_specs=in_specs, out_specs=out_specs, check_vma=False
    )
```

```python
import functools
import math

import jax
import jax.numpy as jnp
import numpy as np
from jax import lax
from jax.experimental import pallas as pl
from jax.experimental.pallas import tpu as pltpu
from jax.sharding import PartitionSpec as P

HEADS = 16
GROUPS = 4
HEAD_DIM = 64
FF = 1024


(
    f_qZ, f_qp0, f_qp1, f_qp2, f_qp3, f_qe0, f_qe1, f_qe2, f_qe3, f_qc0, f_qc1, f_qc2, f_qc3,
    f_qz0, f_qz1, f_qz2, f_qz3, f_dZ, f_dp0, f_dp1, f_dp2, f_dp3, f_de0, f_de1, f_de2, f_de3,
    f_dc0, f_dc1, f_dc2, f_dc3, f_dz0, f_dz1, f_dz2, f_dz3, f_gZ, f_gp0, f_gp1, f_gp2, f_gp3,
    f_ge0, f_ge1, f_ge2, f_ge3, f_gc0, f_gc1, f_gc2, f_gc3, f_gz0, f_gz1, f_gz2, f_gz3, f_qs0,
    f_qs1, f_qs2, f_qs3, f_gs0, f_gs1, f_gs2, f_gs3, f_ds0, f_ds1, f_ds2, f_ds3, f_oc0, f_oc1,
    f_oc2, f_oc3, f_oz00, f_oz01, f_oz02, f_oz03, f_oz10, f_oz11, f_oz12, f_oz13, f_oz20, f_oz21,
    f_oz22, f_oz23, f_oz30, f_oz31, f_oz32, f_oz33, f_kc0, f_kc1, f_kc2, f_kc3, f_kz00, f_kz01,
    f_kz02, f_kz03, f_kz10, f_kz11, f_kz12, f_kz13, f_kz20, f_kz21, f_kz22, f_kz23, f_kz30,
    f_kz31, f_kz32, f_kz33, f_kP, f_kZ, f_ke, f_kD, f_A, f_norm, f_trig, f_turn, f_keys, f_query,
    f_kve, f_kvc, f_unpack, f_mix, f_res, f_norm2, f_turn2, f_gate, f_act, f_y, f_oP, f_oZ, f_oe,
    f_oD,
) = range(127)

(
    b_df, b_da0, b_da1, b_da2, b_da3, b_db0, b_db1, b_db2, b_db3, b_dd0, b_dd1, b_dd2, b_dd3,
    b_dx0, b_dx1, b_dx2, b_dx3, b_dz0, b_dz1, b_dz2, b_dz3, b_gf, b_ga0, b_ga1, b_ga2, b_ga3,
    b_gb0, b_gb1, b_gb2, b_gb3, b_gd0, b_gd1, b_gd2, b_gd3, b_gx0, b_gx1, b_gx2, b_gx3, b_gz0,
    b_gz1, b_gz2, b_gz3, b_qf, b_qa0, b_qa1, b_qa2, b_qa3, b_qb0, b_qb1, b_qb2, b_qb3, b_qd0,
    b_qd1, b_qd2, b_qd3, b_qx0, b_qx1, b_qx2, b_qx3, b_qz0, b_qz1, b_qz2, b_qz3, b_rf, b_ra0,
    b_ra1, b_ra2, b_ra3, b_rb0, b_rb1, b_rb2, b_rb3, b_rd0, b_rd1, b_rd2, b_rd3, b_rx0, b_rx1,
    b_rx2, b_rx3, b_rz0, b_rz1, b_rz2, b_rz3, b_dw0, b_dw1, b_dw2, b_dw3, b_gw0, b_gw1, b_gw2,
    b_gw3, b_ow0, b_ow1, b_ow2, b_ow3, b_qw0, b_qw1, b_qw2, b_qw3, b_rw0, b_rw1, b_rw2, b_rw3,
    b_oa0, b_oa1, b_oa2, b_oa3, b_oo0, b_oo1, b_oo2, b_oo3, b_hs0, b_hs1, b_hs2, b_he0, b_he1,
    b_he2, b_oz00, b_oz01, b_oz02, b_oz03, b_oz10, b_oz11, b_oz12, b_oz13, b_oz20, b_oz21, b_oz22,
    b_oz23, b_ka0, b_ka1, b_ka2, b_ka3, b_ko0, b_ko1, b_ko2, b_ko3, b_kz00, b_kz01, b_kz02,
    b_kz03, b_kz10, b_kz11, b_kz12, b_kz13, b_kz20, b_kz21, b_kz22, b_kz23, b_kS, b_ke, b_kf, b_H,
    b_B, b_Q, b_G, b_h, b_nb, b_m, b_att, b_kvs, b_kvc, b_kve, b_kvf, b_oS, b_oe, b_of, b_lm,
    b_ll, b_qs, b_qe, b_qk, b_g, b_nb2, b_rs, b_re,
) = range(177)

FORWARD_ORDER = [
    f_kP, f_qZ, f_qp0, f_oP, f_norm, f_oZ, f_qz1, f_qp1, f_qe0, f_qz2, f_trig, f_oz10, f_dZ,
    f_qp2, f_oz20, f_qz3, f_qe1, f_qp3, f_turn, f_gZ, f_qe2, f_ke, f_kZ, f_qc0, f_qe3, f_oe,
    f_qc1, f_qs0, f_gp0, f_qc2, f_qc3, f_qs1, f_qs2, f_oD, f_gz1, f_dz1, f_qs3, f_keys, f_dz2,
    f_dp2, f_gz2, f_dp1, f_kve, f_gp1, f_gz3, f_kz11, f_query, f_de1, f_gp2, f_dz3, f_oz12,
    f_kz10, f_oz11, f_oz13, f_kvc, f_dp0, f_oz22, f_kz12, f_ge0, f_kD, f_gp3, f_unpack, f_oz23,
    *[f_A] * 5, f_kz22, *[f_A] * 2, f_oz21, *[f_A] * 3, f_ge2, f_oc1, f_ge1, f_A, f_oz30,
    *[f_A] * 5, f_kz20, f_gc0, *[f_A] * 2, f_oz31, f_A, f_de2, *[f_A] * 3, f_oc2, f_dp3, f_oz32,
    *[f_A] * 6, f_oz33, f_oc3, f_dc1, *[f_A] * 2, f_kz13, f_ge3, f_kc1, f_gc2, f_kz32, *[f_A] * 2,
    f_gc1, f_de0, f_dc2, f_kz30, f_res, f_kz21, f_de3, f_mix, f_kz23, f_gc3, f_norm2, f_kz33,
    f_gs0, f_dc0, f_gs1, f_kz31, f_kc3, f_gs2, f_dc3, f_kc2, f_turn2, f_ds0, f_gs3, f_ds1, f_ds2,
    f_ds3, f_gate, f_act, f_y,
]

BACKWARD_ORDER = [
    b_dw0, b_ka0, b_gw0, b_gw1, b_dw1, b_ga0, b_dw2, b_gb0, b_dw3, b_da1, b_h, *[b_H] * 2, b_kz00,
    b_da0, *[b_H] * 3, b_kz03, b_H, b_ka1, b_da2, *[b_H] * 2, b_nb, b_gw2, b_gw3, b_ga3, b_kz02,
    b_db1, b_lm, b_ka2, b_m, b_att, b_ll, b_ow0, b_ga1, b_ga2, b_dd0, b_oa0, b_kz12, b_kz13,
    *[b_B] * 2, b_ow1, b_oa1, b_B, b_gd0, b_B, b_kz22, *[b_B] * 3, b_db0, b_gd2, b_oz00, b_oz01,
    b_B, b_kz10, b_B, b_ow2, b_gb2, b_gd3, b_kz20, b_gx0, b_gb1, b_oa2, b_B, b_gd1, *[b_B] * 3,
    b_gb3, b_ow3, b_oz02, b_kz01, b_oa3, *[b_B] * 3, b_kz11, b_dx0, b_kvs, b_Q, b_dd1, b_oz12,
    b_oz11, b_db2, b_oz22, b_oz10, b_Q, b_db3, b_dd2, b_Q, b_oz03, b_da3, b_gx1, *[b_Q] * 3,
    b_kz21, b_oz13, b_gx2, b_ko0, b_kvc, b_dx1, b_ko2, b_oz21, b_dz0, *[b_Q] * 2, b_qs, b_kve,
    b_qe, b_kz23, b_qw0, b_qw1, b_qw2, b_dz1, b_qb2, b_qa0, b_qa1, b_oz23, b_qb1, b_qw3, b_qa2,
    b_gz0, b_kvf, b_qb0, b_qk, b_rw0, b_rw1, b_ra0, b_rw2, b_ra2, b_rb2, b_rb0, b_dx2, b_g, b_ka3,
    b_dd3, b_oz20, b_gz1, b_qd1, b_ra1, *[b_G] * 2, b_oo3, b_rw3, b_G, b_rb1, *[b_G] * 2, b_gz2,
    b_qd0, *[b_G] * 2, b_rd0, b_G, b_ko1, b_qd2, b_ko3, b_rb3, b_rd2, b_ra3, b_nb2, b_oo0, b_rd1,
    b_kS, b_dz2, b_qa3, b_qx0, b_hs0, b_qz0, b_he0, b_qx2, b_rx0, b_rz0, b_hs1, b_oo2, b_oo1,
    b_qx1, b_oS, b_qz1, b_ke, b_rx1, b_rz1, b_qz2, b_he1, b_rx2, b_rz2, b_hs2, b_gf, b_oe, b_rd3,
    b_he2, b_qd3, b_df, b_rs, b_qb3, b_qf, b_re, b_rf, b_kf, b_of,
]


f32 = jnp.float32
bf16 = jnp.bfloat16
MESH = pl.DeviceIdType.MESH
NZ = 4
EPS = 1e-06


class Place:
    def __init__(self):
        self.z = lax.axis_index("dp")
        spot = lax.axis_index("ctx")
        self.core = spot % 2
        self.x = (spot // 2) % 2
        self.y = spot // 4

    def at(self, z=None, y=None, x=None, core=None):
        z = self.z if z is None else z
        y = self.y if y is None else y
        x = self.x if x is None else x
        core = self.core if core is None else core
        return (z, y * 4 + x * 2 + core)

    def xn(self):
        return self.at(x=1 - self.x)

    def yn(self):
        return self.at(y=1 - self.y)

    def sn(self):
        return self.at(core=1 - self.core)

    def up(self):
        return self.at(z=self.z + 1)

    def down(self):
        return self.at(z=self.z - 1)


def barrier(pc):
    bar = pltpu.get_barrier_semaphore()

    def greet(device):
        pl.semaphore_signal(bar, inc=1, device_id=device, device_id_type=MESH)

    for device in (pc.xn(), pc.yn(), pc.sn()):
        greet(device)

    @pl.when(pc.z < NZ - 1)
    def _():
        greet(pc.up())

    @pl.when(pc.z > 0)
    def _():
        greet(pc.down())

    pl.semaphore_wait(bar, 3 + (1 - pc.z // (NZ - 1)) + (pc.z + NZ - 1) // NZ)


def far(z, i):
    m = z // 2
    zz = z + m * (3 - 2 * z)
    lo = 3 - i if i < 2 else (1 - zz if i == 2 else zz)
    return lo + m * (3 - 2 * lo)


def near(z, i):
    return far(z, NZ - 1 - i)


def remote(src, dst, dev, send, recv):
    return pltpu.make_async_remote_copy(
        src_ref=src, dst_ref=dst, send_sem=send, recv_sem=recv, device_id=dev, device_id_type=MESH
    )


def halves(rows):
    return pl.ds(0, rows // 2), pl.ds(rows // 2, rows // 2)


def cuts(shape, some=None):
    rows, columns = shape[-2:]
    if some is None:
        return (pl.ds(0, rows),), tuple((h,) for h in halves(rows))
    return (some,), tuple((some, h) for h in halves(columns))


KZ, KX, KY, KD0, KD1, KS, KU = range(7)


class Gather:
    def __init__(self, pc, buf, send, recv, some=None):
        self.pc, self.buf, self.send, self.recv = pc, buf, send, recv
        self.full, self.h = cuts(buf.shape, some)

    def cp(self, idx, dev, ks, kr, slot):
        ref = self.buf.at[idx]
        return remote(ref, ref, dev, self.send.at[ks, slot], self.recv.at[kr, slot])

    def c_up(self, z0):
        p = self.pc
        return self.cp((z0, p.y, p.x, p.core, *self.full), p.up(), KU, KZ, z0)

    def c_down(self, z0):
        p = self.pc
        return self.cp((z0, p.y, p.x, p.core, *self.full), p.down(), KZ, KZ, z0)

    def c_x(self, z0):
        p = self.pc
        return self.cp((z0, p.y, p.x, p.core, *self.full), p.xn(), KX, KX, z0)

    def c_y(self, z0):
        p = self.pc
        return self.cp((z0, p.y, p.x, p.core, *self.full), p.yn(), KY, KY, z0)

    def c_d0(self, z0):
        p = self.pc
        return self.cp((z0, p.y, 1 - p.x, p.core, *self.h[0]), p.yn(), KD0, KD0, z0)

    def c_d1(self, z0):
        p = self.pc
        return self.cp((z0, 1 - p.y, p.x, p.core, *self.h[1]), p.xn(), KD1, KD1, z0)

    def c_s(self, z0):
        p = self.pc
        return self.cp((z0, slice(None), slice(None), p.core, *self.full), p.sn(), KS, KS, z0)

    def plane_send(self, i):
        z0 = near(self.pc.z, i)
        self.c_x(z0).start()
        self.c_y(z0).start()

    def own_z(self):
        z = self.pc.z

        @pl.when(z < NZ - 1)
        def _():
            self.c_up(z).start()

        @pl.when(z > 0)
        def _():
            self.c_down(z).start()

    def z_event(self, i, plane=True):
        z = self.pc.z
        z0 = near(z, i)

        @pl.when(z0 < z)
        def _():
            self.c_up(z0).wait_recv()

            @pl.when(z < NZ - 1)
            def _():
                self.c_up(z0).start()

        @pl.when(z0 > z)
        def _():
            self.c_down(z0).wait_recv()

            @pl.when(z > 0)
            def _():
                self.c_down(z0).start()

        if plane:
            self.plane_send(i)

    def plane_event(self, i):
        z0 = near(self.pc.z, i)
        self.c_x(z0).wait_recv()
        self.c_d0(z0).start()
        self.c_y(z0).wait_recv()
        self.c_d1(z0).start()

    def core_event(self, i):
        z0 = near(self.pc.z, i)
        self.c_d0(z0).wait_recv()
        self.c_d1(z0).wait_recv()
        self.c_s(z0).start()

    def done_event(self, i):
        self.c_s(near(self.pc.z, i)).wait_recv()

    def finish(self):
        z = self.pc.z
        for z0 in range(NZ):
            for c in (self.c_x, self.c_y, self.c_d0, self.c_d1, self.c_s):
                c(z0).wait_send()

            @pl.when((z < NZ - 1) & (z0 <= z))
            def _():
                self.c_up(z0).wait_send()

            @pl.when((z > 0) & (z0 >= z))
            def _():
                self.c_down(z0).wait_send()


class GatherPlane:
    def __init__(self, pc, buf, send, recv, some=None):
        self.pc, self.buf, self.send, self.recv = pc, buf, send, recv
        self.full, self.h = cuts(buf.shape, some)

    def cp(self, idx, dev, s, r):
        ref = self.buf.at[idx]
        return remote(ref, ref, dev, self.send.at[s], self.recv.at[r])

    def yx(self, k):
        p = self.pc
        return (p.y if k < 2 else 1 - p.y), (p.x if k % 2 == 0 else 1 - p.x)

    def c_x(self):
        p = self.pc
        return self.cp((p.z, p.y, p.x, p.core, *self.full), p.xn(), (KX, 0), (KX, 0))

    def c_y(self):
        p = self.pc
        return self.cp((p.z, p.y, p.x, p.core, *self.full), p.yn(), (KY, 0), (KY, 0))

    def c_d0(self):
        p = self.pc
        return self.cp((p.z, p.y, 1 - p.x, p.core, *self.h[0]), p.yn(), (KD0, 0), (KD0, 0))

    def c_d1(self):
        p = self.pc
        return self.cp((p.z, 1 - p.y, p.x, p.core, *self.h[1]), p.xn(), (KD1, 0), (KD1, 0))

    def c_up(self, z0, k):
        p = self.pc
        y, x = self.yx(k)
        return self.cp((z0, y, x, p.core, *self.full), p.up(), (10 + z0, k), (10 + z0, k))

    def c_down(self, z0, k):
        p = self.pc
        y, x = self.yx(k)
        return self.cp((z0, y, x, p.core, *self.full), p.down(), (14 + z0, k), (10 + z0, k))

    def c_s(self, z0):
        p = self.pc
        return self.cp((z0, slice(None), slice(None), p.core, *self.full), p.sn(), (KS, z0), (KS, z0))

    def z_send(self, k):
        z = self.pc.z

        @pl.when(z < NZ - 1)
        def _():
            self.c_up(z, k).start()

        @pl.when(z > 0)
        def _():
            self.c_down(z, k).start()

    def own_plane(self):
        self.c_x().start()
        self.c_y().start()

    def own_z(self):
        self.z_send(0)

    def plane_event(self):
        self.c_x().wait_recv()
        self.c_d0().start()
        self.z_send(1)
        self.c_y().wait_recv()
        self.c_d1().start()
        self.z_send(2)

    def diag_event(self):
        self.c_d0().wait_recv()
        self.c_d1().wait_recv()
        self.z_send(3)
        self.c_s(self.pc.z).start()

    def z_event(self, i, k):
        z = self.pc.z
        z0 = near(z, i)

        @pl.when(z0 < z)
        def _():
            self.c_up(z0, k).wait_recv()

            @pl.when(z < NZ - 1)
            def _():
                self.c_up(z0, k).start()

        @pl.when(z0 > z)
        def _():
            self.c_down(z0, k).wait_recv()

            @pl.when(z > 0)
            def _():
                self.c_down(z0, k).start()

    def core_event(self, i):
        self.c_s(near(self.pc.z, i)).start()

    def done_event(self, i):
        self.c_s(near(self.pc.z, i)).wait_recv()

    def finish(self):
        z = self.pc.z
        for c in (self.c_x, self.c_y, self.c_d0, self.c_d1):
            c().wait_send()
        for z0 in range(NZ):
            self.c_s(z0).wait_send()
            for k in range(4):

                @pl.when((z < NZ - 1) & (z0 <= z))
                def _():
                    self.c_up(z0, k).wait_send()

                @pl.when((z > 0) & (z0 >= z))
                def _():
                    self.c_down(z0, k).wait_send()


class GatherSequence:
    def __init__(self, pc, buf, send, recv):
        self.pc, self.buf, self.send, self.recv = pc, buf, send, recv
        rows = buf.shape[-2]
        self.h = (pl.ds(0, 128), pl.ds(128, rows - 128))

    def cp(self, idx, dev, k):
        ref = self.buf.at[idx]
        return remote(ref, ref, dev, self.send.at[k], self.recv.at[k])

    def c_x(self):
        p = self.pc
        return self.cp((p.y, p.x, p.core), p.xn(), 0)

    def c_y(self):
        p = self.pc
        return self.cp((p.y, p.x, p.core), p.yn(), 1)

    def c_d0(self):
        p = self.pc
        return self.cp((p.y, 1 - p.x, p.core, self.h[0]), p.yn(), 2)

    def c_d1(self):
        p = self.pc
        return self.cp((1 - p.y, p.x, p.core, self.h[1]), p.xn(), 3)

    def c_s(self, k):
        p = self.pc
        y, x = (p.y if k < 2 else 1 - p.y), (p.x if k % 2 == 0 else 1 - p.x)
        return self.cp((y, x, p.core), p.sn(), 4 + k)

    def own(self):
        for c in (self.c_x(), self.c_y(), self.c_s(0)):
            c.start()

    def plane_event(self):
        self.c_x().wait_recv()
        self.c_d0().start()
        self.c_s(1).start()
        self.c_y().wait_recv()
        self.c_d1().start()
        self.c_s(2).start()

    def core_event(self):
        self.c_d0().wait_recv()
        self.c_d1().wait_recv()
        self.c_s(3).start()

    def done_event(self):
        for k in range(4):
            self.c_s(k).wait_recv()

    def finish(self):
        for c in (self.c_x(), self.c_y(), self.c_d0(), self.c_d1()):
            c.wait_send()
        for k in range(4):
            self.c_s(k).wait_send()


LOG2E = math.log2(math.e)
VMEM = pltpu.VMEM


def dot(a, b):
    return jnp.dot(a, b, preferred_element_type=f32)


def dot_t(a, b):
    return lax.dot_general(a, b, (((1,), (1,)), ((), ())), preferred_element_type=f32)


def lanes(shape):
    return lax.broadcasted_iota(jnp.int32, shape, 1)


def roll_half(v):
    return pltpu.roll(v, 64, 1)


def swap_rot(v):
    first = lanes(v.shape) % 64 < 32
    return jnp.where(first, pltpu.roll(v, 96, 1), pltpu.roll(v, 32, 1))


def head_sums(v):
    row = lax.broadcasted_iota(jnp.int32, (128, 128), 0) // 64
    col = lax.broadcasted_iota(jnp.int32, (128, 128), 1) // 64
    ones = jnp.where(row == col, 1.0, 0.0).astype(bf16)
    high = v.astype(bf16)
    low = (v - high.astype(f32)).astype(bf16)
    return dot(high, ones) + dot(low, ones)


def twice(gain):
    return jnp.concatenate([gain[...], gain[...]], axis=1)


def cols(i, width):
    return pl.ds(pl.multiple_of(i * width, width), width)


def norm_into(src, gain, dst):
    def body(i, _):
        rows = pl.ds(pl.multiple_of(i * 32, 32), 32)
        v = src[rows, :].astype(f32)
        scale = lax.rsqrt(jnp.mean(v * v, axis=-1, keepdims=True) + EPS)
        dst[rows, :] = (v * scale * gain[...]).astype(dst.dtype)
        return 0

    lax.fori_loop(0, src.shape[0] // 32, body, 0)


def run_steps(order, steps, loops):
    order = list(order)
    while order:
        name = order.pop(0)
        if name not in loops:
            steps[name]()
            continue
        count, body = loops[name]
        ticks, seen = {}, 1
        while seen < count:
            inner = order.pop(0)
            if inner == name:
                seen += 1
            else:
                ticks.setdefault(seen - 1, []).append(inner)

        def tick(i, _, body=body, ticks=ticks):
            body(i)
            for k, inner in ticks.items():

                @pl.when(i == k)
                def _(inner=inner):
                    for step in inner:
                        steps[step]()

            return 0

        lax.fori_loop(0, count, tick, 0)


def line_steps(first, g):
    part = functools.partial
    steps = {first: g.own_z}
    for i in range(NZ):
        steps[first + 1 + i] = part(g.plane_send, i)
        steps[first + 5 + i] = part(g.plane_event, i)
        steps[first + 9 + i] = part(g.core_event, i)
        if i:
            steps[first + 13 + i] = part(g.z_event, i, False)
    return steps


def turn(src, rows, core, mine, theirs):
    def body(t, _):
        v = jnp.transpose(src[:, cols(t, 128)])
        for k in range(64 // rows):
            a, b = v[2 * k * rows : (2 * k + 1) * rows], v[(2 * k + 1) * rows : (2 * k + 2) * rows]
            own, other = jnp.where(core == 0, a, b), jnp.where(core == 0, b, a)
            spot = t * (64 // rows) + k
            mine[spot, :, pl.ds(0, v.shape[1])] = own
            theirs[spot, pl.ds(0, rows), :] = other
        return 0

    lax.fori_loop(0, src.shape[1] // 128, body, 0)


def forward_kernel(dims, *refs):
    (tok, width, n_dev, heads_w, kv_w, ff) = dims
    (
        x_ref, cot_ref, place_ref, freq_ref, g_attn, one_q, one_k, g_ffn,
        s_qkv, s_out, s_down, s_gu,
        o_y, o_tattn, o_tmix, o_tffn, o_tact, o_cot, o_ggu, o_kv, o_q2, o_linv, o_mixf, o_res,
        o_kk, o_va, o_mask, o_wqkv, o_wout, o_wgu, o_cos, o_sin,
        w_qkv, w_out, w_down, w_gu, kk, va, mask, mask_t, o2, gu, gact,
        y_ref, hattn_ref, qkv_ref, q2_ref, kvb, linv_ref, mixf_ref, mixb_ref, res_ref, hffn_ref,
        act_ref, cot2, ggu2, cos_ref, sin_ref, t_attn, t_mix, t_ffn, t_act, turn_a, turn_b,
        send, recv, kv_send, kv_recv, lsem, osem, ex_send, ex_recv,
    ) = refs
    pc = Place()
    shards = (s_qkv, s_out, s_down, s_gu)
    bufs = (w_qkv, w_out, w_down, w_gu)
    local = [
        pltpu.make_async_copy(s, b.at[pc.z, pc.y, pc.x, pc.core], lsem.at[k])
        for k, (s, b) in enumerate(zip(shards, bufs))
    ]
    for c in local:
        c.start()
    barrier(pc)
    for c in local:
        c.wait()
    qkv = Gather(pc, w_qkv, send.at[0], recv.at[0])
    out = GatherPlane(pc, w_out, send.at[1], recv.at[1])
    half = s_down.shape[0] // 2
    down = Gather(pc, w_down, send.at[2], recv.at[2], pl.ds(0, half))
    rest = GatherPlane(pc, w_down, send.at[4], recv.at[4], pl.ds(half, half))
    gateup = Gather(pc, w_gu, send.at[3], recv.at[3])
    seq = GatherSequence(pc, kvb, kv_send, kv_recv)
    part = functools.partial
    z = pc.z
    emitted = []

    def emit(src, dst):
        c = pltpu.make_async_copy(src, dst, osem.at[len(emitted)])
        emitted.append(c)
        c.start()

    def exchange(k, src, dst):
        return remote(src, dst, pc.sn(), ex_send.at[k], ex_recv.at[k])

    back = pl.ds(tok, tok)
    sent_cot = exchange(0, cot_ref, cot2.at[back, :])
    sent_attn = exchange(1, turn_a, t_attn.at[:, :, back])
    sent_mix = exchange(2, turn_b.at[:, pl.ds(0, s_out.shape[0]), :], t_mix.at[:, :, back])
    sent_ffn = exchange(3, turn_a, t_ffn.at[:, :, back])
    sent_act = exchange(4, turn_b.at[:, pl.ds(0, s_down.shape[0]), :], t_act.at[:, :, back])
    sent_ggu = exchange(5, ggu2.at[pl.ds(0, tok), :], ggu2.at[back, :])

    g_q, g_k = twice(one_q), twice(one_k)

    def block_row(a):
        return jnp.right_shift(place_ref[:, a * (tok // 2) : (a + 1) * (tok // 2)], 7).astype(f32)

    def tables():
        step = tok // 2
        sign = jnp.where(lanes((step, 128)) % 64 < 32, -1.0, 1.0)
        row = lax.broadcasted_iota(jnp.int32, (step, 128), 0).astype(f32)
        for a in range(2):
            angle = (block_row(a) * 128.0 + row) * freq_ref[...]
            cos_ref[pl.ds(a * step, step), :] = jnp.cos(angle)
            sin_ref[pl.ds(a * step, step), :] = sign * jnp.sin(angle)
        emit(cos_ref, o_cos)
        emit(sin_ref, o_sin)

    def first_norm():
        norm_into(x_ref, g_attn, hattn_ref)

    def first_turn():
        sent_cot.start()
        cot2[pl.ds(0, tok), :] = cot_ref[...]
        turn(hattn_ref, s_qkv.shape[0], pc.core, t_attn, turn_a)
        sent_attn.start()

    def columns_step(g, i, left, right, total, depth):
        g.done_event(i)
        z0 = near(z, i)

        def body(n, _):
            c = cols(n, 256)
            w = right[z0, :, :, :, :, c].reshape(depth, 256)
            prod = dot(left[:, cols(z0, depth)], w)
            if i == 0:
                total[:, c] = prod
            else:
                total[:, c] += prod
            return 0

        lax.fori_loop(0, total.shape[1] // 256, body, 0)

    def grad_act_step(i):
        down.done_event(i)
        rest.done_event(i)
        z0 = near(z, i)
        depth = ff // NZ
        gact[:, cols(z0, depth)] = dot_t(cot_ref[...], w_down[z0].reshape(depth, width))

    low = lanes((tok, 128)) < 64

    def head_tile(t, gain):
        u = qkv_ref[:, cols(t, 128)]
        n = u * lax.rsqrt(head_sums(u * u) * (1.0 / 64) + EPS) * gain
        return n * cos_ref[...] + swap_rot(n) * sin_ref[...]

    def keys_out():
        for t in range(kv_w // 128):
            kvb[pc.y, pc.x, pc.core, pl.ds(0, tok), pl.ds(t * 128, 128)] = head_tile(
                heads_w // 128 + t, g_k
            ).astype(bf16)
        kvb[pc.y, pc.x, pc.core, pl.ds(0, tok), pl.ds(kv_w, kv_w)] = qkv_ref[
            :, pl.ds(heads_w + kv_w, kv_w)
        ].astype(bf16)
        both_rows = jnp.concatenate([block_row(0), block_row(1)], axis=1)
        blocks_row = jnp.broadcast_to(both_rows, (16, tok)).astype(bf16)
        kvb[pc.y, pc.x, pc.core, pl.ds(tok, 16), pl.ds(0, tok)] = blocks_row
        kvb[pc.y, pc.x, pc.core, pl.ds(tok, 16), pl.ds(tok, tok)] = blocks_row
        seq.own()

    def query_tile(t, _):
        q = (head_tile(t, g_q) * 0.125).astype(bf16)
        zero = jnp.zeros_like(q)
        q2_ref[t, pl.ds(0, tok), :] = jnp.where(low, q, zero)
        q2_ref[t, pl.ds(tok, tok), :] = jnp.where(low, zero, q)
        return 0

    def queries():
        lax.fori_loop(0, heads_w // 128, query_tile, 0)
        emit(qkv_ref, o_kv)
        emit(q2_ref, o_q2)
        emit(w_qkv, o_wqkv)
        sent_cot.wait_recv()
        emit(cot2, o_cot)
        sent_attn.wait_recv()
        emit(t_attn, o_tattn)

    def unpack(b, _):
        y, x, c = b // 4, (b // 2) % 2, b % 2
        rows = pl.ds(pl.multiple_of(b * tok, tok), tok)
        for t in range(kv_w // 128):
            k = kvb[y, x, c, pl.ds(0, tok), pl.ds(t * 128, 128)].astype(f32)
            v = kvb[y, x, c, pl.ds(0, tok), pl.ds(kv_w + t * 128, 128)].astype(f32)
            k_r, v_r = roll_half(k), roll_half(v)
            kk[2 * t, rows, :] = jnp.where(low, k, k_r).astype(bf16)
            kk[2 * t + 1, rows, :] = jnp.where(low, k_r, k).astype(bf16)
            va[2 * t, rows, :] = jnp.where(low, v, 1.0).astype(bf16)
            va[2 * t + 1, rows, :] = jnp.where(low, v_r, 1.0).astype(bf16)
        step = tok // 2
        key_hi = kvb[y, x, c, pl.ds(tok, 16), pl.ds(0, tok)].astype(f32)[:1, :]
        for a in range(2):
            own = block_row(a)
            row = lax.broadcasted_iota(jnp.int32, (step, step), 0).astype(f32)
            col = lanes((step, step)).astype(f32)
            for d in range(2):
                theirs = key_hi[:, d * step : (d + 1) * step]
                gap = (own - theirs) * float(step) + row - col
                place = pl.ds(pl.multiple_of(b * tok + d * step, step), step)
                mask[pl.ds(a * step, step), place] = jnp.where(gap >= 0, 1.0, 0.0).astype(bf16)
                gap = (own - theirs) * float(step) + col - row
                mask_t[place, pl.ds(a * step, step)] = jnp.where(gap >= 0, 1.0, 0.0).astype(bf16)
        return 0

    def unpack_all():
        seq.done_event()
        lax.fori_loop(0, n_dev, unpack, 0)
        emit(kk, o_kk)
        emit(va, o_va)
        emit(mask_t, o_mask)

    chunk = 512
    n_chunk = n_dev * tok // chunk

    def attend(tick):
        t, kc = tick // n_chunk, tick % n_chunk
        g = t // 2
        rows = pl.ds(pl.multiple_of(kc * chunk, chunk), chunk)
        s = dot_t(q2_ref[t], kk[g, rows, :])
        e = jnp.exp2(s * LOG2E).astype(bf16).reshape(2, tok, chunk) * mask[:, rows][None]
        o = dot(e.reshape(2 * tok, chunk), va[g, rows, :])

        @pl.when(kc == 0)
        def _():
            o2[...] = o

        @pl.when(kc > 0)
        def _():
            o2[...] += o

        @pl.when(kc == n_chunk - 1)
        def _():
            even, odd = o2[pl.ds(0, tok), :], o2[pl.ds(tok, tok), :]
            total = jnp.where(low, roll_half(even), odd)
            inv = 1.0 / total
            mixed = jnp.where(low, even, roll_half(odd)) * inv
            linv_ref[:, cols(t, 128)] = inv
            mixf_ref[:, cols(t, 128)] = mixed
            mixb_ref[:, cols(t, 128)] = mixed.astype(bf16)

    def mix_out():
        emit(linv_ref, o_linv)
        emit(mixf_ref, o_mixf)
        turn(mixb_ref, s_out.shape[0], pc.core, t_mix, turn_b)
        sent_mix.start()

    def residual_step(n, _):
        c = cols(n, 256)
        w = w_out[:, :, :, :, :, c].reshape(heads_w, 256)
        res_ref[:, c] = x_ref[:, c].astype(f32) + dot(mixb_ref[...], w)
        return 0

    def residual():
        for i in range(NZ):
            out.done_event(i)
        emit(w_out, o_wout)
        lax.fori_loop(0, width // 256, residual_step, 0)

    def second_norm():
        norm_into(res_ref, g_ffn, hffn_ref)

    def second_turn():
        emit(res_ref, o_res)
        sent_mix.wait_recv()
        emit(t_mix, o_tmix)
        sent_attn.wait_send()
        turn(hffn_ref, s_gu.shape[0], pc.core, t_ffn, turn_a)
        sent_ffn.start()

    def gate_step(n, _):
        c = cols(n, 256)
        c2 = cols(n + ff // 256, 256)
        gate, up, grad = gu[:, c], gu[:, c2], gact[:, c]
        sig = 1.0 / (1.0 + jnp.exp(-gate))
        silu = gate * sig
        act_ref[:, c] = (silu * up).astype(bf16)
        ggu2[pl.ds(0, tok), c] = (grad * up * (sig * (1.0 + gate * (1.0 - sig)))).astype(bf16)
        ggu2[pl.ds(0, tok), c2] = (grad * silu).astype(bf16)
        return 0

    def gates():
        lax.fori_loop(0, ff // 256, gate_step, 0)
        sent_ggu.start()
        emit(w_gu, o_wgu)

    def act_out():
        sent_mix.wait_send()
        turn(act_ref, s_down.shape[0], pc.core, t_act, turn_b)
        sent_act.start()
        sent_ffn.wait_recv()
        emit(t_ffn, o_tffn)

    def output_step(n, _):
        c = cols(n, 256)
        w = w_down[:, :, :, :, :, c].reshape(ff, 256)
        y_ref[:, c] = (res_ref[:, c] + dot(act_ref[...], w)).astype(bf16)
        return 0

    def outputs():
        lax.fori_loop(0, width // 256, output_step, 0)
        emit(y_ref, o_y)
        sent_ggu.wait_recv()
        emit(ggu2, o_ggu)
        sent_act.wait_recv()
        emit(t_act, o_tact)

    steps = {
        f_norm: first_norm, f_trig: tables, f_turn: first_turn, f_keys: keys_out, f_query: queries,
        f_kve: seq.plane_event, f_kvc: seq.core_event, f_unpack: unpack_all, f_mix: mix_out,
        f_res: residual, f_norm2: second_norm, f_turn2: second_turn, f_gate: gates,
        f_act: act_out, f_y: outputs, f_oP: out.own_plane, f_oZ: out.own_z, f_oe: out.plane_event,
        f_oD: out.diag_event, f_kP: rest.own_plane, f_kZ: rest.own_z, f_ke: rest.plane_event,
        f_kD: rest.diag_event,
    }
    for first, g in ((f_qZ, qkv), (f_dZ, down), (f_gZ, gateup)):
        steps.update(line_steps(first, g))
    for i in range(NZ):
        steps[f_qs0 + i] = part(columns_step, qkv, i, hattn_ref, w_qkv, qkv_ref, width // NZ)
        steps[f_gs0 + i] = part(columns_step, gateup, i, hffn_ref, w_gu, gu, width // NZ)
        steps[f_ds0 + i] = part(grad_act_step, i)
        if i:
            steps[f_oc0 + i] = part(out.core_event, i)
            steps[f_kc0 + i] = part(rest.core_event, i)
            for k in range(4):
                steps[f_oz00 + 4 * i + k] = part(out.z_event, i, k)
                steps[f_kz00 + 4 * i + k] = part(rest.z_event, i, k)
    run_steps(FORWARD_ORDER, steps, {f_A: (heads_w // 128 * n_chunk, attend)})
    for g in (qkv, out, down, rest, gateup, seq):
        g.finish()
    for c in (sent_cot, sent_ffn, sent_act, sent_ggu):
        c.wait_send()
    for c in emitted:
        c.wait()


def forward(x, cot, places, frequency, g_attn, g_q, g_k, g_ffn, s_qkv, s_out, s_down, s_gu, n_dev):
    tok, width = x.shape
    heads_w, kv_w = HEADS * HEAD_DIM, GROUPS * HEAD_DIM
    ff = s_down.shape[0] * n_dev * NZ
    length = n_dev * tok
    tiles = heads_w // 128
    shape = jax.ShapeDtypeStruct
    seven = [(NZ, 2, 2, 2) + s.shape for s in (s_qkv, s_out, s_down, s_gu)]
    qkv_rows, out_rows, down_rows, gu_rows = [s.shape[0] for s in (s_qkv, s_out, s_down, s_gu)]
    spots = n_dev * NZ // 2
    kv_buf = ((2, 2, 2, tok + 16, 2 * kv_w), bf16)
    turned = [((spots, r, 2 * tok), bf16) for r in (qkv_rows, out_rows, gu_rows, down_rows)]
    keep = [
        ((tok, width), bf16),
        *turned,
        ((2 * tok, width), bf16),
        ((2 * tok, 2 * ff), bf16),
        ((tok, s_qkv.shape[1]), f32),
        ((tiles, 2 * tok, 128), bf16),
        ((tok, heads_w), f32),
        ((tok, heads_w), f32),
        ((tok, width), f32),
        ((GROUPS, length, 128), bf16),
        ((GROUPS, length, 128), bf16),
        ((length, tok), bf16),
        (seven[0], bf16),
        (seven[1], bf16),
        (seven[3], bf16),
        ((tok, 128), f32),
        ((tok, 128), f32),
    ]
    outs = [shape(*k) for k in keep]
    vm = pl.BlockSpec(memory_space=VMEM)
    anyw = pl.BlockSpec(memory_space=pl.ANY)
    dma = pltpu.SemaphoreType.DMA
    flops = 2 * tok * (width * (s_qkv.shape[1] + heads_w + 2 * ff + 2 * ff) + 2 * heads_w * length)
    return pl.pallas_call(
        functools.partial(forward_kernel, (tok, width, n_dev, heads_w, kv_w, ff)),
        out_shape=outs,
        in_specs=[vm] * 8 + [anyw] * 4,
        out_specs=[anyw] * len(outs),
        scratch_shapes=[VMEM(s, bf16) for s in seven]
        + [
            VMEM((GROUPS, length, 128), bf16),
            VMEM((GROUPS, length, 128), bf16),
            VMEM((tok, length), bf16),
            VMEM((length, tok), bf16),
            VMEM((2 * tok, 128), f32),
            VMEM((tok, 2 * ff), f32),
            VMEM((tok, ff), f32),
            VMEM((tok, width), bf16),
            VMEM((tok, width), bf16),
            VMEM((tok, s_qkv.shape[1]), f32),
            VMEM((tiles, 2 * tok, 128), bf16),
            VMEM(*kv_buf),
            VMEM((tok, heads_w), f32),
            VMEM((tok, heads_w), f32),
            VMEM((tok, heads_w), bf16),
            VMEM((tok, width), f32),
            VMEM((tok, width), bf16),
            VMEM((tok, ff), bf16),
            VMEM((2 * tok, width), bf16),
            VMEM((2 * tok, 2 * ff), bf16),
            VMEM((tok, 128), f32),
            VMEM((tok, 128), f32),
            *[VMEM(*t) for t in turned],
            VMEM((spots, qkv_rows, tok), bf16),
            VMEM((spots, out_rows, tok), bf16),
            dma((5, 18, NZ)),
            dma((5, 14, NZ)),
            dma((8,)),
            dma((8,)),
            dma((4,)),
            dma((len(outs),)),
            dma((6,)),
            dma((6,)),
        ],
        compiler_params=pltpu.CompilerParams(
            collective_id=0, has_side_effects=True, vmem_limit_bytes=60 << 20
        ),
        cost_estimate=pl.CostEstimate(flops=flops, bytes_accessed=50 << 20, transcendentals=0),
        name="forward",
    )(x, cot, places, frequency, g_attn, g_q, g_k, g_ffn, s_qkv, s_out, s_down, s_gu)


SD0, SD1, SX0, SX1, SY0, SY1, SA, SB = range(8)


class PlaneSum:
    def plane_setup(self, pc, rd, rx, ry, send, recv):
        self.pc, self.rd, self.rx, self.ry, self.send, self.recv = pc, rd, rx, ry, send, recv

    def cp(self, src, dst, dev, k, s):
        return remote(src, dst, dev, self.send.at[k, s], self.recv.at[k, s])

    def d0(self, s):
        p = self.pc
        return self.cp(self.piece(s, 1 - p.y, 1 - p.x, 0), self.rd.at[s, 0], p.yn(), SD0, s)

    def d1(self, s):
        p = self.pc
        return self.cp(self.piece(s, 1 - p.y, 1 - p.x, 1), self.rd.at[s, 1], p.xn(), SD1, s)

    def x1(self, s):
        p = self.pc
        return self.cp(self.piece(s, p.y, 1 - p.x, 1), self.rx.at[s, 1], p.xn(), SX1, s)

    def y0(self, s):
        p = self.pc
        return self.cp(self.piece(s, 1 - p.y, p.x, 0), self.ry.at[s, 0], p.yn(), SY0, s)

    def x0(self, s):
        return self.cp(self.rd.at[s, 0], self.rx.at[s, 0], self.pc.xn(), SX0, s)

    def y1(self, s):
        return self.cp(self.rd.at[s, 1], self.ry.at[s, 1], self.pc.yn(), SY1, s)

    def plane_far(self, s):
        self.d0(s).start()
        self.d1(s).start()

    def plane_near(self, s):
        self.x1(s).start()
        self.y0(s).start()

    def plane_first(self, s):
        self.plane_far(s)
        self.plane_near(s)

    def plane_second(self, s):
        p = self.pc
        self.d0(s).wait_recv()
        self.rd[s, 0] = self.rd[s, 0] + self.piece(s, p.y, 1 - p.x, 0)[...]
        self.x0(s).start()
        self.d1(s).wait_recv()
        self.rd[s, 1] = self.rd[s, 1] + self.piece(s, 1 - p.y, p.x, 1)[...]
        self.y1(s).start()

    def plane_arrived(self, s):
        for c in (self.x1, self.y0, self.x0, self.y1):
            c(s).wait_recv()

    def plane_total(self, s, k):
        p = self.pc
        own = self.piece(s, p.y, p.x, k)[...].astype(f32)
        return own + self.rx[s, k].astype(f32) + self.ry[s, k].astype(f32)

    def plane_finish(self, s):
        for c in (self.d0, self.d1, self.x1, self.y0, self.x0, self.y1):
            c(s).wait_send()


class Scatter(PlaneSum):
    def __init__(self, pc, part, bufs, out, send, recv, some=None):
        rd, rx, ry, self.zz = bufs
        self.plane_setup(pc, rd, rx, ry, send, recv)
        self.part, self.out = part, out
        self.full, self.h = cuts(part.shape, some)

    @staticmethod
    def scratch(rows, columns, wide=True):
        shape = (2, rows // 2, columns) if wide else (2, rows, columns // 2)
        half = VMEM((NZ, *shape), bf16)
        return [half, half, half, VMEM((NZ + 1, *shape), bf16)]

    def piece(self, s, y, x, k):
        return self.part.at[(s, y, x, *self.h[k])]

    def down(self, zp):
        return self.cp(self.rx.at[zp], self.zz.at[zp], self.pc.down(), SA, zp)

    def up(self, zp):
        gap = zp - (self.pc.z + 1)
        spot = zp + (1 - (gap + NZ - 1) // NZ) * (NZ - zp)
        return self.cp(self.rx.at[zp], self.zz.at[spot], self.pc.up(), SB, zp)

    def far_event(self, i):
        self.plane_far(far(self.pc.z, i))

    def near_event(self, i):
        self.plane_near(far(self.pc.z, i))

    def d_event(self, i):
        self.plane_second(far(self.pc.z, i))

    def xy_event(self, i):
        zp = far(self.pc.z, i)
        self.plane_arrived(zp)
        for k in range(2):
            self.rx[zp, k] = self.plane_total(zp, k).astype(bf16)

    def z_event(self, i):
        z = self.pc.z
        zp = far(z, i)

        @pl.when(zp < z)
        def _():
            @pl.when(z < NZ - 1)
            def _():
                self.down(zp).wait_recv()
                self.rx[zp] = self.rx[zp] + self.zz[zp]

            self.down(zp).start()

        @pl.when(zp > z)
        def _():
            @pl.when(z > 0)
            def _():
                self.up(zp).wait_recv()
                self.rx[zp] = self.rx[zp] + self.zz[zp]

            self.up(zp).start()

    def final(self):
        z = self.pc.z
        self.plane_arrived(z)
        for k in range(2):
            self.out[self.h[k]] = self.plane_total(z, k)

        @pl.when(z < NZ - 1)
        def _():
            self.down(z).wait_recv()
            for k in range(2):
                self.out[self.h[k]] += self.zz[z, k].astype(f32)

        @pl.when(z > 0)
        def _():
            self.up(z).wait_recv()
            for k in range(2):
                self.out[self.h[k]] += self.zz[NZ, k].astype(f32)

    def finish(self):
        z = self.pc.z
        for zp in range(NZ):
            self.plane_finish(zp)

            @pl.when(zp < z)
            def _():
                self.down(zp).wait_send()

            @pl.when(zp > z)
            def _():
                self.up(zp).wait_send()


class ScatterZ(PlaneSum):
    def __init__(self, pc, part, bufs, out, send, recv, some=None):
        rd, rx, ry, self.zz, self.sm = bufs
        wide = some is None
        whole = pl.ds(0, self.sm.shape[-2])
        axis = self.sm.shape[-2 if wide else -1]
        self.inner = [(h,) if wide else (whole, h) for h in halves(axis)]
        self.plane_setup(pc, rd, rx, ry, send, recv)
        self.part, self.out = part, out
        self.full, self.h = cuts(part.shape, some)

    @staticmethod
    def scratch(rows, columns, wide=True):
        half = VMEM((1, 2, rows // 2, columns) if wide else (1, 2, rows, columns // 2), bf16)
        return [half, half, half, VMEM((NZ + 1, 4, rows, columns), bf16), VMEM((4, rows, columns), bf16)]

    def piece(self, s, y, x, k):
        return self.sm.at[(y * 2 + x, *self.inner[k])]

    def down(self, zp, k, src):
        return self.cp(src, self.zz.at[zp, k], self.pc.down(), 8 + zp, k)

    def up(self, zp, k, src):
        gap = zp - (self.pc.z + 1)
        spot = zp + (1 - (gap + NZ - 1) // NZ) * (NZ - zp)
        return self.cp(src, self.zz.at[spot, k], self.pc.up(), 12 + zp, k)

    def first(self, i):
        z = self.pc.z
        zp = far(z, i)
        for k in range(4):
            src = self.part.at[(zp, k // 2, k % 2, *self.full)]

            @pl.when((z == NZ - 1) & (zp < z))
            def _():
                self.down(zp, k, src).start()

            @pl.when((z == 0) & (zp > z))
            def _():
                self.up(zp, k, src).start()

    def z_event(self, i, k):
        z = self.pc.z
        zp = far(z, i)
        held = self.zz.at[zp, k]

        @pl.when((zp < z) & (z < NZ - 1))
        def _():
            self.down(zp, k, held).wait_recv()
            self.zz[zp, k] = self.zz[zp, k] + self.part[(zp, k // 2, k % 2, *self.full)]
            self.down(zp, k, held).start()

        @pl.when((zp > z) & (z > 0))
        def _():
            self.up(zp, k, held).wait_recv()
            self.zz[zp, k] = self.zz[zp, k] + self.part[(zp, k // 2, k % 2, *self.full)]
            self.up(zp, k, held).start()

    def own_event(self, k):
        z = self.pc.z

        @pl.when(z < NZ - 1)
        def _():
            self.down(z, k, self.zz.at[z, k]).wait_recv()

        @pl.when(z > 0)
        def _():
            self.up(z, k, self.zz.at[z, k]).wait_recv()

        own = self.part[(z, k // 2, k % 2, *self.full)].astype(f32)

        @pl.when(z == 0)
        def _():
            self.sm[k] = (own + self.zz[z, k].astype(f32)).astype(bf16)

        @pl.when(z == NZ - 1)
        def _():
            self.sm[k] = (own + self.zz[NZ, k].astype(f32)).astype(bf16)

        @pl.when((z > 0) & (z < NZ - 1))
        def _():
            both = self.zz[z, k].astype(f32) + self.zz[NZ, k].astype(f32)
            self.sm[k] = (own + both).astype(bf16)

    def plane_send(self):
        self.plane_first(0)

    def plane_event(self):
        self.plane_second(0)

    def final(self):
        self.plane_arrived(0)
        for k in range(2):
            self.out[self.h[k]] = self.plane_total(0, k)

    def finish(self):
        z = self.pc.z
        self.plane_finish(0)
        for zp in range(NZ):
            for k in range(4):

                @pl.when(zp < z)
                def _():
                    self.down(zp, k, self.zz.at[zp, k]).wait_send()

                @pl.when(zp > z)
                def _():
                    self.up(zp, k, self.zz.at[zp, k]).wait_send()


class SequenceSum(PlaneSum):
    def __init__(self, pc, terms, bufs, send, recv, core_send, core_recv):
        rd, rx, ry, self.theirs = bufs
        self.plane_setup(pc, rd, rx, ry, send, recv)
        self.terms, self.core_send, self.core_recv = terms, core_send, core_recv
        self.h = halves(terms.shape[-2])

    @staticmethod
    def scratch(rows, columns):
        half = VMEM((1, 2, rows // 2, columns), bf16)
        return [half, half, half, VMEM((2, 2, rows, columns), bf16)]

    def piece(self, s, y, x, k):
        return self.theirs.at[y, x, self.h[k]]

    def swap(self):
        p = self.pc
        return remote(
            self.terms.at[:, :, 1 - p.core], self.theirs, p.sn(), self.core_send, self.core_recv
        )

    def core_event(self):
        p = self.pc
        self.swap().wait_recv()
        for y in range(2):
            for x in range(2):
                self.theirs[y, x] = self.theirs[y, x] + self.terms[y, x, p.core]
        self.plane_first(0)

    def finish(self):
        self.swap().wait_send()
        self.plane_finish(0)


def norm_back(src, gain, grad, part_ref, part_row, emit):
    part_ref[pl.ds(part_row, 1), :] = jnp.zeros((1, part_ref.shape[1]), f32)

    def body(i, _):
        rows = pl.ds(pl.multiple_of(i * 32, 32), 32)
        v, g = src[rows, :].astype(f32), grad[rows, :]
        inv = lax.rsqrt(jnp.mean(v * v, axis=-1, keepdims=True) + EPS)
        unit = v * inv
        part_ref[pl.ds(part_row, 1), :] += jnp.sum(g * unit, axis=0, keepdims=True)
        gg = g * gain[...]
        emit(rows, inv * (gg - unit * jnp.mean(gg * unit, axis=-1, keepdims=True)))
        return 0

    lax.fori_loop(0, grad.shape[0] // 32, body, 0)


def sum_steps(first, g):
    part = functools.partial
    steps = {first: g.final}
    for i in range(NZ):
        steps[first + 1 + i] = part(g.far_event, i)
        steps[first + 5 + i] = part(g.near_event, i)
        steps[first + 9 + i] = part(g.d_event, i)
        if i < NZ - 1:
            steps[first + 13 + i] = part(g.xy_event, i)
            steps[first + 17 + i] = part(g.z_event, i)
    return steps


def weight_grad(left, zp, right, part, first=0):
    rows, columns = part.shape[-2:]
    lhs = left[pl.ds(zp * 4, 4)].reshape(4 * rows, left.shape[-1])
    step = 512

    def body(n, _):
        c = cols(n, step)
        grad = dot(lhs, right[:, cols(n + first // step, step)])
        part[zp, :, :, :, c] = grad.astype(bf16).reshape(2, 2, rows, step)
        return 0

    lax.fori_loop(0, columns // step, body, 0)


LOADS = [
    "act", "cot", "ffn", "ggu", "wgu", "res", "mix", "mixf", "linv", "q2", "kk", "va", "mask",
    "qkv", "wout", "attn", "wqkv", "x",
]


def backward_kernel(dims, *refs):
    (tok, width, n_dev, heads_w, kv_w, ff) = dims
    (
        cos_ref, sin_ref, g_attn, one_q, one_k, g_ffn,
        i_x, i_tattn, i_tmix, i_tffn, i_tact, i_cot, i_ggu, i_qkv, i_q2, i_linv, i_mixf, i_res,
        i_kk, i_va, i_mask, i_wqkv, i_wout, i_wgu,
        o_dx, o_attn, o_q, o_k, o_ffn, out_wqkv, out_wout, out_wgu, out_wdown,
        t_ffn, t_act, cot2, ggu2, qkv, q2, linv, kk, va, mask_t, w_gu,
        part_q, part_kv, part_out, part_gu, part_down, res, gains, came, gh, gattn2, acc_q,
        aug, gm, terms,
        send, recv, kv_send, kv_recv, ex_send, ex_recv, g_send, g_recv, lsem,
    ) = refs[:67]
    bufs = refs[67:]
    g_q, g_k = twice(one_q), twice(one_k)
    pc = Place()
    z = pc.z
    part = functools.partial
    loads = {}

    def load(name, src, dst):
        def copy():
            return pltpu.make_async_copy(src(), dst(), lsem.at[LOADS.index(name)])

        loads[name] = lambda: copy().wait()
        copy().start()

    load("act", lambda: i_tact, lambda: t_act)
    load("cot", lambda: i_cot, lambda: cot2)
    load("ffn", lambda: i_tffn, lambda: t_ffn)
    load("ggu", lambda: i_ggu, lambda: ggu2)
    load("wgu", lambda: i_wgu, lambda: w_gu)
    load("res", lambda: i_res, lambda: res)
    load("linv", lambda: i_linv, lambda: linv)
    load("q2", lambda: i_q2, lambda: q2)
    load("kk", lambda: i_kk, lambda: kk)
    load("va", lambda: i_va, lambda: va)
    load("mask", lambda: i_mask, lambda: mask_t)
    load("qkv", lambda: i_qkv, lambda: qkv)
    bar = pltpu.get_barrier_semaphore()
    for device in (pc.xn(), pc.yn(), pc.sn()):
        pl.semaphore_signal(bar, inc=1, device_id=device, device_id_type=MESH)
    for k in range(1, NZ):
        there = pc.at(z=(z + k) % NZ)
        pl.semaphore_signal(bar, inc=1, device_id=there, device_id_type=MESH)
    pl.semaphore_wait(bar, 3 + NZ - 1)
    cut = part_down.shape[-2] // 2
    down = Scatter(pc, part_down, bufs[0:4], out_wdown, send.at[0], recv.at[0], pl.ds(0, cut))
    rest = ScatterZ(pc, part_down, bufs[21:26], out_wdown, send.at[4], recv.at[4], pl.ds(cut, cut))
    gateup = Scatter(pc, part_gu, bufs[4:8], out_wgu, send.at[1], recv.at[1])
    out = ScatterZ(pc, part_out, bufs[8:13], out_wout, send.at[2], recv.at[2])
    out_q, out_kv = out_wqkv.at[:, pl.ds(0, heads_w)], out_wqkv.at[:, pl.ds(heads_w, 2 * kv_w)]
    last = Scatter(pc, part_q, bufs[17:21], out_q, send.at[3], recv.at[3])
    last_kv = Scatter(pc, part_kv, bufs[26:30], out_kv, send.at[5], recv.at[5])
    seq = SequenceSum(pc, terms, bufs[13:17], kv_send, kv_recv, ex_send.at[2], ex_recv.at[2])

    own = pl.ds(0, tok)
    back = pl.ds(tok, tok)

    def rows_of(left, right, term, names, i, first=0):
        for name in names:
            if name in loads:
                loads.pop(name)()
        weight_grad(left, far(z, i), right, term, first)

    def h_step(n):
        w = w_gu[n // 2, n % 2].reshape(width // 8, 2 * ff)
        gh[:, cols(n, width // 8)] = dot_t(ggu2[own, :], w)

    def start_h():
        loads.pop("wgu")()
        loads.pop("res")()

    def keep_residual(rows, grad):
        total = cot2[rows, :].astype(f32) + grad
        res[rows, :] = total
        gattn2[rows, :] = total.astype(bf16)

    sent_attn = remote(gattn2.at[own, :], gattn2.at[back, :], pc.sn(), ex_send.at[0], ex_recv.at[0])

    def residual_back():
        load("wout", lambda: i_wout, lambda: w_gu.at[:, :, :, :, pl.ds(0, part_out.shape[-2]), :])
        gains[...] = jnp.zeros_like(gains)
        norm_back(res, g_ffn, gh, gains, 1, keep_residual)
        load("mixf", lambda: i_mixf, lambda: gh.at[:, pl.ds(heads_w, heads_w)])
        sent_attn.start()
        loads.pop("wout")()

    columns = heads_w + 2 * kv_w
    some = pl.ds(0, columns)

    def load_mix():
        load("mix", lambda: i_tmix, lambda: t_act)

    def load_last():
        load("attn", lambda: i_tattn, lambda: t_ffn)
        load("wqkv", lambda: i_wqkv, lambda: w_gu.at[:, :, :, :, :, some])
        load("x", lambda: i_x, lambda: cot2.at[own, :])

    def m_step(n, _):
        w = w_gu[n, :, :, :, pl.ds(0, part_out.shape[-2]), :].reshape(heads_w // NZ, width)
        gm[:, cols(n, heads_w // NZ)] = dot_t(gattn2[own, :], w).astype(bf16)
        return 0

    def mixed_back():
        lax.fori_loop(0, NZ, m_step, 0)
        sent_attn.wait()

    def start_attention():
        for name in ("mixf", "linv", "q2", "kk", "va", "mask", "qkv"):
            loads.pop(name)()

    low = lanes((tok, 128)) < 64
    chunk = 512
    n_chunk = n_dev * tok // chunk
    def attend(tick):
        g, kc = tick // n_chunk, tick % n_chunk
        rows = pl.ds(pl.multiple_of(kc * chunk, chunk), chunk)

        @pl.when(kc == 0)
        def _():
            lane = lanes((tok, 128))
            for k in range(2):
                c = cols(2 * g + k, 128)
                grad = gm[:, c].astype(f32)
                mixed = gh[:, cols(2 * g + k + heads_w // 128, 128)]
                delta = head_sums(grad * mixed) * linv[:, c]
                grad = grad * linv[:, c]
                for half in range(2):
                    d = roll_half(delta) if half == 0 else delta
                    v = grad if half == 0 else roll_half(grad)
                    high = d.astype(bf16).astype(f32)
                    rest = jnp.where(lane == 64, -high, jnp.where(lane == 65, high - d, 0.0))
                    aug[pl.ds((2 * k + half) * tok, tok), :] = jnp.where(low, v, rest).astype(bf16)

        q = q2[pl.ds(2 * g, 2)].reshape(4 * tok, 128)
        seen = mask_t[rows, :]
        e = jnp.exp2(dot_t(kk[g, rows, :], q) * LOG2E).astype(bf16)
        e = e * jnp.concatenate([seen] * 4, axis=1)
        ds = e * dot_t(va[g, rows, :], aug[...]).astype(bf16)
        dv = dot(e, aug[...])
        dk = dot(ds, q)
        dq = lax.dot_general(kk[g, rows, :], ds, (((0,), (0,)), ((), ())), preferred_element_type=f32)
        dk = dk + roll_half(dk)
        lower = lanes((chunk, 128)) < 64
        dv = jnp.where(lower, dv, roll_half(dv))
        mine = (lanes((chunk, 128)) // 64) == (g % 2)
        for b in range(chunk // tok):
            spot = kc * (chunk // tok) + b
            y, x, c = spot // 4, (spot // 2) % 2, spot % 2
            cut = slice(b * tok, (b + 1) * tok)
            for base, value in ((0, dk), (kv_w, dv)):
                place = pl.ds(pl.multiple_of(base + (g // 2) * 128, 128), 128)
                old = terms[y, x, c, :, place].astype(f32)
                terms[y, x, c, :, place] = jnp.where(mine[cut], value[cut], old).astype(bf16)

        @pl.when(kc == 0)
        def _():
            acc_q[...] = dq

        @pl.when(kc > 0)
        def _():
            acc_q[...] += dq

        @pl.when(kc == n_chunk - 1)
        def _():
            turned = jnp.transpose(acc_q[...])
            for k in range(2):
                even, odd = [turned[(2 * k + h) * tok : (2 * k + h + 1) * tok] for h in range(2)]
                gh[:, cols(2 * g + k, 128)] = jnp.where(low, even, odd) * 0.125

    def head_back(t, grad, gain, row):
        c = cols(t, 128)
        u = qkv[:, c]
        inv = lax.rsqrt(head_sums(u * u) * (1.0 / 64) + EPS)
        unit = u * inv
        grad = grad * cos_ref[...] - swap_rot(grad) * sin_ref[...]
        gains[pl.ds(row, 1), pl.ds(0, 128)] += jnp.sum(grad * unit, axis=0, keepdims=True)
        gg = grad * gain
        gattn2[own, c] = (inv * (gg - unit * head_sums(gg * unit) * (1.0 / 64))).astype(bf16)

    def query_back(t):
        head_back(t, gh[:, cols(t, 128)], g_q, 2)

    def swap_columns(k, c):
        return remote(
            gattn2.at[own, c], gattn2.at[back, c], pc.sn(), ex_send.at[k], ex_recv.at[k]
        )

    sent_q = swap_columns(1, pl.ds(0, heads_w))
    sent_kv = swap_columns(3, pl.ds(heads_w, 2 * kv_w))

    def keys_back():
        seq.plane_arrived(0)
        for k in range(2):
            gh[seq.h[k], pl.ds(0, 2 * kv_w)] = seq.plane_total(0, k)
        for t in range(kv_w // 128):
            head_back(heads_w // 128 + t, gh[:, pl.ds(t * 128, 128)], g_k, 3)
        gattn2[own, pl.ds(heads_w + kv_w, kv_w)] = gh[:, pl.ds(kv_w, kv_w)].astype(bf16)
        sent_kv.start()

    def g_step(n):
        w = w_gu[n // 2, n % 2, :, :, :, some].reshape(width // 8, columns)
        gh[:, cols(n, width // 8)] = dot_t(gattn2[own, some], w)

    def keep_input(rows, grad):
        cot2[pl.ds(rows.start + tok, rows.size), :] = (res[rows, :] + grad).astype(bf16)

    sent_dx = pltpu.make_async_copy(cot2.at[back, :], o_dx, lsem.at[len(LOADS)])

    def input_back():
        loads.pop("x")()
        norm_back(cot2, g_attn, gh, gains, 0, keep_input)
        sent_dx.start()

    def start_g():
        loads.pop("wqkv")()

    def hop(k):
        device = (pc.sn(), pc.xn(), pc.yn())[k]
        return remote(gains, came.at[k], device, g_send.at[k], g_recv.at[k])

    def hop_end(k):
        hop(k).wait()
        gains[...] += came[k]

    def ring(k):
        there = pc.at(z=(z + k) % NZ)
        return remote(gains, came.at[3 + z], there, g_send.at[2 + k], g_recv.at[3 + z])

    def ring_start():
        came[3 + z] = gains[...]
        for k in range(1, NZ):
            ring(k).start()

    def ring_end():
        for k in range(1, NZ):
            there = (z + k) % NZ
            slot = came.at[3 + there]
            remote(gains, slot, pc.at(z=there), g_send.at[2 + k], g_recv.at[3 + there]).wait_recv()
        total = came[3]
        for k in range(1, NZ):
            total = total + came[3 + k]
        o_attn[...] = total[0:1]
        o_ffn[...] = total[1:2]
        for o, row in ((o_q, 2), (o_k, 3)):
            v = total[:, :128]
            o[...] = (v + roll_half(v))[row : row + 1, :64]

    steps = {
        b_h: start_h, b_nb: residual_back, b_m: mixed_back, b_att: start_attention,
        b_kvs: seq.swap().start, b_kvc: seq.core_event, b_kve: part(seq.plane_second, 0),
        b_kvf: keys_back, b_oS: out.plane_send, b_oe: out.plane_event, b_of: out.final, b_kS: rest.plane_send,
        b_ke: rest.plane_event, b_kf: rest.final,
        b_lm: load_mix, b_ll: load_last, b_qs: sent_q.start, b_qe: sent_q.wait_recv, b_qk: sent_kv.wait_recv, b_g: start_g,
        b_nb2: input_back, b_rs: ring_start, b_re: ring_end,
    }
    steps.update(sum_steps(b_qf, last))
    steps.update(sum_steps(b_rf, last_kv))
    steps.update(sum_steps(b_df, down))
    steps.update(sum_steps(b_gf, gateup))
    for i in range(NZ):
        steps[b_dw0 + i] = part(rows_of, t_act, cot2, part_down, ("act", "cot"), i)
        steps[b_gw0 + i] = part(rows_of, t_ffn, ggu2, part_gu, ("ffn", "ggu"), i)
        steps[b_ow0 + i] = part(rows_of, t_act, gattn2, part_out, ("mix",), i)
        steps[b_qw0 + i] = part(rows_of, t_ffn, gattn2, part_q, ("attn",), i)
        steps[b_rw0 + i] = part(rows_of, t_ffn, gattn2, part_kv, ("attn",), i, heads_w)
        steps[b_oa0 + i] = part(out.first, i)
        steps[b_oo0 + i] = part(out.own_event, i)
        steps[b_ka0 + i] = part(rest.first, i)
        steps[b_ko0 + i] = part(rest.own_event, i)
        if i < NZ - 1:
            for k in range(4):
                steps[b_oz00 + 4 * i + k] = part(out.z_event, i, k)
                steps[b_kz00 + 4 * i + k] = part(rest.z_event, i, k)
            steps[b_hs0 + i] = hop(i).start
            steps[b_he0 + i] = part(hop_end, i)
    loops = {
        b_H: (8, h_step),
        b_B: (GROUPS * n_chunk, attend),
        b_Q: (heads_w // 128, query_back),
        b_G: (8, g_step),
    }
    run_steps(BACKWARD_ORDER, steps, loops)
    for g in (down, rest, gateup, out, seq, last, last_kv):
        g.finish()
    sent_q.wait_send()
    sent_kv.wait_send()
    for k in range(1, NZ):
        ring(k).wait_send()
    sent_dx.wait()


def backward(x, g_attn, g_q, g_k, g_ffn, kept, rows, n_dev):
    (t_attn, t_mix, t_ffn, t_act, cot2, ggu2, qkv, q2, linv, mixf, res, kk, va, mask_t, w_qkv, w_out, w_gu, cosine, sine) = kept
    tok, width = x.shape
    heads_w, kv_w = HEADS * HEAD_DIM, GROUPS * HEAD_DIM
    ff = ggu2.shape[1] // 2
    length = n_dev * tok
    columns = qkv.shape[1]
    dims = (tok, width, n_dev, heads_w, kv_w, ff)
    shape = jax.ShapeDtypeStruct
    vm = pl.BlockSpec(memory_space=VMEM)
    anyw = pl.BlockSpec(memory_space=pl.ANY)
    dma = pltpu.SemaphoreType.DMA
    r_qkv, r_out, r_gu, r_down = rows
    partial = [
        VMEM((NZ, 2, 2, r, c), bf16)
        for r, c in ((r_qkv, heads_w), (r_qkv, 2 * kv_w), (r_out, width), (r_gu, width), (r_down, width))
    ]
    like = [
        VMEM(v.shape, v.dtype)
        for v in (t_ffn, t_act, cot2, ggu2, qkv, q2, linv, kk, va, mask_t, w_gu)
    ]
    return pl.pallas_call(
        functools.partial(backward_kernel, dims),
        out_shape=[
            shape((tok, width), bf16),
            shape((1, width), f32),
            shape((1, 64), f32),
            shape((1, 64), f32),
            shape((1, width), f32),
            shape((r_qkv, columns), f32),
            shape((r_out, width), f32),
            shape((r_gu, width), f32),
            shape((r_down, width), f32),
        ],
        in_specs=[vm] * 6 + [anyw] * 18,
        out_specs=[anyw] + [vm] * 8,
        scratch_shapes=like
        + partial
        + [
            VMEM((tok, width), f32),
            VMEM((8, width), f32),
            VMEM((3 + NZ, 8, width), f32),
            VMEM((tok, width), f32),
            VMEM((2 * tok, width), bf16),
            VMEM((128, 4 * tok), f32),
            VMEM((4 * tok, 128), bf16),
            VMEM((tok, heads_w), bf16),
            VMEM((2, 2, 2, tok, 2 * kv_w), bf16),
            dma((6, 16, NZ)),
            dma((6, 16, NZ)),
            dma((8, 1)),
            dma((8, 1)),
            dma((4,)),
            dma((4,)),
            dma((3 + NZ,)),
            dma((3 + NZ,)),
            dma((len(LOADS) + 1,)),
        ]
        + Scatter.scratch(r_down // 2, width, False)
        + Scatter.scratch(r_gu, width)
        + ScatterZ.scratch(r_out, width)
        + SequenceSum.scratch(tok, 2 * kv_w)
        + Scatter.scratch(r_qkv, heads_w)
        + ScatterZ.scratch(r_down // 2, width, False)
        + Scatter.scratch(r_qkv, 2 * kv_w),
        compiler_params=pltpu.CompilerParams(
            collective_id=1, has_side_effects=True, vmem_limit_bytes=64 << 20
        ),
        cost_estimate=pl.CostEstimate(
            flops=20 * tok * width * width, bytes_accessed=60 << 20, transcendentals=0
        ),
        name="backward",
    )(
        cosine, sine, g_attn, g_q, g_k, g_ffn, x, t_attn, t_mix, t_ffn, t_act, cot2, ggu2, qkv, q2,
        linv, mixf, res, kk, va, mask_t, w_qkv, w_out, w_gu,
    )


def settle_kernel(count, *refs):
    copies = [
        pltpu.make_async_copy(a, b, refs[-1].at[k])
        for k, (a, b) in enumerate(zip(refs[:count], refs[count : 2 * count]))
    ]
    for c in copies:
        c.start()
    for c in copies:
        c.wait()


def settle(arrays):
    count = len(arrays)
    anyw = pl.BlockSpec(memory_space=pl.ANY)
    return pl.pallas_call(
        functools.partial(settle_kernel, count),
        out_shape=[jax.ShapeDtypeStruct(a.shape, a.dtype) for a in arrays],
        in_specs=[pl.BlockSpec(memory_space=VMEM)] * count,
        out_specs=[anyw] * count,
        scratch_shapes=[pltpu.SemaphoreType.DMA((count,))],
        name="settle",
    )(*arrays)


epsilon = 1e-06


def norm_rows(values, gain_vec):
    return (
        values * lax.rsqrt(jnp.mean(values * values, axis=-1, keepdims=True) + epsilon) * gain_vec
    )


def rotate(values, positions):
    half_dim = values.shape[-1] // 2
    frequency = jnp.exp(
        jnp.arange(half_dim).astype(jnp.float32) * (-2.0 * math.log(10000.0) / values.shape[-1])
    )
    angles = positions.astype(jnp.float32)[:, None] * frequency[None, :]
    cosine = jnp.cos(angles)[:, None, :]
    sine = jnp.sin(angles)[:, None, :]
    first = values[..., :half_dim]
    second = values[..., half_dim:]
    return jnp.concatenate(
        [first * cosine - second * sine, second * cosine + first * sine], axis=-1
    )


def project_heads(qkv_all, positions, q_gain, k_gain):
    tok_rows = qkv_all.shape[0]
    q_cols = HEADS * HEAD_DIM
    k_cols = GROUPS * HEAD_DIM
    queries = qkv_all[:, :q_cols].reshape(tok_rows, HEADS, HEAD_DIM)
    keys_raw = qkv_all[:, q_cols : q_cols + k_cols].reshape(tok_rows, GROUPS, HEAD_DIM)
    values = qkv_all[:, q_cols + k_cols :].reshape(tok_rows, GROUPS, HEAD_DIM)
    return (
        rotate(norm_rows(queries, q_gain), positions),
        rotate(norm_rows(keys_raw, k_gain), positions),
        values,
    )


def gated(gate_up):
    return jax.nn.silu(gate_up[:, :FF]) * gate_up[:, FF:]


def per_device_plain(
    inputs, places, cotangent, attn_gain, w_qkv, q_gain, k_gain, w_out, ffn_gain, w_gateup, w_down
):
    tok_rows = inputs.shape[1]
    repeat = HEADS // GROUPS
    score_scale = HEAD_DIM ** (-0.5)
    here_f = inputs[0].astype(jnp.float32)
    own_places = places[0]
    qkv_w, out_w = (
        lax.all_gather(w_qkv, ("dp", "ctx"), axis=0, tiled=True),
        lax.all_gather(w_out, ("dp", "ctx"), axis=0, tiled=True),
    )
    h_attn_f, pull_attn = jax.vjp(norm_rows, here_f, attn_gain)
    h_attn = h_attn_f.astype(jnp.bfloat16)
    qkv_all = jnp.dot(h_attn, qkv_w, preferred_element_type=jnp.float32)

    def heads_of(qkv_in, gain_q, gain_k):
        return project_heads(qkv_in, own_places, gain_q, gain_k)

    (queries, keys_f, values), pull_heads = jax.vjp(heads_of, qkv_all, q_gain, k_gain)
    query_b = queries.astype(jnp.bfloat16).reshape(tok_rows, GROUPS, repeat, HEAD_DIM)
    key_b = keys_f.astype(jnp.bfloat16)
    value_b = values.astype(jnp.bfloat16)
    all_keys, all_values = (
        lax.all_gather(key_b, "ctx", axis=0, tiled=True),
        lax.all_gather(value_b, "ctx", axis=0, tiled=True),
    )
    all_places = lax.all_gather(own_places, "ctx", axis=0, tiled=True)
    blocks = lax.axis_size("ctx")
    key_blocks = all_keys.reshape(blocks, tok_rows, GROUPS, HEAD_DIM)
    value_blocks = all_values.reshape(blocks, tok_rows, GROUPS, HEAD_DIM)
    place_blocks = all_places.reshape(blocks, tok_rows)

    def score_block(key_blk, place_blk):
        scores = (
            jnp.einsum("igrd,jgd->grij", query_b, key_blk, preferred_element_type=jnp.float32)
            * score_scale
        )
        allowed = place_blk[None, :] <= own_places[:, None]
        return (scores, allowed)

    def max_step(state_pair, entries):
        row_top, row_total = state_pair
        scores, allowed = score_block(entries[0], entries[1])
        scores = jnp.where(allowed, scores, -1e30)
        new_top = jnp.maximum(row_top, jnp.max(scores, axis=-1))
        row_total = row_total * jnp.exp(row_top - new_top) + jnp.sum(
            jnp.where(allowed, jnp.exp(scores - new_top[..., None]), 0.0), axis=-1
        )
        return ((new_top, row_total), None)

    start_pair = (
        jnp.full((GROUPS, repeat, tok_rows), -1e30, jnp.float32),
        jnp.zeros((GROUPS, repeat, tok_rows), jnp.float32),
    )
    (row_top, row_total), _ = lax.scan(max_step, start_pair, (key_blocks, place_blocks))
    log_total = row_top + jnp.log(row_total)

    def out_step(accum, entries):
        scores, allowed = score_block(entries[0], entries[1])
        weights_b = jnp.where(allowed, jnp.exp(scores - log_total[..., None]), 0.0).astype(
            jnp.bfloat16
        )
        return (
            accum
            + jnp.einsum(
                "grij,jgd->igrd", weights_b, entries[2], preferred_element_type=jnp.float32
            ),
            None,
        )

    mixed_f, _ = lax.scan(
        out_step,
        jnp.zeros((tok_rows, GROUPS, repeat, HEAD_DIM), jnp.float32),
        (key_blocks, place_blocks, value_blocks),
    )
    mixed_b = mixed_f.reshape(tok_rows, HEADS * HEAD_DIM).astype(jnp.bfloat16)
    attn_out = jnp.dot(mixed_b, out_w, preferred_element_type=jnp.float32)
    residual = here_f + attn_out
    gateup_w, down_w = (
        lax.all_gather(w_gateup, ("dp", "ctx"), axis=0, tiled=True),
        lax.all_gather(w_down, ("dp", "ctx"), axis=0, tiled=True),
    )
    h_ffn_f, pull_ffn = jax.vjp(norm_rows, residual, ffn_gain)
    h_ffn = h_ffn_f.astype(jnp.bfloat16)
    gate_up = jnp.dot(h_ffn, gateup_w, preferred_element_type=jnp.float32)
    act_f, pull_gate = jax.vjp(gated, gate_up)
    act_b = act_f.astype(jnp.bfloat16)
    result = residual + jnp.dot(act_b, down_w, preferred_element_type=jnp.float32)
    layer_output = result.astype(jnp.bfloat16)[None]
    gateup_w, down_w = (
        lax.all_gather(w_gateup, ("dp", "ctx"), axis=0, tiled=True),
        lax.all_gather(w_down, ("dp", "ctx"), axis=0, tiled=True),
    )
    grad_out = cotangent[0]
    grad_act = jnp.dot(grad_out, down_w.T, preferred_element_type=jnp.float32)
    grad_down = jnp.dot(act_b.T, grad_out, preferred_element_type=jnp.float32)
    grad_gu_b = pull_gate(grad_act)[0].astype(jnp.bfloat16)
    grad_gateup = jnp.dot(h_ffn.T, grad_gu_b, preferred_element_type=jnp.float32)
    grad_h_ffn = jnp.dot(grad_gu_b, gateup_w.T, preferred_element_type=jnp.float32)
    grad_resid_part, grad_ffn_gain = pull_ffn(grad_h_ffn)
    grad_residual = grad_out.astype(jnp.float32) + grad_resid_part
    grad_gateup_own, grad_down_own = (
        lax.psum_scatter(grad_gateup, ("dp", "ctx"), scatter_dimension=0, tiled=True),
        lax.psum_scatter(grad_down, ("dp", "ctx"), scatter_dimension=0, tiled=True),
    )
    qkv_w, out_w = (
        lax.all_gather(w_qkv, ("dp", "ctx"), axis=0, tiled=True),
        lax.all_gather(w_out, ("dp", "ctx"), axis=0, tiled=True),
    )
    grad_attn_b = grad_residual.astype(jnp.bfloat16)
    grad_out_w = jnp.dot(mixed_b.T, grad_attn_b, preferred_element_type=jnp.float32)
    grad_mixed_b = (
        jnp.dot(grad_attn_b, out_w.T, preferred_element_type=jnp.float32)
        .astype(jnp.bfloat16)
        .reshape(tok_rows, GROUPS, repeat, HEAD_DIM)
    )
    row_delta = jnp.transpose(
        jnp.sum(grad_mixed_b.astype(jnp.float32) * mixed_f, axis=-1), (1, 2, 0)
    )

    def back_step(grad_query, entries):
        key_blk, place_blk, value_blk = entries
        scores, allowed = score_block(key_blk, place_blk)
        weights_f = jnp.where(allowed, jnp.exp(scores - log_total[..., None]), 0.0)
        weights_b = weights_f.astype(jnp.bfloat16)
        grad_value = jnp.einsum(
            "grij,igrd->jgd", weights_b, grad_mixed_b, preferred_element_type=jnp.float32
        )
        grad_prob = jnp.einsum(
            "igrd,jgd->grij", grad_mixed_b, value_blk, preferred_element_type=jnp.float32
        )
        grad_score = (weights_f * (grad_prob - row_delta[..., None])).astype(jnp.bfloat16)
        grad_query = grad_query + jnp.einsum(
            "grij,jgd->igrd", grad_score, key_blk, preferred_element_type=jnp.float32
        )
        grad_key = (
            jnp.einsum("grij,igrd->jgd", grad_score, query_b, preferred_element_type=jnp.float32)
            * score_scale
        )
        return (
            grad_query,
            jnp.concatenate(
                [
                    grad_key.reshape(tok_rows, GROUPS * HEAD_DIM),
                    grad_value.reshape(tok_rows, GROUPS * HEAD_DIM),
                ],
                axis=1,
            ),
        )

    grad_query, kv_terms = lax.scan(
        back_step,
        jnp.zeros((tok_rows, GROUPS, repeat, HEAD_DIM), jnp.float32),
        (key_blocks, place_blocks, value_blocks),
    )
    grad_query = grad_query * score_scale
    kv_own = lax.psum_scatter(
        kv_terms.reshape(blocks * tok_rows, 2 * GROUPS * HEAD_DIM).astype(jnp.bfloat16),
        "ctx",
        scatter_dimension=0,
        tiled=True,
    ).astype(jnp.float32)
    grad_key_own = kv_own[:, : GROUPS * HEAD_DIM].reshape(tok_rows, GROUPS, HEAD_DIM)
    grad_value_own = kv_own[:, GROUPS * HEAD_DIM :].reshape(tok_rows, GROUPS, HEAD_DIM)
    grad_qkv_f, grad_q_gain, grad_k_gain = pull_heads(
        (grad_query.reshape(tok_rows, HEADS, HEAD_DIM), grad_key_own, grad_value_own)
    )
    grad_qkv_b = grad_qkv_f.astype(jnp.bfloat16)
    grad_qkv_w = jnp.dot(h_attn.T, grad_qkv_b, preferred_element_type=jnp.float32)
    grad_h_attn = jnp.dot(grad_qkv_b, qkv_w.T, preferred_element_type=jnp.float32)
    grad_here_part, grad_attn_gain = pull_attn(grad_h_attn)
    grad_inputs = (grad_residual + grad_here_part).astype(jnp.bfloat16)[None]
    grad_qkv_own, grad_out_own = (
        lax.psum_scatter(grad_qkv_w, ("dp", "ctx"), scatter_dimension=0, tiled=True),
        lax.psum_scatter(grad_out_w, ("dp", "ctx"), scatter_dimension=0, tiled=True),
    )
    gain_attn, gain_query, gain_key, gain_ffn = lax.psum(
        (grad_attn_gain, grad_q_gain, grad_k_gain, grad_ffn_gain), ("dp", "ctx")
    )
    return (
        layer_output,
        grad_inputs,
        gain_attn,
        grad_qkv_own,
        gain_query,
        gain_key,
        grad_out_own,
        gain_ffn,
        grad_gateup_own,
        grad_down_own,
    )


def per_device_fast(
    inputs, places, cotangent, attn_gain, w_qkv, q_gain, k_gain, w_out, ffn_gain, w_gateup, w_down
):
    n_dev = lax.axis_size("ctx")
    half = HEAD_DIM // 2
    spot = np.arange(128) % half
    step = np.float32(-2.0 * math.log(10000.0) / HEAD_DIM)
    frequency = np.exp(spot.astype(np.float32) * step).astype(np.float32)[None]
    gain_q, gain_k = q_gain[None], k_gain[None]
    layer_output, *kept = forward(
        inputs[0], cotangent[0], places, frequency, attn_gain[None], gain_q, gain_k,
        ffn_gain[None], w_qkv, w_out, w_down, w_gateup, n_dev,
    )
    rows = [w.shape[0] for w in (w_qkv, w_out, w_gateup, w_down)]
    grads = backward(inputs[0], attn_gain[None], gain_q, gain_k, ffn_gain[None], kept, rows, n_dev)
    layer_output, dx, g_attn, g_q, g_k, g_ffn, d_qkv, d_out, d_gu, d_down = settle(
        [layer_output, *grads]
    )
    return (
        layer_output[None], dx[None], g_attn[0], d_qkv, g_q[0], g_k[0], d_out, g_ffn[0], d_gu, d_down
    )


def solution(mesh):
    in_specs = (
        P("dp", "ctx", None),
        P("dp", "ctx"),
        P("dp", "ctx", None),
        P(),
        P(("dp", "ctx"), None),
        P(),
        P(),
        P(("dp", "ctx"), None),
        P(),
        P(("dp", "ctx"), None),
        P(("dp", "ctx"), None),
    )
    out_specs = (
        P("dp", "ctx", None),
        P("dp", "ctx", None),
        P(),
        P(("dp", "ctx"), None),
        P(),
        P(),
        P(("dp", "ctx"), None),
        P(),
        P(("dp", "ctx"), None),
        P(("dp", "ctx"), None),
    )
    fast = dict(mesh.shape) == {"dp": 4, "ctx": 8}
    per_device = per_device_fast if fast else per_device_plain
    return jax.shard_map(
        per_device, mesh=mesh, in_specs=in_specs, out_specs=out_specs, check_vma=False
    )
```
